32 devices in a mesh: seq: 8 (over y, x, core), rows: 4 (over z).
Axes of the slice: x: 2, y: 2, z: 4, core: 2. Of those that a mesh axis runs over, the one named last changes fastest.
Arguments:
- tokens: bfloat16 [8, 512, 2048], P('rows', 'seq'), may hold values from -6 to 6
- doc_starts: int32 [8, 4], P('rows'), may hold values from 0 to 511, as said below
- grad_out: bfloat16 [8, 512, 2048], P('rows', 'seq'), may hold values from -6 to 6
- qkv_master: float32 [2048, 3072], P(('seq', 'rows')), may hold values from -0.125 to 0.125
- out_master: float32 [2048, 2048], P(('seq', 'rows')), may hold values from -0.75 to 0.75
- gate_up_master: float32 [2048, 16384], P(('seq', 'rows')), may hold values from -0.125 to 0.125
- down_master: float32 [8192, 2048], P(('seq', 'rows')), may hold values from -0.0625 to 0.0625
- gains: float32 [4224], replicated, may hold values from 0.3 to 2.4
- qkv_rows: float32 [2048], P(('seq', 'rows')), may hold values from 1146 to 9216
- out_rows: float32 [2048], P(('seq', 'rows')), may hold values from 17 to 144
- gate_up_rows: float32 [2048], P(('seq', 'rows')), may hold values from 34 to 278
- down_rows: float32 [8192], P(('seq', 'rows')), may hold values from 139 to 1105
- col_moments: float32 [23552], replicated, may hold values from 34 to 9216
- gain_moments: float32 [4224], replicated, may hold values from 204 to 143360
Outputs:
- output: bfloat16 [8, 512, 2048], P('rows', 'seq')
- grad_tokens: bfloat16 [8, 512, 2048], P('rows', 'seq')
- grad_qkv: float32 [2048, 3072], P(('seq', 'rows'))
- grad_out_proj: float32 [2048, 2048], P(('seq', 'rows'))
- grad_gate_up: float32 [2048, 16384], P(('seq', 'rows'))
- grad_down: float32 [8192, 2048], P(('seq', 'rows'))
- grad_gains: float32 [4224], replicated
- qkv_rows_new: float32 [2048], P(('seq', 'rows'))
- out_rows_new: float32 [2048], P(('seq', 'rows'))
- gate_up_rows_new: float32 [2048], P(('seq', 'rows'))
- down_rows_new: float32 [8192], P(('seq', 'rows'))
- col_moments_new: float32 [23552], replicated
- gain_moments_new: float32 [4224], replicated
- qkv_new: float32 [2048, 3072], P(('seq', 'rows'))
- out_new: float32 [2048, 2048], P(('seq', 'rows'))
- gate_up_new: float32 [2048, 16384], P(('seq', 'rows'))
- down_new: float32 [8192, 2048], P(('seq', 'rows'))
- qkv_copy: bfloat16 [2048, 3072], P(('seq', 'rows'))
- out_copy: bfloat16 [2048, 2048], P(('seq', 'rows'))
- gate_up_copy: bfloat16 [2048, 16384], P(('seq', 'rows'))
- down_copy: bfloat16 [8192, 2048], P(('seq', 'rows'))
- gains_new: float32 [4224], replicated
- update_rms: float32 [8], replicated
The draws below stay inside these ranges and needn't reach their ends.
Inputs may be any that keep to these rules, and one draw needn't show every extreme that they name: `doc_starts`: each row's first entry is 0 and its entries rise strictly. In each aligned block of 2 rows (the rows of one device) one row, which one drawn from the seed, has its first document running from position 0 into the last 64 positions.
All inputs are finite; a program needn't handle non-finite values.
Results may differ from the reference program's by a relative error of at most 0.018.
Values may be sent and summed in bfloat16 or wider, within the bound.
A program may use at most 512 MiB of HBM per device.

```python
import math
import jax
import jax.numpy as jnp
from jax import lax

D = 2048
HEADS = 32
KV_HEADS = 8
HEAD_DIM = 64
FF = 8192
SEQ_DEV = 64
ROWS_DEV = 2
DOCS = 4
STEP = 10
LENGTH = 512
ROWS = 8
TOKENS = 4096
ATT = 2048
QKV = 3072
COLS = 23552
GAINS = 4224


def draw_doc_starts(key, part):
    key = jax.random.fold_in(key, 5)
    pick_key, rows_key, tail_key = jax.random.split(key, 3)
    chosen = jax.random.randint(pick_key, (ROWS // ROWS_DEV,), 0, ROWS_DEV)
    row_ids = jnp.arange(ROWS, dtype=jnp.int32)
    is_long = row_ids % ROWS_DEV == chosen[row_ids // ROWS_DEV]

    def spread_cuts(row_key):
        return jnp.sort(jax.random.permutation(row_key, LENGTH - 1)[:DOCS - 1] + 1)

    def tail_cuts(row_key):
        return jnp.sort(jax.random.permutation(row_key, SEQ_DEV - 1)[:DOCS - 1] + 1 + LENGTH - SEQ_DEV)
    spread = jax.vmap(spread_cuts)(jax.random.split(rows_key, ROWS)).astype(jnp.int32)
    tails = jax.vmap(tail_cuts)(jax.random.split(tail_key, ROWS)).astype(jnp.int32)
    cuts = jnp.where(is_long[:, None], tails, spread)
    return jnp.concatenate([jnp.zeros((ROWS, 1), jnp.int32), cuts], axis=1)


def draw_gains(key, part):
    key = jax.random.fold_in(key, 11)
    noise_key, head_key = jax.random.split(key)
    ramp = jnp.arange(D, dtype=jnp.float32) / (D - 1)
    bottom, height = (0.6, 1.2)
    noise = 1.0 + 0.05 * jnp.clip(jax.random.normal(noise_key, (2, D), jnp.float32), -3.0, 3.0)
    wide = (bottom + height * ramp)[None, :] * noise
    heads = jax.random.uniform(head_key, (2 * HEAD_DIM,), jnp.float32, 0.7, 1.3)
    return jnp.concatenate([wide[0], wide[1], heads])


def draw_gain_moments(key, part):
    key = jax.random.fold_in(key, 17)
    levels = jnp.concatenate([jnp.full((D,), 3.2, jnp.float32), jnp.full((D,), 0.72, jnp.float32), jnp.full((2 * HEAD_DIM,), 46.0, jnp.float32)])
    factor = jnp.exp(jax.random.uniform(key, (GAINS,), jnp.float32, jnp.log(0.094), jnp.log(0.75)))
    return levels * factor * TOKENS


def steps_of(own_key, extent, shards, smallest, top_value):
    level, own = 1.0, jax.random.fold_in(own_key, 6)
    for dim, shards_of in shards:
        draws = jnp.exp(jax.random.uniform(jax.random.fold_in(own, dim), (shards_of,), jnp.float32, smallest / len(shards), top_value / len(shards)))
        level = level * jnp.repeat(draws, extent[dim] // shards_of).reshape([-1 if axis == dim else 1 for axis in range(len(extent))])
    return level


def centred(key, dims, scale, reach, cuts=(), kind=jnp.bfloat16):
    factor_of = steps_of(key, dims, cuts, -0.22, 0.18) if cuts else 1.0
    array = jax.random.normal(key, dims, jnp.float32) * scale * factor_of
    return jnp.minimum(jnp.maximum(array, -reach), reach).astype(kind)


def setup_inputs(seed: int = 0) -> dict:
    seeds = jax.random.split(jax.random.key(seed), 15)
    return {
        "tokens": centred(seeds[0], (ROWS, LENGTH, D), 1.0, 6.0, ((0, 4), (1, 8))),
        "doc_starts": draw_doc_starts(jax.random.fold_in(seeds[14], 71), 0),
        "grad_out": centred(seeds[2], (ROWS, LENGTH, D), 1.0, 6.0, ((0, 4), (1, 8))),
        "qkv_master": centred(seeds[3], (D, QKV), D ** -0.5, 0.125, ((0, 32),), jnp.float32),
        "out_master": centred(seeds[4], (ATT, D), (max(D * DOCS * 4 // LENGTH, 1)) ** -0.5, 0.75, ((0, 32),), jnp.float32),
        "gate_up_master": centred(seeds[5], (D, 2 * FF), D ** -0.5, 0.125, ((0, 32),), jnp.float32),
        "down_master": centred(seeds[6], (FF, D), FF ** -0.5, 0.0625, ((0, 32),), jnp.float32),
        "gains": draw_gains(jax.random.fold_in(seeds[14], 71), 0),
        "qkv_rows": jnp.clip(jnp.exp(math.log(9216.0) - 2.0846635 * jax.random.uniform(seeds[8], (D,), jnp.float32) ** steps_of(seeds[8], (D,), ((0, 32),), -0.2, 0.2)), 1146.0, 9216.0),
        "out_rows": jnp.clip(jnp.exp(math.log(144.0) - 2.1366 * jax.random.uniform(seeds[9], (ATT,), jnp.float32) ** steps_of(seeds[9], (ATT,), ((0, 32),), -0.2, 0.2)), 17.0, 144.0),
        "gate_up_rows": jnp.clip(jnp.exp(math.log(278.0) - 2.1012606 * jax.random.uniform(seeds[10], (D,), jnp.float32) ** steps_of(seeds[10], (D,), ((0, 32),), -0.2, 0.2)), 34.0, 278.0),
        "down_rows": jnp.clip(jnp.exp(math.log(1105.0) - 2.0731267 * jax.random.uniform(seeds[11], (FF,), jnp.float32) ** steps_of(seeds[11], (FF,), ((0, 32),), -0.2, 0.2)), 139.0, 1105.0),
        "col_moments": jnp.clip(jnp.exp(jax.random.uniform(seeds[12], (COLS,), jnp.float32, math.log(34.0), math.log(9216.0))), 34.0, 9216.0),
        "gain_moments": draw_gain_moments(jax.random.fold_in(seeds[14], 71), 0),
    }


EPSILON = 1e-06
ROPE_BASE = 10000.0
MASKED_SCORE = -1e+30
STEP_RATE = 0.3
CLIP_LEVEL = 1.0
SQUARE_EPSILON = 1e-30
SCALE_EPSILON = 0.001
PRECISE = lax.Precision.HIGHEST

@jax.custom_vjp
def low(v):
    return lax.optimization_barrier(v.astype(jnp.bfloat16)).astype(jnp.float32)

@jax.custom_vjp
def low_back(v):
    return v

def low_keep(v):
    return (low(v), None)

def low_pass(kept, grad):
    return (grad,)

def back_keep(v):
    return (v, None)

def back_low(kept, grad):
    return (low(grad),)
low.defvjp(low_keep, low_pass)
low_back.defvjp(back_keep, back_low)

def norm_rows(entries, gain):
    return entries * lax.rsqrt(lax.optimization_barrier(jnp.mean(entries * entries, axis=-1, keepdims=True)) + EPSILON) * gain

def turn(entries, cos_wide, sin_wide):
    half_width = entries.shape[-1] // 2
    turned = jnp.concatenate([-entries[..., half_width:], entries[..., :half_width]], axis=-1)
    return entries * cos_wide + turned * sin_wide

def doc_tables(doc_starts, places):
    before = doc_starts[:, None, :] <= places[None, :, None]
    doc_ids = lax.optimization_barrier(jnp.sum(before.astype(jnp.int32), axis=-1))
    doc_first = lax.optimization_barrier(jnp.max(jnp.where(before, doc_starts[:, None, :], 0), axis=-1))
    return (doc_ids, places[None, :] - doc_first)

def rotary(offsets):
    frequency = ROPE_BASE ** (-(jnp.arange(HEAD_DIM // 2, dtype=jnp.float32) * 2.0 / HEAD_DIM))
    angles = offsets.astype(jnp.float32)[..., None] * frequency
    cos_table = jnp.concatenate([jnp.cos(angles), jnp.cos(angles)], axis=-1)
    sin_table = jnp.concatenate([jnp.sin(angles), jnp.sin(angles)], axis=-1)
    return (cos_table, sin_table)

def queries_keys(cos_table, sin_table, projected, gain_query, gain_key):
    rows_here, seq_here = (projected.shape[0], projected.shape[1])
    att_width = HEADS * HEAD_DIM
    queries = projected[..., :att_width].reshape(rows_here, seq_here, HEADS, HEAD_DIM)
    keys_rot = projected[..., att_width:att_width + KV_HEADS * HEAD_DIM].reshape(rows_here, seq_here, KV_HEADS, HEAD_DIM)
    cos_wide = cos_table[:, :, None, :]
    sin_wide = sin_table[:, :, None, :]
    queries = turn(norm_rows(queries, gain_query), cos_wide, sin_wide) * HEAD_DIM ** (-0.5)
    keys_rot = turn(norm_rows(keys_rot, gain_key), cos_wide, sin_wide)
    return (queries, keys_rot)

def mask_of(query_docs, query_places, key_docs, key_places):
    same_doc = query_docs[:, :, None] == key_docs[:, None, :]
    causal = query_places[None, :, None] >= key_places[None, None, :]
    return (same_doc & causal)[:, None, None, :, :]

def row_forward(params, row_tokens, row_starts):
    w_qkv, w_out, w_gate_up, w_down, gains = params
    group_size = HEADS // KV_HEADS
    att_width = HEADS * HEAD_DIM
    kv_width = KV_HEADS * HEAD_DIM
    block_rows = min(512, LENGTH)
    places = jnp.arange(LENGTH, dtype=jnp.int32)
    doc_ids, offsets = doc_tables(row_starts[None, :], places)
    cos_table, sin_table = rotary(offsets)
    tokens_wide = row_tokens[None]
    normed = low(norm_rows(tokens_wide, gains[:D]))
    projected = low_back(jnp.einsum('rtd,de->rte', normed, w_qkv, precision=PRECISE))
    queries, keys_rot = queries_keys(cos_table, sin_table, projected, gains[2 * D:2 * D + HEAD_DIM], gains[2 * D + HEAD_DIM:])
    queries = low(queries).reshape(1, LENGTH, KV_HEADS, group_size, HEAD_DIM)
    keys_rot = low(keys_rot)
    values = low(projected[..., att_width + kv_width:].reshape(1, LENGTH, KV_HEADS, HEAD_DIM))

    def attend_block(block_index):
        begin_at = block_index * block_rows
        query_block = lax.dynamic_slice_in_dim(queries, begin_at, block_rows, 1)
        query_places = begin_at + jnp.arange(block_rows, dtype=jnp.int32)
        query_docs = lax.dynamic_slice_in_dim(doc_ids, begin_at, block_rows, 1)
        allowed = mask_of(query_docs, query_places, doc_ids, places)
        scores = low_back(jnp.einsum('rqkgh,rtkh->rkgqt', query_block, keys_rot, precision=PRECISE))
        scores = jnp.where(allowed, scores, MASKED_SCORE)
        probs = jax.nn.softmax(scores, axis=-1)
        return jnp.einsum('rkgqt,rtkh->rqkgh', low(probs), values, precision=PRECISE)
    pieces = lax.map(jax.checkpoint(attend_block), jnp.arange(LENGTH // block_rows, dtype=jnp.int32))
    attended = pieces.transpose(1, 0, 2, 3, 4, 5).reshape(1, LENGTH, att_width)
    attended = low(low_back(attended))
    branch = low_back(jnp.einsum('rtc,cd->rtd', attended, w_out, precision=PRECISE))
    hidden_in = tokens_wide + branch
    normed2 = low(norm_rows(hidden_in, gains[D:2 * D]))
    gate_up = low_back(jnp.einsum('rtd,df->rtf', normed2, w_gate_up, precision=PRECISE))
    hidden = low(jax.nn.silu(gate_up[..., :FF]) * gate_up[..., FF:])
    result = hidden_in + low_back(jnp.einsum('rtf,fd->rtd', hidden, w_down, precision=PRECISE))
    return result[0]

def factored(gradient, master, row_state, col_state):
    beta = 1.0 - STEP ** (-0.8)
    square = gradient * gradient + SQUARE_EPSILON
    row_new = beta * row_state + (1.0 - beta) * lax.optimization_barrier(jnp.mean(square, axis=1))
    col_new = beta * col_state + (1.0 - beta) * lax.optimization_barrier(jnp.mean(square, axis=0))
    unit = gradient * lax.rsqrt(row_new / jnp.mean(row_new))[:, None] * lax.rsqrt(col_new)[None, :]
    spread = jnp.sqrt(jnp.mean(unit * unit))
    scale = STEP_RATE * jnp.maximum(SCALE_EPSILON, jnp.sqrt(jnp.mean(master * master)))
    return (row_new, col_new, master - scale * unit / jnp.maximum(1.0, spread / CLIP_LEVEL), spread)

def unfactored(gradient, gain, moment):
    beta = 1.0 - STEP ** (-0.8)
    moment_new = beta * moment + (1.0 - beta) * (gradient * gradient + SQUARE_EPSILON)
    unit = gradient * lax.rsqrt(moment_new)
    spread = jnp.sqrt(jnp.mean(unit * unit))
    scale = STEP_RATE * jnp.maximum(SCALE_EPSILON, jnp.sqrt(jnp.mean(gain * gain)))
    return (moment_new, gain - scale * unit / jnp.maximum(1.0, spread / CLIP_LEVEL), spread)

def reference(tokens, doc_starts, grad_out, qkv_master, out_master, gate_up_master, down_master, gains, qkv_rows, out_rows, gate_up_rows, down_rows, col_moments, gain_moments):

    def layer(tokens_wide, w_qkv, w_out, w_gate_up, w_down, gains_wide):
        params = (w_qkv, w_out, w_gate_up, w_down, gains_wide)

        def one_row(packed):
            return row_forward(params, packed[0], packed[1])
        return lax.map(jax.checkpoint(one_row), (tokens_wide, doc_starts))
    output, back = jax.vjp(layer, tokens.astype(jnp.float32), low(qkv_master), low(out_master), low(gate_up_master), low(down_master), gains)
    grad_x, grad_qkv, grad_out_proj, grad_gate_up, grad_down, grad_gains = back(grad_out.astype(jnp.float32))
    col_widths = (QKV, D, 2 * FF, D)
    col_parts = []
    begin_at = 0
    for col_width in col_widths:
        col_parts.append(col_moments[begin_at:begin_at + col_width])
        begin_at = begin_at + col_width
    qkv_rows_new, qkv_cols, qkv_new, qkv_spread = factored(grad_qkv, qkv_master, qkv_rows, col_parts[0])
    out_rows_new, out_cols, out_new, out_spread = factored(grad_out_proj, out_master, out_rows, col_parts[1])
    gate_up_rows_new, gate_up_cols, gate_up_new, gate_up_spread = factored(grad_gate_up, gate_up_master, gate_up_rows, col_parts[2])
    down_rows_new, down_cols, down_new, down_spread = factored(grad_down, down_master, down_rows, col_parts[3])
    bounds = (0, D, 2 * D, 2 * D + HEAD_DIM, 2 * D + 2 * HEAD_DIM)
    moment_parts, gain_parts, spreads = ([], [], [qkv_spread, out_spread, gate_up_spread, down_spread])
    for segment in range(4):
        moment_new, gain_new, spread = unfactored(grad_gains[bounds[segment]:bounds[segment + 1]], gains[bounds[segment]:bounds[segment + 1]], gain_moments[bounds[segment]:bounds[segment + 1]])
        moment_parts.append(moment_new)
        gain_parts.append(gain_new)
        spreads.append(spread)
    return (output.astype(jnp.bfloat16), grad_x.astype(jnp.bfloat16), grad_qkv, grad_out_proj, grad_gate_up, grad_down, grad_gains, qkv_rows_new, out_rows_new, gate_up_rows_new, down_rows_new, jnp.concatenate([qkv_cols, out_cols, gate_up_cols, down_cols]), jnp.concatenate(moment_parts), qkv_new, out_new, gate_up_new, down_new, qkv_new.astype(jnp.bfloat16), out_new.astype(jnp.bfloat16), gate_up_new.astype(jnp.bfloat16), down_new.astype(jnp.bfloat16), jnp.concatenate(gain_parts), jnp.stack(spreads))
```

```python
from functools import partial

import jax
import jax.numpy as jnp
from jax import lax
from jax.experimental import pallas as pl
from jax.experimental.pallas import tpu as pltpu
from jax.sharding import PartitionSpec as P

D = 2048
HEADS = 32
KV_HEADS = 8
HEAD_DIM = 64
FF = 8192
STEP = 10
QKV = 3072


EPSILON = 1e-06
ROPE_BASE = 10000.0
MASKED_SCORE = -1e30
STEP_RATE = 0.3
CLIP_LEVEL = 1.0
SQUARE_EPSILON = 1e-30
SCALE_EPSILON = 0.001


def from_behind(value, axis, steps):
    count = lax.axis_size(axis)
    pairs = [(source, (source + steps) % count) for source in range(count)]
    return lax.ppermute(value, axis, pairs)


def norm_rows(entries, gain):
    return entries * lax.rsqrt(jnp.mean(entries * entries, axis=-1, keepdims=True) + EPSILON) * gain


def turn(entries, cos_wide, sin_wide):
    half_width = entries.shape[-1] // 2
    turned = jnp.concatenate([-entries[..., half_width:], entries[..., :half_width]], axis=-1)
    return entries * cos_wide + turned * sin_wide


def doc_tables(doc_starts, places):
    before = doc_starts[:, None, :] <= places[None, :, None]
    doc_ids = jnp.sum(before.astype(jnp.int32), axis=-1)
    doc_first = jnp.max(jnp.where(before, doc_starts[:, None, :], 0), axis=-1)
    return (doc_ids, places[None, :] - doc_first)


def rotary(offsets):
    frequency = ROPE_BASE ** (-(jnp.arange(HEAD_DIM // 2, dtype=jnp.float32) * 2.0 / HEAD_DIM))
    angles = offsets.astype(jnp.float32)[..., None] * frequency
    cos_table = jnp.concatenate([jnp.cos(angles), jnp.cos(angles)], axis=-1)
    sin_table = jnp.concatenate([jnp.sin(angles), jnp.sin(angles)], axis=-1)
    return (cos_table, sin_table)


def queries_keys(
    cos_table, sin_table, projected, gain_query, gain_key, heads=HEADS, kv_heads=KV_HEADS
):
    rows_here, seq_here = (projected.shape[0], projected.shape[1])
    att_width = heads * HEAD_DIM
    queries = projected[..., :att_width].reshape(rows_here, seq_here, heads, HEAD_DIM)
    keys_rot = projected[..., att_width : att_width + kv_heads * HEAD_DIM].reshape(
        rows_here, seq_here, kv_heads, HEAD_DIM
    )
    cos_wide = cos_table[:, :, None, :]
    sin_wide = sin_table[:, :, None, :]
    queries = turn(norm_rows(queries, gain_query), cos_wide, sin_wide) * HEAD_DIM ** (-0.5)
    keys_rot = turn(norm_rows(keys_rot, gain_key), cos_wide, sin_wide)
    return (queries, keys_rot)


def mask_of(query_docs, query_places, key_docs, key_places):
    same_doc = query_docs[:, :, None] == key_docs[:, None, :]
    causal = query_places[None, :, None] >= key_places[None, None, :]
    return (same_doc & causal)[:, None, None, :, :]


def gathered_local(
    tokens,
    doc_starts,
    grad_out,
    qkv_master,
    out_master,
    gate_up_master,
    down_master,
    gains,
    qkv_rows,
    out_rows,
    gate_up_rows,
    down_rows,
    col_moments,
    gain_moments,
):
    cycle_size = lax.axis_size("seq")
    seq_index = lax.axis_index("seq")
    rows_dev, seq_dev = (tokens.shape[0], tokens.shape[1])
    group_size = HEADS // KV_HEADS
    att_width = HEADS * HEAD_DIM
    kv_width = KV_HEADS * HEAD_DIM
    gain_attn = gains[:D]
    gain_ffn = gains[D : 2 * D]
    gain_query = gains[2 * D : 2 * D + HEAD_DIM]
    gain_key = gains[2 * D + HEAD_DIM :]
    local_places = jnp.arange(seq_dev, dtype=jnp.int32)
    places = seq_index * seq_dev + local_places
    query_docs, offsets = doc_tables(doc_starts, places)
    cos_table, sin_table = rotary(offsets)
    copies = (
        qkv_master.astype(jnp.bfloat16),
        out_master.astype(jnp.bfloat16),
        gate_up_master.astype(jnp.bfloat16),
        down_master.astype(jnp.bfloat16),
    )
    w_qkv, w_out, w_gate_up, w_down = (
        lax.all_gather(copies[0], ("seq", "rows"), axis=0, tiled=True),
        lax.all_gather(copies[1], ("seq", "rows"), axis=0, tiled=True),
        lax.all_gather(copies[2], ("seq", "rows"), axis=0, tiled=True),
        lax.all_gather(copies[3], ("seq", "rows"), axis=0, tiled=True),
    )
    tokens_wide = tokens.astype(jnp.float32)
    normed = norm_rows(tokens_wide, gain_attn).astype(jnp.bfloat16)
    projected = jnp.einsum("rtd,de->rte", normed, w_qkv, preferred_element_type=jnp.float32)
    head_fn = partial(queries_keys, cos_table, sin_table)
    queries, keys_rot = head_fn(projected, gain_query, gain_key)
    query16 = queries.astype(jnp.bfloat16).reshape(
        rows_dev, seq_dev, KV_HEADS, group_size, HEAD_DIM
    )
    keys16 = keys_rot.astype(jnp.bfloat16).reshape(rows_dev, seq_dev, kv_width)
    values16 = projected[..., att_width + kv_width :].astype(jnp.bfloat16)
    stat_shape = (rows_dev, KV_HEADS, group_size, seq_dev)
    initial = (
        jnp.full(stat_shape, MASKED_SCORE, jnp.float32),
        jnp.zeros(stat_shape, jnp.float32),
        jnp.zeros(stat_shape + (HEAD_DIM,), jnp.float32),
    )
    carry = initial
    key_piece = lax.all_gather(keys16, "seq", axis=1, tiled=True)
    value_piece = lax.all_gather(values16, "seq", axis=1, tiled=True)
    key_count = key_piece.shape[1]

    def absorb_block(state, block_index):
        best, total, summed = state
        block_begin = block_index * seq_dev
        key_block = lax.dynamic_slice_in_dim(key_piece, block_begin, seq_dev, 1).reshape(
            rows_dev, seq_dev, KV_HEADS, HEAD_DIM
        )
        value_block = lax.dynamic_slice_in_dim(value_piece, block_begin, seq_dev, 1).reshape(
            rows_dev, seq_dev, KV_HEADS, HEAD_DIM
        )
        key_places = block_begin + jnp.arange(seq_dev, dtype=jnp.int32)
        key_docs, _ = doc_tables(doc_starts, key_places)
        allowed = mask_of(query_docs, places, key_docs, key_places)
        scores = jnp.einsum(
            "rqkgh,rtkh->rkgqt", query16, key_block, preferred_element_type=jnp.float32
        )
        scores = jnp.where(allowed, scores, MASKED_SCORE)
        best_new = jnp.maximum(best, jnp.max(scores, axis=-1))
        weights = jnp.where(allowed, jnp.exp(scores - best_new[..., None]), 0.0)
        factor = jnp.exp(best - best_new)
        total = total * factor + jnp.sum(weights, axis=-1)
        summed = summed * factor[..., None] + jnp.einsum(
            "rkgqt,rtkh->rkgqh",
            weights.astype(jnp.bfloat16),
            value_block,
            preferred_element_type=jnp.float32,
        )
        return ((best_new, total, summed), None)

    carry, _ = lax.scan(absorb_block, carry, jnp.arange(key_count // seq_dev, dtype=jnp.int32))
    best, total, summed = carry
    log_total = best + jnp.log(total)
    attended = summed / total[..., None]
    attended16 = (
        attended.transpose(0, 3, 1, 2, 4).reshape(rows_dev, seq_dev, att_width).astype(jnp.bfloat16)
    )
    branch = jnp.einsum("rtc,cd->rtd", attended16, w_out, preferred_element_type=jnp.float32)
    hidden_in = tokens_wide + branch
    normed2 = norm_rows(hidden_in, gain_ffn).astype(jnp.bfloat16)
    gate_up = jnp.einsum("rtd,df->rtf", normed2, w_gate_up, preferred_element_type=jnp.float32)
    gate_part, up_part = (gate_up[..., :FF], gate_up[..., FF:])
    hidden = (jax.nn.silu(gate_part) * up_part).astype(jnp.bfloat16)
    output = hidden_in + jnp.einsum(
        "rtf,fd->rtd", hidden, w_down, preferred_element_type=jnp.float32
    )
    d_hidden = jnp.einsum("rtd,fd->rtf", grad_out, w_down, preferred_element_type=jnp.float32)
    silu_value, silu_back = jax.vjp(jax.nn.silu, gate_part)
    d_gate = silu_back(d_hidden * up_part)[0]
    d_gate_up = jnp.concatenate([d_gate, d_hidden * silu_value], axis=-1).astype(jnp.bfloat16)
    d_normed2 = jnp.einsum("rtf,df->rtd", d_gate_up, w_gate_up, preferred_element_type=jnp.float32)
    _, ffn_norm_back = jax.vjp(norm_rows, hidden_in, gain_ffn)
    d_inner, grad_gain_ffn = ffn_norm_back(d_normed2)
    d_hidden_in = grad_out.astype(jnp.float32) + d_inner
    term_down = jnp.einsum("rtf,rtd->fd", hidden, grad_out, preferred_element_type=jnp.float32)
    grad_down = lax.psum_scatter(term_down, ("seq", "rows"), scatter_dimension=0, tiled=True)
    term_gate_up = jnp.einsum("rtd,rtf->df", normed2, d_gate_up, preferred_element_type=jnp.float32)
    grad_gate_up = lax.psum_scatter(term_gate_up, ("seq", "rows"), scatter_dimension=0, tiled=True)
    d_branch = d_hidden_in.astype(jnp.bfloat16)
    term_out = jnp.einsum("rtc,rtd->cd", attended16, d_branch, preferred_element_type=jnp.float32)
    d_attended = jnp.einsum(
        "rtd,cd->rtc", d_branch, w_out, preferred_element_type=jnp.float32
    ).astype(jnp.bfloat16)
    d_heads = d_attended.reshape(rows_dev, seq_dev, KV_HEADS, group_size, HEAD_DIM).transpose(
        0, 2, 3, 1, 4
    )
    delta = jnp.sum(d_heads.astype(jnp.float32) * attended, axis=-1)

    def cycle_turn(turn_index, carry):
        pair16, grad_pair, d_queries = carry
        source = (seq_index + turn_index) % cycle_size
        key_places = source * seq_dev + local_places
        key_docs, _ = doc_tables(doc_starts, key_places)
        allowed = mask_of(query_docs, places, key_docs, key_places)
        key_block = pair16[0].reshape(rows_dev, seq_dev, KV_HEADS, HEAD_DIM)
        value_block = pair16[1].reshape(rows_dev, seq_dev, KV_HEADS, HEAD_DIM)
        scores = jnp.einsum(
            "rqkgh,rtkh->rkgqt", query16, key_block, preferred_element_type=jnp.float32
        )
        scores = jnp.where(allowed, scores, MASKED_SCORE)
        probs = jnp.where(allowed, jnp.exp(scores - log_total[..., None]), 0.0)
        d_values = jnp.einsum(
            "rkgqt,rkgqh->rtkh",
            probs.astype(jnp.bfloat16),
            d_heads,
            preferred_element_type=jnp.float32,
        )
        d_probs = jnp.einsum(
            "rkgqh,rtkh->rkgqt", d_heads, value_block, preferred_element_type=jnp.float32
        )
        d_scores = (probs * (d_probs - delta[..., None])).astype(jnp.bfloat16)
        d_queries = d_queries + jnp.einsum(
            "rkgqt,rtkh->rkgqh", d_scores, key_block, preferred_element_type=jnp.float32
        )
        d_keys = jnp.einsum(
            "rkgqt,rqkgh->rtkh", d_scores, query16, preferred_element_type=jnp.float32
        )
        grad_pair = grad_pair + jnp.stack(
            [
                d_keys.reshape(rows_dev, seq_dev, kv_width),
                d_values.reshape(rows_dev, seq_dev, kv_width),
            ]
        )
        grad_pair = from_behind(grad_pair.astype(jnp.bfloat16), "seq", -1).astype(grad_pair.dtype)
        pair16 = from_behind(pair16, "seq", -1)
        return (pair16, grad_pair, d_queries)

    start_pair = jnp.stack([keys16, values16])
    start_grads = jnp.zeros((2, rows_dev, seq_dev, kv_width), jnp.float32)
    start_queries = jnp.zeros(stat_shape + (HEAD_DIM,), jnp.float32)
    _, grad_pair, d_queries = lax.fori_loop(
        0, cycle_size, cycle_turn, (start_pair, start_grads, start_queries)
    )
    d_queries = d_queries.transpose(0, 3, 1, 2, 4).reshape(rows_dev, seq_dev, HEADS, HEAD_DIM)
    d_keys_home = grad_pair[0].reshape(rows_dev, seq_dev, KV_HEADS, HEAD_DIM)
    _, heads_back = jax.vjp(head_fn, projected, gain_query, gain_key)
    d_projected, grad_gain_query, grad_gain_key = heads_back((d_queries, d_keys_home))
    d_projected = jnp.concatenate(
        [d_projected[..., : att_width + kv_width], grad_pair[1]], axis=-1
    ).astype(jnp.bfloat16)
    term_qkv = jnp.einsum("rtd,rte->de", normed, d_projected, preferred_element_type=jnp.float32)
    d_normed = jnp.einsum("rte,de->rtd", d_projected, w_qkv, preferred_element_type=jnp.float32)
    _, attn_norm_back = jax.vjp(norm_rows, tokens_wide, gain_attn)
    d_tokens_part, grad_gain_attn = attn_norm_back(d_normed)
    grad_tokens = (d_hidden_in + d_tokens_part).astype(jnp.bfloat16)
    grad_qkv, grad_out_proj = (
        lax.psum_scatter(term_qkv, ("seq", "rows"), scatter_dimension=0, tiled=True),
        lax.psum_scatter(term_out, ("seq", "rows"), scatter_dimension=0, tiled=True),
    )
    gain_local = jnp.concatenate([grad_gain_attn, grad_gain_ffn, grad_gain_query, grad_gain_key])
    grads = (grad_qkv, grad_out_proj, grad_gate_up, grad_down)
    updated = optimizer_step(
        grads, gain_local, (qkv_master, out_master, gate_up_master, down_master), gains,
        (qkv_rows, out_rows, gate_up_rows, down_rows), col_moments, gain_moments,
        lambda vector: lax.psum(vector, ("seq", "rows")),
    )
    return (output.astype(jnp.bfloat16), grad_tokens, *grads, *updated)


MESH = pl.DeviceIdType.MESH
PLACES = 32
VMEM_BYTES = 56 * 1024 * 1024
CHUNK = 16


def here():
    seq = lax.axis_index("seq")
    return lax.div(seq, 2), lax.rem(seq, 2), lax.axis_index("rows")


def flips(chip):
    return (chip + 1 - 2 * lax.rem(chip, 2), lax.rem(chip + 2, 4), 3 - chip)


def ahead(z, step):
    return lax.rem(z + step, 4)


def at_place(chip, core, z):
    return (2 * chip + core, z)


def greet(peers):
    barrier = pltpu.get_barrier_semaphore()
    for peer in peers:
        pl.semaphore_signal(barrier, inc=1, device_id=peer, device_id_type=MESH)
    pl.semaphore_wait(barrier, len(peers))


class Mover:
    def __init__(self, send_sem, recv_sem, local_sem):
        self.send_sem, self.recv_sem, self.local_sem = send_sem, recv_sem, local_sem
        self.remote, self.own = [], []

    def send(self, src, dst, peer):
        slot = len(self.remote)
        copy = pltpu.make_async_remote_copy(
            src_ref=src,
            dst_ref=dst,
            send_sem=self.send_sem.at[slot],
            recv_sem=self.recv_sem.at[slot],
            device_id=peer,
            device_id_type=MESH,
        )
        copy.start()
        handle = [copy, False, copy.wait_recv]
        self.remote.append(handle)
        return handle

    def keep(self, src, dst):
        copy = pltpu.make_async_copy(src, dst, self.local_sem.at[len(self.own)])
        copy.start()
        handle = [copy, False, copy.wait]
        self.own.append(handle)
        return handle

    def arrive(self, *handles):
        for handle in handles:
            if not handle[1]:
                handle[1] = True
                handle[2]()

    def finish(self):
        self.arrive(*self.own, *self.remote)
        for handle in self.remote:
            handle[0].wait_send()


def semaphores(remote, own):
    return [
        pltpu.SemaphoreType.DMA((remote,)),
        pltpu.SemaphoreType.DMA((remote,)),
        pltpu.SemaphoreType.DMA((max(own, 1),)),
    ]


def exchange(kernel, ident, inputs, outputs, scratch, copies, moved):
    vmem, anywhere = pl.BlockSpec(memory_space=pltpu.VMEM), pl.BlockSpec(memory_space=pl.ANY)
    return pl.pallas_call(
        kernel,
        out_shape=[jax.ShapeDtypeStruct(shape, kind) for shape, kind, _ in outputs],
        in_specs=[vmem if near else anywhere for _, near in inputs],
        out_specs=[vmem if near else anywhere for _, _, near in outputs],
        scratch_shapes=scratch + semaphores(*copies),
        compiler_params=pltpu.CompilerParams(
            collective_id=ident, has_side_effects=True, vmem_limit_bytes=VMEM_BYTES
        ),
        cost_estimate=pl.CostEstimate(flops=0, bytes_accessed=moved, transcendentals=0),
    )(*[array for array, _ in inputs])


def chunks(length, body):
    @pl.loop(0, length // CHUNK)
    def _(step):
        body(pl.ds(pl.multiple_of(step * CHUNK, CHUNK), CHUNK))


def attention_weights_kernel(tok, wq, wo, all_tok, all_wq, all_wo, *sems):
    chip, core, z = here()
    others = flips(chip)
    other = 1 - core
    plane = [at_place(chip, other, z)]
    for peer_chip in others:
        plane += [at_place(peer_chip, core, z), at_place(peer_chip, other, z)]
    along = [at_place(chip, core, ahead(z, step)) for step in (2, 1, 3)]
    greet(plane + along)
    move = Mover(*sems)
    me = 2 * chip + core
    for peer in along:
        move.send(wo, all_wo.at[z], peer)
    parts = [move.keep(wq.at[me], all_wq.at[me, z])]
    for peer in plane:
        parts.append(move.send(wq.at[peer[0]], all_wq.at[me, z], peer))
    came = []
    for peer_chip in others:
        came.append(move.send(tok, all_tok.at[:, me], at_place(peer_chip, core, z)))
    partner = at_place(chip, other, z)
    move.send(tok, all_tok.at[:, me], partner)
    move.keep(tok, all_tok.at[:, me])
    move.keep(wo, all_wo.at[z])
    move.arrive(*parts)
    for peer in along:
        move.send(all_wq.at[:, z], all_wq.at[:, z], peer)
    for peer_chip, handle in zip(others, came):
        move.arrive(handle)
        block = all_tok.at[:, 2 * peer_chip + core]
        move.send(block, block, partner)
    move.finish()


def add_blocks(first, second, result):
    for row in range(2):

        def body(part):
            total = first[row, part].astype(jnp.float32) + second[row, part].astype(jnp.float32)
            result[row, part] = total.astype(result.dtype)

        chunks(64, body)


def add_flat(first, second, result):
    def body(part):
        total = first[part].astype(jnp.float32) + second[part].astype(jnp.float32)
        result[part] = total.astype(result.dtype)

    chunks(128, body)


def ffn_weights_kernel(
    branch, tok, gain, wg, wd, grad_out,
    hidden_in, all_norm, all_out, all_wg, all_wd,
    from_partner, summed, came, normed, *sems,
):
    chip, core, z = here()
    others = flips(chip)
    other = 1 - core
    partner = at_place(chip, other, z)
    plane = [at_place(peer_chip, core, z) for peer_chip in others]
    steps = (2, 1, 3)
    line = [at_place(chip, core, ahead(z, step)) for step in steps]
    cross = [at_place(chip, other, ahead(z, step)) for step in steps]
    greet([partner] + plane + line + cross)
    move = Mover(*sems)
    order = tuple(others) + (chip,)
    halves = [
        move.send(branch.at[:, 2 * to + other], from_partner.at[to], partner) for to in order
    ]
    shared = []
    for step, peer in zip(steps, line):
        shared.append((move.send(grad_out, all_out.at[z, core], peer), step))
    move.send(grad_out, all_out.at[z, core], partner)
    move.keep(grad_out, all_out.at[z, core])
    turned = [move.keep(wg.at[z, core], all_wg.at[chip, core, z])]
    turned.append(move.send(wg.at[z, other], all_wg.at[chip, core, z], partner))
    for step, peer, peer_cross in zip(steps, line, cross):
        to = ahead(z, step)
        turned.append(move.send(wg.at[to, core], all_wg.at[chip, core, z], peer))
        turned.append(move.send(wg.at[to, other], all_wg.at[chip, core, z], peer_cross))
    sums = []
    for to, half, peer in zip(others, halves, plane):
        move.arrive(half)
        add_blocks(branch.at[:, 2 * to + core], from_partner.at[to], summed.at[to])
        sums.append(move.send(summed.at[to], came.at[chip], peer))
    for peer in plane:
        move.send(wd, all_wd.at[chip], peer)
    move.keep(wd, all_wd.at[chip])
    move.arrive(halves[3], *sums)
    for row in range(2):

        def body(part):
            total = tok[row, part].astype(jnp.float32)
            total += branch[row, 2 * chip + core, part].astype(jnp.float32)
            total += from_partner[chip, row, part].astype(jnp.float32)
            for peer_chip in others:
                total += came[peer_chip, row, part].astype(jnp.float32)
            hidden_in[row, part] = total
            scale = lax.rsqrt(jnp.mean(total * total, axis=-1, keepdims=True) + EPSILON)
            normed[row, part] = (total * scale * gain[...]).astype(jnp.bfloat16)

        chunks(64, body)
    for step, peer in zip(steps, line):
        shared.append((move.send(normed, all_norm.at[z, core], peer), step))
    move.send(normed, all_norm.at[z, core], partner)
    move.keep(normed, all_norm.at[z, core])
    move.arrive(*turned)
    for peer in plane:
        move.send(all_wg.at[chip], all_wg.at[chip], peer)
    for index, (handle, step) in enumerate(shared):
        move.arrive(handle)
        target = all_out if index < 3 else all_norm
        block = target.at[ahead(z, 4 - step), core]
        move.send(block, block, partner)
    move.finish()


def line_sums(move, partial, from_partner, summed, came, partner, line, steps, core, z):
    other = 1 - core
    halves = [
        move.send(partial.at[ahead(z, step), other], from_partner.at[ahead(z, step)], partner)
        for step in steps + (0,)
    ]
    sums = []
    for step, half, peer in zip(steps, halves, line):
        to = ahead(z, step)
        move.arrive(half)
        add_flat(partial.at[to, core], from_partner.at[to], summed.at[to])
        sums.append(move.send(summed.at[to], came.at[z], peer))
    return sums + [halves[3]]


def ffn_back_kernel(
    d_norm, out_part, down_part, hidden_in, grad_out, gain,
    all_branch, d_hidden_in, out_sum, gain_part, down_came,
    from_partner, summed, came, from_partner2, summed2, came2, d_branch, *sems,
):
    chip, core, z = here()
    others = flips(chip)
    other = 1 - core
    partner = at_place(chip, other, z)
    plane = [at_place(peer_chip, core, z) for peer_chip in others]
    steps = (2, 1, 3)
    line = [at_place(chip, core, ahead(z, step)) for step in steps]
    greet([partner] + plane + line)
    move = Mover(*sems)
    first = line_sums(move, d_norm, from_partner, summed, came, partner, line, steps, core, z)
    for to, peer in zip(others, plane):
        move.send(down_part.at[to], down_came.at[chip], peer)
    move.keep(down_part.at[chip], down_came.at[chip])
    move.arrive(*first)
    gain_part[...] = jnp.zeros_like(gain_part)

    def body(part):
        total = d_norm[z, core, part].astype(jnp.float32)
        total += from_partner[z, part].astype(jnp.float32)
        for step in steps:
            total += came[ahead(z, step), part].astype(jnp.float32)
        entries = hidden_in[part]
        scale = lax.rsqrt(jnp.mean(entries * entries, axis=-1, keepdims=True) + EPSILON)
        gain_part[...] += jnp.sum(total * entries * scale, axis=0, keepdims=True)
        total = total * gain[...]
        inner = jnp.mean(total * entries, axis=-1, keepdims=True) * (scale * scale * scale)
        grad = grad_out[part].astype(jnp.float32) + total * scale - entries * inner
        d_hidden_in[part] = grad
        d_branch[part] = grad.astype(jnp.bfloat16)

    chunks(128, body)
    me = 2 * chip + core
    shared = [move.send(d_branch, all_branch.at[me], peer) for peer in plane]
    move.send(d_branch, all_branch.at[me], partner)
    move.keep(d_branch, all_branch.at[me])
    second = line_sums(
        move, out_part, from_partner2, summed2, came2, partner, line, steps, core, z
    )
    for peer_chip, handle in zip(others, shared):
        move.arrive(handle)
        block = all_branch.at[2 * peer_chip + core]
        move.send(block, block, partner)
    move.arrive(*second)

    def body2(part):
        total = out_part[z, core, part].astype(jnp.float32)
        total += from_partner2[z, part].astype(jnp.float32)
        total += hidden_in[part]
        for step in steps:
            total += came2[ahead(z, step), part].astype(jnp.float32)
        out_sum[part] = total.astype(jnp.bfloat16)

    chunks(128, body2)
    move.finish()


def gradients_kernel(
    d_norm, gate_up_part, qkv_part, out_part,
    d_norm_came, gate_up_came, qkv_came, out_came,
    from_partner, summed, gate_up_in, gate_up_sum, qkv_in, qkv_sum, *sems,
):
    chip, core, z = here()
    others = flips(chip)
    other = 1 - core
    me = 2 * chip + core
    partner = at_place(chip, other, z)
    plane = [at_place(peer_chip, core, z) for peer_chip in others]
    plane_cross = [at_place(peer_chip, other, z) for peer_chip in others]
    steps = (2, 1, 3)
    line = [at_place(chip, core, ahead(z, step)) for step in steps]
    cross = [at_place(chip, other, ahead(z, step)) for step in steps]
    greet([partner] + plane + plane_cross + line + cross)
    move = Mover(*sems)
    pieces = [
        move.send(gate_up_part.at[to], gate_up_in.at[chip], peer)
        for to, peer in zip(others, plane)
    ]
    order = tuple(others) + (chip,)
    halves = [
        move.send(d_norm.at[:, 2 * to + other], from_partner.at[to], partner) for to in order
    ]
    qkv_pieces = []
    for step, peer in zip(steps, line):
        qkv_pieces.append(move.send(qkv_part.at[:, ahead(z, step)], qkv_in.at[z], peer))
        move.send(out_part.at[ahead(z, step)], out_came.at[z], peer)
    move.keep(out_part.at[z], out_came.at[z])
    for to, half in zip(order, halves):
        move.arrive(half)
        add_blocks(d_norm.at[:, 2 * to + core], from_partner.at[to], summed.at[to])
    for to, peer in zip(others, plane):
        move.send(summed.at[to], d_norm_came.at[chip], peer)
    move.keep(summed.at[chip], d_norm_came.at[chip])
    move.arrive(*qkv_pieces)

    @pl.loop(0, 8)
    def _(block):
        def body(part):
            total = qkv_part[block, z, part].astype(jnp.float32)
            for step in steps:
                total += qkv_in[ahead(z, step), block, part].astype(jnp.float32)
            qkv_sum[block, part] = total.astype(jnp.bfloat16)

        chunks(64, body)

    for peer in [partner] + plane + plane_cross:
        move.send(qkv_sum.at[peer[0]], qkv_came.at[me], peer)
    move.keep(qkv_sum.at[me], qkv_came.at[me])
    move.arrive(*pieces)

    @pl.loop(0, 8)
    def _(block):
        to_core, to_z = lax.div(block, 4), lax.rem(block, 4)

        def body(part):
            total = gate_up_part[chip, to_core, to_z, part].astype(jnp.float32)
            for peer_chip in others:
                total += gate_up_in[peer_chip, to_core, to_z, part].astype(jnp.float32)
            gate_up_sum[to_core, to_z, part] = total.astype(jnp.bfloat16)

        chunks(64, body)

    for step, peer, peer_cross in zip(steps, line, cross):
        to = ahead(z, step)
        move.send(gate_up_sum.at[core, to], gate_up_came.at[z, core], peer)
        move.send(gate_up_sum.at[other, to], gate_up_came.at[z, core], peer_cross)
    move.send(gate_up_sum.at[other, z], gate_up_came.at[z, core], partner)
    move.keep(gate_up_sum.at[core, z], gate_up_came.at[z, core])
    move.finish()


def total_kernel(parts, totals, came, mine, *sems):
    seq, z = lax.axis_index("seq"), lax.axis_index("rows")
    me = seq * 4 + z
    places = [lax.rem(me + step, PLACES) for step in range(1, PLACES)]
    peers = [(lax.div(place, 4), lax.rem(place, 4)) for place in places]
    greet(peers)
    move = Mover(*sems)
    pieces = [
        move.send(parts.at[place], came.at[me], peer) for place, peer in zip(places, peers)
    ]
    came[me] = parts[me]
    move.arrive(*pieces)
    total = came[0]
    for place in range(1, PLACES):
        total = total + came[place]
    mine[...] = total
    for peer in peers:
        move.send(mine, totals.at[me], peer)
    totals[me] = total
    move.finish()


def total_of(vector):
    length = vector.shape[0]
    width = -(-length // (PLACES * 1024)) * 1024
    padded = jnp.pad(vector, (0, PLACES * width - length)).reshape(PLACES, width // 128, 128)
    shape = (PLACES, width // 128, 128)
    totals = exchange(
        total_kernel, 4, [(padded, True)], [(shape, jnp.float32, True)],
        [pltpu.VMEM(shape, jnp.float32), pltpu.VMEM(shape[1:], jnp.float32)],
        (2 * (PLACES - 1), 0), 2 * PLACES * width * 4,
    )[0]
    return totals.reshape(-1)[:length]


def ffn_split(entries):
    rows = entries.shape[0]
    return entries.reshape(rows, 2, 4, 2, 4, 256).transpose(4, 3, 0, 1, 2, 5).reshape(4, 2, rows, 2048)


def ffn_join(blocks):
    rows = blocks.shape[2]
    return blocks.reshape(4, 2, rows, 2, 4, 256).transpose(2, 3, 4, 1, 0, 5).reshape(rows, 16384)


def head_split(entries):
    rows = entries.shape[0]
    parts = (
        entries[:, :2048].reshape(rows, 8, 256),
        entries[:, 2048:2560].reshape(rows, 8, 64),
        entries[:, 2560:].reshape(rows, 8, 64),
    )
    return jnp.concatenate(parts, axis=2).transpose(1, 0, 2)


def head_join(blocks):
    rows = blocks.shape[1]
    blocks = blocks.transpose(1, 0, 2)
    parts = (blocks[..., :256], blocks[..., 256:320], blocks[..., 320:])
    return jnp.concatenate([part.reshape(rows, -1) for part in parts], axis=1)


def split_local(
    tokens, doc_starts, grad_out, qkv_master, out_master, gate_up_master, down_master, gains,
    qkv_rows, out_rows, gate_up_rows, down_rows, col_moments, gain_moments,
):
    half, full = jnp.bfloat16, jnp.float32
    gain_attn = gains[:D]
    gain_ffn = gains[D : 2 * D]
    gain_query = gains[2 * D : 2 * D + HEAD_DIM]
    gain_key = gains[2 * D + HEAD_DIM :]
    length, group = 512, 4
    tokens_wide = tokens.astype(full)
    normed = norm_rows(tokens_wide, gain_attn).astype(half)
    all_tok, all_wq, all_wo = exchange(
        attention_weights_kernel, 0,
        [(normed, False), (head_split(qkv_master.astype(half)), False), (out_master.astype(half), False)],
        [((2, 8, 64, D), half, False), ((8, 4, 64, 384), half, False), ((4, 64, D), half, False)],
        [], (23, 3), 16 << 20,
    )
    all_tok = all_tok.reshape(2, length, D)
    w_qkv = all_wq.reshape(D, 384)
    w_out = all_wo.reshape(256, D)

    places = jnp.arange(length, dtype=jnp.int32)
    docs, offsets = doc_tables(doc_starts, places)
    cos_table, sin_table = rotary(offsets)
    allowed = mask_of(docs, places, docs, places)[:, 0]
    projected = jnp.einsum("rtd,de->rte", all_tok, w_qkv, preferred_element_type=full)
    head_fn = partial(queries_keys, cos_table, sin_table, heads=group, kv_heads=1)
    queries, keys = head_fn(projected[..., :320], gain_query, gain_key)
    query16 = queries.astype(half)
    keys16 = keys.astype(half)[:, :, 0]
    values16 = projected[..., 320:].astype(half)
    scores = jnp.einsum("rqgh,rth->rgqt", query16, keys16, preferred_element_type=full)
    scores = jnp.where(allowed, scores, MASKED_SCORE)
    best = jnp.max(scores, axis=-1, keepdims=True)
    weights = jnp.where(allowed, jnp.exp(scores - best), 0.0)
    probs = weights / jnp.sum(weights, axis=-1, keepdims=True)
    probs16 = probs.astype(half)
    attended = jnp.einsum("rgqt,rth->rqgh", probs16, values16, preferred_element_type=full)
    attended16 = attended.astype(half).reshape(2, length, 256)
    branch = jnp.einsum("rtc,cd->rtd", attended16, w_out, preferred_element_type=full)

    hidden_in, all_norm, all_grad, all_wg, all_wd = exchange(
        ffn_weights_kernel, 1,
        [
            (branch.astype(half).reshape(2, 8, 64, D), True), (tokens, True), (gain_ffn[None], True),
            (ffn_split(gate_up_master.astype(half)), False), (down_master.astype(half), False),
            (grad_out.reshape(128, D), False),
        ],
        [
            ((2, 64, D), full, True), ((4, 2, 2, 64, D), half, False), ((4, 2, 128, D), half, False),
            ((4, 2, 4, 64, 2048), half, False), ((4, 256, D), half, False),
        ],
        [
            pltpu.VMEM((4, 2, 64, D), half), pltpu.VMEM((4, 2, 64, D), half),
            pltpu.VMEM((4, 2, 64, D), half), pltpu.VMEM((2, 64, D), half),
        ],
        (34, 4), 64 << 20,
    )
    hidden_in = hidden_in.reshape(128, D)
    normed2 = all_norm.reshape(1024, D)
    grad16 = all_grad.reshape(1024, D)
    w_gate_up = all_wg.reshape(D, 2048)
    w_down = all_wd.reshape(1024, D)
    gate_up = jnp.einsum("td,df->tf", normed2, w_gate_up, preferred_element_type=full)
    gate_part, up_part = gate_up[:, :1024], gate_up[:, 1024:]
    hidden = (jax.nn.silu(gate_part) * up_part).astype(half)
    out_part = jnp.einsum("tf,fd->td", hidden, w_down, preferred_element_type=full).astype(half)
    d_hidden = jnp.einsum("td,fd->tf", grad16, w_down, preferred_element_type=full)
    silu_value, silu_back = jax.vjp(jax.nn.silu, gate_part)
    d_gate = silu_back(d_hidden * up_part)[0]
    d_gate_up = jnp.concatenate([d_gate, d_hidden * silu_value], axis=-1).astype(half)
    d_normed2 = jnp.einsum("tf,df->td", d_gate_up, w_gate_up, preferred_element_type=full).astype(half)
    term_down = jnp.einsum("tf,td->fd", hidden, grad16, preferred_element_type=full).astype(half)
    term_gate_up = jnp.einsum("td,tf->df", normed2, d_gate_up, preferred_element_type=full).astype(half)

    line_scratch = [pltpu.VMEM((4, 128, D), half)] * 3
    all_branch, d_hidden_in, output, grad_gain_ffn, down_came = exchange(
        ffn_back_kernel, 2,
        [
            (d_normed2.reshape(4, 2, 128, D), True), (out_part.reshape(4, 2, 128, D), True),
            (term_down.reshape(4, 256, D), False), (hidden_in, True), (grad_out.reshape(128, D), True),
            (gain_ffn[None], True),
        ],
        [
            ((8, 128, D), half, False), ((128, D), full, True), ((128, D), half, True),
            ((1, D), full, True), ((4, 256, D), half, False),
        ],
        line_scratch * 2 + [pltpu.VMEM((128, D), half)],
        (24, 2), 32 << 20,
    )
    d_branch = all_branch.reshape(8, 2, 64, D).transpose(1, 0, 2, 3).reshape(2, length, D)
    term_out = jnp.einsum("rtc,rtd->cd", attended16, d_branch, preferred_element_type=full).astype(half)
    d_heads = jnp.einsum("rtd,cd->rtc", d_branch, w_out, preferred_element_type=full).astype(half)
    d_heads = d_heads.reshape(2, length, group, HEAD_DIM)
    delta = jnp.sum(d_heads.astype(full) * attended, axis=-1).transpose(0, 2, 1)
    d_values = jnp.einsum("rgqt,rqgh->rth", probs16, d_heads, preferred_element_type=full)
    d_probs = jnp.einsum("rqgh,rth->rgqt", d_heads, values16, preferred_element_type=full)
    d_scores = (probs * (d_probs - delta[..., None])).astype(half)
    d_queries = jnp.einsum("rgqt,rth->rqgh", d_scores, keys16, preferred_element_type=full)
    d_keys = jnp.einsum("rgqt,rqgh->rth", d_scores, query16, preferred_element_type=full)
    _, heads_back = jax.vjp(head_fn, projected[..., :320], gain_query, gain_key)
    d_heads_in, grad_gain_query, grad_gain_key = heads_back((d_queries, d_keys[:, :, None]))
    d_projected = jnp.concatenate([d_heads_in, d_values], axis=-1).astype(half)
    term_qkv = jnp.einsum("rtd,rte->de", all_tok, d_projected, preferred_element_type=full).astype(half)
    d_normed = jnp.einsum("rte,de->rtd", d_projected, w_qkv, preferred_element_type=full).astype(half)

    d_norm_came, gate_up_came, qkv_came, out_came = exchange(
        gradients_kernel, 3,
        [
            (d_normed.reshape(2, 8, 64, D), True), (term_gate_up.reshape(4, 2, 4, 64, 2048), True),
            (term_qkv.reshape(8, 4, 64, 384), True), (term_out.reshape(4, 64, D), False),
        ],
        [
            ((4, 2, 64, D), half, False), ((4, 2, 64, 2048), half, False),
            ((8, 64, 384), half, False), ((4, 64, D), half, False),
        ],
        [
            pltpu.VMEM((4, 2, 64, D), half), pltpu.VMEM((4, 2, 64, D), half),
            pltpu.VMEM((4, 2, 4, 64, 2048), half), pltpu.VMEM((2, 4, 64, 2048), half),
            pltpu.VMEM((4, 8, 64, 384), half), pltpu.VMEM((8, 64, 384), half),
        ],
        (30, 4), 48 << 20,
    )
    d_normed = jnp.sum(d_norm_came.astype(full), axis=0)
    _, attn_norm_back = jax.vjp(norm_rows, tokens_wide, gain_attn)
    d_tokens_part, grad_gain_attn = attn_norm_back(d_normed)
    grad_tokens = (d_hidden_in.reshape(2, 64, D) + d_tokens_part).astype(half)
    grads = (
        head_join(qkv_came).astype(full),
        jnp.sum(out_came.astype(full), axis=0),
        ffn_join(gate_up_came).astype(full),
        jnp.sum(down_came.astype(full), axis=0),
    )
    gain_local = jnp.concatenate([grad_gain_attn, grad_gain_ffn[0], grad_gain_query, grad_gain_key])
    updated = optimizer_step(
        grads, gain_local, (qkv_master, out_master, gate_up_master, down_master), gains,
        (qkv_rows, out_rows, gate_up_rows, down_rows), col_moments, gain_moments, total_of,
    )
    return (output.reshape(2, 64, D), grad_tokens, *grads, *updated)


def optimizer_step(
    grads, gain_local, masters, gains, row_states, col_moments, gain_moments, total_fn
):
    beta = 1.0 - STEP ** (-0.8)
    col_widths = (QKV, D, 2 * FF, D)
    row_totals = (D, HEADS * HEAD_DIM, D, FF)
    squares = [gradient * gradient + SQUARE_EPSILON for gradient in grads]
    rows_new = [
        beta * row_state + (1.0 - beta) * jnp.mean(square, axis=1)
        for row_state, square in zip(row_states, squares)
    ]
    col_local = [jnp.sum(square, axis=0) for square in squares]
    weighted_local = [
        jnp.sum(gradient * gradient / row_new[:, None], axis=0)
        for gradient, row_new in zip(grads, rows_new)
    ]
    stats_local = jnp.stack(
        [jnp.sum(row_new) for row_new in rows_new]
        + [jnp.sum(master * master) for master in masters]
    )
    totals = total_fn(jnp.concatenate(col_local + weighted_local + [stats_local, gain_local]))
    cols = sum(col_widths)
    col_sums, weighted = totals[:cols], totals[cols : 2 * cols]
    stats, grad_gains = totals[2 * cols : 2 * cols + 8], totals[2 * cols + 8 :]
    col_divisor = jnp.concatenate(
        [
            jnp.full((col_width,), float(row_total), jnp.float32)
            for col_width, row_total in zip(col_widths, row_totals)
        ]
    )
    cols_new = beta * col_moments + (1.0 - beta) * col_sums / col_divisor
    new_masters = []
    spreads = []
    begin_at = 0
    for slot in range(4):
        col_part = cols_new[begin_at : begin_at + col_widths[slot]]
        weighted_part = weighted[begin_at : begin_at + col_widths[slot]]
        begin_at = begin_at + col_widths[slot]
        mean_rows = stats[slot] / row_totals[slot]
        unit = (
            grads[slot]
            * lax.rsqrt(rows_new[slot] / mean_rows)[:, None]
            * lax.rsqrt(col_part)[None, :]
        )
        entries_all = float(row_totals[slot] * col_widths[slot])
        spread = jnp.sqrt(mean_rows * jnp.sum(weighted_part / col_part) / entries_all)
        scale = STEP_RATE * jnp.maximum(SCALE_EPSILON, jnp.sqrt(stats[4 + slot] / entries_all))
        new_masters.append(masters[slot] - scale * unit / jnp.maximum(1.0, spread / CLIP_LEVEL))
        spreads.append(spread)
    bounds = (0, D, 2 * D, 2 * D + HEAD_DIM, 2 * D + 2 * HEAD_DIM)
    moment_parts, gain_parts = ([], [])
    for segment in range(4):
        gradient = grad_gains[bounds[segment] : bounds[segment + 1]]
        gain_old = gains[bounds[segment] : bounds[segment + 1]]
        moment_new = beta * gain_moments[bounds[segment] : bounds[segment + 1]] + (1.0 - beta) * (
            gradient * gradient + SQUARE_EPSILON
        )
        unit = gradient * lax.rsqrt(moment_new)
        spread = jnp.sqrt(jnp.mean(unit * unit))
        scale = STEP_RATE * jnp.maximum(SCALE_EPSILON, jnp.sqrt(jnp.mean(gain_old * gain_old)))
        moment_parts.append(moment_new)
        gain_parts.append(gain_old - scale * unit / jnp.maximum(1.0, spread / CLIP_LEVEL))
        spreads.append(spread)
    return (
        grad_gains,
        *rows_new,
        cols_new,
        jnp.concatenate(moment_parts),
        *new_masters,
        *[master.astype(jnp.bfloat16) for master in new_masters],
        jnp.concatenate(gain_parts),
        jnp.stack(spreads),
    )


def solution(mesh):
    split = mesh.shape["seq"] == 8 and mesh.shape["rows"] == 4
    return jax.shard_map(
        split_local if split else gathered_local,
        mesh=mesh,
        in_specs=(
            P("rows", "seq", None),
            P("rows", None),
            P("rows", "seq", None),
            P(("seq", "rows"), None),
            P(("seq", "rows"), None),
            P(("seq", "rows"), None),
            P(("seq", "rows"), None),
            P(),
            P(("seq", "rows")),
            P(("seq", "rows")),
            P(("seq", "rows")),
            P(("seq", "rows")),
            P(),
            P(),
        ),
        out_specs=(
            P("rows", "seq", None),
            P("rows", "seq", None),
            P(("seq", "rows"), None),
            P(("seq", "rows"), None),
            P(("seq", "rows"), None),
            P(("seq", "rows"), None),
            P(),
            P(("seq", "rows")),
            P(("seq", "rows")),
            P(("seq", "rows")),
            P(("seq", "rows")),
            P(),
            P(),
            P(("seq", "rows"), None),
            P(("seq", "rows"), None),
            P(("seq", "rows"), None),
            P(("seq", "rows"), None),
            P(("seq", "rows"), None),
            P(("seq", "rows"), None),
            P(("seq", "rows"), None),
            P(("seq", "rows"), None),
            P(),
            P(),
        ),
        check_vma=False,
    )
```

```python
from functools import partial

import jax
import jax.numpy as jnp
from jax import lax
from jax.experimental import pallas as pl
from jax.experimental.pallas import tpu as pltpu
from jax.sharding import PartitionSpec as P

D = 2048
HEADS = 32
KV_HEADS = 8
HEAD_DIM = 64
FF = 8192
STEP = 10
QKV = 3072


EPSILON = 1e-06
ROPE_BASE = 10000.0
MASKED_SCORE = -1e30
STEP_RATE = 0.3
CLIP_LEVEL = 1.0
SQUARE_EPSILON = 1e-30
SCALE_EPSILON = 0.001


def from_behind(value, axis, steps):
    count = lax.axis_size(axis)
    pairs = [(source, (source + steps) % count) for source in range(count)]
    return lax.ppermute(value, axis, pairs)


def norm_rows(entries, gain):
    return entries * lax.rsqrt(jnp.mean(entries * entries, axis=-1, keepdims=True) + EPSILON) * gain


def turn(entries, cos_wide, sin_wide):
    half_width = entries.shape[-1] // 2
    turned = jnp.concatenate([-entries[..., half_width:], entries[..., :half_width]], axis=-1)
    return entries * cos_wide + turned * sin_wide


def doc_tables(doc_starts, places):
    before = doc_starts[:, None, :] <= places[None, :, None]
    doc_ids = jnp.sum(before.astype(jnp.int32), axis=-1)
    doc_first = jnp.max(jnp.where(before, doc_starts[:, None, :], 0), axis=-1)
    return (doc_ids, places[None, :] - doc_first)


def rotary(offsets):
    frequency = ROPE_BASE ** (-(jnp.arange(HEAD_DIM // 2, dtype=jnp.float32) * 2.0 / HEAD_DIM))
    angles = offsets.astype(jnp.float32)[..., None] * frequency
    cos_table = jnp.concatenate([jnp.cos(angles), jnp.cos(angles)], axis=-1)
    sin_table = jnp.concatenate([jnp.sin(angles), jnp.sin(angles)], axis=-1)
    return (cos_table, sin_table)


def queries_keys(
    cos_table, sin_table, projected, gain_query, gain_key, heads=HEADS, kv_heads=KV_HEADS
):
    rows_here, seq_here = (projected.shape[0], projected.shape[1])
    att_width = heads * HEAD_DIM
    queries = projected[..., :att_width].reshape(rows_here, seq_here, heads, HEAD_DIM)
    keys_rot = projected[..., att_width : att_width + kv_heads * HEAD_DIM].reshape(
        rows_here, seq_here, kv_heads, HEAD_DIM
    )
    cos_wide = cos_table[:, :, None, :]
    sin_wide = sin_table[:, :, None, :]
    queries = turn(norm_rows(queries, gain_query), cos_wide, sin_wide) * HEAD_DIM ** (-0.5)
    keys_rot = turn(norm_rows(keys_rot, gain_key), cos_wide, sin_wide)
    return (queries, keys_rot)


def mask_of(query_docs, query_places, key_docs, key_places):
    same_doc = query_docs[:, :, None] == key_docs[:, None, :]
    causal = query_places[None, :, None] >= key_places[None, None, :]
    return (same_doc & causal)[:, None, None, :, :]


def gathered_local(
    tokens,
    doc_starts,
    grad_out,
    qkv_master,
    out_master,
    gate_up_master,
    down_master,
    gains,
    qkv_rows,
    out_rows,
    gate_up_rows,
    down_rows,
    col_moments,
    gain_moments,
):
    cycle_size = lax.axis_size("seq")
    seq_index = lax.axis_index("seq")
    rows_dev, seq_dev = (tokens.shape[0], tokens.shape[1])
    group_size = HEADS // KV_HEADS
    att_width = HEADS * HEAD_DIM
    kv_width = KV_HEADS * HEAD_DIM
    gain_attn = gains[:D]
    gain_ffn = gains[D : 2 * D]
    gain_query = gains[2 * D : 2 * D + HEAD_DIM]
    gain_key = gains[2 * D + HEAD_DIM :]
    local_places = jnp.arange(seq_dev, dtype=jnp.int32)
    places = seq_index * seq_dev + local_places
    query_docs, offsets = doc_tables(doc_starts, places)
    cos_table, sin_table = rotary(offsets)
    copies = (
        qkv_master.astype(jnp.bfloat16),
        out_master.astype(jnp.bfloat16),
        gate_up_master.astype(jnp.bfloat16),
        down_master.astype(jnp.bfloat16),
    )
    w_qkv, w_out, w_gate_up, w_down = (
        lax.all_gather(copies[0], ("seq", "rows"), axis=0, tiled=True),
        lax.all_gather(copies[1], ("seq", "rows"), axis=0, tiled=True),
        lax.all_gather(copies[2], ("seq", "rows"), axis=0, tiled=True),
        lax.all_gather(copies[3], ("seq", "rows"), axis=0, tiled=True),
    )
    tokens_wide = tokens.astype(jnp.float32)
    normed = norm_rows(tokens_wide, gain_attn).astype(jnp.bfloat16)
    projected = jnp.einsum("rtd,de->rte", normed, w_qkv, preferred_element_type=jnp.float32)
    head_fn = partial(queries_keys, cos_table, sin_table)
    queries, keys_rot = head_fn(projected, gain_query, gain_key)
    query16 = queries.astype(jnp.bfloat16).reshape(
        rows_dev, seq_dev, KV_HEADS, group_size, HEAD_DIM
    )
    keys16 = keys_rot.astype(jnp.bfloat16).reshape(rows_dev, seq_dev, kv_width)
    values16 = projected[..., att_width + kv_width :].astype(jnp.bfloat16)
    stat_shape = (rows_dev, KV_HEADS, group_size, seq_dev)
    initial = (
        jnp.full(stat_shape, MASKED_SCORE, jnp.float32),
        jnp.zeros(stat_shape, jnp.float32),
        jnp.zeros(stat_shape + (HEAD_DIM,), jnp.float32),
    )
    carry = initial
    key_piece = lax.all_gather(keys16, "seq", axis=1, tiled=True)
    value_piece = lax.all_gather(values16, "seq", axis=1, tiled=True)
    key_count = key_piece.shape[1]

    def absorb_block(state, block_index):
        best, total, summed = state
        block_begin = block_index * seq_dev
        key_block = lax.dynamic_slice_in_dim(key_piece, block_begin, seq_dev, 1).reshape(
            rows_dev, seq_dev, KV_HEADS, HEAD_DIM
        )
        value_block = lax.dynamic_slice_in_dim(value_piece, block_begin, seq_dev, 1).reshape(
            rows_dev, seq_dev, KV_HEADS, HEAD_DIM
        )
        key_places = block_begin + jnp.arange(seq_dev, dtype=jnp.int32)
        key_docs, _ = doc_tables(doc_starts, key_places)
        allowed = mask_of(query_docs, places, key_docs, key_places)
        scores = jnp.einsum(
            "rqkgh,rtkh->rkgqt", query16, key_block, preferred_element_type=jnp.float32
        )
        scores = jnp.where(allowed, scores, MASKED_SCORE)
        best_new = jnp.maximum(best, jnp.max(scores, axis=-1))
        weights = jnp.where(allowed, jnp.exp(scores - best_new[..., None]), 0.0)
        factor = jnp.exp(best - best_new)
        total = total * factor + jnp.sum(weights, axis=-1)
        summed = summed * factor[..., None] + jnp.einsum(
            "rkgqt,rtkh->rkgqh",
            weights.astype(jnp.bfloat16),
            value_block,
            preferred_element_type=jnp.float32,
        )
        return ((best_new, total, summed), None)

    carry, _ = lax.scan(absorb_block, carry, jnp.arange(key_count // seq_dev, dtype=jnp.int32))
    best, total, summed = carry
    log_total = best + jnp.log(total)
    attended = summed / total[..., None]
    attended16 = (
        attended.transpose(0, 3, 1, 2, 4).reshape(rows_dev, seq_dev, att_width).astype(jnp.bfloat16)
    )
    branch = jnp.einsum("rtc,cd->rtd", attended16, w_out, preferred_element_type=jnp.float32)
    hidden_in = tokens_wide + branch
    normed2 = norm_rows(hidden_in, gain_ffn).astype(jnp.bfloat16)
    gate_up = jnp.einsum("rtd,df->rtf", normed2, w_gate_up, preferred_element_type=jnp.float32)
    gate_part, up_part = (gate_up[..., :FF], gate_up[..., FF:])
    hidden = (jax.nn.silu(gate_part) * up_part).astype(jnp.bfloat16)
    output = hidden_in + jnp.einsum(
        "rtf,fd->rtd", hidden, w_down, preferred_element_type=jnp.float32
    )
    d_hidden = jnp.einsum("rtd,fd->rtf", grad_out, w_down, preferred_element_type=jnp.float32)
    silu_value, silu_back = jax.vjp(jax.nn.silu, gate_part)
    d_gate = silu_back(d_hidden * up_part)[0]
    d_gate_up = jnp.concatenate([d_gate, d_hidden * silu_value], axis=-1).astype(jnp.bfloat16)
    d_normed2 = jnp.einsum("rtf,df->rtd", d_gate_up, w_gate_up, preferred_element_type=jnp.float32)
    _, ffn_norm_back = jax.vjp(norm_rows, hidden_in, gain_ffn)
    d_inner, grad_gain_ffn = ffn_norm_back(d_normed2)
    d_hidden_in = grad_out.astype(jnp.float32) + d_inner
    term_down = jnp.einsum("rtf,rtd->fd", hidden, grad_out, preferred_element_type=jnp.float32)
    grad_down = lax.psum_scatter(term_down, ("seq", "rows"), scatter_dimension=0, tiled=True)
    term_gate_up = jnp.einsum("rtd,rtf->df", normed2, d_gate_up, preferred_element_type=jnp.float32)
    grad_gate_up = lax.psum_scatter(term_gate_up, ("seq", "rows"), scatter_dimension=0, tiled=True)
    d_branch = d_hidden_in.astype(jnp.bfloat16)
    term_out = jnp.einsum("rtc,rtd->cd", attended16, d_branch, preferred_element_type=jnp.float32)
    d_attended = jnp.einsum(
        "rtd,cd->rtc", d_branch, w_out, preferred_element_type=jnp.float32
    ).astype(jnp.bfloat16)
    d_heads = d_attended.reshape(rows_dev, seq_dev, KV_HEADS, group_size, HEAD_DIM).transpose(
        0, 2, 3, 1, 4
    )
    delta = jnp.sum(d_heads.astype(jnp.float32) * attended, axis=-1)

    def cycle_turn(turn_index, carry):
        pair16, grad_pair, d_queries = carry
        source = (seq_index + turn_index) % cycle_size
        key_places = source * seq_dev + local_places
        key_docs, _ = doc_tables(doc_starts, key_places)
        allowed = mask_of(query_docs, places, key_docs, key_places)
        key_block = pair16[0].reshape(rows_dev, seq_dev, KV_HEADS, HEAD_DIM)
        value_block = pair16[1].reshape(rows_dev, seq_dev, KV_HEADS, HEAD_DIM)
        scores = jnp.einsum(
            "rqkgh,rtkh->rkgqt", query16, key_block, preferred_element_type=jnp.float32
        )
        scores = jnp.where(allowed, scores, MASKED_SCORE)
        probs = jnp.where(allowed, jnp.exp(scores - log_total[..., None]), 0.0)
        d_values = jnp.einsum(
            "rkgqt,rkgqh->rtkh",
            probs.astype(jnp.bfloat16),
            d_heads,
            preferred_element_type=jnp.float32,
        )
        d_probs = jnp.einsum(
            "rkgqh,rtkh->rkgqt", d_heads, value_block, preferred_element_type=jnp.float32
        )
        d_scores = (probs * (d_probs - delta[..., None])).astype(jnp.bfloat16)
        d_queries = d_queries + jnp.einsum(
            "rkgqt,rtkh->rkgqh", d_scores, key_block, preferred_element_type=jnp.float32
        )
        d_keys = jnp.einsum(
            "rkgqt,rqkgh->rtkh", d_scores, query16, preferred_element_type=jnp.float32
        )
        grad_pair = grad_pair + jnp.stack(
            [
                d_keys.reshape(rows_dev, seq_dev, kv_width),
                d_values.reshape(rows_dev, seq_dev, kv_width),
            ]
        )
        grad_pair = from_behind(grad_pair.astype(jnp.bfloat16), "seq", -1).astype(grad_pair.dtype)
        pair16 = from_behind(pair16, "seq", -1)
        return (pair16, grad_pair, d_queries)

    start_pair = jnp.stack([keys16, values16])
    start_grads = jnp.zeros((2, rows_dev, seq_dev, kv_width), jnp.float32)
    start_queries = jnp.zeros(stat_shape + (HEAD_DIM,), jnp.float32)
    _, grad_pair, d_queries = lax.fori_loop(
        0, cycle_size, cycle_turn, (start_pair, start_grads, start_queries)
    )
    d_queries = d_queries.transpose(0, 3, 1, 2, 4).reshape(rows_dev, seq_dev, HEADS, HEAD_DIM)
    d_keys_home = grad_pair[0].reshape(rows_dev, seq_dev, KV_HEADS, HEAD_DIM)
    _, heads_back = jax.vjp(head_fn, projected, gain_query, gain_key)
    d_projected, grad_gain_query, grad_gain_key = heads_back((d_queries, d_keys_home))
    d_projected = jnp.concatenate(
        [d_projected[..., : att_width + kv_width], grad_pair[1]], axis=-1
    ).astype(jnp.bfloat16)
    term_qkv = jnp.einsum("rtd,rte->de", normed, d_projected, preferred_element_type=jnp.float32)
    d_normed = jnp.einsum("rte,de->rtd", d_projected, w_qkv, preferred_element_type=jnp.float32)
    _, attn_norm_back = jax.vjp(norm_rows, tokens_wide, gain_attn)
    d_tokens_part, grad_gain_attn = attn_norm_back(d_normed)
    grad_tokens = (d_hidden_in + d_tokens_part).astype(jnp.bfloat16)
    grad_qkv, grad_out_proj = (
        lax.psum_scatter(term_qkv, ("seq", "rows"), scatter_dimension=0, tiled=True),
        lax.psum_scatter(term_out, ("seq", "rows"), scatter_dimension=0, tiled=True),
    )
    gain_local = jnp.concatenate([grad_gain_attn, grad_gain_ffn, grad_gain_query, grad_gain_key])
    grads = (grad_qkv, grad_out_proj, grad_gate_up, grad_down)
    updated = optimizer_step(
        grads, gain_local, (qkv_master, out_master, gate_up_master, down_master), gains,
        (qkv_rows, out_rows, gate_up_rows, down_rows), col_moments, gain_moments,
        lambda vector: lax.psum(vector, ("seq", "rows")),
    )
    return (output.astype(jnp.bfloat16), grad_tokens, *grads, *updated)


MESH = pl.DeviceIdType.MESH
PLACES = 32
VMEM_BYTES = 56 * 1024 * 1024
CHUNK = 16


def here():
    seq = lax.axis_index("seq")
    return lax.div(seq, 2), lax.rem(seq, 2), lax.axis_index("rows")


def flips(chip):
    return (chip + 1 - 2 * lax.rem(chip, 2), lax.rem(chip + 2, 4), 3 - chip)


def ahead(z, step):
    return lax.rem(z + step, 4)


def at_place(chip, core, z):
    return (2 * chip + core, z)


def greet(peers):
    barrier = pltpu.get_barrier_semaphore()
    for peer in peers:
        pl.semaphore_signal(barrier, inc=1, device_id=peer, device_id_type=MESH)
    pl.semaphore_wait(barrier, len(peers))


class Mover:
    def __init__(self, send_sem, recv_sem, local_sem):
        self.send_sem, self.recv_sem, self.local_sem = send_sem, recv_sem, local_sem
        self.remote, self.own = [], []

    def send(self, src, dst, peer):
        slot = len(self.remote)
        copy = pltpu.make_async_remote_copy(
            src_ref=src,
            dst_ref=dst,
            send_sem=self.send_sem.at[slot],
            recv_sem=self.recv_sem.at[slot],
            device_id=peer,
            device_id_type=MESH,
        )
        copy.start()
        handle = [copy, False, copy.wait_recv]
        self.remote.append(handle)
        return handle

    def send_parts(self, pairs, whole, peer):
        slot = len(self.remote)

        def copy_of(src, dst):
            return pltpu.make_async_remote_copy(
                src_ref=src,
                dst_ref=dst,
                send_sem=self.send_sem.at[slot],
                recv_sem=self.recv_sem.at[slot],
                device_id=peer,
                device_id_type=MESH,
            )

        for src, dst in pairs:
            copy_of(src, dst).start()
        copy = copy_of(whole, whole)
        handle = [copy, False, copy.wait_recv]
        self.remote.append(handle)
        return handle

    def keep_parts(self, pairs, whole):
        sem = self.local_sem.at[len(self.own)]
        for src, dst in pairs:
            pltpu.make_async_copy(src, dst, sem).start()
        copy = pltpu.make_async_copy(whole, whole, sem)
        handle = [copy, False, copy.wait]
        self.own.append(handle)
        return handle

    def keep(self, src, dst):
        copy = pltpu.make_async_copy(src, dst, self.local_sem.at[len(self.own)])
        copy.start()
        handle = [copy, False, copy.wait]
        self.own.append(handle)
        return handle

    def arrive(self, *handles):
        for handle in handles:
            if not handle[1]:
                handle[1] = True
                handle[2]()

    def finish(self):
        self.arrive(*self.own, *self.remote)
        for handle in self.remote:
            handle[0].wait_send()


def semaphores(remote, own):
    return [
        pltpu.SemaphoreType.DMA((remote,)),
        pltpu.SemaphoreType.DMA((remote,)),
        pltpu.SemaphoreType.DMA((max(own, 1),)),
    ]


def exchange(kernel, ident, inputs, outputs, scratch, copies, moved):
    vmem, anywhere = pl.BlockSpec(memory_space=pltpu.VMEM), pl.BlockSpec(memory_space=pl.ANY)
    return pl.pallas_call(
        kernel,
        out_shape=[jax.ShapeDtypeStruct(shape, kind) for shape, kind, _ in outputs],
        in_specs=[vmem if near else anywhere for _, near in inputs],
        out_specs=[vmem if near else anywhere for _, _, near in outputs],
        scratch_shapes=scratch + semaphores(*copies),
        compiler_params=pltpu.CompilerParams(
            collective_id=ident, has_side_effects=True, vmem_limit_bytes=VMEM_BYTES
        ),
        cost_estimate=pl.CostEstimate(flops=0, bytes_accessed=moved, transcendentals=0),
    )(*[array for array, _ in inputs])


def chunks(length, body):
    @pl.loop(0, length // CHUNK)
    def _(step):
        body(pl.ds(pl.multiple_of(step * CHUNK, CHUNK), CHUNK))


def segments(core, z):
    for part in range(2):
        for chip in range(4):
            start = part * FF + ((2 * chip + core) * 4 + z) * 256
            yield pl.ds(pl.multiple_of(start, 256), 256), pl.ds(part * 1024 + chip * 256, 256)


def attention_weights_kernel(tok, wq, wo, wd, all_tok, all_wq, all_wo, all_wd, *sems):
    chip, core, z = here()
    others = flips(chip)
    other = 1 - core
    plane = [at_place(chip, other, z)]
    for peer_chip in others:
        plane += [at_place(peer_chip, core, z), at_place(peer_chip, other, z)]
    along = [at_place(chip, core, ahead(z, step)) for step in (2, 1, 3)]
    greet(plane + along)
    move = Mover(*sems)
    me = 2 * chip + core
    for peer in along:
        move.send(wo, all_wo.at[z], peer)
    parts = [move.keep(wq.at[me], all_wq.at[me, z])]
    for peer in plane:
        parts.append(move.send(wq.at[peer[0]], all_wq.at[me, z], peer))
    came = []
    for peer_chip in others:
        came.append(move.send(tok, all_tok.at[:, me], at_place(peer_chip, core, z)))
    partner = at_place(chip, other, z)
    move.send(tok, all_tok.at[:, me], partner)
    for peer_chip in others:
        move.send(wd, all_wd.at[chip], at_place(peer_chip, core, z))
    move.keep(tok, all_tok.at[:, me])
    move.keep(wo, all_wo.at[z])
    move.keep(wd, all_wd.at[chip])
    move.arrive(*parts)
    for peer in along:
        move.send(all_wq.at[:, z], all_wq.at[:, z], peer)
    for peer_chip, handle in zip(others, came):
        move.arrive(handle)
        block = all_tok.at[:, 2 * peer_chip + core]
        move.send(block, block, partner)
    move.finish()


def add_blocks(first, second, result):
    for row in range(2):

        def body(part):
            total = first[row, part].astype(jnp.float32) + second[row, part].astype(jnp.float32)
            result[row, part] = total.astype(result.dtype)

        chunks(64, body)


def add_flat(first, second, result):
    def body(part):
        total = first[part].astype(jnp.float32) + second[part].astype(jnp.float32)
        result[part] = total.astype(result.dtype)

    chunks(128, body)


def ffn_weights_kernel(
    branch, tok, gain, wg, grad_out,
    hidden_in, all_norm, all_out, all_wg,
    from_partner, came, normed, *sems,
):
    chip, core, z = here()
    others = flips(chip)
    other = 1 - core
    partner = at_place(chip, other, z)
    plane = [at_place(peer_chip, core, z) for peer_chip in others]
    steps = (2, 1, 3)
    line = [at_place(chip, core, ahead(z, step)) for step in steps]
    cross = [at_place(chip, other, ahead(z, step)) for step in steps]
    greet([partner] + plane + line + cross)
    move = Mover(*sems)
    order = tuple(others) + (chip,)
    halves = [
        move.send(branch.at[:, 2 * to + other], from_partner.at[to], partner) for to in order
    ]

    def turn_block(to_core, to_z):
        whole = all_wg.at[chip, core, z]
        return [(wg.at[:, src], whole.at[:, dst]) for src, dst in segments(to_core, to_z)], whole

    turned = [[move.keep_parts(*turn_block(core, z))], []]
    turned[1].append(move.send_parts(*turn_block(other, z), partner))
    for step, peer, peer_cross in zip(steps, line, cross):
        to = ahead(z, step)
        turned[0].append(move.send_parts(*turn_block(core, to), peer))
        turned[1].append(move.send_parts(*turn_block(other, to), peer_cross))
    shared = []
    for step, peer in zip(steps, line):
        shared.append((move.send(grad_out, all_out.at[z, core], peer), step))
    move.send(grad_out, all_out.at[z, core], partner)
    move.keep(grad_out, all_out.at[z, core])
    sums = []
    for to, half, peer in zip(others, halves, plane):
        move.arrive(half)
        add_blocks(branch.at[:, 2 * to + core], from_partner.at[to], from_partner.at[to])
        sums.append(move.send(from_partner.at[to], came.at[chip], peer))
    move.arrive(halves[3], *sums)
    for row in range(2):

        def body(part):
            total = tok[row, part].astype(jnp.float32)
            total += branch[row, 2 * chip + core, part].astype(jnp.float32)
            total += from_partner[chip, row, part].astype(jnp.float32)
            for peer_chip in others:
                total += came[peer_chip, row, part].astype(jnp.float32)
            hidden_in[row, part] = total
            scale = lax.rsqrt(jnp.mean(total * total, axis=-1, keepdims=True) + EPSILON)
            normed[row, part] = (total * scale * gain[...]).astype(jnp.bfloat16)

        chunks(64, body)
    for step, peer in zip(steps, line):
        shared.append((move.send(normed, all_norm.at[z, core], peer), step))
    move.send(normed, all_norm.at[z, core], partner)
    move.keep(normed, all_norm.at[z, core])
    move.arrive(*turned[0], *turned[1])
    by_x, by_y = plane[0], plane[1]
    first, second = all_wg.at[chip, 0], all_wg.at[chip, 1]
    from_x = move.send(first, first, by_x)
    from_y = move.send(second, second, by_y)
    move.send(second, second, by_x)
    move.send(first, first, by_y)
    for index, (handle, step) in enumerate(shared):
        if index == 3:
            move.arrive(from_x, from_y)
            first, second = all_wg.at[others[0], 0], all_wg.at[others[1], 1]
            move.send(first, first, by_y)
            move.send(second, second, by_x)
        move.arrive(handle)
        target = all_out if index < 3 else all_norm
        block = target.at[ahead(z, 4 - step), core]
        move.send(block, block, partner)
    move.finish()


def line_sums(move, partial, from_partner, summed, came, partner, line, steps, core, z):
    other = 1 - core
    halves = [
        move.send(partial.at[ahead(z, step), other], from_partner.at[ahead(z, step)], partner)
        for step in steps + (0,)
    ]
    sums = []
    for step, half, peer in zip(steps, halves, line):
        to = ahead(z, step)
        move.arrive(half)
        add_flat(partial.at[to, core], from_partner.at[to], summed.at[to])
        sums.append(move.send(summed.at[to], came.at[z], peer))
    return sums + [halves[3]]


def ffn_back_kernel(
    d_norm, out_part, down_part, hidden_in, grad_out, gain,
    all_branch, d_hidden_in, out_sum, gain_part, down_came,
    from_partner, summed, came, from_partner2, summed2, came2, d_branch, *sems,
):
    chip, core, z = here()
    others = flips(chip)
    other = 1 - core
    partner = at_place(chip, other, z)
    plane = [at_place(peer_chip, core, z) for peer_chip in others]
    steps = (2, 1, 3)
    line = [at_place(chip, core, ahead(z, step)) for step in steps]
    greet([partner] + plane + line)
    move = Mover(*sems)
    first = line_sums(move, d_norm, from_partner, summed, came, partner, line, steps, core, z)
    for to, peer in zip(others, plane):
        move.send(down_part.at[to], down_came.at[chip], peer)
    move.keep(down_part.at[chip], down_came.at[chip])
    move.arrive(*first)
    gain_part[...] = jnp.zeros_like(gain_part)

    def body(part):
        total = d_norm[z, core, part].astype(jnp.float32)
        total += from_partner[z, part].astype(jnp.float32)
        for step in steps:
            total += came[ahead(z, step), part].astype(jnp.float32)
        entries = hidden_in[part]
        scale = lax.rsqrt(jnp.mean(entries * entries, axis=-1, keepdims=True) + EPSILON)
        gain_part[...] += jnp.sum(total * entries * scale, axis=0, keepdims=True)
        total = total * gain[...]
        inner = jnp.mean(total * entries, axis=-1, keepdims=True) * (scale * scale * scale)
        grad = grad_out[part].astype(jnp.float32) + total * scale - entries * inner
        d_hidden_in[part] = grad
        d_branch[part] = grad.astype(jnp.bfloat16)

    chunks(128, body)
    me = 2 * chip + core
    shared = [move.send(d_branch, all_branch.at[me], peer) for peer in plane]
    move.send(d_branch, all_branch.at[me], partner)
    move.keep(d_branch, all_branch.at[me])
    second = line_sums(
        move, out_part, from_partner2, summed2, came2, partner, line, steps, core, z
    )
    for peer_chip, handle in zip(others, shared):
        move.arrive(handle)
        block = all_branch.at[2 * peer_chip + core]
        move.send(block, block, partner)
    move.arrive(*second)

    def body2(part):
        total = out_part[z, core, part].astype(jnp.float32)
        total += from_partner2[z, part].astype(jnp.float32)
        total += hidden_in[part]
        for step in steps:
            total += came2[ahead(z, step), part].astype(jnp.float32)
        out_sum[part] = total.astype(jnp.bfloat16)

    chunks(128, body2)
    move.finish()


def gradients_kernel(
    d_norm, gate_up_part, qkv_part, out_part,
    d_norm_came, gate_up_came, qkv_came, out_came,
    from_partner, summed, gate_up_in, gate_up_sum, qkv_in, qkv_sum, *sems,
):
    chip, core, z = here()
    others = flips(chip)
    other = 1 - core
    me = 2 * chip + core
    partner = at_place(chip, other, z)
    plane = [at_place(peer_chip, core, z) for peer_chip in others]
    plane_cross = [at_place(peer_chip, other, z) for peer_chip in others]
    steps = (2, 1, 3)
    line = [at_place(chip, core, ahead(z, step)) for step in steps]
    cross = [at_place(chip, other, ahead(z, step)) for step in steps]
    greet([partner] + plane + plane_cross + line + cross)
    move = Mover(*sems)
    pieces = [
        move.send(gate_up_part.at[to], gate_up_in.at[chip], peer)
        for to, peer in zip(others, plane)
    ]
    order = tuple(others) + (chip,)
    halves = [
        move.send(d_norm.at[:, 2 * to + other], from_partner.at[to], partner) for to in order
    ]
    qkv_pieces = []
    for step, peer in zip(steps, line):
        qkv_pieces.append(move.send(qkv_part.at[:, ahead(z, step)], qkv_in.at[z], peer))
        move.send(out_part.at[ahead(z, step)], out_came.at[z], peer)
    move.keep(out_part.at[z], out_came.at[z])
    for to, half in zip(order, halves):
        move.arrive(half)
        add_blocks(d_norm.at[:, 2 * to + core], from_partner.at[to], summed.at[to])
    for to, peer in zip(others, plane):
        move.send(summed.at[to], d_norm_came.at[chip], peer)
    move.keep(summed.at[chip], d_norm_came.at[chip])
    move.arrive(*qkv_pieces)

    @pl.loop(0, 8)
    def _(block):
        def body(part):
            total = qkv_part[block, z, part].astype(jnp.float32)
            for step in steps:
                total += qkv_in[ahead(z, step), block, part].astype(jnp.float32)
            qkv_sum[block, part] = total.astype(jnp.bfloat16)

        chunks(64, body)

    for peer in [partner] + plane + plane_cross:
        move.send(qkv_sum.at[peer[0]], qkv_came.at[me], peer)
    move.keep(qkv_sum.at[me], qkv_came.at[me])
    move.arrive(*pieces)

    @pl.loop(0, 8)
    def _(block):
        to_core, to_z = lax.div(block, 4), lax.rem(block, 4)

        def body(part):
            total = gate_up_part[chip, to_core, to_z, part].astype(jnp.float32)
            for peer_chip in others:
                total += gate_up_in[peer_chip, to_core, to_z, part].astype(jnp.float32)
            gate_up_sum[to_core, to_z, part] = total.astype(jnp.bfloat16)

        chunks(64, body)

    def turn_block(to_core, to_z):
        whole = gate_up_sum.at[to_core, to_z]
        return [
            (whole.at[:, src], gate_up_came.at[:, dst]) for dst, src in segments(core, z)
        ], whole

    for step, peer, peer_cross in zip(steps, line, cross):
        to = ahead(z, step)
        move.send_parts(*turn_block(core, to), peer)
        move.send_parts(*turn_block(other, to), peer_cross)
    move.send_parts(*turn_block(other, z), partner)
    move.keep_parts(*turn_block(core, z))
    move.finish()


COL_ROWS, GAIN_ROWS = 184, 33
MATRICES = ((64, QKV, 0, 0), (64, D, 64, 24), (64, 2 * FF, 128, 40), (256, D, 192, 168))
ROW_TOTALS = (D, HEADS * HEAD_DIM, D, FF)
BETA = 1.0 - STEP ** (-0.8)


def lane_value(vector, lane):
    lanes = lax.broadcasted_iota(jnp.int32, (1, 128), 1)
    return jnp.sum(jnp.where(lanes == lane, vector, 0.0), axis=-1, keepdims=True)


def statistics_kernel(
    d_norm, tok, d_hidden_in, gain, gain_ffn, gain_qk, qkv, out, gate_up, down, rows,
    m_qkv, m_out, m_gate_up, m_down,
    grad_tok, g_qkv, g_out, g_gate_up, g_down, rows_new, packed,
    gain_part, sums, inverse,
):
    gain_part[...] = jnp.zeros_like(gain_part)

    @pl.loop(0, 128 // CHUNK)
    def _(step):
        part = pl.ds(pl.multiple_of(step * CHUNK, CHUNK), CHUNK)
        total = d_norm[0, part].astype(jnp.float32)
        for slot in range(1, 4):
            total += d_norm[slot, part].astype(jnp.float32)
        entries = tok[part].astype(jnp.float32)
        scale = lax.rsqrt(jnp.mean(entries * entries, axis=-1, keepdims=True) + EPSILON)
        gain_part[...] += jnp.sum(total * entries * scale, axis=0, keepdims=True)
        total = total * gain[...]
        inner = jnp.mean(total * entries, axis=-1, keepdims=True) * (scale * scale * scale)
        grad_tok[part] = (d_hidden_in[part] + total * scale - entries * inner).astype(jnp.bfloat16)

    first = 2 * COL_ROWS
    for slot in range(16):
        lanes = pl.ds(slot * 128, 128)
        packed[first + slot : first + slot + 1] = gain_part[:, lanes]
        packed[first + 16 + slot : first + 17 + slot] = gain_ffn[:, lanes]
    packed[first + 32 : first + 33] = gain_qk[...]
    lane = lax.broadcasted_iota(jnp.int32, (64, 128), 1)

    def wide(step):
        return pl.ds(pl.multiple_of(step * 128, 128), 128)

    def read_qkv(step):
        return g_qkv[:, wide(step)]

    for head in range(8):
        for half in range(2):
            g_qkv[:, pl.ds(head * 256 + half * 128, 128)] = qkv[
                head, :, pl.ds(half * 128, 128)
            ].astype(jnp.float32)
    for pair in range(4):
        low = qkv[2 * pair, :, pl.ds(256, 128)].astype(jnp.float32)
        high = qkv[2 * pair + 1, :, pl.ds(256, 128)].astype(jnp.float32)
        g_qkv[:, pl.ds(2048 + pair * 128, 128)] = jnp.where(lane < 64, low, pltpu.roll(high, 64, 1))
        g_qkv[:, pl.ds(2560 + pair * 128, 128)] = jnp.where(lane < 64, pltpu.roll(low, 64, 1), high)

    def read_out(step):
        total = out[0, :, wide(step)].astype(jnp.float32)
        for slot in range(1, 4):
            total += out[slot, :, wide(step)].astype(jnp.float32)
        return total

    def read_gate_up(step):
        return gate_up[:, wide(step)].astype(jnp.float32)

    def read_down(step):
        total = down[0, :, wide(step)].astype(jnp.float32)
        for slot in range(1, 4):
            total += down[slot, :, wide(step)].astype(jnp.float32)
        return total

    readers = (read_qkv, read_out, read_gate_up, read_down)
    grads = (g_qkv, g_out, g_gate_up, g_down)
    masters = (m_qkv, m_out, m_gate_up, m_down)
    stats = jnp.zeros((1, 128), jnp.float32)
    lanes = lax.broadcasted_iota(jnp.int32, (1, 128), 1)
    for slot, (count, width, row_at, col_at) in enumerate(MATRICES):
        own = pl.ds(0, count)
        sums[0, own] = jnp.zeros((count, 128), jnp.float32)
        sums[1, own] = jnp.zeros((count, 128), jnp.float32)

        @pl.loop(0, width // 128)
        def _(step, slot=slot, own=own):
            entries = readers[slot](step)
            if slot > 0:
                grads[slot][:, wide(step)] = entries
            sums[0, own] += entries * entries
            weight = masters[slot][:, wide(step)]
            sums[1, own] += weight * weight

        mean = jnp.sum(sums[0, own], axis=-1, keepdims=True) / width + SQUARE_EPSILON
        here_rows = pl.ds(row_at, count)
        new = BETA * rows[here_rows] + (1.0 - BETA) * mean
        rows_new[here_rows] = new
        inverse[own] = jnp.broadcast_to(1.0 / new, (count, 128))
        weight_sum = jnp.sum(jnp.sum(sums[1, own], axis=-1, keepdims=True), axis=0, keepdims=True)
        stats = jnp.where(lanes == slot, jnp.sum(new, axis=0, keepdims=True), stats)
        stats = jnp.where(lanes == 4 + slot, weight_sum, stats)

        @pl.loop(0, width // 128)
        def _(step, slot=slot, own=own, count=count, col_at=col_at):
            entries = grads[slot][:, wide(step)]
            square = entries * entries
            packed[pl.ds(col_at + step, 1)] = (
                jnp.sum(square, axis=0, keepdims=True) + count * SQUARE_EPSILON
            )
            packed[pl.ds(COL_ROWS + col_at + step, 1)] = jnp.sum(
                square * inverse[own], axis=0, keepdims=True
            )

    packed[first + 33 : first + 34] = stats
    packed[first + 34 : 512] = jnp.zeros((512 - first - 34, 128), jnp.float32)


def total_kernel(
    parts, col_moments, gain_moments, gains,
    cols_new, col_factors, moments_new, gains_new, grad_gains, spreads,
    totals, plane_came, line_came, plane_sum, line_sum, line_all, *sems,
):
    chip, core, z = here()
    me = 2 * chip + core
    other = 1 - core
    plane = [at_place(chip, other, z)]
    for peer_chip in flips(chip):
        plane += [at_place(peer_chip, core, z), at_place(peer_chip, other, z)]
    line = [at_place(chip, core, ahead(z, step)) for step in (2, 1, 3)]
    greet(plane + line)
    move = Mover(*sems)
    pieces = [move.send(parts.at[peer[0]], plane_came.at[me], peer) for peer in plane]
    plane_came[me] = parts[me]
    move.arrive(*pieces)
    total = plane_came[0]
    for slot in range(1, 8):
        total = total + plane_came[slot]
    plane_sum[...] = total
    pieces = [move.send(plane_sum.at[peer[1]], line_came.at[z], peer) for peer in line]
    line_came[z] = plane_sum[z]
    move.arrive(*pieces)
    line_sum[...] = line_came[0] + line_came[1] + line_came[2] + line_came[3]
    pieces = [move.send(line_sum, line_all.at[z], peer) for peer in line]
    line_all[z] = line_sum[...]
    move.arrive(*pieces)
    for peer in plane:
        move.send(line_all, totals.at[me], peer)
    totals[me] = line_all[...]
    move.finish()
    flat = totals.reshape(512, 128)
    first = 2 * COL_ROWS
    stats = flat[first + 33 : first + 34]
    lanes = lax.broadcasted_iota(jnp.int32, (1, 128), 1)
    out = jnp.zeros((1, 128), jnp.float32)
    for slot, (_, width, _, col_at) in enumerate(MATRICES):
        own = pl.ds(col_at, width // 128)
        entries_all = float(ROW_TOTALS[slot] * width)
        new = BETA * col_moments[own] + (1.0 - BETA) * (flat[own] / ROW_TOTALS[slot])
        cols_new[own] = new
        mean_rows = lane_value(stats, slot) / ROW_TOTALS[slot]
        ratio = flat[pl.ds(COL_ROWS + col_at, width // 128)] / new
        ratio = jnp.sum(jnp.sum(ratio, axis=-1, keepdims=True), axis=0, keepdims=True)
        spread = jnp.sqrt(mean_rows * ratio / entries_all)
        scale = STEP_RATE * jnp.maximum(
            SCALE_EPSILON, jnp.sqrt(lane_value(stats, 4 + slot) / entries_all)
        )
        factor = scale * jnp.sqrt(mean_rows) / jnp.maximum(1.0, spread / CLIP_LEVEL)
        col_factors[own] = lax.rsqrt(new) * factor
        out = jnp.where(lanes == slot, spread, out)
    gradient = flat[first : first + GAIN_ROWS]
    grad_gains[...] = gradient
    old = gains[...]
    new = BETA * gain_moments[...] + (1.0 - BETA) * (gradient * gradient + SQUARE_EPSILON)
    moments_new[...] = new
    unit = gradient * lax.rsqrt(new)
    row = lax.broadcasted_iota(jnp.int32, (GAIN_ROWS, 128), 0)
    lane = lax.broadcasted_iota(jnp.int32, (GAIN_ROWS, 128), 1)
    segment = jnp.where(row < 16, 0, jnp.where(row < 32, 1, jnp.where(lane < 64, 2, 3)))
    factors = jnp.zeros((GAIN_ROWS, 128), jnp.float32)

    def mean_of(square, mask, count):
        picked = jnp.where(mask, square, 0.0)
        return jnp.sum(jnp.sum(picked, axis=-1, keepdims=True), axis=0, keepdims=True) / count

    for slot, count in enumerate((D, D, HEAD_DIM, HEAD_DIM)):
        mask = segment == slot
        spread = jnp.sqrt(mean_of(unit * unit, mask, count))
        scale = STEP_RATE * jnp.maximum(SCALE_EPSILON, jnp.sqrt(mean_of(old * old, mask, count)))
        factors = jnp.where(mask, scale / jnp.maximum(1.0, spread / CLIP_LEVEL), factors)
        out = jnp.where(lanes == 4 + slot, spread, out)
    gains_new[...] = old - factors * unit
    spreads[...] = out


def head_split(entries):
    rows = entries.shape[0]
    parts = (
        entries[:, :2048].reshape(rows, 8, 256),
        entries[:, 2048:2560].reshape(rows, 8, 64),
        entries[:, 2560:].reshape(rows, 8, 64),
    )
    return jnp.concatenate(parts, axis=2).transpose(1, 0, 2)


def head_join(blocks):
    rows = blocks.shape[1]
    blocks = blocks.transpose(1, 0, 2)
    parts = (blocks[..., :256], blocks[..., 256:320], blocks[..., 320:])
    return jnp.concatenate([part.reshape(rows, -1) for part in parts], axis=1)


def split_local(
    tokens, doc_starts, grad_out, qkv_master, out_master, gate_up_master, down_master, gains,
    qkv_rows, out_rows, gate_up_rows, down_rows, col_moments, gain_moments,
):
    half, full = jnp.bfloat16, jnp.float32
    gain_attn = gains[:D]
    gain_ffn = gains[D : 2 * D]
    gain_query = gains[2 * D : 2 * D + HEAD_DIM]
    gain_key = gains[2 * D + HEAD_DIM :]
    length, group = 512, 4
    tokens_wide = tokens.astype(full)
    normed = norm_rows(tokens_wide, gain_attn).astype(half)
    all_tok, all_wq, all_wo, all_wd = exchange(
        attention_weights_kernel, 0,
        [
            (normed, False), (head_split(qkv_master.astype(half)), False),
            (out_master.astype(half), False), (down_master.astype(half), False),
        ],
        [
            ((2, 8, 64, D), half, False), ((8, 4, 64, 384), half, False), ((4, 64, D), half, False),
            ((4, 256, D), half, False),
        ],
        [], (23, 4), 16 << 20,
    )
    all_tok = all_tok.reshape(2, length, D)
    w_qkv = all_wq.reshape(D, 384)
    w_out = all_wo.reshape(256, D)

    places = jnp.arange(length, dtype=jnp.int32)
    docs, offsets = doc_tables(doc_starts, places)
    cos_table, sin_table = rotary(offsets)
    allowed = mask_of(docs, places, docs, places)[:, 0]
    projected = jnp.einsum("rtd,de->rte", all_tok, w_qkv, preferred_element_type=full)
    head_fn = partial(queries_keys, cos_table, sin_table, heads=group, kv_heads=1)
    queries, keys = head_fn(projected[..., :320], gain_query, gain_key)
    query16 = queries.astype(half)
    keys16 = keys.astype(half)[:, :, 0]
    values16 = projected[..., 320:].astype(half)
    scores = jnp.einsum("rqgh,rth->rgqt", query16, keys16, preferred_element_type=full)
    scores = jnp.where(allowed, scores, MASKED_SCORE)
    best = jnp.max(scores, axis=-1, keepdims=True)
    weights = jnp.where(allowed, jnp.exp(scores - best), 0.0)
    probs = weights / jnp.sum(weights, axis=-1, keepdims=True)
    probs16 = probs.astype(half)
    attended = jnp.einsum("rgqt,rth->rqgh", probs16, values16, preferred_element_type=full)
    attended16 = attended.astype(half).reshape(2, length, 256)
    branch = jnp.einsum("rtc,cd->rtd", attended16, w_out, preferred_element_type=full)

    hidden_in, all_norm, all_grad, all_wg = exchange(
        ffn_weights_kernel, 1,
        [
            (branch.astype(half).reshape(2, 8, 64, D), True), (tokens, True), (gain_ffn[None], True),
            (gate_up_master.astype(half), False), (grad_out.reshape(128, D), False),
        ],
        [
            ((2, 64, D), full, True), ((4, 2, 2, 64, D), half, False), ((4, 2, 128, D), half, False),
            ((4, 2, 4, 64, 2048), half, False),
        ],
        [
            pltpu.VMEM((4, 2, 64, D), half), pltpu.VMEM((4, 2, 64, D), half),
            pltpu.VMEM((2, 64, D), half),
        ],
        (34, 4), 64 << 20,
    )
    hidden_in = hidden_in.reshape(128, D)
    normed2 = all_norm.reshape(1024, D)
    grad16 = all_grad.reshape(1024, D)
    w_gate_up = all_wg.reshape(D, 2048)
    w_down = all_wd.reshape(1024, D)
    gate_up = jnp.einsum("td,df->tf", normed2, w_gate_up, preferred_element_type=full)
    gate_part, up_part = gate_up[:, :1024], gate_up[:, 1024:]
    hidden = (jax.nn.silu(gate_part) * up_part).astype(half)
    out_part = jnp.einsum("tf,fd->td", hidden, w_down, preferred_element_type=full).astype(half)
    d_hidden = jnp.einsum("td,fd->tf", grad16, w_down, preferred_element_type=full)
    silu_value, silu_back = jax.vjp(jax.nn.silu, gate_part)
    d_gate = silu_back(d_hidden * up_part)[0]
    d_gate_up = jnp.concatenate([d_gate, d_hidden * silu_value], axis=-1).astype(half)
    d_normed2 = jnp.einsum("tf,df->td", d_gate_up, w_gate_up, preferred_element_type=full).astype(half)
    term_down = jnp.einsum("tf,td->fd", hidden, grad16, preferred_element_type=full).astype(half)
    term_gate_up = jnp.einsum("td,tf->df", normed2, d_gate_up, preferred_element_type=full).astype(half)

    line_scratch = [pltpu.VMEM((4, 128, D), half)] * 3
    all_branch, d_hidden_in, output, grad_gain_ffn, down_came = exchange(
        ffn_back_kernel, 2,
        [
            (d_normed2.reshape(4, 2, 128, D), True), (out_part.reshape(4, 2, 128, D), True),
            (term_down.reshape(4, 256, D), False), (hidden_in, True), (grad_out.reshape(128, D), True),
            (gain_ffn[None], True),
        ],
        [
            ((8, 128, D), half, False), ((128, D), full, True), ((128, D), half, True),
            ((1, D), full, True), ((4, 256, D), half, False),
        ],
        line_scratch * 2 + [pltpu.VMEM((128, D), half)],
        (24, 2), 32 << 20,
    )
    d_branch = all_branch.reshape(8, 2, 64, D).transpose(1, 0, 2, 3).reshape(2, length, D)
    term_out = jnp.einsum("rtc,rtd->cd", attended16, d_branch, preferred_element_type=full).astype(half)
    d_heads = jnp.einsum("rtd,cd->rtc", d_branch, w_out, preferred_element_type=full).astype(half)
    d_heads = d_heads.reshape(2, length, group, HEAD_DIM)
    delta = jnp.sum(d_heads.astype(full) * attended, axis=-1).transpose(0, 2, 1)
    d_values = jnp.einsum("rgqt,rqgh->rth", probs16, d_heads, preferred_element_type=full)
    d_probs = jnp.einsum("rqgh,rth->rgqt", d_heads, values16, preferred_element_type=full)
    d_scores = (probs * (d_probs - delta[..., None])).astype(half)
    d_queries = jnp.einsum("rgqt,rth->rqgh", d_scores, keys16, preferred_element_type=full)
    d_keys = jnp.einsum("rgqt,rqgh->rth", d_scores, query16, preferred_element_type=full)
    _, heads_back = jax.vjp(head_fn, projected[..., :320], gain_query, gain_key)
    d_heads_in, grad_gain_query, grad_gain_key = heads_back((d_queries, d_keys[:, :, None]))
    d_projected = jnp.concatenate([d_heads_in, d_values], axis=-1).astype(half)
    term_qkv = jnp.einsum("rtd,rte->de", all_tok, d_projected, preferred_element_type=full).astype(half)
    d_normed = jnp.einsum("rte,de->rtd", d_projected, w_qkv, preferred_element_type=full).astype(half)

    d_norm_came, gate_up_came, qkv_came, out_came = exchange(
        gradients_kernel, 3,
        [
            (d_normed.reshape(2, 8, 64, D), True), (term_gate_up.reshape(4, 2, 4, 64, 2048), True),
            (term_qkv.reshape(8, 4, 64, 384), True), (term_out.reshape(4, 64, D), False),
        ],
        [
            ((4, 2, 64, D), half, False), ((64, 2 * FF), half, False),
            ((8, 64, 384), half, False), ((4, 64, D), half, False),
        ],
        [
            pltpu.VMEM((4, 2, 64, D), half), pltpu.VMEM((4, 2, 64, D), half),
            pltpu.VMEM((4, 2, 4, 64, 2048), half), pltpu.VMEM((2, 4, 64, 2048), half),
            pltpu.VMEM((4, 8, 64, 384), half), pltpu.VMEM((8, 64, 384), half),
        ],
        (30, 4), 48 << 20,
    )
    row_states = jnp.concatenate([qkv_rows, out_rows, gate_up_rows, down_rows])[:, None]
    masters = (qkv_master, out_master, gate_up_master, down_master)
    grad_tokens, *grads, rows_new, packed = pl.pallas_call(
        statistics_kernel,
        out_shape=[
            jax.ShapeDtypeStruct((128, D), half),
            *[jax.ShapeDtypeStruct((count, width), full) for count, width, _, _ in MATRICES],
            jax.ShapeDtypeStruct((448, 1), full),
            jax.ShapeDtypeStruct((512, 128), full),
        ],
        scratch_shapes=[
            pltpu.VMEM((1, D), full), pltpu.VMEM((2, 256, 128), full), pltpu.VMEM((256, 128), full),
        ],
        compiler_params=pltpu.CompilerParams(vmem_limit_bytes=VMEM_BYTES),
    )(
        d_norm_came.reshape(4, 128, D), tokens.reshape(128, D), d_hidden_in, gain_attn[None],
        grad_gain_ffn, jnp.concatenate([grad_gain_query, grad_gain_key])[None],
        qkv_came, out_came, gate_up_came, down_came, row_states, *masters,
    )
    shape = (8, 4, 16, 128)
    cols_new, col_factors, moments_new, gains_new, grad_gains, spreads = exchange(
        total_kernel, 4,
        [
            (packed.reshape(shape), True), (col_moments.reshape(-1, 128), True),
            (gain_moments.reshape(-1, 128), True), (gains.reshape(-1, 128), True),
        ],
        [
            ((COL_ROWS, 128), full, True), ((COL_ROWS, 128), full, True),
            ((GAIN_ROWS, 128), full, True), ((GAIN_ROWS, 128), full, True),
            ((GAIN_ROWS, 128), full, True), ((1, 128), full, True),
        ],
        [
            pltpu.VMEM(shape, full), pltpu.VMEM(shape, full), pltpu.VMEM(shape[1:], full),
            pltpu.VMEM(shape[1:], full), pltpu.VMEM(shape[2:], full), pltpu.VMEM(shape[1:], full),
        ],
        (20, 0), 1 << 20,
    )
    col_factors = col_factors.reshape(-1)
    row_factors = lax.rsqrt(rows_new[:, 0])
    new_masters = []
    for slot, (count, width, row_at, col_at) in enumerate(MATRICES):
        row_factor = row_factors[row_at : row_at + count]
        col_factor = col_factors[col_at * 128 : col_at * 128 + width]
        new_masters.append(
            masters[slot] - grads[slot] * row_factor[:, None] * col_factor[None, :]
        )
    return (
        output.reshape(2, 64, D),
        grad_tokens.reshape(2, 64, D),
        *grads,
        grad_gains.reshape(-1),
        *[rows_new[row_at : row_at + count, 0] for count, _, row_at, _ in MATRICES],
        cols_new.reshape(-1),
        moments_new.reshape(-1),
        *new_masters,
        *[master.astype(half) for master in new_masters],
        gains_new.reshape(-1),
        spreads[0, :8],
    )


def optimizer_step(
    grads, gain_local, masters, gains, row_states, col_moments, gain_moments, total_fn
):
    beta = 1.0 - STEP ** (-0.8)
    col_widths = (QKV, D, 2 * FF, D)
    row_totals = (D, HEADS * HEAD_DIM, D, FF)
    squares = [gradient * gradient + SQUARE_EPSILON for gradient in grads]
    rows_new = [
        beta * row_state + (1.0 - beta) * jnp.mean(square, axis=1)
        for row_state, square in zip(row_states, squares)
    ]
    col_local = [jnp.sum(square, axis=0) for square in squares]
    weighted_local = [
        jnp.sum(gradient * gradient / row_new[:, None], axis=0)
        for gradient, row_new in zip(grads, rows_new)
    ]
    stats_local = jnp.stack(
        [jnp.sum(row_new) for row_new in rows_new]
        + [jnp.sum(master * master) for master in masters]
    )
    totals = total_fn(jnp.concatenate(col_local + weighted_local + [stats_local, gain_local]))
    cols = sum(col_widths)
    col_sums, weighted = totals[:cols], totals[cols : 2 * cols]
    stats, grad_gains = totals[2 * cols : 2 * cols + 8], totals[2 * cols + 8 :]
    col_divisor = jnp.concatenate(
        [
            jnp.full((col_width,), float(row_total), jnp.float32)
            for col_width, row_total in zip(col_widths, row_totals)
        ]
    )
    cols_new = beta * col_moments + (1.0 - beta) * col_sums / col_divisor
    new_masters = []
    spreads = []
    begin_at = 0
    for slot in range(4):
        col_part = cols_new[begin_at : begin_at + col_widths[slot]]
        weighted_part = weighted[begin_at : begin_at + col_widths[slot]]
        begin_at = begin_at + col_widths[slot]
        mean_rows = stats[slot] / row_totals[slot]
        unit = (
            grads[slot]
            * lax.rsqrt(rows_new[slot] / mean_rows)[:, None]
            * lax.rsqrt(col_part)[None, :]
        )
        entries_all = float(row_totals[slot] * col_widths[slot])
        spread = jnp.sqrt(mean_rows * jnp.sum(weighted_part / col_part) / entries_all)
        scale = STEP_RATE * jnp.maximum(SCALE_EPSILON, jnp.sqrt(stats[4 + slot] / entries_all))
        new_masters.append(masters[slot] - scale * unit / jnp.maximum(1.0, spread / CLIP_LEVEL))
        spreads.append(spread)
    bounds = (0, D, 2 * D, 2 * D + HEAD_DIM, 2 * D + 2 * HEAD_DIM)
    moment_parts, gain_parts = ([], [])
    for segment in range(4):
        gradient = grad_gains[bounds[segment] : bounds[segment + 1]]
        gain_old = gains[bounds[segment] : bounds[segment + 1]]
        moment_new = beta * gain_moments[bounds[segment] : bounds[segment + 1]] + (1.0 - beta) * (
            gradient * gradient + SQUARE_EPSILON
        )
        unit = gradient * lax.rsqrt(moment_new)
        spread = jnp.sqrt(jnp.mean(unit * unit))
        scale = STEP_RATE * jnp.maximum(SCALE_EPSILON, jnp.sqrt(jnp.mean(gain_old * gain_old)))
        moment_parts.append(moment_new)
        gain_parts.append(gain_old - scale * unit / jnp.maximum(1.0, spread / CLIP_LEVEL))
        spreads.append(spread)
    return (
        grad_gains,
        *rows_new,
        cols_new,
        jnp.concatenate(moment_parts),
        *new_masters,
        *[master.astype(jnp.bfloat16) for master in new_masters],
        jnp.concatenate(gain_parts),
        jnp.stack(spreads),
    )


def solution(mesh):
    split = mesh.shape["seq"] == 8 and mesh.shape["rows"] == 4
    return jax.shard_map(
        split_local if split else gathered_local,
        mesh=mesh,
        in_specs=(
            P("rows", "seq", None),
            P("rows", None),
            P("rows", "seq", None),
            P(("seq", "rows"), None),
            P(("seq", "rows"), None),
            P(("seq", "rows"), None),
            P(("seq", "rows"), None),
            P(),
            P(("seq", "rows")),
            P(("seq", "rows")),
            P(("seq", "rows")),
            P(("seq", "rows")),
            P(),
            P(),
        ),
        out_specs=(
            P("rows", "seq", None),
            P("rows", "seq", None),
            P(("seq", "rows"), None),
            P(("seq", "rows"), None),
            P(("seq", "rows"), None),
            P(("seq", "rows"), None),
            P(),
            P(("seq", "rows")),
            P(("seq", "rows")),
            P(("seq", "rows")),
            P(("seq", "rows")),
            P(),
            P(),
            P(("seq", "rows"), None),
            P(("seq", "rows"), None),
            P(("seq", "rows"), None),
            P(("seq", "rows"), None),
            P(("seq", "rows"), None),
            P(("seq", "rows"), None),
            P(("seq", "rows"), None),
            P(("seq", "rows"), None),
            P(),
            P(),
        ),
        check_vma=False,
    )
```

```python
from functools import partial

import jax
import jax.numpy as jnp
from jax import lax
from jax.experimental import pallas as pl
from jax.experimental.pallas import tpu as pltpu
from jax.sharding import PartitionSpec as P

D = 2048
HEADS = 32
KV_HEADS = 8
HEAD_DIM = 64
FF = 8192
STEP = 10
QKV = 3072


EPSILON = 1e-06
ROPE_BASE = 10000.0
MASKED_SCORE = -1e30
STEP_RATE = 0.3
CLIP_LEVEL = 1.0
SQUARE_EPSILON = 1e-30
SCALE_EPSILON = 0.001


def from_behind(value, axis, steps):
    count = lax.axis_size(axis)
    pairs = [(source, (source + steps) % count) for source in range(count)]
    return lax.ppermute(value, axis, pairs)


def norm_rows(entries, gain):
    return entries * lax.rsqrt(jnp.mean(entries * entries, axis=-1, keepdims=True) + EPSILON) * gain


def turn(entries, cos_wide, sin_wide):
    half_width = entries.shape[-1] // 2
    turned = jnp.concatenate([-entries[..., half_width:], entries[..., :half_width]], axis=-1)
    return entries * cos_wide + turned * sin_wide


def doc_tables(doc_starts, places):
    before = doc_starts[:, None, :] <= places[None, :, None]
    doc_ids = jnp.sum(before.astype(jnp.int32), axis=-1)
    doc_first = jnp.max(jnp.where(before, doc_starts[:, None, :], 0), axis=-1)
    return (doc_ids, places[None, :] - doc_first)


def rotary(offsets):
    frequency = ROPE_BASE ** (-(jnp.arange(HEAD_DIM // 2, dtype=jnp.float32) * 2.0 / HEAD_DIM))
    angles = offsets.astype(jnp.float32)[..., None] * frequency
    cos_table = jnp.concatenate([jnp.cos(angles), jnp.cos(angles)], axis=-1)
    sin_table = jnp.concatenate([jnp.sin(angles), jnp.sin(angles)], axis=-1)
    return (cos_table, sin_table)


def queries_keys(
    cos_table, sin_table, projected, gain_query, gain_key, heads=HEADS, kv_heads=KV_HEADS
):
    rows_here, seq_here = (projected.shape[0], projected.shape[1])
    att_width = heads * HEAD_DIM
    queries = projected[..., :att_width].reshape(rows_here, seq_here, heads, HEAD_DIM)
    keys_rot = projected[..., att_width : att_width + kv_heads * HEAD_DIM].reshape(
        rows_here, seq_here, kv_heads, HEAD_DIM
    )
    cos_wide = cos_table[:, :, None, :]
    sin_wide = sin_table[:, :, None, :]
    queries = turn(norm_rows(queries, gain_query), cos_wide, sin_wide) * HEAD_DIM ** (-0.5)
    keys_rot = turn(norm_rows(keys_rot, gain_key), cos_wide, sin_wide)
    return (queries, keys_rot)


def mask_of(query_docs, query_places, key_docs, key_places):
    same_doc = query_docs[:, :, None] == key_docs[:, None, :]
    causal = query_places[None, :, None] >= key_places[None, None, :]
    return (same_doc & causal)[:, None, None, :, :]


def gathered_local(
    tokens,
    doc_starts,
    grad_out,
    qkv_master,
    out_master,
    gate_up_master,
    down_master,
    gains,
    qkv_rows,
    out_rows,
    gate_up_rows,
    down_rows,
    col_moments,
    gain_moments,
):
    cycle_size = lax.axis_size("seq")
    seq_index = lax.axis_index("seq")
    rows_dev, seq_dev = (tokens.shape[0], tokens.shape[1])
    group_size = HEADS // KV_HEADS
    att_width = HEADS * HEAD_DIM
    kv_width = KV_HEADS * HEAD_DIM
    gain_attn = gains[:D]
    gain_ffn = gains[D : 2 * D]
    gain_query = gains[2 * D : 2 * D + HEAD_DIM]
    gain_key = gains[2 * D + HEAD_DIM :]
    local_places = jnp.arange(seq_dev, dtype=jnp.int32)
    places = seq_index * seq_dev + local_places
    query_docs, offsets = doc_tables(doc_starts, places)
    cos_table, sin_table = rotary(offsets)
    copies = (
        qkv_master.astype(jnp.bfloat16),
        out_master.astype(jnp.bfloat16),
        gate_up_master.astype(jnp.bfloat16),
        down_master.astype(jnp.bfloat16),
    )
    w_qkv, w_out, w_gate_up, w_down = (
        lax.all_gather(copies[0], ("seq", "rows"), axis=0, tiled=True),
        lax.all_gather(copies[1], ("seq", "rows"), axis=0, tiled=True),
        lax.all_gather(copies[2], ("seq", "rows"), axis=0, tiled=True),
        lax.all_gather(copies[3], ("seq", "rows"), axis=0, tiled=True),
    )
    tokens_wide = tokens.astype(jnp.float32)
    normed = norm_rows(tokens_wide, gain_attn).astype(jnp.bfloat16)
    projected = jnp.einsum("rtd,de->rte", normed, w_qkv, preferred_element_type=jnp.float32)
    head_fn = partial(queries_keys, cos_table, sin_table)
    queries, keys_rot = head_fn(projected, gain_query, gain_key)
    query16 = queries.astype(jnp.bfloat16).reshape(
        rows_dev, seq_dev, KV_HEADS, group_size, HEAD_DIM
    )
    keys16 = keys_rot.astype(jnp.bfloat16).reshape(rows_dev, seq_dev, kv_width)
    values16 = projected[..., att_width + kv_width :].astype(jnp.bfloat16)
    stat_shape = (rows_dev, KV_HEADS, group_size, seq_dev)
    initial = (
        jnp.full(stat_shape, MASKED_SCORE, jnp.float32),
        jnp.zeros(stat_shape, jnp.float32),
        jnp.zeros(stat_shape + (HEAD_DIM,), jnp.float32),
    )
    carry = initial
    key_piece = lax.all_gather(keys16, "seq", axis=1, tiled=True)
    value_piece = lax.all_gather(values16, "seq", axis=1, tiled=True)
    key_count = key_piece.shape[1]

    def absorb_block(state, block_index):
        best, total, summed = state
        block_begin = block_index * seq_dev
        key_block = lax.dynamic_slice_in_dim(key_piece, block_begin, seq_dev, 1).reshape(
            rows_dev, seq_dev, KV_HEADS, HEAD_DIM
        )
        value_block = lax.dynamic_slice_in_dim(value_piece, block_begin, seq_dev, 1).reshape(
            rows_dev, seq_dev, KV_HEADS, HEAD_DIM
        )
        key_places = block_begin + jnp.arange(seq_dev, dtype=jnp.int32)
        key_docs, _ = doc_tables(doc_starts, key_places)
        allowed = mask_of(query_docs, places, key_docs, key_places)
        scores = jnp.einsum(
            "rqkgh,rtkh->rkgqt", query16, key_block, preferred_element_type=jnp.float32
        )
        scores = jnp.where(allowed, scores, MASKED_SCORE)
        best_new = jnp.maximum(best, jnp.max(scores, axis=-1))
        weights = jnp.where(allowed, jnp.exp(scores - best_new[..., None]), 0.0)
        factor = jnp.exp(best - best_new)
        total = total * factor + jnp.sum(weights, axis=-1)
        summed = summed * factor[..., None] + jnp.einsum(
            "rkgqt,rtkh->rkgqh",
            weights.astype(jnp.bfloat16),
            value_block,
            preferred_element_type=jnp.float32,
        )
        return ((best_new, total, summed), None)

    carry, _ = lax.scan(absorb_block, carry, jnp.arange(key_count // seq_dev, dtype=jnp.int32))
    best, total, summed = carry
    log_total = best + jnp.log(total)
    attended = summed / total[..., None]
    attended16 = (
        attended.transpose(0, 3, 1, 2, 4).reshape(rows_dev, seq_dev, att_width).astype(jnp.bfloat16)
    )
    branch = jnp.einsum("rtc,cd->rtd", attended16, w_out, preferred_element_type=jnp.float32)
    hidden_in = tokens_wide + branch
    normed2 = norm_rows(hidden_in, gain_ffn).astype(jnp.bfloat16)
    gate_up = jnp.einsum("rtd,df->rtf", normed2, w_gate_up, preferred_element_type=jnp.float32)
    gate_part, up_part = (gate_up[..., :FF], gate_up[..., FF:])
    hidden = (jax.nn.silu(gate_part) * up_part).astype(jnp.bfloat16)
    output = hidden_in + jnp.einsum(
        "rtf,fd->rtd", hidden, w_down, preferred_element_type=jnp.float32
    )
    d_hidden = jnp.einsum("rtd,fd->rtf", grad_out, w_down, preferred_element_type=jnp.float32)
    silu_value, silu_back = jax.vjp(jax.nn.silu, gate_part)
    d_gate = silu_back(d_hidden * up_part)[0]
    d_gate_up = jnp.concatenate([d_gate, d_hidden * silu_value], axis=-1).astype(jnp.bfloat16)
    d_normed2 = jnp.einsum("rtf,df->rtd", d_gate_up, w_gate_up, preferred_element_type=jnp.float32)
    _, ffn_norm_back = jax.vjp(norm_rows, hidden_in, gain_ffn)
    d_inner, grad_gain_ffn = ffn_norm_back(d_normed2)
    d_hidden_in = grad_out.astype(jnp.float32) + d_inner
    term_down = jnp.einsum("rtf,rtd->fd", hidden, grad_out, preferred_element_type=jnp.float32)
    grad_down = lax.psum_scatter(term_down, ("seq", "rows"), scatter_dimension=0, tiled=True)
    term_gate_up = jnp.einsum("rtd,rtf->df", normed2, d_gate_up, preferred_element_type=jnp.float32)
    grad_gate_up = lax.psum_scatter(term_gate_up, ("seq", "rows"), scatter_dimension=0, tiled=True)
    d_branch = d_hidden_in.astype(jnp.bfloat16)
    term_out = jnp.einsum("rtc,rtd->cd", attended16, d_branch, preferred_element_type=jnp.float32)
    d_attended = jnp.einsum(
        "rtd,cd->rtc", d_branch, w_out, preferred_element_type=jnp.float32
    ).astype(jnp.bfloat16)
    d_heads = d_attended.reshape(rows_dev, seq_dev, KV_HEADS, group_size, HEAD_DIM).transpose(
        0, 2, 3, 1, 4
    )
    delta = jnp.sum(d_heads.astype(jnp.float32) * attended, axis=-1)

    def cycle_turn(turn_index, carry):
        pair16, grad_pair, d_queries = carry
        source = (seq_index + turn_index) % cycle_size
        key_places = source * seq_dev + local_places
        key_docs, _ = doc_tables(doc_starts, key_places)
        allowed = mask_of(query_docs, places, key_docs, key_places)
        key_block = pair16[0].reshape(rows_dev, seq_dev, KV_HEADS, HEAD_DIM)
        value_block = pair16[1].reshape(rows_dev, seq_dev, KV_HEADS, HEAD_DIM)
        scores = jnp.einsum(
            "rqkgh,rtkh->rkgqt", query16, key_block, preferred_element_type=jnp.float32
        )
        scores = jnp.where(allowed, scores, MASKED_SCORE)
        probs = jnp.where(allowed, jnp.exp(scores - log_total[..., None]), 0.0)
        d_values = jnp.einsum(
            "rkgqt,rkgqh->rtkh",
            probs.astype(jnp.bfloat16),
            d_heads,
            preferred_element_type=jnp.float32,
        )
        d_probs = jnp.einsum(
            "rkgqh,rtkh->rkgqt", d_heads, value_block, preferred_element_type=jnp.float32
        )
        d_scores = (probs * (d_probs - delta[..., None])).astype(jnp.bfloat16)
        d_queries = d_queries + jnp.einsum(
            "rkgqt,rtkh->rkgqh", d_scores, key_block, preferred_element_type=jnp.float32
        )
        d_keys = jnp.einsum(
            "rkgqt,rqkgh->rtkh", d_scores, query16, preferred_element_type=jnp.float32
        )
        grad_pair = grad_pair + jnp.stack(
            [
                d_keys.reshape(rows_dev, seq_dev, kv_width),
                d_values.reshape(rows_dev, seq_dev, kv_width),
            ]
        )
        grad_pair = from_behind(grad_pair.astype(jnp.bfloat16), "seq", -1).astype(grad_pair.dtype)
        pair16 = from_behind(pair16, "seq", -1)
        return (pair16, grad_pair, d_queries)

    start_pair = jnp.stack([keys16, values16])
    start_grads = jnp.zeros((2, rows_dev, seq_dev, kv_width), jnp.float32)
    start_queries = jnp.zeros(stat_shape + (HEAD_DIM,), jnp.float32)
    _, grad_pair, d_queries = lax.fori_loop(
        0, cycle_size, cycle_turn, (start_pair, start_grads, start_queries)
    )
    d_queries = d_queries.transpose(0, 3, 1, 2, 4).reshape(rows_dev, seq_dev, HEADS, HEAD_DIM)
    d_keys_home = grad_pair[0].reshape(rows_dev, seq_dev, KV_HEADS, HEAD_DIM)
    _, heads_back = jax.vjp(head_fn, projected, gain_query, gain_key)
    d_projected, grad_gain_query, grad_gain_key = heads_back((d_queries, d_keys_home))
    d_projected = jnp.concatenate(
        [d_projected[..., : att_width + kv_width], grad_pair[1]], axis=-1
    ).astype(jnp.bfloat16)
    term_qkv = jnp.einsum("rtd,rte->de", normed, d_projected, preferred_element_type=jnp.float32)
    d_normed = jnp.einsum("rte,de->rtd", d_projected, w_qkv, preferred_element_type=jnp.float32)
    _, attn_norm_back = jax.vjp(norm_rows, tokens_wide, gain_attn)
    d_tokens_part, grad_gain_attn = attn_norm_back(d_normed)
    grad_tokens = (d_hidden_in + d_tokens_part).astype(jnp.bfloat16)
    grad_qkv, grad_out_proj = (
        lax.psum_scatter(term_qkv, ("seq", "rows"), scatter_dimension=0, tiled=True),
        lax.psum_scatter(term_out, ("seq", "rows"), scatter_dimension=0, tiled=True),
    )
    gain_local = jnp.concatenate([grad_gain_attn, grad_gain_ffn, grad_gain_query, grad_gain_key])
    grads = (grad_qkv, grad_out_proj, grad_gate_up, grad_down)
    updated = optimizer_step(
        grads, gain_local, (qkv_master, out_master, gate_up_master, down_master), gains,
        (qkv_rows, out_rows, gate_up_rows, down_rows), col_moments, gain_moments,
        lambda vector: lax.psum(vector, ("seq", "rows")),
    )
    return (output.astype(jnp.bfloat16), grad_tokens, *grads, *updated)


MESH = pl.DeviceIdType.MESH
PLACES = 32
VMEM_BYTES = 56 * 1024 * 1024
CHUNK = 16


def here():
    seq = lax.axis_index("seq")
    return lax.div(seq, 2), lax.rem(seq, 2), lax.axis_index("rows")


def flips(chip):
    return (chip + 1 - 2 * lax.rem(chip, 2), lax.rem(chip + 2, 4), 3 - chip)


def ahead(z, step):
    return lax.rem(z + step, 4)


def at_place(chip, core, z):
    return (2 * chip + core, z)


def greet(peers):
    barrier = pltpu.get_barrier_semaphore()
    for peer in peers:
        pl.semaphore_signal(barrier, inc=1, device_id=peer, device_id_type=MESH)
    pl.semaphore_wait(barrier, len(peers))


class Mover:
    def __init__(self, send_sem, recv_sem, local_sem):
        self.send_sem, self.recv_sem, self.local_sem = send_sem, recv_sem, local_sem
        self.remote, self.own = [], []

    def send(self, src, dst, peer):
        slot = len(self.remote)
        copy = pltpu.make_async_remote_copy(
            src_ref=src,
            dst_ref=dst,
            send_sem=self.send_sem.at[slot],
            recv_sem=self.recv_sem.at[slot],
            device_id=peer,
            device_id_type=MESH,
        )
        copy.start()
        handle = [copy, False, copy.wait_recv, False]
        self.remote.append(handle)
        return handle

    def send_parts(self, pairs, whole, peer):
        slot = len(self.remote)

        def copy_of(src, dst):
            return pltpu.make_async_remote_copy(
                src_ref=src,
                dst_ref=dst,
                send_sem=self.send_sem.at[slot],
                recv_sem=self.recv_sem.at[slot],
                device_id=peer,
                device_id_type=MESH,
            )

        for src, dst in pairs:
            copy_of(src, dst).start()
        copy = copy_of(whole, whole)
        handle = [copy, False, copy.wait_recv, False]
        self.remote.append(handle)
        return handle

    def keep_parts(self, pairs, whole):
        sem = self.local_sem.at[len(self.own)]
        for src, dst in pairs:
            pltpu.make_async_copy(src, dst, sem).start()
        copy = pltpu.make_async_copy(whole, whole, sem)
        handle = [copy, False, copy.wait]
        self.own.append(handle)
        return handle

    def keep(self, src, dst):
        copy = pltpu.make_async_copy(src, dst, self.local_sem.at[len(self.own)])
        copy.start()
        handle = [copy, False, copy.wait]
        self.own.append(handle)
        return handle

    def arrive(self, *handles):
        for handle in handles:
            if not handle[1]:
                handle[1] = True
                handle[2]()

    def sent(self, *handles):
        for handle in handles:
            if not handle[3]:
                handle[3] = True
                handle[0].wait_send()

    def finish(self):
        self.arrive(*self.own, *self.remote)
        self.sent(*self.remote)


def semaphores(remote, own):
    return [
        pltpu.SemaphoreType.DMA((remote,)),
        pltpu.SemaphoreType.DMA((remote,)),
        pltpu.SemaphoreType.DMA((max(own, 1),)),
    ]


def exchange(kernel, ident, inputs, outputs, scratch, copies, moved, flops=0):
    vmem, anywhere = pl.BlockSpec(memory_space=pltpu.VMEM), pl.BlockSpec(memory_space=pl.ANY)
    return pl.pallas_call(
        kernel,
        out_shape=[jax.ShapeDtypeStruct(shape, kind) for shape, kind, _ in outputs],
        in_specs=[vmem if near else anywhere for _, near in inputs],
        out_specs=[vmem if near else anywhere for _, _, near in outputs],
        scratch_shapes=scratch + semaphores(*copies),
        compiler_params=pltpu.CompilerParams(
            collective_id=ident, has_side_effects=True, vmem_limit_bytes=VMEM_BYTES
        ),
        cost_estimate=pl.CostEstimate(flops=flops, bytes_accessed=moved, transcendentals=0),
    )(*[array for array, _ in inputs])


def chunks(length, body):
    @pl.loop(0, length // CHUNK)
    def _(step):
        body(pl.ds(pl.multiple_of(step * CHUNK, CHUNK), CHUNK))


def segments(core, z):
    for part in range(2):
        for chip in range(4):
            start = part * FF + ((2 * chip + core) * 4 + z) * 256
            yield pl.ds(pl.multiple_of(start, 256), 256), pl.ds(part * 1024 + chip * 256, 256)


def attention_weights_kernel(tok, wq, wo, wd, all_tok, all_wq, all_wo, all_wd, *sems):
    chip, core, z = here()
    others = flips(chip)
    other = 1 - core
    plane = [at_place(chip, other, z)]
    for peer_chip in others:
        plane += [at_place(peer_chip, core, z), at_place(peer_chip, other, z)]
    along = [at_place(chip, core, ahead(z, step)) for step in (2, 1, 3)]
    greet(plane + along)
    move = Mover(*sems)
    me = 2 * chip + core
    for peer in along:
        move.send(wo, all_wo.at[z], peer)
    parts = [move.keep(wq.at[me], all_wq.at[me, z])]
    for peer in plane:
        parts.append(move.send(wq.at[peer[0]], all_wq.at[me, z], peer))
    came = []
    for peer_chip in others:
        came.append(move.send(tok, all_tok.at[:, me], at_place(peer_chip, core, z)))
    partner = at_place(chip, other, z)
    move.send(tok, all_tok.at[:, me], partner)
    for peer_chip in others:
        move.send(wd, all_wd.at[chip], at_place(peer_chip, core, z))
    move.keep(tok, all_tok.at[:, me])
    move.keep(wo, all_wo.at[z])
    move.keep(wd, all_wd.at[chip])
    move.arrive(*parts)
    for peer in along:
        move.send(all_wq.at[:, z], all_wq.at[:, z], peer)
    for peer_chip, handle in zip(others, came):
        move.arrive(handle)
        block = all_tok.at[:, 2 * peer_chip + core]
        move.send(block, block, partner)
    move.finish()


def add_blocks(first, second, result):
    for row in range(2):

        def body(part):
            total = first[row, part].astype(jnp.float32) + second[row, part].astype(jnp.float32)
            result[row, part] = total.astype(result.dtype)

        chunks(64, body)


def ffn_kernel(
    branch, tok, gain, wg, wd_all, grad_out,
    all_branch, d_hidden_in, out_sum, gain_part, down_part, gate_up_in,
    from_partner, came, normed, hidden_in, all_norm, all_out, all_wg, wd, hidden, d_gate_up,
    partial, from_partner2, came2, d_branch, *sems,
):
    half, full = jnp.bfloat16, jnp.float32
    chip, core, z = here()
    others = flips(chip)
    other = 1 - core
    me = 2 * chip + core
    partner = at_place(chip, other, z)
    plane = [at_place(peer_chip, core, z) for peer_chip in others]
    steps = (2, 1, 3)
    line = [at_place(chip, core, ahead(z, step)) for step in steps]
    cross = [at_place(chip, other, ahead(z, step)) for step in steps]
    greet([partner] + plane + line + cross)
    move = Mover(*sems)
    order = tuple(others) + (chip,)
    halves = [
        move.send(branch.at[:, 2 * to + other], from_partner.at[to], partner) for to in order
    ]

    def turn_block(to_core, to_z):
        whole = all_wg.at[chip, core, z]
        return [(wg.at[:, src], whole.at[:, dst]) for src, dst in segments(to_core, to_z)], whole

    turned = [move.keep_parts(*turn_block(core, z)), move.send_parts(*turn_block(other, z), partner)]
    for step, peer, peer_cross in zip(steps, line, cross):
        to = ahead(z, step)
        turned.append(move.send_parts(*turn_block(core, to), peer))
        turned.append(move.send_parts(*turn_block(other, to), peer_cross))
    grads = [move.send(grad_out, all_out.at[z, core], peer) for peer in line]
    own = [
        move.keep(wd_all, wd),
        move.keep(grad_out, all_out.at[z, core]),
        move.send(grad_out, all_out.at[z, core], partner),
    ]
    sums = []
    for to, arrived, peer in zip(others, halves, plane):
        move.arrive(arrived)
        add_blocks(branch.at[:, 2 * to + core], from_partner.at[to], from_partner.at[to])
        sums.append(move.send(from_partner.at[to], came.at[chip], peer))
    move.arrive(halves[3], *sums)
    for row in range(2):

        def body(part):
            total = tok[row, part].astype(full)
            total += branch[row, me, part].astype(full)
            total += from_partner[chip, row, part].astype(full)
            for peer_chip in others:
                total += came[peer_chip, row, part].astype(full)
            hidden_in[row, part] = total
            scale = lax.rsqrt(jnp.mean(total * total, axis=-1, keepdims=True) + EPSILON)
            normed[row, part] = (total * scale * gain[...]).astype(half)

        chunks(64, body)
    move.sent(*sums)
    norms = [move.send(normed, all_norm.at[z, core], peer) for peer in line]
    own.append(move.send(normed, all_norm.at[z, core], partner))
    own.append(move.keep(normed, all_norm.at[z, core]))

    move.arrive(*turned)
    by_x, by_y = plane[0], plane[1]
    first, second = all_wg.at[chip, 0], all_wg.at[chip, 1]
    from_x = move.send(first, first, by_x)
    from_y = move.send(second, second, by_y)
    weights = [from_x, from_y, move.send(second, second, by_x), move.send(first, first, by_y)]

    def share(handles, target):
        shared = []
        for step, handle in zip(steps, handles):
            move.arrive(handle)
            block = target.at[ahead(z, 4 - step), core]
            shared.append(move.send(block, block, partner))
        return shared

    shared = share(grads, all_out)
    move.arrive(from_x, from_y)
    first, second = all_wg.at[others[0], 0], all_wg.at[others[1], 1]
    weights += [move.send(first, first, by_y), move.send(second, second, by_x)]
    shared += share(norms, all_norm)
    move.arrive(*weights, *own, *shared)

    flat_wg = all_wg.reshape(D, 2048)
    flat_wd = wd.reshape(1024, D)

    def wide(start, size):
        return pl.ds(pl.multiple_of(start, size), size)

    def across(left, right):
        return lax.dot_general(left, right, (((1,), (1,)), ((), ())), preferred_element_type=full)

    def down(left, right):
        return lax.dot_general(left, right, (((0,), (0,)), ((), ())), preferred_element_type=full)

    def block_of(zb):
        @pl.loop(0, 4)
        def _(step):
            cols, ups = wide(step * 256, 256), wide(1024 + step * 256, 256)
            rows = all_norm[zb].reshape(256, D)
            gate = jnp.dot(rows, flat_wg[:, cols], preferred_element_type=full)
            up = jnp.dot(rows, flat_wg[:, ups], preferred_element_type=full)
            d_hidden = across(all_out[zb].reshape(256, D), flat_wd[cols])
            sigmoid = 1.0 / (1.0 + jnp.exp(-gate))
            silu = gate * sigmoid
            hidden[zb, :, cols] = (silu * up).astype(half)
            d_gate = d_hidden * up * (sigmoid * (1.0 + gate * (1.0 - sigmoid)))
            d_gate_up[zb, :, cols] = d_gate.astype(half)
            d_gate_up[zb, :, ups] = (d_hidden * silu).astype(half)

        @pl.loop(0, 8)
        def _(step):
            cols = wide(step * 256, 256)
            block = across(d_gate_up[zb], flat_wg[cols])
            partial[zb, :, :, :, cols] = block.reshape(2, 2, 64, 256).astype(half)

    def pair_sum(zb, handle, into):
        move.arrive(handle)
        add_blocks(partial.at[zb, core], into.at[zb], into.at[zb])

    to_partner, sums = [], []
    walk = [ahead(z, step) for step in steps] + [z]
    for index, zb in enumerate(walk):
        block_of(zb)
        to_partner.append(move.send(partial.at[zb, other], from_partner.at[zb], partner))
        if index > 0:
            pair_sum(walk[index - 1], to_partner[index - 1], from_partner)
            sums.append(
                move.send(from_partner.at[walk[index - 1]], came.at[z], line[index - 1])
            )
    pair_sum(z, to_partner[3], from_partner)

    flat_norm, flat_grads = all_norm.reshape(1024, D), all_out.reshape(1024, D)
    flat_hidden, flat_d = hidden.reshape(1024, 1024), d_gate_up.reshape(1024, 2048)
    move.sent(*weights)
    for to, peer in zip((others[2], others[0], others[1], chip), (plane[2], plane[0], plane[1], None)):
        rows = wide(to * 512, 512)

        @pl.loop(0, 4)
        def _(step, rows=rows):
            cols = wide(step * 512, 512)
            flat_wg[rows, cols] = down(flat_norm[:, rows], flat_d[:, cols]).astype(half)

        if peer is None:
            move.keep(all_wg.at[to], gate_up_in.at[chip])
        else:
            move.send(all_wg.at[to], gate_up_in.at[chip], peer)

    move.arrive(*sums)
    gain_part[...] = jnp.zeros_like(gain_part)
    for row in range(2):

        def body2(part):
            total = from_partner[z, row, part].astype(full)
            for step in steps:
                total += came[ahead(z, step), row, part].astype(full)
            entries = hidden_in[row, part]
            scale = lax.rsqrt(jnp.mean(entries * entries, axis=-1, keepdims=True) + EPSILON)
            gain_part[...] += jnp.sum(total * entries * scale, axis=0, keepdims=True)
            total = total * gain[...]
            inner = jnp.mean(total * entries, axis=-1, keepdims=True) * (scale * scale * scale)
            grad = grad_out[row, part].astype(full) + total * scale - entries * inner
            d_hidden_in[row, part] = grad
            d_branch[row, part] = grad.astype(half)

        chunks(64, body2)
    branches = [move.send(d_branch, all_branch.at[me], peer) for peer in plane]
    move.send(d_branch, all_branch.at[me], partner)
    move.keep(d_branch, all_branch.at[me])

    move.sent(*to_partner)
    to_partner, sums = [], []
    for index, zb in enumerate(walk):

        @pl.loop(0, 4)
        def _(step, zb=zb):
            cols = wide(step * 512, 512)
            block = jnp.dot(hidden[zb], flat_wd[:, cols], preferred_element_type=full)
            partial[zb, :, :, :, cols] = block.reshape(2, 2, 64, 512).astype(half)

        to_partner.append(move.send(partial.at[zb, other], from_partner2.at[zb], partner))
        if index > 0:
            pair_sum(walk[index - 1], to_partner[index - 1], from_partner2)
            sums.append(
                move.send(from_partner2.at[walk[index - 1]], came2.at[z], line[index - 1])
            )
    pair_sum(z, to_partner[3], from_partner2)

    @pl.loop(0, 4)
    def _(to):
        rows = wide(to * 256, 256)

        @pl.loop(0, 4)
        def _(step):
            cols = wide(step * 512, 512)
            flat_wd[rows, cols] = down(flat_hidden[:, rows], flat_grads[:, cols]).astype(half)

    move.keep(wd, down_part)
    for peer_chip, handle in zip(others, branches):
        move.arrive(handle)
        block = all_branch.at[2 * peer_chip + core]
        move.send(block, block, partner)
    move.arrive(*sums)
    for row in range(2):

        def body3(part):
            total = hidden_in[row, part] + from_partner2[z, row, part].astype(full)
            for step in steps:
                total += came2[ahead(z, step), row, part].astype(full)
            out_sum[row, part] = total.astype(half)

        chunks(64, body3)
    move.finish()


def gradients_kernel(
    d_norm, gate_up_in, qkv_part, out_part, down_part,
    d_norm_came, gate_up_came, qkv_came, out_came, down_came,
    from_partner, summed, gate_up_sum, qkv_in, qkv_sum, *sems,
):
    chip, core, z = here()
    others = flips(chip)
    other = 1 - core
    me = 2 * chip + core
    partner = at_place(chip, other, z)
    plane = [at_place(peer_chip, core, z) for peer_chip in others]
    plane_cross = [at_place(peer_chip, other, z) for peer_chip in others]
    steps = (2, 1, 3)
    line = [at_place(chip, core, ahead(z, step)) for step in steps]
    cross = [at_place(chip, other, ahead(z, step)) for step in steps]
    greet([partner] + plane + plane_cross + line + cross)
    move = Mover(*sems)
    order = tuple(others) + (chip,)
    halves = [
        move.send(d_norm.at[:, 2 * to + other], from_partner.at[to], partner) for to in order
    ]
    qkv_pieces = []
    for step, peer in zip(steps, line):
        qkv_pieces.append(move.send(qkv_part.at[:, ahead(z, step)], qkv_in.at[z], peer))
        move.send(out_part.at[ahead(z, step)], out_came.at[z], peer)
    move.keep(out_part.at[z], out_came.at[z])
    for to, half in zip(order, halves):
        move.arrive(half)
        add_blocks(d_norm.at[:, 2 * to + core], from_partner.at[to], summed.at[to])
    for to, peer in zip(others, plane):
        move.send(summed.at[to], d_norm_came.at[chip], peer)
    move.keep(summed.at[chip], d_norm_came.at[chip])
    for to, peer in zip(others, plane):
        move.send(down_part.at[to], down_came.at[chip], peer)
    move.keep(down_part.at[chip], down_came.at[chip])

    @pl.loop(0, 8)
    def _(block):
        to_core, to_z = lax.div(block, 4), lax.rem(block, 4)

        def body(part):
            total = gate_up_in[0, to_core, to_z, part].astype(jnp.float32)
            for slot in range(1, 4):
                total += gate_up_in[slot, to_core, to_z, part].astype(jnp.float32)
            gate_up_sum[to_core, to_z, part] = total.astype(jnp.bfloat16)

        chunks(64, body)

    def turn_block(to_core, to_z):
        whole = gate_up_sum.at[to_core, to_z]
        return [
            (whole.at[:, src], gate_up_came.at[:, dst]) for dst, src in segments(core, z)
        ], whole

    for step, peer, peer_cross in zip(steps, line, cross):
        to = ahead(z, step)
        move.send_parts(*turn_block(core, to), peer)
        move.send_parts(*turn_block(other, to), peer_cross)
    move.send_parts(*turn_block(other, z), partner)
    move.keep_parts(*turn_block(core, z))
    move.arrive(*qkv_pieces)

    @pl.loop(0, 8)
    def _(block):
        def body(part):
            total = qkv_part[block, z, part].astype(jnp.float32)
            for step in steps:
                total += qkv_in[ahead(z, step), block, part].astype(jnp.float32)
            qkv_sum[block, part] = total.astype(jnp.bfloat16)

        chunks(64, body)

    for peer in [partner] + plane + plane_cross:
        move.send(qkv_sum.at[peer[0]], qkv_came.at[me], peer)
    move.keep(qkv_sum.at[me], qkv_came.at[me])
    move.finish()


COL_ROWS, GAIN_ROWS = 184, 33
MATRICES = ((64, QKV, 0, 0), (64, D, 64, 24), (64, 2 * FF, 128, 40), (256, D, 192, 168))
ROW_TOTALS = (D, HEADS * HEAD_DIM, D, FF)
BETA = 1.0 - STEP ** (-0.8)


def lane_value(vector, lane):
    lanes = lax.broadcasted_iota(jnp.int32, (1, 128), 1)
    return jnp.sum(jnp.where(lanes == lane, vector, 0.0), axis=-1, keepdims=True)


def statistics_kernel(
    d_norm, tok, d_hidden_in, gain, gain_ffn, gain_qk, qkv, out, gate_up, down, rows,
    m_qkv, m_out, m_gate_up, m_down,
    grad_tok, g_qkv, g_out, g_gate_up, g_down, rows_new, packed,
    gain_part, sums, inverse,
):
    gain_part[...] = jnp.zeros_like(gain_part)

    @pl.loop(0, 128 // CHUNK)
    def _(step):
        part = pl.ds(pl.multiple_of(step * CHUNK, CHUNK), CHUNK)
        total = d_norm[0, part].astype(jnp.float32)
        for slot in range(1, 4):
            total += d_norm[slot, part].astype(jnp.float32)
        entries = tok[part].astype(jnp.float32)
        scale = lax.rsqrt(jnp.mean(entries * entries, axis=-1, keepdims=True) + EPSILON)
        gain_part[...] += jnp.sum(total * entries * scale, axis=0, keepdims=True)
        total = total * gain[...]
        inner = jnp.mean(total * entries, axis=-1, keepdims=True) * (scale * scale * scale)
        grad_tok[part] = (d_hidden_in[part] + total * scale - entries * inner).astype(jnp.bfloat16)

    first = 2 * COL_ROWS
    for slot in range(16):
        lanes = pl.ds(slot * 128, 128)
        packed[first + slot : first + slot + 1] = gain_part[:, lanes]
        packed[first + 16 + slot : first + 17 + slot] = gain_ffn[:, lanes]
    packed[first + 32 : first + 33] = gain_qk[...]
    lane = lax.broadcasted_iota(jnp.int32, (64, 128), 1)

    def wide(step):
        return pl.ds(pl.multiple_of(step * 128, 128), 128)

    def read_qkv(step):
        return g_qkv[:, wide(step)]

    for head in range(8):
        for half in range(2):
            g_qkv[:, pl.ds(head * 256 + half * 128, 128)] = qkv[
                head, :, pl.ds(half * 128, 128)
            ].astype(jnp.float32)
    for pair in range(4):
        low = qkv[2 * pair, :, pl.ds(256, 128)].astype(jnp.float32)
        high = qkv[2 * pair + 1, :, pl.ds(256, 128)].astype(jnp.float32)
        g_qkv[:, pl.ds(2048 + pair * 128, 128)] = jnp.where(lane < 64, low, pltpu.roll(high, 64, 1))
        g_qkv[:, pl.ds(2560 + pair * 128, 128)] = jnp.where(lane < 64, pltpu.roll(low, 64, 1), high)

    def read_out(step):
        total = out[0, :, wide(step)].astype(jnp.float32)
        for slot in range(1, 4):
            total += out[slot, :, wide(step)].astype(jnp.float32)
        return total

    def read_gate_up(step):
        return gate_up[:, wide(step)].astype(jnp.float32)

    def read_down(step):
        total = down[0, :, wide(step)].astype(jnp.float32)
        for slot in range(1, 4):
            total += down[slot, :, wide(step)].astype(jnp.float32)
        return total

    readers = (read_qkv, read_out, read_gate_up, read_down)
    grads = (g_qkv, g_out, g_gate_up, g_down)
    masters = (m_qkv, m_out, m_gate_up, m_down)
    stats = jnp.zeros((1, 128), jnp.float32)
    lanes = lax.broadcasted_iota(jnp.int32, (1, 128), 1)
    for slot, (count, width, row_at, col_at) in enumerate(MATRICES):
        own = pl.ds(0, count)
        sums[0, own] = jnp.zeros((count, 128), jnp.float32)
        sums[1, own] = jnp.zeros((count, 128), jnp.float32)

        @pl.loop(0, width // 128)
        def _(step, slot=slot, own=own):
            entries = readers[slot](step)
            if slot > 0:
                grads[slot][:, wide(step)] = entries
            sums[0, own] += entries * entries
            weight = masters[slot][:, wide(step)]
            sums[1, own] += weight * weight

        mean = jnp.sum(sums[0, own], axis=-1, keepdims=True) / width + SQUARE_EPSILON
        here_rows = pl.ds(row_at, count)
        new = BETA * rows[here_rows] + (1.0 - BETA) * mean
        rows_new[here_rows] = new
        inverse[own] = jnp.broadcast_to(1.0 / new, (count, 128))
        weight_sum = jnp.sum(jnp.sum(sums[1, own], axis=-1, keepdims=True), axis=0, keepdims=True)
        stats = jnp.where(lanes == slot, jnp.sum(new, axis=0, keepdims=True), stats)
        stats = jnp.where(lanes == 4 + slot, weight_sum, stats)

        @pl.loop(0, width // 128)
        def _(step, slot=slot, own=own, count=count, col_at=col_at):
            entries = grads[slot][:, wide(step)]
            square = entries * entries
            packed[pl.ds(col_at + step, 1)] = (
                jnp.sum(square, axis=0, keepdims=True) + count * SQUARE_EPSILON
            )
            packed[pl.ds(COL_ROWS + col_at + step, 1)] = jnp.sum(
                square * inverse[own], axis=0, keepdims=True
            )

    packed[first + 33 : first + 34] = stats
    packed[first + 34 : 512] = jnp.zeros((512 - first - 34, 128), jnp.float32)


def total_kernel(
    parts, col_moments, gain_moments, gains,
    cols_new, col_factors, moments_new, gains_new, grad_gains, spreads,
    totals, plane_came, line_came, plane_sum, line_sum, line_all, *sems,
):
    chip, core, z = here()
    me = 2 * chip + core
    other = 1 - core
    plane = [at_place(chip, other, z)]
    for peer_chip in flips(chip):
        plane += [at_place(peer_chip, core, z), at_place(peer_chip, other, z)]
    line = [at_place(chip, core, ahead(z, step)) for step in (2, 1, 3)]
    greet(plane + line)
    move = Mover(*sems)
    pieces = [move.send(parts.at[peer[0]], plane_came.at[me], peer) for peer in plane]
    plane_came[me] = parts[me]
    move.arrive(*pieces)
    total = plane_came[0]
    for slot in range(1, 8):
        total = total + plane_came[slot]
    plane_sum[...] = total
    pieces = [move.send(plane_sum.at[peer[1]], line_came.at[z], peer) for peer in line]
    line_came[z] = plane_sum[z]
    move.arrive(*pieces)
    line_sum[...] = line_came[0] + line_came[1] + line_came[2] + line_came[3]
    pieces = [move.send(line_sum, line_all.at[z], peer) for peer in line]
    line_all[z] = line_sum[...]
    move.arrive(*pieces)
    for peer in plane:
        move.send(line_all, totals.at[me], peer)
    totals[me] = line_all[...]
    move.finish()
    flat = totals.reshape(512, 128)
    first = 2 * COL_ROWS
    stats = flat[first + 33 : first + 34]
    lanes = lax.broadcasted_iota(jnp.int32, (1, 128), 1)
    out = jnp.zeros((1, 128), jnp.float32)
    for slot, (_, width, _, col_at) in enumerate(MATRICES):
        own = pl.ds(col_at, width // 128)
        entries_all = float(ROW_TOTALS[slot] * width)
        new = BETA * col_moments[own] + (1.0 - BETA) * (flat[own] / ROW_TOTALS[slot])
        cols_new[own] = new
        mean_rows = lane_value(stats, slot) / ROW_TOTALS[slot]
        ratio = flat[pl.ds(COL_ROWS + col_at, width // 128)] / new
        ratio = jnp.sum(jnp.sum(ratio, axis=-1, keepdims=True), axis=0, keepdims=True)
        spread = jnp.sqrt(mean_rows * ratio / entries_all)
        scale = STEP_RATE * jnp.maximum(
            SCALE_EPSILON, jnp.sqrt(lane_value(stats, 4 + slot) / entries_all)
        )
        factor = scale * jnp.sqrt(mean_rows) / jnp.maximum(1.0, spread / CLIP_LEVEL)
        col_factors[own] = lax.rsqrt(new) * factor
        out = jnp.where(lanes == slot, spread, out)
    gradient = flat[first : first + GAIN_ROWS]
    grad_gains[...] = gradient
    old = gains[...]
    new = BETA * gain_moments[...] + (1.0 - BETA) * (gradient * gradient + SQUARE_EPSILON)
    moments_new[...] = new
    unit = gradient * lax.rsqrt(new)
    row = lax.broadcasted_iota(jnp.int32, (GAIN_ROWS, 128), 0)
    lane = lax.broadcasted_iota(jnp.int32, (GAIN_ROWS, 128), 1)
    segment = jnp.where(row < 16, 0, jnp.where(row < 32, 1, jnp.where(lane < 64, 2, 3)))
    factors = jnp.zeros((GAIN_ROWS, 128), jnp.float32)

    def mean_of(square, mask, count):
        picked = jnp.where(mask, square, 0.0)
        return jnp.sum(jnp.sum(picked, axis=-1, keepdims=True), axis=0, keepdims=True) / count

    for slot, count in enumerate((D, D, HEAD_DIM, HEAD_DIM)):
        mask = segment == slot
        spread = jnp.sqrt(mean_of(unit * unit, mask, count))
        scale = STEP_RATE * jnp.maximum(SCALE_EPSILON, jnp.sqrt(mean_of(old * old, mask, count)))
        factors = jnp.where(mask, scale / jnp.maximum(1.0, spread / CLIP_LEVEL), factors)
        out = jnp.where(lanes == 4 + slot, spread, out)
    gains_new[...] = old - factors * unit
    spreads[...] = out


def head_split(entries):
    rows = entries.shape[0]
    parts = (
        entries[:, :2048].reshape(rows, 8, 256),
        entries[:, 2048:2560].reshape(rows, 8, 64),
        entries[:, 2560:].reshape(rows, 8, 64),
    )
    return jnp.concatenate(parts, axis=2).transpose(1, 0, 2)


def head_join(blocks):
    rows = blocks.shape[1]
    blocks = blocks.transpose(1, 0, 2)
    parts = (blocks[..., :256], blocks[..., 256:320], blocks[..., 320:])
    return jnp.concatenate([part.reshape(rows, -1) for part in parts], axis=1)


def split_local(
    tokens, doc_starts, grad_out, qkv_master, out_master, gate_up_master, down_master, gains,
    qkv_rows, out_rows, gate_up_rows, down_rows, col_moments, gain_moments,
):
    half, full = jnp.bfloat16, jnp.float32
    gain_attn = gains[:D]
    gain_ffn = gains[D : 2 * D]
    gain_query = gains[2 * D : 2 * D + HEAD_DIM]
    gain_key = gains[2 * D + HEAD_DIM :]
    length, group = 512, 4
    tokens_wide = tokens.astype(full)
    normed = norm_rows(tokens_wide, gain_attn).astype(half)
    all_tok, all_wq, all_wo, all_wd = exchange(
        attention_weights_kernel, 0,
        [
            (normed, False), (head_split(qkv_master.astype(half)), False),
            (out_master.astype(half), False), (down_master.astype(half), False),
        ],
        [
            ((2, 8, 64, D), half, False), ((8, 4, 64, 384), half, False), ((4, 64, D), half, False),
            ((4, 256, D), half, False),
        ],
        [], (23, 4), 16 << 20,
    )
    all_tok = all_tok.reshape(2, length, D)
    w_qkv = all_wq.reshape(D, 384)
    w_out = all_wo.reshape(256, D)

    places = jnp.arange(length, dtype=jnp.int32)
    docs, offsets = doc_tables(doc_starts, places)
    cos_table, sin_table = rotary(offsets)
    allowed = mask_of(docs, places, docs, places)[:, 0]
    projected = jnp.einsum("rtd,de->rte", all_tok, w_qkv, preferred_element_type=full)
    head_fn = partial(queries_keys, cos_table, sin_table, heads=group, kv_heads=1)
    queries, keys = head_fn(projected[..., :320], gain_query, gain_key)
    query16 = queries.astype(half)
    keys16 = keys.astype(half)[:, :, 0]
    values16 = projected[..., 320:].astype(half)
    scores = jnp.einsum("rqgh,rth->rgqt", query16, keys16, preferred_element_type=full)
    scores = jnp.where(allowed, scores, MASKED_SCORE)
    best = jnp.max(scores, axis=-1, keepdims=True)
    weights = jnp.where(allowed, jnp.exp(scores - best), 0.0)
    probs = weights / jnp.sum(weights, axis=-1, keepdims=True)
    probs16 = probs.astype(half)
    attended = jnp.einsum("rgqt,rth->rqgh", probs16, values16, preferred_element_type=full)
    attended16 = attended.astype(half).reshape(2, length, 256)
    branch = jnp.einsum("rtc,cd->rtd", attended16, w_out, preferred_element_type=full)

    def near(*shape, kind=half):
        return pltpu.VMEM(shape, kind)

    all_branch, d_hidden_in, output, grad_gain_ffn, down_part, gate_up_in = exchange(
        ffn_kernel, 1,
        [
            (branch.astype(half).reshape(2, 8, 64, D), True), (tokens, True), (gain_ffn[None], True),
            (gate_up_master.astype(half), False), (all_wd, False), (grad_out, True),
        ],
        [
            ((8, 2, 64, D), half, False), ((2, 64, D), full, True), ((2, 64, D), half, True),
            ((1, D), full, True), ((4, 256, D), half, False), ((4, 2, 4, 64, 2048), half, False),
        ],
        [
            near(4, 2, 64, D), near(4, 2, 64, D), near(2, 64, D), near(2, 64, D, kind=full),
            near(4, 2, 2, 64, D), near(4, 2, 2, 64, D), near(4, 2, 4, 64, 2048), near(4, 256, D),
            near(4, 256, 1024), near(4, 256, 2048), near(4, 2, 2, 64, D),
            near(4, 2, 64, D), near(4, 2, 64, D), near(2, 64, D),
        ],
        (60, 8), 64 << 20, 39 << 30,
    )
    d_branch = all_branch.reshape(8, 2, 64, D).transpose(1, 0, 2, 3).reshape(2, length, D)
    term_out = jnp.einsum("rtc,rtd->cd", attended16, d_branch, preferred_element_type=full).astype(half)
    d_heads = jnp.einsum("rtd,cd->rtc", d_branch, w_out, preferred_element_type=full).astype(half)
    d_heads = d_heads.reshape(2, length, group, HEAD_DIM)
    delta = jnp.sum(d_heads.astype(full) * attended, axis=-1).transpose(0, 2, 1)
    d_values = jnp.einsum("rgqt,rqgh->rth", probs16, d_heads, preferred_element_type=full)
    d_probs = jnp.einsum("rqgh,rth->rgqt", d_heads, values16, preferred_element_type=full)
    d_scores = (probs * (d_probs - delta[..., None])).astype(half)
    d_queries = jnp.einsum("rgqt,rth->rqgh", d_scores, keys16, preferred_element_type=full)
    d_keys = jnp.einsum("rgqt,rqgh->rth", d_scores, query16, preferred_element_type=full)
    _, heads_back = jax.vjp(head_fn, projected[..., :320], gain_query, gain_key)
    d_heads_in, grad_gain_query, grad_gain_key = heads_back((d_queries, d_keys[:, :, None]))
    d_projected = jnp.concatenate([d_heads_in, d_values], axis=-1).astype(half)
    term_qkv = jnp.einsum("rtd,rte->de", all_tok, d_projected, preferred_element_type=full).astype(half)
    d_normed = jnp.einsum("rte,de->rtd", d_projected, w_qkv, preferred_element_type=full).astype(half)

    d_norm_came, gate_up_came, qkv_came, out_came, down_came = exchange(
        gradients_kernel, 3,
        [
            (d_normed.reshape(2, 8, 64, D), True), (gate_up_in, True),
            (term_qkv.reshape(8, 4, 64, 384), True), (term_out.reshape(4, 64, D), False),
            (down_part, False),
        ],
        [
            ((4, 2, 64, D), half, False), ((64, 2 * FF), half, False),
            ((8, 64, 384), half, False), ((4, 64, D), half, False), ((4, 256, D), half, False),
        ],
        [
            near(4, 2, 64, D), near(4, 2, 64, D), near(2, 4, 64, 2048),
            near(4, 8, 64, 384), near(8, 64, 384),
        ],
        (30, 5), 48 << 20,
    )
    row_states = jnp.concatenate([qkv_rows, out_rows, gate_up_rows, down_rows])[:, None]
    masters = (qkv_master, out_master, gate_up_master, down_master)
    grad_tokens, *grads, rows_new, packed = pl.pallas_call(
        statistics_kernel,
        out_shape=[
            jax.ShapeDtypeStruct((128, D), half),
            *[jax.ShapeDtypeStruct((count, width), full) for count, width, _, _ in MATRICES],
            jax.ShapeDtypeStruct((448, 1), full),
            jax.ShapeDtypeStruct((512, 128), full),
        ],
        scratch_shapes=[
            pltpu.VMEM((1, D), full), pltpu.VMEM((2, 256, 128), full), pltpu.VMEM((256, 128), full),
        ],
        compiler_params=pltpu.CompilerParams(vmem_limit_bytes=VMEM_BYTES),
    )(
        d_norm_came.reshape(4, 128, D), tokens.reshape(128, D), d_hidden_in.reshape(128, D), gain_attn[None],
        grad_gain_ffn, jnp.concatenate([grad_gain_query, grad_gain_key])[None],
        qkv_came, out_came, gate_up_came, down_came, row_states, *masters,
    )
    shape = (8, 4, 16, 128)
    cols_new, col_factors, moments_new, gains_new, grad_gains, spreads = exchange(
        total_kernel, 4,
        [
            (packed.reshape(shape), True), (col_moments.reshape(-1, 128), True),
            (gain_moments.reshape(-1, 128), True), (gains.reshape(-1, 128), True),
        ],
        [
            ((COL_ROWS, 128), full, True), ((COL_ROWS, 128), full, True),
            ((GAIN_ROWS, 128), full, True), ((GAIN_ROWS, 128), full, True),
            ((GAIN_ROWS, 128), full, True), ((1, 128), full, True),
        ],
        [
            pltpu.VMEM(shape, full), pltpu.VMEM(shape, full), pltpu.VMEM(shape[1:], full),
            pltpu.VMEM(shape[1:], full), pltpu.VMEM(shape[2:], full), pltpu.VMEM(shape[1:], full),
        ],
        (20, 0), 1 << 20,
    )
    col_factors = col_factors.reshape(-1)
    row_factors = lax.rsqrt(rows_new[:, 0])
    new_masters = []
    for slot, (count, width, row_at, col_at) in enumerate(MATRICES):
        row_factor = row_factors[row_at : row_at + count]
        col_factor = col_factors[col_at * 128 : col_at * 128 + width]
        new_masters.append(
            masters[slot] - grads[slot] * row_factor[:, None] * col_factor[None, :]
        )
    return (
        output,
        grad_tokens.reshape(2, 64, D),
        *grads,
        grad_gains.reshape(-1),
        *[rows_new[row_at : row_at + count, 0] for count, _, row_at, _ in MATRICES],
        cols_new.reshape(-1),
        moments_new.reshape(-1),
        *new_masters,
        *[master.astype(half) for master in new_masters],
        gains_new.reshape(-1),
        spreads[0, :8],
    )


def optimizer_step(
    grads, gain_local, masters, gains, row_states, col_moments, gain_moments, total_fn
):
    beta = 1.0 - STEP ** (-0.8)
    col_widths = (QKV, D, 2 * FF, D)
    row_totals = (D, HEADS * HEAD_DIM, D, FF)
    squares = [gradient * gradient + SQUARE_EPSILON for gradient in grads]
    rows_new = [
        beta * row_state + (1.0 - beta) * jnp.mean(square, axis=1)
        for row_state, square in zip(row_states, squares)
    ]
    col_local = [jnp.sum(square, axis=0) for square in squares]
    weighted_local = [
        jnp.sum(gradient * gradient / row_new[:, None], axis=0)
        for gradient, row_new in zip(grads, rows_new)
    ]
    stats_local = jnp.stack(
        [jnp.sum(row_new) for row_new in rows_new]
        + [jnp.sum(master * master) for master in masters]
    )
    totals = total_fn(jnp.concatenate(col_local + weighted_local + [stats_local, gain_local]))
    cols = sum(col_widths)
    col_sums, weighted = totals[:cols], totals[cols : 2 * cols]
    stats, grad_gains = totals[2 * cols : 2 * cols + 8], totals[2 * cols + 8 :]
    col_divisor = jnp.concatenate(
        [
            jnp.full((col_width,), float(row_total), jnp.float32)
            for col_width, row_total in zip(col_widths, row_totals)
        ]
    )
    cols_new = beta * col_moments + (1.0 - beta) * col_sums / col_divisor
    new_masters = []
    spreads = []
    begin_at = 0
    for slot in range(4):
        col_part = cols_new[begin_at : begin_at + col_widths[slot]]
        weighted_part = weighted[begin_at : begin_at + col_widths[slot]]
        begin_at = begin_at + col_widths[slot]
        mean_rows = stats[slot] / row_totals[slot]
        unit = (
            grads[slot]
            * lax.rsqrt(rows_new[slot] / mean_rows)[:, None]
            * lax.rsqrt(col_part)[None, :]
        )
        entries_all = float(row_totals[slot] * col_widths[slot])
        spread = jnp.sqrt(mean_rows * jnp.sum(weighted_part / col_part) / entries_all)
        scale = STEP_RATE * jnp.maximum(SCALE_EPSILON, jnp.sqrt(stats[4 + slot] / entries_all))
        new_masters.append(masters[slot] - scale * unit / jnp.maximum(1.0, spread / CLIP_LEVEL))
        spreads.append(spread)
    bounds = (0, D, 2 * D, 2 * D + HEAD_DIM, 2 * D + 2 * HEAD_DIM)
    moment_parts, gain_parts = ([], [])
    for segment in range(4):
        gradient = grad_gains[bounds[segment] : bounds[segment + 1]]
        gain_old = gains[bounds[segment] : bounds[segment + 1]]
        moment_new = beta * gain_moments[bounds[segment] : bounds[segment + 1]] + (1.0 - beta) * (
            gradient * gradient + SQUARE_EPSILON
        )
        unit = gradient * lax.rsqrt(moment_new)
        spread = jnp.sqrt(jnp.mean(unit * unit))
        scale = STEP_RATE * jnp.maximum(SCALE_EPSILON, jnp.sqrt(jnp.mean(gain_old * gain_old)))
        moment_parts.append(moment_new)
        gain_parts.append(gain_old - scale * unit / jnp.maximum(1.0, spread / CLIP_LEVEL))
        spreads.append(spread)
    return (
        grad_gains,
        *rows_new,
        cols_new,
        jnp.concatenate(moment_parts),
        *new_masters,
        *[master.astype(jnp.bfloat16) for master in new_masters],
        jnp.concatenate(gain_parts),
        jnp.stack(spreads),
    )


def solution(mesh):
    split = mesh.shape["seq"] == 8 and mesh.shape["rows"] == 4
    return jax.shard_map(
        split_local if split else gathered_local,
        mesh=mesh,
        in_specs=(
            P("rows", "seq", None),
            P("rows", None),
            P("rows", "seq", None),
            P(("seq", "rows"), None),
            P(("seq", "rows"), None),
            P(("seq", "rows"), None),
            P(("seq", "rows"), None),
            P(),
            P(("seq", "rows")),
            P(("seq", "rows")),
            P(("seq", "rows")),
            P(("seq", "rows")),
            P(),
            P(),
        ),
        out_specs=(
            P("rows", "seq", None),
            P("rows", "seq", None),
            P(("seq", "rows"), None),
            P(("seq", "rows"), None),
            P(("seq", "rows"), None),
            P(("seq", "rows"), None),
            P(),
            P(("seq", "rows")),
            P(("seq", "rows")),
            P(("seq", "rows")),
            P(("seq", "rows")),
            P(),
            P(),
            P(("seq", "rows"), None),
            P(("seq", "rows"), None),
            P(("seq", "rows"), None),
            P(("seq", "rows"), None),
            P(("seq", "rows"), None),
            P(("seq", "rows"), None),
            P(("seq", "rows"), None),
            P(("seq", "rows"), None),
            P(),
            P(),
        ),
        check_vma=False,
    )
```

```python
from functools import partial

import jax
import jax.numpy as jnp
from jax import lax
from jax.experimental import pallas as pl
from jax.experimental.pallas import tpu as pltpu
from jax.sharding import PartitionSpec as P

D = 2048
HEADS = 32
KV_HEADS = 8
HEAD_DIM = 64
FF = 8192
STEP = 10
QKV = 3072


EPSILON = 1e-06
ROPE_BASE = 10000.0
MASKED_SCORE = -1e30
STEP_RATE = 0.3
CLIP_LEVEL = 1.0
SQUARE_EPSILON = 1e-30
SCALE_EPSILON = 0.001


def from_behind(value, axis, steps):
    count = lax.axis_size(axis)
    pairs = [(source, (source + steps) % count) for source in range(count)]
    return lax.ppermute(value, axis, pairs)


def norm_rows(entries, gain):
    return entries * lax.rsqrt(jnp.mean(entries * entries, axis=-1, keepdims=True) + EPSILON) * gain


def turn(entries, cos_wide, sin_wide):
    half_width = entries.shape[-1] // 2
    turned = jnp.concatenate([-entries[..., half_width:], entries[..., :half_width]], axis=-1)
    return entries * cos_wide + turned * sin_wide


def doc_tables(doc_starts, places):
    before = doc_starts[:, None, :] <= places[None, :, None]
    doc_ids = jnp.sum(before.astype(jnp.int32), axis=-1)
    doc_first = jnp.max(jnp.where(before, doc_starts[:, None, :], 0), axis=-1)
    return (doc_ids, places[None, :] - doc_first)


def rotary(offsets):
    frequency = ROPE_BASE ** (-(jnp.arange(HEAD_DIM // 2, dtype=jnp.float32) * 2.0 / HEAD_DIM))
    angles = offsets.astype(jnp.float32)[..., None] * frequency
    cos_table = jnp.concatenate([jnp.cos(angles), jnp.cos(angles)], axis=-1)
    sin_table = jnp.concatenate([jnp.sin(angles), jnp.sin(angles)], axis=-1)
    return (cos_table, sin_table)


def queries_keys(
    cos_table, sin_table, projected, gain_query, gain_key, heads=HEADS, kv_heads=KV_HEADS
):
    rows_here, seq_here = (projected.shape[0], projected.shape[1])
    att_width = heads * HEAD_DIM
    queries = projected[..., :att_width].reshape(rows_here, seq_here, heads, HEAD_DIM)
    keys_rot = projected[..., att_width : att_width + kv_heads * HEAD_DIM].reshape(
        rows_here, seq_here, kv_heads, HEAD_DIM
    )
    cos_wide = cos_table[:, :, None, :]
    sin_wide = sin_table[:, :, None, :]
    queries = turn(norm_rows(queries, gain_query), cos_wide, sin_wide) * HEAD_DIM ** (-0.5)
    keys_rot = turn(norm_rows(keys_rot, gain_key), cos_wide, sin_wide)
    return (queries, keys_rot)


def mask_of(query_docs, query_places, key_docs, key_places):
    same_doc = query_docs[:, :, None] == key_docs[:, None, :]
    causal = query_places[None, :, None] >= key_places[None, None, :]
    return (same_doc & causal)[:, None, None, :, :]


def gathered_local(
    tokens,
    doc_starts,
    grad_out,
    qkv_master,
    out_master,
    gate_up_master,
    down_master,
    gains,
    qkv_rows,
    out_rows,
    gate_up_rows,
    down_rows,
    col_moments,
    gain_moments,
):
    cycle_size = lax.axis_size("seq")
    seq_index = lax.axis_index("seq")
    rows_dev, seq_dev = (tokens.shape[0], tokens.shape[1])
    group_size = HEADS // KV_HEADS
    att_width = HEADS * HEAD_DIM
    kv_width = KV_HEADS * HEAD_DIM
    gain_attn = gains[:D]
    gain_ffn = gains[D : 2 * D]
    gain_query = gains[2 * D : 2 * D + HEAD_DIM]
    gain_key = gains[2 * D + HEAD_DIM :]
    local_places = jnp.arange(seq_dev, dtype=jnp.int32)
    places = seq_index * seq_dev + local_places
    query_docs, offsets = doc_tables(doc_starts, places)
    cos_table, sin_table = rotary(offsets)
    copies = (
        qkv_master.astype(jnp.bfloat16),
        out_master.astype(jnp.bfloat16),
        gate_up_master.astype(jnp.bfloat16),
        down_master.astype(jnp.bfloat16),
    )
    w_qkv, w_out, w_gate_up, w_down = (
        lax.all_gather(copies[0], ("seq", "rows"), axis=0, tiled=True),
        lax.all_gather(copies[1], ("seq", "rows"), axis=0, tiled=True),
        lax.all_gather(copies[2], ("seq", "rows"), axis=0, tiled=True),
        lax.all_gather(copies[3], ("seq", "rows"), axis=0, tiled=True),
    )
    tokens_wide = tokens.astype(jnp.float32)
    normed = norm_rows(tokens_wide, gain_attn).astype(jnp.bfloat16)
    projected = jnp.einsum("rtd,de->rte", normed, w_qkv, preferred_element_type=jnp.float32)
    head_fn = partial(queries_keys, cos_table, sin_table)
    queries, keys_rot = head_fn(projected, gain_query, gain_key)
    query16 = queries.astype(jnp.bfloat16).reshape(
        rows_dev, seq_dev, KV_HEADS, group_size, HEAD_DIM
    )
    keys16 = keys_rot.astype(jnp.bfloat16).reshape(rows_dev, seq_dev, kv_width)
    values16 = projected[..., att_width + kv_width :].astype(jnp.bfloat16)
    stat_shape = (rows_dev, KV_HEADS, group_size, seq_dev)
    initial = (
        jnp.full(stat_shape, MASKED_SCORE, jnp.float32),
        jnp.zeros(stat_shape, jnp.float32),
        jnp.zeros(stat_shape + (HEAD_DIM,), jnp.float32),
    )
    carry = initial
    key_piece = lax.all_gather(keys16, "seq", axis=1, tiled=True)
    value_piece = lax.all_gather(values16, "seq", axis=1, tiled=True)
    key_count = key_piece.shape[1]

    def absorb_block(state, block_index):
        best, total, summed = state
        block_begin = block_index * seq_dev
        key_block = lax.dynamic_slice_in_dim(key_piece, block_begin, seq_dev, 1).reshape(
            rows_dev, seq_dev, KV_HEADS, HEAD_DIM
        )
        value_block = lax.dynamic_slice_in_dim(value_piece, block_begin, seq_dev, 1).reshape(
            rows_dev, seq_dev, KV_HEADS, HEAD_DIM
        )
        key_places = block_begin + jnp.arange(seq_dev, dtype=jnp.int32)
        key_docs, _ = doc_tables(doc_starts, key_places)
        allowed = mask_of(query_docs, places, key_docs, key_places)
        scores = jnp.einsum(
            "rqkgh,rtkh->rkgqt", query16, key_block, preferred_element_type=jnp.float32
        )
        scores = jnp.where(allowed, scores, MASKED_SCORE)
        best_new = jnp.maximum(best, jnp.max(scores, axis=-1))
        weights = jnp.where(allowed, jnp.exp(scores - best_new[..., None]), 0.0)
        factor = jnp.exp(best - best_new)
        total = total * factor + jnp.sum(weights, axis=-1)
        summed = summed * factor[..., None] + jnp.einsum(
            "rkgqt,rtkh->rkgqh",
            weights.astype(jnp.bfloat16),
            value_block,
            preferred_element_type=jnp.float32,
        )
        return ((best_new, total, summed), None)

    carry, _ = lax.scan(absorb_block, carry, jnp.arange(key_count // seq_dev, dtype=jnp.int32))
    best, total, summed = carry
    log_total = best + jnp.log(total)
    attended = summed / total[..., None]
    attended16 = (
        attended.transpose(0, 3, 1, 2, 4).reshape(rows_dev, seq_dev, att_width).astype(jnp.bfloat16)
    )
    branch = jnp.einsum("rtc,cd->rtd", attended16, w_out, preferred_element_type=jnp.float32)
    hidden_in = tokens_wide + branch
    normed2 = norm_rows(hidden_in, gain_ffn).astype(jnp.bfloat16)
    gate_up = jnp.einsum("rtd,df->rtf", normed2, w_gate_up, preferred_element_type=jnp.float32)
    gate_part, up_part = (gate_up[..., :FF], gate_up[..., FF:])
    hidden = (jax.nn.silu(gate_part) * up_part).astype(jnp.bfloat16)
    output = hidden_in + jnp.einsum(
        "rtf,fd->rtd", hidden, w_down, preferred_element_type=jnp.float32
    )
    d_hidden = jnp.einsum("rtd,fd->rtf", grad_out, w_down, preferred_element_type=jnp.float32)
    silu_value, silu_back = jax.vjp(jax.nn.silu, gate_part)
    d_gate = silu_back(d_hidden * up_part)[0]
    d_gate_up = jnp.concatenate([d_gate, d_hidden * silu_value], axis=-1).astype(jnp.bfloat16)
    d_normed2 = jnp.einsum("rtf,df->rtd", d_gate_up, w_gate_up, preferred_element_type=jnp.float32)
    _, ffn_norm_back = jax.vjp(norm_rows, hidden_in, gain_ffn)
    d_inner, grad_gain_ffn = ffn_norm_back(d_normed2)
    d_hidden_in = grad_out.astype(jnp.float32) + d_inner
    term_down = jnp.einsum("rtf,rtd->fd", hidden, grad_out, preferred_element_type=jnp.float32)
    grad_down = lax.psum_scatter(term_down, ("seq", "rows"), scatter_dimension=0, tiled=True)
    term_gate_up = jnp.einsum("rtd,rtf->df", normed2, d_gate_up, preferred_element_type=jnp.float32)
    grad_gate_up = lax.psum_scatter(term_gate_up, ("seq", "rows"), scatter_dimension=0, tiled=True)
    d_branch = d_hidden_in.astype(jnp.bfloat16)
    term_out = jnp.einsum("rtc,rtd->cd", attended16, d_branch, preferred_element_type=jnp.float32)
    d_attended = jnp.einsum(
        "rtd,cd->rtc", d_branch, w_out, preferred_element_type=jnp.float32
    ).astype(jnp.bfloat16)
    d_heads = d_attended.reshape(rows_dev, seq_dev, KV_HEADS, group_size, HEAD_DIM).transpose(
        0, 2, 3, 1, 4
    )
    delta = jnp.sum(d_heads.astype(jnp.float32) * attended, axis=-1)

    def cycle_turn(turn_index, carry):
        pair16, grad_pair, d_queries = carry
        source = (seq_index + turn_index) % cycle_size
        key_places = source * seq_dev + local_places
        key_docs, _ = doc_tables(doc_starts, key_places)
        allowed = mask_of(query_docs, places, key_docs, key_places)
        key_block = pair16[0].reshape(rows_dev, seq_dev, KV_HEADS, HEAD_DIM)
        value_block = pair16[1].reshape(rows_dev, seq_dev, KV_HEADS, HEAD_DIM)
        scores = jnp.einsum(
            "rqkgh,rtkh->rkgqt", query16, key_block, preferred_element_type=jnp.float32
        )
        scores = jnp.where(allowed, scores, MASKED_SCORE)
        probs = jnp.where(allowed, jnp.exp(scores - log_total[..., None]), 0.0)
        d_values = jnp.einsum(
            "rkgqt,rkgqh->rtkh",
            probs.astype(jnp.bfloat16),
            d_heads,
            preferred_element_type=jnp.float32,
        )
        d_probs = jnp.einsum(
            "rkgqh,rtkh->rkgqt", d_heads, value_block, preferred_element_type=jnp.float32
        )
        d_scores = (probs * (d_probs - delta[..., None])).astype(jnp.bfloat16)
        d_queries = d_queries + jnp.einsum(
            "rkgqt,rtkh->rkgqh", d_scores, key_block, preferred_element_type=jnp.float32
        )
        d_keys = jnp.einsum(
            "rkgqt,rqkgh->rtkh", d_scores, query16, preferred_element_type=jnp.float32
        )
        grad_pair = grad_pair + jnp.stack(
            [
                d_keys.reshape(rows_dev, seq_dev, kv_width),
                d_values.reshape(rows_dev, seq_dev, kv_width),
            ]
        )
        grad_pair = from_behind(grad_pair.astype(jnp.bfloat16), "seq", -1).astype(grad_pair.dtype)
        pair16 = from_behind(pair16, "seq", -1)
        return (pair16, grad_pair, d_queries)

    start_pair = jnp.stack([keys16, values16])
    start_grads = jnp.zeros((2, rows_dev, seq_dev, kv_width), jnp.float32)
    start_queries = jnp.zeros(stat_shape + (HEAD_DIM,), jnp.float32)
    _, grad_pair, d_queries = lax.fori_loop(
        0, cycle_size, cycle_turn, (start_pair, start_grads, start_queries)
    )
    d_queries = d_queries.transpose(0, 3, 1, 2, 4).reshape(rows_dev, seq_dev, HEADS, HEAD_DIM)
    d_keys_home = grad_pair[0].reshape(rows_dev, seq_dev, KV_HEADS, HEAD_DIM)
    _, heads_back = jax.vjp(head_fn, projected, gain_query, gain_key)
    d_projected, grad_gain_query, grad_gain_key = heads_back((d_queries, d_keys_home))
    d_projected = jnp.concatenate(
        [d_projected[..., : att_width + kv_width], grad_pair[1]], axis=-1
    ).astype(jnp.bfloat16)
    term_qkv = jnp.einsum("rtd,rte->de", normed, d_projected, preferred_element_type=jnp.float32)
    d_normed = jnp.einsum("rte,de->rtd", d_projected, w_qkv, preferred_element_type=jnp.float32)
    _, attn_norm_back = jax.vjp(norm_rows, tokens_wide, gain_attn)
    d_tokens_part, grad_gain_attn = attn_norm_back(d_normed)
    grad_tokens = (d_hidden_in + d_tokens_part).astype(jnp.bfloat16)
    grad_qkv, grad_out_proj = (
        lax.psum_scatter(term_qkv, ("seq", "rows"), scatter_dimension=0, tiled=True),
        lax.psum_scatter(term_out, ("seq", "rows"), scatter_dimension=0, tiled=True),
    )
    gain_local = jnp.concatenate([grad_gain_attn, grad_gain_ffn, grad_gain_query, grad_gain_key])
    grads = (grad_qkv, grad_out_proj, grad_gate_up, grad_down)
    updated = optimizer_step(
        grads, gain_local, (qkv_master, out_master, gate_up_master, down_master), gains,
        (qkv_rows, out_rows, gate_up_rows, down_rows), col_moments, gain_moments,
        lambda vector: lax.psum(vector, ("seq", "rows")),
    )
    return (output.astype(jnp.bfloat16), grad_tokens, *grads, *updated)


MESH = pl.DeviceIdType.MESH
PLACES = 32
VMEM_BYTES = 56 * 1024 * 1024
CHUNK = 16


def here():
    seq = lax.axis_index("seq")
    return lax.div(seq, 2), lax.rem(seq, 2), lax.axis_index("rows")


def flips(chip):
    return (chip + 1 - 2 * lax.rem(chip, 2), lax.rem(chip + 2, 4), 3 - chip)


def ahead(z, step):
    return lax.rem(z + step, 4)


def at_place(chip, core, z):
    return (2 * chip + core, z)


def greet(peers):
    barrier = pltpu.get_barrier_semaphore()
    for peer in peers:
        pl.semaphore_signal(barrier, inc=1, device_id=peer, device_id_type=MESH)
    pl.semaphore_wait(barrier, len(peers))


class Mover:
    def __init__(self, send_sem, recv_sem, local_sem):
        self.send_sem, self.recv_sem, self.local_sem = send_sem, recv_sem, local_sem
        self.remote, self.own = [], []

    def send(self, src, dst, peer):
        slot = len(self.remote)
        copy = pltpu.make_async_remote_copy(
            src_ref=src,
            dst_ref=dst,
            send_sem=self.send_sem.at[slot],
            recv_sem=self.recv_sem.at[slot],
            device_id=peer,
            device_id_type=MESH,
        )
        copy.start()
        handle = [copy, False, copy.wait_recv, False]
        self.remote.append(handle)
        return handle

    def send_parts(self, pairs, whole, peer):
        slot = len(self.remote)

        def copy_of(src, dst):
            return pltpu.make_async_remote_copy(
                src_ref=src,
                dst_ref=dst,
                send_sem=self.send_sem.at[slot],
                recv_sem=self.recv_sem.at[slot],
                device_id=peer,
                device_id_type=MESH,
            )

        for src, dst in pairs:
            copy_of(src, dst).start()
        copy = copy_of(whole, whole)
        handle = [copy, False, copy.wait_recv, False]
        self.remote.append(handle)
        return handle

    def keep_parts(self, pairs, whole):
        sem = self.local_sem.at[len(self.own)]
        for src, dst in pairs:
            pltpu.make_async_copy(src, dst, sem).start()
        copy = pltpu.make_async_copy(whole, whole, sem)
        handle = [copy, False, copy.wait]
        self.own.append(handle)
        return handle

    def keep(self, src, dst):
        copy = pltpu.make_async_copy(src, dst, self.local_sem.at[len(self.own)])
        copy.start()
        handle = [copy, False, copy.wait]
        self.own.append(handle)
        return handle

    def arrive(self, *handles):
        for handle in handles:
            if not handle[1]:
                handle[1] = True
                handle[2]()

    def sent(self, *handles):
        for handle in handles:
            if not handle[3]:
                handle[3] = True
                handle[0].wait_send()

    def finish(self):
        self.arrive(*self.own, *self.remote)
        self.sent(*self.remote)


def semaphores(remote, own):
    return [
        pltpu.SemaphoreType.DMA((remote,)),
        pltpu.SemaphoreType.DMA((remote,)),
        pltpu.SemaphoreType.DMA((max(own, 1),)),
    ]


def exchange(kernel, ident, inputs, outputs, scratch, copies, moved, flops=0):
    vmem, anywhere = pl.BlockSpec(memory_space=pltpu.VMEM), pl.BlockSpec(memory_space=pl.ANY)
    return pl.pallas_call(
        kernel,
        out_shape=[jax.ShapeDtypeStruct(shape, kind) for shape, kind, _ in outputs],
        in_specs=[vmem if near else anywhere for _, near in inputs],
        out_specs=[vmem if near else anywhere for _, _, near in outputs],
        scratch_shapes=scratch + semaphores(*copies),
        compiler_params=pltpu.CompilerParams(
            collective_id=ident, has_side_effects=True, vmem_limit_bytes=VMEM_BYTES
        ),
        cost_estimate=pl.CostEstimate(flops=flops, bytes_accessed=moved, transcendentals=0),
    )(*[array for array, _ in inputs])


def chunks(length, body):
    @pl.loop(0, length // CHUNK)
    def _(step):
        body(pl.ds(pl.multiple_of(step * CHUNK, CHUNK), CHUNK))


def segments(core, z):
    for part in range(2):
        for chip in range(4):
            start = part * FF + ((2 * chip + core) * 4 + z) * 256
            yield pl.ds(pl.multiple_of(start, 256), 256), pl.ds(part * 1024 + chip * 256, 256)


def add_blocks(first, second, result):
    for row in range(2):

        def body(part):
            total = first[row, part].astype(jnp.float32) + second[row, part].astype(jnp.float32)
            result[row, part] = total.astype(result.dtype)

        chunks(64, body)


def head_tables(doc_starts, length):
    places = jnp.arange(length, dtype=jnp.int32)
    _, offsets = doc_tables(doc_starts, places)
    cos_table, sin_table = rotary(offsets)
    signs = jnp.where(jnp.arange(HEAD_DIM) < HEAD_DIM // 2, -1.0, 1.0)
    tables = []
    for table in (cos_table, sin_table * signs):
        wide = jnp.concatenate([table, table], axis=-1)
        tables.append(wide.reshape(2, 8, 64, 128).transpose(1, 0, 2, 3))
    return (*tables, (places[None, :] - offsets)[..., None])


def lower_half(shape):
    return lax.broadcasted_iota(jnp.int32, shape, len(shape) - 1) < 64


def swap_halves(entries):
    lane = lax.broadcasted_iota(jnp.int32, entries.shape, 1)
    return jnp.where(lax.rem(lane, 64) < 32, pltpu.roll(entries, 96, 1), pltpu.roll(entries, 32, 1))


def head_means(entries):
    lower = lower_half(entries.shape)
    low = jnp.sum(jnp.where(lower, entries, 0.0), axis=-1, keepdims=True)
    high = jnp.sum(jnp.where(lower, 0.0, entries), axis=-1, keepdims=True)
    return jnp.where(lower, low, high) * (1.0 / HEAD_DIM)


def wide(start, size):
    return pl.ds(pl.multiple_of(start, size), size)


def plain(left, right):
    return jnp.dot(left, right, preferred_element_type=jnp.float32)


def across(left, right):
    return lax.dot_general(
        left, right, (((1,), (1,)), ((), ())), preferred_element_type=jnp.float32
    )


def down(left, right):
    return lax.dot_general(
        left, right, (((0,), (0,)), ((), ())), preferred_element_type=jnp.float32
    )


def attention_probs(queries, keys, first, part):
    scores = across(queries, keys)
    place = lax.broadcasted_iota(jnp.int32, scores.shape, 1)
    query = lax.broadcasted_iota(jnp.int32, scores.shape, 0) + part * 128
    allowed = (place >= first) & (place <= query)
    scores = jnp.where(allowed, scores, MASKED_SCORE)
    best = jnp.max(scores, axis=-1, keepdims=True)
    weights = jnp.where(allowed, jnp.exp(scores - best), 0.0)
    return weights / jnp.sum(weights, axis=-1, keepdims=True)


def forward_kernel(
    tok, gain_attn, gain_ffn, gain_heads, cosines, sines, first, qkv_master, wo, wd_own, wg, grad_out,
    all_branch, d_hidden_in, out_sum, gain_part, down_part, gate_up_in,
    kept_tok, kept_wq, kept_wo, projected, queries, keys_values, attended,
    wq_send, normed, all_tok, all_wq, all_wo, partial, from_partner, came,
    hidden_in, all_norm, all_out, all_wg, wd, hidden, d_gate_up, d_branch, *sems,
):
    half, full = jnp.bfloat16, jnp.float32
    chip, core, z = here()
    others = flips(chip)
    other = 1 - core
    me = 2 * chip + core
    partner = at_place(chip, other, z)
    plane = [at_place(peer_chip, core, z) for peer_chip in others]
    plane_cross = [at_place(peer_chip, other, z) for peer_chip in others]
    steps = (2, 1, 3)
    line = [at_place(chip, core, ahead(z, step)) for step in steps]
    cross = [at_place(chip, other, ahead(z, step)) for step in steps]
    everyone = [partner] + plane + plane_cross
    greet(everyone + line + cross)
    move = Mover(*sems)

    for head in range(8):
        wq_send[head, :, pl.ds(0, 256)] = qkv_master[:, pl.ds(head * 256, 256)].astype(half)
    low = lower_half((64, 128))
    for pair in range(4):
        keys = qkv_master[:, pl.ds(2048 + pair * 128, 128)]
        values = qkv_master[:, pl.ds(2560 + pair * 128, 128)]
        tail = pl.ds(256, 128)
        wq_send[2 * pair, :, tail] = jnp.where(low, keys, pltpu.roll(values, 64, 1)).astype(half)
        wq_send[2 * pair + 1, :, tail] = jnp.where(low, pltpu.roll(keys, 64, 1), values).astype(half)
    heads = [move.keep(wq_send.at[me], all_wq.at[me, z])]
    for peer in everyone:
        heads.append(move.send(wq_send.at[peer[0]], all_wq.at[me, z], peer))

    for row in range(2):

        def body0(part):
            total = tok[row, part].astype(full)
            scale = lax.rsqrt(jnp.mean(total * total, axis=-1, keepdims=True) + EPSILON)
            normed[row, part] = (total * scale * gain_attn[...]).astype(half)

        chunks(64, body0)
    token_copies = [move.send(normed, all_tok.at[me], peer) for peer in plane]
    token_copies.append(move.send(normed, all_tok.at[me], partner))
    tokens_here = move.keep(normed, all_tok.at[me])
    move.arrive(*heads)
    weights = [move.send(all_wq.at[:, z], all_wq.at[:, z], peer) for peer in line]
    weights += [move.send(wo, all_wo.at[z], peer) for peer in line]
    weights.append(move.keep(wo, all_wo.at[z]))

    def turn_block(to_core, to_z):
        whole = all_wg.at[chip, core, z]
        return [(wg.at[:, src], whole.at[:, dst]) for src, dst in segments(to_core, to_z)], whole

    turned = []
    for step, peer, peer_cross in zip(steps, line, cross):
        to = ahead(z, step)
        turned.append(move.send_parts(*turn_block(core, to), peer))
        turned.append(move.send_parts(*turn_block(other, to), peer_cross))
    turned += [move.keep_parts(*turn_block(core, z)), move.send_parts(*turn_block(other, z), partner)]
    grads = [move.send(grad_out, all_out.at[z, core], peer) for peer in line]
    own = [
        move.keep(wd_own, wd.at[chip]),
        move.keep(grad_out, all_out.at[z, core]),
        move.send(grad_out, all_out.at[z, core], partner),
    ]
    own += [move.send(wd_own, wd.at[chip], peer) for peer in plane]
    for peer_chip, handle in zip(others, tuple(token_copies)):
        move.arrive(handle)
        block = all_tok.at[2 * peer_chip + core]
        token_copies.append(move.send(block, block, partner))
    move.arrive(tokens_here, *token_copies, *weights)
    saved = [move.keep(all_tok, kept_tok), move.keep(all_wq, kept_wq), move.keep(all_wo, kept_wo)]

    flat_tok, flat_wq = all_tok.reshape(1024, D), all_wq.reshape(D, 384)
    flat_wo = all_wo.reshape(256, D)

    @pl.loop(0, 4)
    def _(step):
        block = plain(flat_tok[wide(step * 256, 256)], flat_wq[...])
        projected[wide(step * 2, 2)] = block.reshape(2, 2, 64, 384)

    @pl.loop(0, 8)
    def _(block):
        for row in range(2):
            cosine, sine = cosines[block, row], sines[block, row]
            places = wide(block * 64, 64)
            for tile in range(3):
                entries = projected[block, row, :, pl.ds(tile * 128, 128)]
                gain = gain_heads[min(tile, 2) // 2 : min(tile, 2) // 2 + 1]
                scale = lax.rsqrt(head_means(entries * entries) + EPSILON)
                turned_entries = entries * scale * gain
                turned_entries = turned_entries * cosine + swap_halves(turned_entries) * sine
                if tile < 2:
                    queries[row, tile, places] = (turned_entries * HEAD_DIM ** (-0.5)).astype(half)
                else:
                    zero = jnp.zeros_like(entries)
                    rolled = pltpu.roll(turned_entries, 64, 1)
                    values = pltpu.roll(entries, 64, 1)
                    keys_values[row, 0, places] = jnp.where(low, turned_entries, zero).astype(half)
                    keys_values[row, 1, places] = jnp.where(low, zero, rolled).astype(half)
                    keys_values[row, 2, places] = jnp.where(low, values, zero).astype(half)
                    keys_values[row, 3, places] = jnp.where(low, zero, entries).astype(half)

    @pl.loop(0, 2)
    def _(row):
        for tile in range(2):
            for part in range(4):
                own_places, upto = pl.ds(part * 128, 128), pl.ds(0, (part + 1) * 128)
                total = jnp.zeros((128, 128), full)
                for side in range(2):
                    probs = attention_probs(
                        queries[row, tile, own_places], keys_values[row, side, upto],
                        first[row, own_places], part,
                    )
                    total += plain(probs.astype(half), keys_values[row, 2 + side, upto])
                attended[pl.ds(2 * part, 2), row, :, pl.ds(tile * 128, 128)] = total.reshape(2, 64, 128)

    flat_attended = attended.reshape(1024, 256)

    @pl.loop(0, 4)
    def _(step):
        rows = flat_attended[wide(step * 256, 256)].astype(half)

        @pl.loop(0, 4)
        def _(col):
            cols = wide(col * 512, 512)
            block = plain(rows, flat_wo[:, cols])
            partial[wide(step * 2, 2), :, :, cols] = block.reshape(2, 2, 64, 512).astype(half)

    order = tuple(others) + (chip,)
    halves = [move.send(partial.at[2 * to + other], from_partner.at[to], partner) for to in order]
    sums = []
    for to, arrived, peer in zip(others, halves, plane):
        move.arrive(arrived)
        add_blocks(partial.at[2 * to + core], from_partner.at[to], from_partner.at[to])
        sums.append(move.send(from_partner.at[to], came.at[chip], peer))
    move.sent(*token_copies)
    move.arrive(halves[3], *sums)
    for row in range(2):

        def body(part):
            total = tok[row, part].astype(full)
            total += partial[me, row, part].astype(full)
            total += from_partner[chip, row, part].astype(full)
            for peer_chip in others:
                total += came[peer_chip, row, part].astype(full)
            hidden_in[row, part] = total
            scale = lax.rsqrt(jnp.mean(total * total, axis=-1, keepdims=True) + EPSILON)
            normed[row, part] = (total * scale * gain_ffn[...]).astype(half)

        chunks(64, body)
    move.sent(*sums, *halves)
    move.arrive(*saved)
    norms = [move.send(normed, all_norm.at[z, core], peer) for peer in line]
    own.append(move.send(normed, all_norm.at[z, core], partner))
    own.append(move.keep(normed, all_norm.at[z, core]))

    move.arrive(*turned)
    by_x, by_y = plane[0], plane[1]
    front, back = all_wg.at[chip, 0], all_wg.at[chip, 1]
    from_x = move.send(front, front, by_x)
    from_y = move.send(back, back, by_y)
    weights = [from_x, from_y, move.send(back, back, by_x), move.send(front, front, by_y)]

    def share(handles, target):
        shared = []
        for step, handle in zip(steps, handles):
            move.arrive(handle)
            block = target.at[ahead(z, 4 - step), core]
            shared.append(move.send(block, block, partner))
        return shared

    shared = share(grads, all_out)
    move.arrive(from_x, from_y)
    front, back = all_wg.at[others[0], 0], all_wg.at[others[1], 1]
    weights += [move.send(front, front, by_y), move.send(back, back, by_x)]
    shared += share(norms, all_norm)
    move.arrive(*weights, *own, *shared)

    flat_wg, flat_wd = all_wg.reshape(D, 2048), wd.reshape(1024, D)

    def block_of(zb):
        @pl.loop(0, 4)
        def _(step):
            cols, ups = wide(step * 256, 256), wide(1024 + step * 256, 256)
            rows = all_norm[zb].reshape(256, D)
            gate = plain(rows, flat_wg[:, cols])
            up = plain(rows, flat_wg[:, ups])
            d_hidden = across(all_out[zb].reshape(256, D), flat_wd[cols])
            sigmoid = 1.0 / (1.0 + jnp.exp(-gate))
            silu = gate * sigmoid
            hidden[zb, :, cols] = (silu * up).astype(half)
            d_gate = d_hidden * up * (sigmoid * (1.0 + gate * (1.0 - sigmoid)))
            d_gate_up[zb, :, cols] = d_gate.astype(half)
            d_gate_up[zb, :, ups] = (d_hidden * silu).astype(half)

        @pl.loop(0, 8)
        def _(step):
            cols = wide(step * 256, 256)
            block = across(d_gate_up[zb], flat_wg[cols])
            partial[pl.ds(2 * zb, 2), :, :, cols] = block.reshape(2, 2, 64, 256).astype(half)

    def pair_sum(zb, handle, into, base):
        move.arrive(handle)
        add_blocks(partial.at[2 * zb + core], into.at[base + zb], into.at[base + zb])

    to_partner, sums = [], []
    walk = [ahead(z, step) for step in steps] + [z]
    for index, zb in enumerate(walk):
        block_of(zb)
        to_partner.append(move.send(partial.at[2 * zb + other], from_partner.at[zb], partner))
        if index > 0:
            before = walk[index - 1]
            pair_sum(before, to_partner[index - 1], from_partner, 0)
            sums.append(move.send(from_partner.at[before], came.at[z], line[index - 1]))
    pair_sum(z, to_partner[3], from_partner, 0)

    flat_norm, flat_grads = all_norm.reshape(1024, D), all_out.reshape(1024, D)
    flat_hidden, flat_d = hidden.reshape(1024, 1024), d_gate_up.reshape(1024, 2048)
    move.sent(*weights)
    for to, peer in zip((others[2], others[0], others[1], chip), (plane[2], plane[0], plane[1], None)):
        rows = wide(to * 512, 512)

        @pl.loop(0, 4)
        def _(step, rows=rows):
            cols = wide(step * 512, 512)
            flat_wg[rows, cols] = down(flat_norm[:, rows], flat_d[:, cols]).astype(half)

        if peer is None:
            move.keep(all_wg.at[to], gate_up_in.at[chip])
        else:
            move.send(all_wg.at[to], gate_up_in.at[chip], peer)

    move.arrive(*sums)
    gain_part[...] = jnp.zeros_like(gain_part)
    for row in range(2):

        def body2(part):
            total = from_partner[z, row, part].astype(full)
            for step in steps:
                total += came[ahead(z, step), row, part].astype(full)
            entries = hidden_in[row, part]
            scale = lax.rsqrt(jnp.mean(entries * entries, axis=-1, keepdims=True) + EPSILON)
            gain_part[...] += jnp.sum(total * entries * scale, axis=0, keepdims=True)
            total = total * gain_ffn[...]
            inner = jnp.mean(total * entries, axis=-1, keepdims=True) * (scale * scale * scale)
            grad = grad_out[row, part].astype(full) + total * scale - entries * inner
            d_hidden_in[row, part] = grad
            d_branch[row, part] = grad.astype(half)

        chunks(64, body2)
    branches = [move.send(d_branch, all_branch.at[me], peer) for peer in plane]
    move.send(d_branch, all_branch.at[me], partner)
    move.keep(d_branch, all_branch.at[me])

    move.sent(*to_partner)
    to_partner, sums = [], []
    for index, zb in enumerate(walk):

        @pl.loop(0, 4)
        def _(step, zb=zb):
            cols = wide(step * 512, 512)
            block = plain(hidden[zb], flat_wd[:, cols])
            partial[pl.ds(2 * zb, 2), :, :, cols] = block.reshape(2, 2, 64, 512).astype(half)

        to_partner.append(move.send(partial.at[2 * zb + other], all_tok.at[zb], partner))
        if index > 0:
            before = walk[index - 1]
            pair_sum(before, to_partner[index - 1], all_tok, 0)
            sums.append(move.send(all_tok.at[before], all_tok.at[4 + z], line[index - 1]))
    pair_sum(z, to_partner[3], all_tok, 0)

    @pl.loop(0, 4)
    def _(to):
        rows = wide(to * 256, 256)

        @pl.loop(0, 4)
        def _(step):
            cols = wide(step * 512, 512)
            flat_wd[rows, cols] = down(flat_hidden[:, rows], flat_grads[:, cols]).astype(half)

    move.keep(wd, down_part)
    for peer_chip, handle in zip(others, branches):
        move.arrive(handle)
        block = all_branch.at[2 * peer_chip + core]
        move.send(block, block, partner)
    move.arrive(*sums)
    for row in range(2):

        def body3(part):
            total = hidden_in[row, part] + all_tok[z, row, part].astype(full)
            for step in steps:
                total += all_tok[4 + ahead(z, step), row, part].astype(full)
            out_sum[row, part] = total.astype(half)

        chunks(64, body3)
    move.finish()


def backward_kernel(
    branch_in, wq_in, wo_in, tok_in, gate_up_in, down_part, projected, queries, keys_values, attended,
    cosines, sines, first, gain_heads,
    d_norm_came, gate_up_came, qkv_came, out_came, down_came, gain_qk,
    d_branch, wq, wo, all_tok, gate_up, d_attended, d_queries, d_keys_values, d_projected,
    qkv_part, out_part, partial, from_partner, gate_up_sum, qkv_in, qkv_sum, *sems,
):
    half, full = jnp.bfloat16, jnp.float32
    chip, core, z = here()
    others = flips(chip)
    other = 1 - core
    me = 2 * chip + core
    partner = at_place(chip, other, z)
    plane = [at_place(peer_chip, core, z) for peer_chip in others]
    plane_cross = [at_place(peer_chip, other, z) for peer_chip in others]
    everyone = [partner] + plane + plane_cross
    steps = (2, 1, 3)
    line = [at_place(chip, core, ahead(z, step)) for step in steps]
    cross = [at_place(chip, other, ahead(z, step)) for step in steps]
    move = Mover(*sems)
    load_gate_up = move.keep(gate_up_in, gate_up)
    loads = [move.keep(branch_in, d_branch), move.keep(wo_in, wo), move.keep(wq_in, wq)]
    load_tok = move.keep(tok_in, all_tok)
    greet(everyone + line + cross)
    for to, peer in zip(others, plane):
        move.send(down_part.at[to], down_came.at[chip], peer)
    move.keep(down_part.at[chip], down_came.at[chip])
    move.arrive(load_gate_up)

    @pl.loop(0, 8)
    def _(block):
        to_core, to_z = lax.div(block, 4), lax.rem(block, 4)

        def body(part):
            total = gate_up[0, to_core, to_z, part].astype(full)
            for slot in range(1, 4):
                total += gate_up[slot, to_core, to_z, part].astype(full)
            gate_up_sum[to_core, to_z, part] = total.astype(half)

        chunks(64, body)

    def turn_block(to_core, to_z):
        whole = gate_up_sum.at[to_core, to_z]
        return [
            (whole.at[:, src], gate_up_came.at[:, dst]) for dst, src in segments(core, z)
        ], whole

    for step, peer, peer_cross in zip(steps, line, cross):
        to = ahead(z, step)
        move.send_parts(*turn_block(core, to), peer)
        move.send_parts(*turn_block(other, to), peer_cross)
    move.send_parts(*turn_block(other, z), partner)
    move.keep_parts(*turn_block(core, z))

    move.arrive(*loads)
    flat_branch, flat_wo = d_branch.reshape(1024, D), wo.reshape(256, D)
    flat_d = d_attended.reshape(1024, 256)

    @pl.loop(0, 4)
    def _(step):
        rows = wide(step * 256, 256)
        flat_d[rows] = across(flat_branch[rows], flat_wo[...]).astype(half)

    d_keys_values[...] = jnp.zeros_like(d_keys_values)
    lower = lower_half((128, 128))

    @pl.loop(0, 2)
    def _(row):
        for tile in range(2):
            for part in range(4):
                own_places, upto = pl.ds(part * 128, 128), pl.ds(0, (part + 1) * 128)
                at = (pl.ds(2 * part, 2), row, slice(None), pl.ds(tile * 128, 128))
                d_heads = d_attended[at].reshape(128, 128)
                products = d_heads.astype(full) * attended[at].reshape(128, 128)
                query = queries[row, tile, own_places]
                total = jnp.zeros((128, 128), full)
                for side in range(2):
                    mask = lower if side == 0 else jnp.logical_not(lower)
                    delta = jnp.sum(jnp.where(mask, products, 0.0), axis=-1, keepdims=True)
                    keys = keys_values[row, side, upto]
                    probs = attention_probs(query, keys, first[row, own_places], part)
                    d_probs = across(d_heads, keys_values[row, 2 + side, upto])
                    d_scores = (probs * (d_probs - delta)).astype(half)
                    total += plain(d_scores, keys)
                    d_keys_values[row, side, upto] += down(d_scores, query)
                    d_keys_values[row, 2 + side, upto] += down(probs.astype(half), d_heads)
                d_queries[row, tile, own_places] = total

    low = lower_half((64, 128))
    gain_qk[...] = jnp.zeros_like(gain_qk)

    @pl.loop(0, 8)
    def _(block):
        for row in range(2):
            cosine, sine = cosines[block, row], sines[block, row]
            places = wide(block * 64, 64)
            for tile in range(3):
                lanes = pl.ds(tile * 128, 128)
                entries = projected[block, row, :, lanes]
                gain = gain_heads[min(tile, 2) // 2 : min(tile, 2) // 2 + 1]
                scale = lax.rsqrt(head_means(entries * entries) + EPSILON)
                if tile < 2:
                    grad = d_queries[row, tile, places] * HEAD_DIM ** (-0.5)
                else:
                    from_low, from_high = d_keys_values[row, 0, places], d_keys_values[row, 1, places]
                    grad = jnp.where(low, from_low + pltpu.roll(from_high, 64, 1), 0.0)
                grad = grad * cosine + swap_halves(grad * sine)
                for_gain = jnp.sum(grad * entries * scale, axis=0, keepdims=True)
                line_low = lower_half((1, 128))
                if tile < 2:
                    for_gain = jnp.where(line_low, for_gain + pltpu.roll(for_gain, 64, 1), 0.0)
                else:
                    for_gain = jnp.where(line_low, 0.0, pltpu.roll(for_gain, 64, 1))
                gain_qk[...] += for_gain
                grad = grad * gain
                inner = head_means(grad * entries) * (scale * scale * scale)
                grad = grad * scale - entries * inner
                if tile == 2:
                    values = pltpu.roll(d_keys_values[row, 2, places], 64, 1)
                    grad = jnp.where(low, grad, values + d_keys_values[row, 3, places])
                d_projected[block, row, :, lanes] = grad.astype(half)

    flat_p, flat_wq = d_projected.reshape(1024, 384), wq.reshape(D, 384)

    @pl.loop(0, 4)
    def _(step):
        rows = flat_p[wide(step * 256, 256)]

        @pl.loop(0, 4)
        def _(col):
            cols = wide(col * 512, 512)
            block = across(rows, flat_wq[cols])
            partial[wide(step * 2, 2), :, :, cols] = block.reshape(2, 2, 64, 512).astype(half)

    order = tuple(others) + (chip,)
    halves = [move.send(partial.at[2 * to + other], from_partner.at[to], partner) for to in order]
    move.arrive(load_tok)
    flat_tok = all_tok.reshape(1024, D)

    @pl.loop(0, 4)
    def _(step):
        block = down(flat_tok[:, wide(step * 512, 512)], flat_p[...])
        qkv_part[wide(step * 2, 2)] = block.reshape(2, 4, 64, 384).astype(half)

    qkv_pieces = [
        move.send(qkv_part.at[:, ahead(z, step)], qkv_in.at[z], peer)
        for step, peer in zip(steps, line)
    ]
    for to, arrived, peer in zip(others, halves, plane):
        move.arrive(arrived)
        add_blocks(partial.at[2 * to + core], from_partner.at[to], from_partner.at[to])
        move.send(from_partner.at[to], d_norm_came.at[chip], peer)
    move.arrive(halves[3])
    add_blocks(partial.at[me], from_partner.at[chip], from_partner.at[chip])
    move.keep(from_partner.at[chip], d_norm_came.at[chip])
    flat_attended = attended.reshape(1024, 256)

    @pl.loop(0, 4)
    def _(step):
        cols = wide(step * 512, 512)
        block = down(flat_attended[...].astype(half), flat_branch[:, cols])
        out_part[:, :, cols] = block.reshape(4, 64, 512).astype(half)

    for step, peer in zip(steps, line):
        move.send(out_part.at[ahead(z, step)], out_came.at[z], peer)
    move.keep(out_part.at[z], out_came.at[z])
    move.arrive(*qkv_pieces)

    @pl.loop(0, 8)
    def _(block):
        def body(part):
            total = qkv_part[block, z, part].astype(full)
            for step in steps:
                total += qkv_in[ahead(z, step), block, part].astype(full)
            qkv_sum[block, part] = total.astype(half)

        chunks(64, body)

    for peer in everyone:
        move.send(qkv_sum.at[peer[0]], qkv_came.at[me], peer)
    move.keep(qkv_sum.at[me], qkv_came.at[me])
    move.finish()


COL_ROWS, GAIN_ROWS = 184, 33
MATRICES = ((64, QKV, 0, 0), (64, D, 64, 24), (64, 2 * FF, 128, 40), (256, D, 192, 168))
ROW_TOTALS = (D, HEADS * HEAD_DIM, D, FF)
BETA = 1.0 - STEP ** (-0.8)


def lane_value(vector, lane):
    lanes = lax.broadcasted_iota(jnp.int32, (1, 128), 1)
    return jnp.sum(jnp.where(lanes == lane, vector, 0.0), axis=-1, keepdims=True)


def statistics_kernel(
    d_norm, tok, d_hidden_in, gain, gain_ffn, gain_qk, qkv, out, gate_up, down, rows,
    m_qkv, m_out, m_gate_up, m_down,
    grad_tok, g_qkv, g_out, g_gate_up, g_down, rows_new, packed,
    gain_part, sums, inverse,
):
    gain_part[...] = jnp.zeros_like(gain_part)

    @pl.loop(0, 128 // CHUNK)
    def _(step):
        part = pl.ds(pl.multiple_of(step * CHUNK, CHUNK), CHUNK)
        total = d_norm[0, part].astype(jnp.float32)
        for slot in range(1, 4):
            total += d_norm[slot, part].astype(jnp.float32)
        entries = tok[part].astype(jnp.float32)
        scale = lax.rsqrt(jnp.mean(entries * entries, axis=-1, keepdims=True) + EPSILON)
        gain_part[...] += jnp.sum(total * entries * scale, axis=0, keepdims=True)
        total = total * gain[...]
        inner = jnp.mean(total * entries, axis=-1, keepdims=True) * (scale * scale * scale)
        grad_tok[part] = (d_hidden_in[part] + total * scale - entries * inner).astype(jnp.bfloat16)

    first = 2 * COL_ROWS
    for slot in range(16):
        lanes = pl.ds(slot * 128, 128)
        packed[first + slot : first + slot + 1] = gain_part[:, lanes]
        packed[first + 16 + slot : first + 17 + slot] = gain_ffn[:, lanes]
    packed[first + 32 : first + 33] = gain_qk[...]
    lane = lax.broadcasted_iota(jnp.int32, (64, 128), 1)

    def wide(step):
        return pl.ds(pl.multiple_of(step * 128, 128), 128)

    def read_qkv(step):
        return g_qkv[:, wide(step)]

    for head in range(8):
        for half in range(2):
            g_qkv[:, pl.ds(head * 256 + half * 128, 128)] = qkv[
                head, :, pl.ds(half * 128, 128)
            ].astype(jnp.float32)
    for pair in range(4):
        low = qkv[2 * pair, :, pl.ds(256, 128)].astype(jnp.float32)
        high = qkv[2 * pair + 1, :, pl.ds(256, 128)].astype(jnp.float32)
        g_qkv[:, pl.ds(2048 + pair * 128, 128)] = jnp.where(lane < 64, low, pltpu.roll(high, 64, 1))
        g_qkv[:, pl.ds(2560 + pair * 128, 128)] = jnp.where(lane < 64, pltpu.roll(low, 64, 1), high)

    def read_out(step):
        total = out[0, :, wide(step)].astype(jnp.float32)
        for slot in range(1, 4):
            total += out[slot, :, wide(step)].astype(jnp.float32)
        return total

    def read_gate_up(step):
        return gate_up[:, wide(step)].astype(jnp.float32)

    def read_down(step):
        total = down[0, :, wide(step)].astype(jnp.float32)
        for slot in range(1, 4):
            total += down[slot, :, wide(step)].astype(jnp.float32)
        return total

    readers = (read_qkv, read_out, read_gate_up, read_down)
    grads = (g_qkv, g_out, g_gate_up, g_down)
    masters = (m_qkv, m_out, m_gate_up, m_down)
    stats = jnp.zeros((1, 128), jnp.float32)
    lanes = lax.broadcasted_iota(jnp.int32, (1, 128), 1)
    for slot, (count, width, row_at, col_at) in enumerate(MATRICES):
        own = pl.ds(0, count)
        sums[0, own] = jnp.zeros((count, 128), jnp.float32)
        sums[1, own] = jnp.zeros((count, 128), jnp.float32)

        @pl.loop(0, width // 128)
        def _(step, slot=slot, own=own):
            entries = readers[slot](step)
            if slot > 0:
                grads[slot][:, wide(step)] = entries
            sums[0, own] += entries * entries
            weight = masters[slot][:, wide(step)]
            sums[1, own] += weight * weight

        mean = jnp.sum(sums[0, own], axis=-1, keepdims=True) / width + SQUARE_EPSILON
        here_rows = pl.ds(row_at, count)
        new = BETA * rows[here_rows] + (1.0 - BETA) * mean
        rows_new[here_rows] = new
        inverse[own] = jnp.broadcast_to(1.0 / new, (count, 128))
        weight_sum = jnp.sum(jnp.sum(sums[1, own], axis=-1, keepdims=True), axis=0, keepdims=True)
        stats = jnp.where(lanes == slot, jnp.sum(new, axis=0, keepdims=True), stats)
        stats = jnp.where(lanes == 4 + slot, weight_sum, stats)

        @pl.loop(0, width // 128)
        def _(step, slot=slot, own=own, count=count, col_at=col_at):
            entries = grads[slot][:, wide(step)]
            square = entries * entries
            packed[pl.ds(col_at + step, 1)] = (
                jnp.sum(square, axis=0, keepdims=True) + count * SQUARE_EPSILON
            )
            packed[pl.ds(COL_ROWS + col_at + step, 1)] = jnp.sum(
                square * inverse[own], axis=0, keepdims=True
            )

    packed[first + 33 : first + 34] = stats
    packed[first + 34 : 512] = jnp.zeros((512 - first - 34, 128), jnp.float32)


def total_kernel(
    parts, col_moments, gain_moments, gains,
    cols_new, col_factors, moments_new, gains_new, grad_gains, spreads,
    totals, plane_came, line_came, plane_sum, line_sum, line_all, *sems,
):
    chip, core, z = here()
    me = 2 * chip + core
    other = 1 - core
    plane = [at_place(chip, other, z)]
    for peer_chip in flips(chip):
        plane += [at_place(peer_chip, core, z), at_place(peer_chip, other, z)]
    line = [at_place(chip, core, ahead(z, step)) for step in (2, 1, 3)]
    greet(plane + line)
    move = Mover(*sems)
    pieces = [move.send(parts.at[peer[0]], plane_came.at[me], peer) for peer in plane]
    plane_came[me] = parts[me]
    move.arrive(*pieces)
    total = plane_came[0]
    for slot in range(1, 8):
        total = total + plane_came[slot]
    plane_sum[...] = total
    pieces = [move.send(plane_sum.at[peer[1]], line_came.at[z], peer) for peer in line]
    line_came[z] = plane_sum[z]
    move.arrive(*pieces)
    line_sum[...] = line_came[0] + line_came[1] + line_came[2] + line_came[3]
    pieces = [move.send(line_sum, line_all.at[z], peer) for peer in line]
    line_all[z] = line_sum[...]
    move.arrive(*pieces)
    for peer in plane:
        move.send(line_all, totals.at[me], peer)
    totals[me] = line_all[...]
    move.finish()
    flat = totals.reshape(512, 128)
    first = 2 * COL_ROWS
    stats = flat[first + 33 : first + 34]
    lanes = lax.broadcasted_iota(jnp.int32, (1, 128), 1)
    out = jnp.zeros((1, 128), jnp.float32)
    for slot, (_, width, _, col_at) in enumerate(MATRICES):
        own = pl.ds(col_at, width // 128)
        entries_all = float(ROW_TOTALS[slot] * width)
        new = BETA * col_moments[own] + (1.0 - BETA) * (flat[own] / ROW_TOTALS[slot])
        cols_new[own] = new
        mean_rows = lane_value(stats, slot) / ROW_TOTALS[slot]
        ratio = flat[pl.ds(COL_ROWS + col_at, width // 128)] / new
        ratio = jnp.sum(jnp.sum(ratio, axis=-1, keepdims=True), axis=0, keepdims=True)
        spread = jnp.sqrt(mean_rows * ratio / entries_all)
        scale = STEP_RATE * jnp.maximum(
            SCALE_EPSILON, jnp.sqrt(lane_value(stats, 4 + slot) / entries_all)
        )
        factor = scale * jnp.sqrt(mean_rows) / jnp.maximum(1.0, spread / CLIP_LEVEL)
        col_factors[own] = lax.rsqrt(new) * factor
        out = jnp.where(lanes == slot, spread, out)
    gradient = flat[first : first + GAIN_ROWS]
    grad_gains[...] = gradient
    old = gains[...]
    new = BETA * gain_moments[...] + (1.0 - BETA) * (gradient * gradient + SQUARE_EPSILON)
    moments_new[...] = new
    unit = gradient * lax.rsqrt(new)
    row = lax.broadcasted_iota(jnp.int32, (GAIN_ROWS, 128), 0)
    lane = lax.broadcasted_iota(jnp.int32, (GAIN_ROWS, 128), 1)
    segment = jnp.where(row < 16, 0, jnp.where(row < 32, 1, jnp.where(lane < 64, 2, 3)))
    factors = jnp.zeros((GAIN_ROWS, 128), jnp.float32)

    def mean_of(square, mask, count):
        picked = jnp.where(mask, square, 0.0)
        return jnp.sum(jnp.sum(picked, axis=-1, keepdims=True), axis=0, keepdims=True) / count

    for slot, count in enumerate((D, D, HEAD_DIM, HEAD_DIM)):
        mask = segment == slot
        spread = jnp.sqrt(mean_of(unit * unit, mask, count))
        scale = STEP_RATE * jnp.maximum(SCALE_EPSILON, jnp.sqrt(mean_of(old * old, mask, count)))
        factors = jnp.where(mask, scale / jnp.maximum(1.0, spread / CLIP_LEVEL), factors)
        out = jnp.where(lanes == 4 + slot, spread, out)
    gains_new[...] = old - factors * unit
    spreads[...] = out


def split_local(
    tokens, doc_starts, grad_out, qkv_master, out_master, gate_up_master, down_master, gains,
    qkv_rows, out_rows, gate_up_rows, down_rows, col_moments, gain_moments,
):
    half, full = jnp.bfloat16, jnp.float32
    gain_attn, gain_ffn = gains[None, :D], gains[None, D : 2 * D]
    gain_query = gains[2 * D : 2 * D + HEAD_DIM]
    gain_key = gains[2 * D + HEAD_DIM :]
    gain_heads = jnp.stack(
        [jnp.concatenate([gain_query, gain_query]), jnp.concatenate([gain_key, gain_key])]
    )
    cosines, sines, first = head_tables(doc_starts, 512)

    def near(*shape, kind=half):
        return pltpu.VMEM(shape, kind)

    (
        all_branch, d_hidden_in, output, grad_gain_ffn, down_part, gate_up_in,
        all_tok, all_wq, all_wo, projected, queries, keys_values, attended,
    ) = exchange(
        forward_kernel, 0,
        [
            (tokens, True), (gain_attn, True), (gain_ffn, True), (gain_heads, True),
            (cosines, True), (sines, True), (first, True), (qkv_master, True),
            (out_master.astype(half), False), (down_master.astype(half), False),
            (gate_up_master.astype(half), False), (grad_out, True),
        ],
        [
            ((8, 2, 64, D), half, False), ((2, 64, D), full, True), ((2, 64, D), half, True),
            ((1, D), full, True), ((4, 256, D), half, False), ((4, 2, 4, 64, 2048), half, False),
            ((8, 2, 64, D), half, False), ((8, 4, 64, 384), half, False), ((4, 64, D), half, False),
            ((8, 2, 64, 384), full, True), ((2, 2, 512, 128), half, True),
            ((2, 4, 512, 128), half, True), ((8, 2, 64, 256), full, True),
        ],
        [
            near(8, 64, 384), near(2, 64, D), near(8, 2, 64, D), near(8, 4, 64, 384), near(4, 64, D),
            near(8, 2, 64, D), near(4, 2, 64, D), near(4, 2, 64, D), near(2, 64, D, kind=full),
            near(4, 2, 2, 64, D), near(4, 2, 2, 64, D), near(4, 2, 4, 64, 2048), near(4, 256, D),
            near(4, 256, 1024), near(4, 256, 2048), near(2, 64, D),
        ],
        (84, 14), 96 << 20, 42 << 30,
    )
    d_norm_came, gate_up_came, qkv_came, out_came, down_came, gain_qk = exchange(
        backward_kernel, 1,
        [
            (all_branch, False), (all_wq, False), (all_wo, False), (all_tok, False),
            (gate_up_in, False), (down_part, False), (projected, True), (queries, True),
            (keys_values, True), (attended, True), (cosines, True), (sines, True), (first, True),
            (gain_heads, True),
        ],
        [
            ((4, 2, 64, D), half, False), ((64, 2 * FF), half, False), ((8, 64, 384), half, False),
            ((4, 64, D), half, False), ((4, 256, D), half, False), ((1, 128), full, True),
        ],
        [
            near(8, 2, 64, D), near(8, 4, 64, 384), near(4, 64, D), near(8, 2, 64, D),
            near(4, 2, 4, 64, 2048), near(8, 2, 64, 256), near(2, 2, 512, 128, kind=full),
            near(2, 4, 512, 128, kind=full), near(8, 2, 64, 384), near(8, 4, 64, 384),
            near(4, 64, D), near(8, 2, 64, D), near(4, 2, 64, D), near(2, 4, 64, 2048),
            near(4, 8, 64, 384), near(8, 64, 384),
        ],
        (34, 12), 64 << 20, 6 << 30,
    )
    row_states = jnp.concatenate([qkv_rows, out_rows, gate_up_rows, down_rows])[:, None]
    masters = (qkv_master, out_master, gate_up_master, down_master)
    grad_tokens, *grads, rows_new, packed = pl.pallas_call(
        statistics_kernel,
        out_shape=[
            jax.ShapeDtypeStruct((128, D), half),
            *[jax.ShapeDtypeStruct((count, width), full) for count, width, _, _ in MATRICES],
            jax.ShapeDtypeStruct((448, 1), full),
            jax.ShapeDtypeStruct((512, 128), full),
        ],
        scratch_shapes=[
            pltpu.VMEM((1, D), full), pltpu.VMEM((2, 256, 128), full), pltpu.VMEM((256, 128), full),
        ],
        compiler_params=pltpu.CompilerParams(vmem_limit_bytes=VMEM_BYTES),
    )(
        d_norm_came.reshape(4, 128, D), tokens.reshape(128, D), d_hidden_in.reshape(128, D), gain_attn,
        grad_gain_ffn, gain_qk,
        qkv_came, out_came, gate_up_came, down_came, row_states, *masters,
    )
    shape = (8, 4, 16, 128)
    cols_new, col_factors, moments_new, gains_new, grad_gains, spreads = exchange(
        total_kernel, 2,
        [
            (packed.reshape(shape), True), (col_moments.reshape(-1, 128), True),
            (gain_moments.reshape(-1, 128), True), (gains.reshape(-1, 128), True),
        ],
        [
            ((COL_ROWS, 128), full, True), ((COL_ROWS, 128), full, True),
            ((GAIN_ROWS, 128), full, True), ((GAIN_ROWS, 128), full, True),
            ((GAIN_ROWS, 128), full, True), ((1, 128), full, True),
        ],
        [
            pltpu.VMEM(shape, full), pltpu.VMEM(shape, full), pltpu.VMEM(shape[1:], full),
            pltpu.VMEM(shape[1:], full), pltpu.VMEM(shape[2:], full), pltpu.VMEM(shape[1:], full),
        ],
        (20, 0), 1 << 20,
    )
    col_factors = col_factors.reshape(-1)
    row_factors = lax.rsqrt(rows_new[:, 0])
    new_masters = []
    for slot, (count, width, row_at, col_at) in enumerate(MATRICES):
        row_factor = row_factors[row_at : row_at + count]
        col_factor = col_factors[col_at * 128 : col_at * 128 + width]
        new_masters.append(
            masters[slot] - grads[slot] * row_factor[:, None] * col_factor[None, :]
        )
    return (
        output,
        grad_tokens.reshape(2, 64, D),
        *grads,
        grad_gains.reshape(-1),
        *[rows_new[row_at : row_at + count, 0] for count, _, row_at, _ in MATRICES],
        cols_new.reshape(-1),
        moments_new.reshape(-1),
        *new_masters,
        *[master.astype(half) for master in new_masters],
        gains_new.reshape(-1),
        spreads[0, :8],
    )


def optimizer_step(
    grads, gain_local, masters, gains, row_states, col_moments, gain_moments, total_fn
):
    beta = 1.0 - STEP ** (-0.8)
    col_widths = (QKV, D, 2 * FF, D)
    row_totals = (D, HEADS * HEAD_DIM, D, FF)
    squares = [gradient * gradient + SQUARE_EPSILON for gradient in grads]
    rows_new = [
        beta * row_state + (1.0 - beta) * jnp.mean(square, axis=1)
        for row_state, square in zip(row_states, squares)
    ]
    col_local = [jnp.sum(square, axis=0) for square in squares]
    weighted_local = [
        jnp.sum(gradient * gradient / row_new[:, None], axis=0)
        for gradient, row_new in zip(grads, rows_new)
    ]
    stats_local = jnp.stack(
        [jnp.sum(row_new) for row_new in rows_new]
        + [jnp.sum(master * master) for master in masters]
    )
    totals = total_fn(jnp.concatenate(col_local + weighted_local + [stats_local, gain_local]))
    cols = sum(col_widths)
    col_sums, weighted = totals[:cols], totals[cols : 2 * cols]
    stats, grad_gains = totals[2 * cols : 2 * cols + 8], totals[2 * cols + 8 :]
    col_divisor = jnp.concatenate(
        [
            jnp.full((col_width,), float(row_total), jnp.float32)
            for col_width, row_total in zip(col_widths, row_totals)
        ]
    )
    cols_new = beta * col_moments + (1.0 - beta) * col_sums / col_divisor
    new_masters = []
    spreads = []
    begin_at = 0
    for slot in range(4):
        col_part = cols_new[begin_at : begin_at + col_widths[slot]]
        weighted_part = weighted[begin_at : begin_at + col_widths[slot]]
        begin_at = begin_at + col_widths[slot]
        mean_rows = stats[slot] / row_totals[slot]
        unit = (
            grads[slot]
            * lax.rsqrt(rows_new[slot] / mean_rows)[:, None]
            * lax.rsqrt(col_part)[None, :]
        )
        entries_all = float(row_totals[slot] * col_widths[slot])
        spread = jnp.sqrt(mean_rows * jnp.sum(weighted_part / col_part) / entries_all)
        scale = STEP_RATE * jnp.maximum(SCALE_EPSILON, jnp.sqrt(stats[4 + slot] / entries_all))
        new_masters.append(masters[slot] - scale * unit / jnp.maximum(1.0, spread / CLIP_LEVEL))
        spreads.append(spread)
    bounds = (0, D, 2 * D, 2 * D + HEAD_DIM, 2 * D + 2 * HEAD_DIM)
    moment_parts, gain_parts = ([], [])
    for segment in range(4):
        gradient = grad_gains[bounds[segment] : bounds[segment + 1]]
        gain_old = gains[bounds[segment] : bounds[segment + 1]]
        moment_new = beta * gain_moments[bounds[segment] : bounds[segment + 1]] + (1.0 - beta) * (
            gradient * gradient + SQUARE_EPSILON
        )
        unit = gradient * lax.rsqrt(moment_new)
        spread = jnp.sqrt(jnp.mean(unit * unit))
        scale = STEP_RATE * jnp.maximum(SCALE_EPSILON, jnp.sqrt(jnp.mean(gain_old * gain_old)))
        moment_parts.append(moment_new)
        gain_parts.append(gain_old - scale * unit / jnp.maximum(1.0, spread / CLIP_LEVEL))
        spreads.append(spread)
    return (
        grad_gains,
        *rows_new,
        cols_new,
        jnp.concatenate(moment_parts),
        *new_masters,
        *[master.astype(jnp.bfloat16) for master in new_masters],
        jnp.concatenate(gain_parts),
        jnp.stack(spreads),
    )


def solution(mesh):
    split = mesh.shape["seq"] == 8 and mesh.shape["rows"] == 4
    return jax.shard_map(
        split_local if split else gathered_local,
        mesh=mesh,
        in_specs=(
            P("rows", "seq", None),
            P("rows", None),
            P("rows", "seq", None),
            P(("seq", "rows"), None),
            P(("seq", "rows"), None),
            P(("seq", "rows"), None),
            P(("seq", "rows"), None),
            P(),
            P(("seq", "rows")),
            P(("seq", "rows")),
            P(("seq", "rows")),
            P(("seq", "rows")),
            P(),
            P(),
        ),
        out_specs=(
            P("rows", "seq", None),
            P("rows", "seq", None),
            P(("seq", "rows"), None),
            P(("seq", "rows"), None),
            P(("seq", "rows"), None),
            P(("seq", "rows"), None),
            P(),
            P(("seq", "rows")),
            P(("seq", "rows")),
            P(("seq", "rows")),
            P(("seq", "rows")),
            P(),
            P(),
            P(("seq", "rows"), None),
            P(("seq", "rows"), None),
            P(("seq", "rows"), None),
            P(("seq", "rows"), None),
            P(("seq", "rows"), None),
            P(("seq", "rows"), None),
            P(("seq", "rows"), None),
            P(("seq", "rows"), None),
            P(),
            P(),
        ),
        check_vma=False,
    )
```

```python
from functools import partial

import jax
import jax.numpy as jnp
from jax import lax
from jax.experimental import pallas as pl
from jax.experimental.pallas import tpu as pltpu
from jax.sharding import PartitionSpec as P

D = 2048
HEADS = 32
KV_HEADS = 8
HEAD_DIM = 64
FF = 8192
STEP = 10
QKV = 3072


EPSILON = 1e-06
ROPE_BASE = 10000.0
MASKED_SCORE = -1e30
STEP_RATE = 0.3
CLIP_LEVEL = 1.0
SQUARE_EPSILON = 1e-30
SCALE_EPSILON = 0.001


def from_behind(value, axis, steps):
    count = lax.axis_size(axis)
    pairs = [(source, (source + steps) % count) for source in range(count)]
    return lax.ppermute(value, axis, pairs)


def norm_rows(entries, gain):
    return entries * lax.rsqrt(jnp.mean(entries * entries, axis=-1, keepdims=True) + EPSILON) * gain


def turn(entries, cos_wide, sin_wide):
    half_width = entries.shape[-1] // 2
    turned = jnp.concatenate([-entries[..., half_width:], entries[..., :half_width]], axis=-1)
    return entries * cos_wide + turned * sin_wide


def doc_tables(doc_starts, places):
    before = doc_starts[:, None, :] <= places[None, :, None]
    doc_ids = jnp.sum(before.astype(jnp.int32), axis=-1)
    doc_first = jnp.max(jnp.where(before, doc_starts[:, None, :], 0), axis=-1)
    return (doc_ids, places[None, :] - doc_first)


def rotary(offsets):
    frequency = ROPE_BASE ** (-(jnp.arange(HEAD_DIM // 2, dtype=jnp.float32) * 2.0 / HEAD_DIM))
    angles = offsets.astype(jnp.float32)[..., None] * frequency
    cos_table = jnp.concatenate([jnp.cos(angles), jnp.cos(angles)], axis=-1)
    sin_table = jnp.concatenate([jnp.sin(angles), jnp.sin(angles)], axis=-1)
    return (cos_table, sin_table)


def queries_keys(
    cos_table, sin_table, projected, gain_query, gain_key, heads=HEADS, kv_heads=KV_HEADS
):
    rows_here, seq_here = (projected.shape[0], projected.shape[1])
    att_width = heads * HEAD_DIM
    queries = projected[..., :att_width].reshape(rows_here, seq_here, heads, HEAD_DIM)
    keys_rot = projected[..., att_width : att_width + kv_heads * HEAD_DIM].reshape(
        rows_here, seq_here, kv_heads, HEAD_DIM
    )
    cos_wide = cos_table[:, :, None, :]
    sin_wide = sin_table[:, :, None, :]
    queries = turn(norm_rows(queries, gain_query), cos_wide, sin_wide) * HEAD_DIM ** (-0.5)
    keys_rot = turn(norm_rows(keys_rot, gain_key), cos_wide, sin_wide)
    return (queries, keys_rot)


def mask_of(query_docs, query_places, key_docs, key_places):
    same_doc = query_docs[:, :, None] == key_docs[:, None, :]
    causal = query_places[None, :, None] >= key_places[None, None, :]
    return (same_doc & causal)[:, None, None, :, :]


def gathered_local(
    tokens,
    doc_starts,
    grad_out,
    qkv_master,
    out_master,
    gate_up_master,
    down_master,
    gains,
    qkv_rows,
    out_rows,
    gate_up_rows,
    down_rows,
    col_moments,
    gain_moments,
):
    cycle_size = lax.axis_size("seq")
    seq_index = lax.axis_index("seq")
    rows_dev, seq_dev = (tokens.shape[0], tokens.shape[1])
    group_size = HEADS // KV_HEADS
    att_width = HEADS * HEAD_DIM
    kv_width = KV_HEADS * HEAD_DIM
    gain_attn = gains[:D]
    gain_ffn = gains[D : 2 * D]
    gain_query = gains[2 * D : 2 * D + HEAD_DIM]
    gain_key = gains[2 * D + HEAD_DIM :]
    local_places = jnp.arange(seq_dev, dtype=jnp.int32)
    places = seq_index * seq_dev + local_places
    query_docs, offsets = doc_tables(doc_starts, places)
    cos_table, sin_table = rotary(offsets)
    copies = (
        qkv_master.astype(jnp.bfloat16),
        out_master.astype(jnp.bfloat16),
        gate_up_master.astype(jnp.bfloat16),
        down_master.astype(jnp.bfloat16),
    )
    w_qkv, w_out, w_gate_up, w_down = (
        lax.all_gather(copies[0], ("seq", "rows"), axis=0, tiled=True),
        lax.all_gather(copies[1], ("seq", "rows"), axis=0, tiled=True),
        lax.all_gather(copies[2], ("seq", "rows"), axis=0, tiled=True),
        lax.all_gather(copies[3], ("seq", "rows"), axis=0, tiled=True),
    )
    tokens_wide = tokens.astype(jnp.float32)
    normed = norm_rows(tokens_wide, gain_attn).astype(jnp.bfloat16)
    projected = jnp.einsum("rtd,de->rte", normed, w_qkv, preferred_element_type=jnp.float32)
    head_fn = partial(queries_keys, cos_table, sin_table)
    queries, keys_rot = head_fn(projected, gain_query, gain_key)
    query16 = queries.astype(jnp.bfloat16).reshape(
        rows_dev, seq_dev, KV_HEADS, group_size, HEAD_DIM
    )
    keys16 = keys_rot.astype(jnp.bfloat16).reshape(rows_dev, seq_dev, kv_width)
    values16 = projected[..., att_width + kv_width :].astype(jnp.bfloat16)
    stat_shape = (rows_dev, KV_HEADS, group_size, seq_dev)
    initial = (
        jnp.full(stat_shape, MASKED_SCORE, jnp.float32),
        jnp.zeros(stat_shape, jnp.float32),
        jnp.zeros(stat_shape + (HEAD_DIM,), jnp.float32),
    )
    carry = initial
    key_piece = lax.all_gather(keys16, "seq", axis=1, tiled=True)
    value_piece = lax.all_gather(values16, "seq", axis=1, tiled=True)
    key_count = key_piece.shape[1]

    def absorb_block(state, block_index):
        best, total, summed = state
        block_begin = block_index * seq_dev
        key_block = lax.dynamic_slice_in_dim(key_piece, block_begin, seq_dev, 1).reshape(
            rows_dev, seq_dev, KV_HEADS, HEAD_DIM
        )
        value_block = lax.dynamic_slice_in_dim(value_piece, block_begin, seq_dev, 1).reshape(
            rows_dev, seq_dev, KV_HEADS, HEAD_DIM
        )
        key_places = block_begin + jnp.arange(seq_dev, dtype=jnp.int32)
        key_docs, _ = doc_tables(doc_starts, key_places)
        allowed = mask_of(query_docs, places, key_docs, key_places)
        scores = jnp.einsum(
            "rqkgh,rtkh->rkgqt", query16, key_block, preferred_element_type=jnp.float32
        )
        scores = jnp.where(allowed, scores, MASKED_SCORE)
        best_new = jnp.maximum(best, jnp.max(scores, axis=-1))
        weights = jnp.where(allowed, jnp.exp(scores - best_new[..., None]), 0.0)
        factor = jnp.exp(best - best_new)
        total = total * factor + jnp.sum(weights, axis=-1)
        summed = summed * factor[..., None] + jnp.einsum(
            "rkgqt,rtkh->rkgqh",
            weights.astype(jnp.bfloat16),
            value_block,
            preferred_element_type=jnp.float32,
        )
        return ((best_new, total, summed), None)

    carry, _ = lax.scan(absorb_block, carry, jnp.arange(key_count // seq_dev, dtype=jnp.int32))
    best, total, summed = carry
    log_total = best + jnp.log(total)
    attended = summed / total[..., None]
    attended16 = (
        attended.transpose(0, 3, 1, 2, 4).reshape(rows_dev, seq_dev, att_width).astype(jnp.bfloat16)
    )
    branch = jnp.einsum("rtc,cd->rtd", attended16, w_out, preferred_element_type=jnp.float32)
    hidden_in = tokens_wide + branch
    normed2 = norm_rows(hidden_in, gain_ffn).astype(jnp.bfloat16)
    gate_up = jnp.einsum("rtd,df->rtf", normed2, w_gate_up, preferred_element_type=jnp.float32)
    gate_part, up_part = (gate_up[..., :FF], gate_up[..., FF:])
    hidden = (jax.nn.silu(gate_part) * up_part).astype(jnp.bfloat16)
    output = hidden_in + jnp.einsum(
        "rtf,fd->rtd", hidden, w_down, preferred_element_type=jnp.float32
    )
    d_hidden = jnp.einsum("rtd,fd->rtf", grad_out, w_down, preferred_element_type=jnp.float32)
    silu_value, silu_back = jax.vjp(jax.nn.silu, gate_part)
    d_gate = silu_back(d_hidden * up_part)[0]
    d_gate_up = jnp.concatenate([d_gate, d_hidden * silu_value], axis=-1).astype(jnp.bfloat16)
    d_normed2 = jnp.einsum("rtf,df->rtd", d_gate_up, w_gate_up, preferred_element_type=jnp.float32)
    _, ffn_norm_back = jax.vjp(norm_rows, hidden_in, gain_ffn)
    d_inner, grad_gain_ffn = ffn_norm_back(d_normed2)
    d_hidden_in = grad_out.astype(jnp.float32) + d_inner
    term_down = jnp.einsum("rtf,rtd->fd", hidden, grad_out, preferred_element_type=jnp.float32)
    grad_down = lax.psum_scatter(term_down, ("seq", "rows"), scatter_dimension=0, tiled=True)
    term_gate_up = jnp.einsum("rtd,rtf->df", normed2, d_gate_up, preferred_element_type=jnp.float32)
    grad_gate_up = lax.psum_scatter(term_gate_up, ("seq", "rows"), scatter_dimension=0, tiled=True)
    d_branch = d_hidden_in.astype(jnp.bfloat16)
    term_out = jnp.einsum("rtc,rtd->cd", attended16, d_branch, preferred_element_type=jnp.float32)
    d_attended = jnp.einsum(
        "rtd,cd->rtc", d_branch, w_out, preferred_element_type=jnp.float32
    ).astype(jnp.bfloat16)
    d_heads = d_attended.reshape(rows_dev, seq_dev, KV_HEADS, group_size, HEAD_DIM).transpose(
        0, 2, 3, 1, 4
    )
    delta = jnp.sum(d_heads.astype(jnp.float32) * attended, axis=-1)

    def cycle_turn(turn_index, carry):
        pair16, grad_pair, d_queries = carry
        source = (seq_index + turn_index) % cycle_size
        key_places = source * seq_dev + local_places
        key_docs, _ = doc_tables(doc_starts, key_places)
        allowed = mask_of(query_docs, places, key_docs, key_places)
        key_block = pair16[0].reshape(rows_dev, seq_dev, KV_HEADS, HEAD_DIM)
        value_block = pair16[1].reshape(rows_dev, seq_dev, KV_HEADS, HEAD_DIM)
        scores = jnp.einsum(
            "rqkgh,rtkh->rkgqt", query16, key_block, preferred_element_type=jnp.float32
        )
        scores = jnp.where(allowed, scores, MASKED_SCORE)
        probs = jnp.where(allowed, jnp.exp(scores - log_total[..., None]), 0.0)
        d_values = jnp.einsum(
            "rkgqt,rkgqh->rtkh",
            probs.astype(jnp.bfloat16),
            d_heads,
            preferred_element_type=jnp.float32,
        )
        d_probs = jnp.einsum(
            "rkgqh,rtkh->rkgqt", d_heads, value_block, preferred_element_type=jnp.float32
        )
        d_scores = (probs * (d_probs - delta[..., None])).astype(jnp.bfloat16)
        d_queries = d_queries + jnp.einsum(
            "rkgqt,rtkh->rkgqh", d_scores, key_block, preferred_element_type=jnp.float32
        )
        d_keys = jnp.einsum(
            "rkgqt,rqkgh->rtkh", d_scores, query16, preferred_element_type=jnp.float32
        )
        grad_pair = grad_pair + jnp.stack(
            [
                d_keys.reshape(rows_dev, seq_dev, kv_width),
                d_values.reshape(rows_dev, seq_dev, kv_width),
            ]
        )
        grad_pair = from_behind(grad_pair.astype(jnp.bfloat16), "seq", -1).astype(grad_pair.dtype)
        pair16 = from_behind(pair16, "seq", -1)
        return (pair16, grad_pair, d_queries)

    start_pair = jnp.stack([keys16, values16])
    start_grads = jnp.zeros((2, rows_dev, seq_dev, kv_width), jnp.float32)
    start_queries = jnp.zeros(stat_shape + (HEAD_DIM,), jnp.float32)
    _, grad_pair, d_queries = lax.fori_loop(
        0, cycle_size, cycle_turn, (start_pair, start_grads, start_queries)
    )
    d_queries = d_queries.transpose(0, 3, 1, 2, 4).reshape(rows_dev, seq_dev, HEADS, HEAD_DIM)
    d_keys_home = grad_pair[0].reshape(rows_dev, seq_dev, KV_HEADS, HEAD_DIM)
    _, heads_back = jax.vjp(head_fn, projected, gain_query, gain_key)
    d_projected, grad_gain_query, grad_gain_key = heads_back((d_queries, d_keys_home))
    d_projected = jnp.concatenate(
        [d_projected[..., : att_width + kv_width], grad_pair[1]], axis=-1
    ).astype(jnp.bfloat16)
    term_qkv = jnp.einsum("rtd,rte->de", normed, d_projected, preferred_element_type=jnp.float32)
    d_normed = jnp.einsum("rte,de->rtd", d_projected, w_qkv, preferred_element_type=jnp.float32)
    _, attn_norm_back = jax.vjp(norm_rows, tokens_wide, gain_attn)
    d_tokens_part, grad_gain_attn = attn_norm_back(d_normed)
    grad_tokens = (d_hidden_in + d_tokens_part).astype(jnp.bfloat16)
    grad_qkv, grad_out_proj = (
        lax.psum_scatter(term_qkv, ("seq", "rows"), scatter_dimension=0, tiled=True),
        lax.psum_scatter(term_out, ("seq", "rows"), scatter_dimension=0, tiled=True),
    )
    gain_local = jnp.concatenate([grad_gain_attn, grad_gain_ffn, grad_gain_query, grad_gain_key])
    grads = (grad_qkv, grad_out_proj, grad_gate_up, grad_down)
    updated = optimizer_step(
        grads, gain_local, (qkv_master, out_master, gate_up_master, down_master), gains,
        (qkv_rows, out_rows, gate_up_rows, down_rows), col_moments, gain_moments,
        lambda vector: lax.psum(vector, ("seq", "rows")),
    )
    return (output.astype(jnp.bfloat16), grad_tokens, *grads, *updated)


MESH = pl.DeviceIdType.MESH
PLACES = 32
VMEM_BYTES = 56 * 1024 * 1024
CHUNK = 16


def here():
    seq = lax.axis_index("seq")
    return lax.div(seq, 2), lax.rem(seq, 2), lax.axis_index("rows")


def flips(chip):
    return (chip + 1 - 2 * lax.rem(chip, 2), lax.rem(chip + 2, 4), 3 - chip)


def ahead(z, step):
    return lax.rem(z + step, 4)


def at_place(chip, core, z):
    return (2 * chip + core, z)


def greet(peers):
    barrier = pltpu.get_barrier_semaphore()
    for peer in peers:
        pl.semaphore_signal(barrier, inc=1, device_id=peer, device_id_type=MESH)
    pl.semaphore_wait(barrier, len(peers))


class Mover:
    def __init__(self, send_sem, recv_sem, local_sem):
        self.send_sem, self.recv_sem, self.local_sem = send_sem, recv_sem, local_sem
        self.remote, self.own, self.lines = [], [], []
        self.used = 0

    def copy_of(self, src, dst, peer, send_slot, recv_slot):
        return pltpu.make_async_remote_copy(
            src_ref=src,
            dst_ref=dst,
            send_sem=self.send_sem.at[send_slot],
            recv_sem=self.recv_sem.at[recv_slot],
            device_id=peer,
            device_id_type=MESH,
        )

    def send_parts(self, pairs, whole, peer):
        slot = self.used
        self.used += 1
        for src, dst in pairs:
            self.copy_of(src, dst, peer, slot, slot).start()
        copy = self.copy_of(whole[0], whole[1], peer, slot, slot)
        handle = [copy, False, copy.wait_recv, False]
        self.remote.append(handle)
        return handle

    def send(self, src, dst, peer):
        return self.send_parts([(src, dst)], (src, dst), peer)

    def keep_parts(self, pairs, whole):
        sem = self.local_sem.at[len(self.own)]
        for src, dst in pairs:
            pltpu.make_async_copy(src, dst, sem).start()
        copy = pltpu.make_async_copy(whole[0], whole[1], sem)
        handle = [copy, False, copy.wait]
        self.own.append(handle)
        return handle

    def keep(self, src, dst):
        return self.keep_parts([(src, dst)], (src, dst))

    def line(self, source, block_of, chip, core, z):
        line = (self.used, block_of, chip, core, z)
        self.used += 5
        base = line[0]
        up, low = at_place(chip, core, z + 1), at_place(chip, core, z - 1)
        rising = self.copy_of(source, block_of(z), up, base, base + 3)
        falling = self.copy_of(source, block_of(z), low, base + 4, base + 1)
        pl.when(z < 3)(rising.start)
        pl.when(z > 0)(falling.start)
        self.lines += [(z < 3, rising), (z > 0, falling)]
        return line

    def arrive_line(self, line, step):
        base, block_of, chip, core, z = line
        block = block_of(ahead(z, step))
        self.copy_of(block, block, at_place(chip, core, ahead(z, step)), base + step, base + step).wait_recv()
        if step > 1:
            copy = self.copy_of(block, block, at_place(chip, core, z + 1), base + step, base + step - 1)
            rises = (z + step >= 4) & (z < 3)
            pl.when(rises)(copy.start)
            self.lines.append((rises, copy))
        if step < 3:
            copy = self.copy_of(block, block, at_place(chip, core, z - 1), base + step, base + step + 1)
            falls = (z + step < 4) & (z > 0)
            pl.when(falls)(copy.start)
            self.lines.append((falls, copy))
        return block

    def arrive(self, *handles):
        for handle in handles:
            if not handle[1]:
                handle[1] = True
                handle[2]()

    def sent(self, *handles):
        for handle in handles:
            if not handle[3]:
                handle[3] = True
                handle[0].wait_send()

    def sent_lines(self):
        for when, copy in self.lines:
            pl.when(when)(copy.wait_send)
        self.lines = []

    def finish(self):
        self.arrive(*self.own, *self.remote)
        self.sent(*self.remote)
        self.sent_lines()


def semaphores(remote, own):
    return [
        pltpu.SemaphoreType.DMA((remote,)),
        pltpu.SemaphoreType.DMA((remote,)),
        pltpu.SemaphoreType.DMA((max(own, 1),)),
    ]


def exchange(kernel, ident, inputs, outputs, scratch, copies, moved, flops=0):
    vmem, anywhere = pl.BlockSpec(memory_space=pltpu.VMEM), pl.BlockSpec(memory_space=pl.ANY)
    return pl.pallas_call(
        kernel,
        out_shape=[jax.ShapeDtypeStruct(shape, kind) for shape, kind, _ in outputs],
        in_specs=[vmem if near else anywhere for _, near in inputs],
        out_specs=[vmem if near else anywhere for _, _, near in outputs],
        scratch_shapes=scratch + semaphores(*copies),
        compiler_params=pltpu.CompilerParams(
            collective_id=ident, has_side_effects=True, vmem_limit_bytes=VMEM_BYTES
        ),
        cost_estimate=pl.CostEstimate(flops=flops, bytes_accessed=moved, transcendentals=0),
    )(*[array for array, _ in inputs])


def chunks(length, body):
    @pl.loop(0, length // CHUNK)
    def _(step):
        body(pl.ds(pl.multiple_of(step * CHUNK, CHUNK), CHUNK))


def segments(core, z):
    for part in range(2):
        for chip in range(4):
            start = part * FF + ((2 * chip + core) * 4 + z) * 256
            yield pl.ds(pl.multiple_of(start, 256), 256), pl.ds(part * 1024 + chip * 256, 256)


def add_blocks(first, second, result):
    for row in range(2):

        def body(part):
            total = first[row, part].astype(jnp.float32) + second[row, part].astype(jnp.float32)
            result[row, part] = total.astype(result.dtype)

        chunks(64, body)


def head_tables(doc_starts, length):
    places = jnp.arange(length, dtype=jnp.int32)
    _, offsets = doc_tables(doc_starts, places)
    cos_table, sin_table = rotary(offsets)
    signs = jnp.where(jnp.arange(HEAD_DIM) < HEAD_DIM // 2, -1.0, 1.0)
    tables = []
    for table in (cos_table, sin_table * signs):
        wide = jnp.concatenate([table, table], axis=-1)
        tables.append(wide.reshape(2, 8, 64, 128).transpose(1, 0, 2, 3))
    return (*tables, (places[None, :] - offsets)[..., None])


def lower_half(shape):
    return lax.broadcasted_iota(jnp.int32, shape, len(shape) - 1) < 64


def swap_halves(entries):
    lane = lax.broadcasted_iota(jnp.int32, entries.shape, 1)
    return jnp.where(lax.rem(lane, 64) < 32, pltpu.roll(entries, 96, 1), pltpu.roll(entries, 32, 1))


def head_means(entries):
    lower = lower_half(entries.shape)
    low = jnp.sum(jnp.where(lower, entries, 0.0), axis=-1, keepdims=True)
    high = jnp.sum(jnp.where(lower, 0.0, entries), axis=-1, keepdims=True)
    return jnp.where(lower, low, high) * (1.0 / HEAD_DIM)


def wide(start, size):
    return pl.ds(pl.multiple_of(start, size), size)


def plain(left, right):
    return jnp.dot(left, right, preferred_element_type=jnp.float32)


def across(left, right):
    return lax.dot_general(
        left, right, (((1,), (1,)), ((), ())), preferred_element_type=jnp.float32
    )


def down(left, right):
    return lax.dot_general(
        left, right, (((0,), (0,)), ((), ())), preferred_element_type=jnp.float32
    )


def attention_probs(queries, keys, first, part):
    scores = across(queries, keys)
    place = lax.broadcasted_iota(jnp.int32, scores.shape, 1)
    query = lax.broadcasted_iota(jnp.int32, scores.shape, 0) + part * 128
    allowed = (place >= first) & (place <= query)
    scores = jnp.where(allowed, scores, MASKED_SCORE)
    best = jnp.max(scores, axis=-1, keepdims=True)
    weights = jnp.where(allowed, jnp.exp(scores - best), 0.0)
    return weights / jnp.sum(weights, axis=-1, keepdims=True)


def forward_kernel(
    tok, gain_attn, gain_ffn, gain_heads, cosines, sines, first, qkv_master, wo, wd_own, wg, grad_out,
    all_branch, d_hidden_in, out_sum, gain_part, down_part, gate_up_in, gate_up_mid,
    kept_tok, kept_wq, kept_wo, projected, queries, keys_values, attended,
    wq_send, normed, all_tok, all_wq, all_wo, partial, from_partner, came,
    hidden_in, all_norm, all_out, all_wg, wd, hidden, d_gate_up, d_branch, *sems,
):
    half, full = jnp.bfloat16, jnp.float32
    chip, core, z = here()
    others = flips(chip)
    other = 1 - core
    me = 2 * chip + core
    partner = at_place(chip, other, z)
    plane = [at_place(peer_chip, core, z) for peer_chip in others]
    plane_cross = [at_place(peer_chip, other, z) for peer_chip in others]
    steps = (2, 1, 3)
    line = [at_place(chip, core, ahead(z, step)) for step in steps]
    cross = [at_place(chip, other, ahead(z, step)) for step in steps]
    everyone = [partner] + plane + plane_cross
    greet(everyone + line + cross)
    move = Mover(*sems)

    for head in range(8):
        wq_send[head, :, pl.ds(0, 256)] = qkv_master[:, pl.ds(head * 256, 256)].astype(half)
    low = lower_half((64, 128))
    for pair in range(4):
        keys = qkv_master[:, pl.ds(2048 + pair * 128, 128)]
        values = qkv_master[:, pl.ds(2560 + pair * 128, 128)]
        tail = pl.ds(256, 128)
        wq_send[2 * pair, :, tail] = jnp.where(low, keys, pltpu.roll(values, 64, 1)).astype(half)
        wq_send[2 * pair + 1, :, tail] = jnp.where(low, pltpu.roll(keys, 64, 1), values).astype(half)
    heads = [move.keep(wq_send.at[me], all_wq.at[me, z])]
    for peer in everyone:
        heads.append(move.send(wq_send.at[peer[0]], all_wq.at[me, z], peer))

    for row in range(2):

        def body0(part):
            total = tok[row, part].astype(full)
            scale = lax.rsqrt(jnp.mean(total * total, axis=-1, keepdims=True) + EPSILON)
            normed[row, part] = (total * scale * gain_attn[...]).astype(half)

        chunks(64, body0)
    token_copies = [move.send(normed, all_tok.at[me], peer) for peer in plane]
    token_copies.append(move.send(normed, all_tok.at[me], partner))
    tokens_here = move.keep(normed, all_tok.at[me])
    move.arrive(*heads)
    hops = (3, 1, 2)
    line_wq = move.line(all_wq.at[:, z], lambda at: all_wq.at[:, at], chip, core, z)
    weights = [move.send(wo, all_wo.at[z], peer) for peer in line]
    weights.append(move.keep(wo, all_wo.at[z]))

    def turn_block(to_core, to_z):
        whole = all_wg.at[chip, core, z]
        pairs = [(wg.at[:, src], whole.at[:, dst]) for src, dst in segments(to_core, to_z)]
        return pairs, (whole, whole)

    own = [
        move.keep(wd_own, wd.at[chip]),
        move.keep(grad_out, all_out.at[z, core]),
        move.send(grad_out, all_out.at[z, core], partner),
    ]
    own += [move.send(wd_own, wd.at[chip], peer) for peer in plane]
    for peer_chip, handle in zip(others, tuple(token_copies)):
        move.arrive(handle)
        block = all_tok.at[2 * peer_chip + core]
        token_copies.append(move.send(block, block, partner))
    for step in hops:
        move.arrive_line(line_wq, step)
    turned = []
    for step, peer, peer_cross in zip(steps, line, cross):
        to = ahead(z, step)
        turned.append(move.send_parts(*turn_block(core, to), peer))
        turned.append(move.send_parts(*turn_block(other, to), peer_cross))
    turned += [move.keep_parts(*turn_block(core, z)), move.send_parts(*turn_block(other, z), partner)]
    line_grads = move.line(grad_out, lambda at: all_out.at[at, core], chip, core, z)
    move.arrive(tokens_here, *token_copies, *weights)
    saved = [move.keep(all_tok, kept_tok), move.keep(all_wq, kept_wq), move.keep(all_wo, kept_wo)]

    flat_tok, flat_wq = all_tok.reshape(1024, D), all_wq.reshape(D, 384)
    flat_wo = all_wo.reshape(256, D)

    @pl.loop(0, 4)
    def _(step):
        block = plain(flat_tok[wide(step * 256, 256)], flat_wq[...])
        projected[wide(step * 2, 2)] = block.reshape(2, 2, 64, 384)

    @pl.loop(0, 8)
    def _(block):
        for row in range(2):
            cosine, sine = cosines[block, row], sines[block, row]
            places = wide(block * 64, 64)
            for tile in range(3):
                entries = projected[block, row, :, pl.ds(tile * 128, 128)]
                gain = gain_heads[min(tile, 2) // 2 : min(tile, 2) // 2 + 1]
                scale = lax.rsqrt(head_means(entries * entries) + EPSILON)
                turned_entries = entries * scale * gain
                turned_entries = turned_entries * cosine + swap_halves(turned_entries) * sine
                if tile < 2:
                    queries[row, tile, places] = (turned_entries * HEAD_DIM ** (-0.5)).astype(half)
                else:
                    zero = jnp.zeros_like(entries)
                    rolled = pltpu.roll(turned_entries, 64, 1)
                    values = pltpu.roll(entries, 64, 1)
                    keys_values[row, 0, places] = jnp.where(low, turned_entries, zero).astype(half)
                    keys_values[row, 1, places] = jnp.where(low, zero, rolled).astype(half)
                    keys_values[row, 2, places] = jnp.where(low, values, zero).astype(half)
                    keys_values[row, 3, places] = jnp.where(low, zero, entries).astype(half)

    @pl.loop(0, 2)
    def _(row):
        for tile in range(2):
            for part in range(4):
                own_places, upto = pl.ds(part * 128, 128), pl.ds(0, (part + 1) * 128)
                total = jnp.zeros((128, 128), full)
                for side in range(2):
                    probs = attention_probs(
                        queries[row, tile, own_places], keys_values[row, side, upto],
                        first[row, own_places], part,
                    )
                    total += plain(probs.astype(half), keys_values[row, 2 + side, upto])
                attended[pl.ds(2 * part, 2), row, :, pl.ds(tile * 128, 128)] = total.reshape(2, 64, 128)

    flat_attended = attended.reshape(1024, 256)

    @pl.loop(0, 4)
    def _(step):
        rows = flat_attended[wide(step * 256, 256)].astype(half)

        @pl.loop(0, 4)
        def _(col):
            cols = wide(col * 512, 512)
            block = plain(rows, flat_wo[:, cols])
            partial[wide(step * 2, 2), :, :, cols] = block.reshape(2, 2, 64, 512).astype(half)

    order = tuple(others) + (chip,)
    halves = [move.send(partial.at[2 * to + other], from_partner.at[to], partner) for to in order]
    sums = []
    for to, arrived, peer in zip(others, halves, plane):
        move.arrive(arrived)
        add_blocks(partial.at[2 * to + core], from_partner.at[to], from_partner.at[to])
        sums.append(move.send(from_partner.at[to], came.at[chip], peer))
    move.sent(*token_copies)
    move.arrive(halves[3], *sums)
    for row in range(2):

        def body(part):
            total = tok[row, part].astype(full)
            total += partial[me, row, part].astype(full)
            total += from_partner[chip, row, part].astype(full)
            for peer_chip in others:
                total += came[peer_chip, row, part].astype(full)
            hidden_in[row, part] = total
            scale = lax.rsqrt(jnp.mean(total * total, axis=-1, keepdims=True) + EPSILON)
            normed[row, part] = (total * scale * gain_ffn[...]).astype(half)

        chunks(64, body)
    move.sent(*sums, *halves)
    move.arrive(*saved)
    line_norms = move.line(normed, lambda at: all_norm.at[at, core], chip, core, z)
    own.append(move.send(normed, all_norm.at[z, core], partner))
    own.append(move.keep(normed, all_norm.at[z, core]))

    move.arrive(*turned)
    by_x, by_y = plane[0], plane[1]
    front, back = all_wg.at[chip, 0], all_wg.at[chip, 1]
    from_x = move.send(front, front, by_x)
    from_y = move.send(back, back, by_y)
    weights = [from_x, from_y, move.send(back, back, by_x), move.send(front, front, by_y)]

    shared = []
    for step in hops:
        if step == 2:
            move.arrive(from_x, from_y)
            front, back = all_wg.at[others[0], 0], all_wg.at[others[1], 1]
            weights += [move.send(front, front, by_y), move.send(back, back, by_x)]
        for line_of in (line_grads, line_norms):
            block = move.arrive_line(line_of, step)
            shared.append(move.send(block, block, partner))
    move.arrive(*weights, *own, *shared)

    flat_wg, flat_wd = all_wg.reshape(D, 2048), wd.reshape(1024, D)

    def block_of(zb):
        @pl.loop(0, 4)
        def _(step):
            cols, ups = wide(step * 256, 256), wide(1024 + step * 256, 256)
            rows = all_norm[zb].reshape(256, D)
            gate = plain(rows, flat_wg[:, cols])
            up = plain(rows, flat_wg[:, ups])
            d_hidden = across(all_out[zb].reshape(256, D), flat_wd[cols])
            sigmoid = 1.0 / (1.0 + jnp.exp(-gate))
            silu = gate * sigmoid
            hidden[zb, :, cols] = (silu * up).astype(half)
            d_gate = d_hidden * up * (sigmoid * (1.0 + gate * (1.0 - sigmoid)))
            d_gate_up[zb, :, cols] = d_gate.astype(half)
            d_gate_up[zb, :, ups] = (d_hidden * silu).astype(half)

        @pl.loop(0, 8)
        def _(step):
            cols = wide(step * 256, 256)
            block = across(d_gate_up[zb], flat_wg[cols])
            partial[pl.ds(2 * zb, 2), :, :, cols] = block.reshape(2, 2, 64, 256).astype(half)

    def pair_sum(zb, handle, into, base):
        move.arrive(handle)
        add_blocks(partial.at[2 * zb + core], into.at[base + zb], into.at[base + zb])

    to_partner, sums = [], []
    walk = [ahead(z, step) for step in steps] + [z]
    for index, zb in enumerate(walk):
        block_of(zb)
        to_partner.append(move.send(partial.at[2 * zb + other], from_partner.at[zb], partner))
        if index > 0:
            before = walk[index - 1]
            pair_sum(before, to_partner[index - 1], from_partner, 0)
            sums.append(move.send(from_partner.at[before], came.at[z], line[index - 1]))
    pair_sum(z, to_partner[3], from_partner, 0)

    flat_norm, flat_grads = all_norm.reshape(1024, D), all_out.reshape(1024, D)
    flat_hidden, flat_d = hidden.reshape(1024, 1024), d_gate_up.reshape(1024, 2048)
    move.sent(*weights)
    move.sent_lines()

    def gate_up_grad(to, side):
        rows, lanes = wide(to * 512, 512), pl.ds(side * 1024, 1024)

        @pl.loop(0, 2)
        def _(step):
            cols = wide(side * 1024 + step * 512, 512)
            flat_wg[rows, cols] = down(flat_norm[:, rows], flat_d[:, cols]).astype(half)

        return flat_wg.at[rows, lanes]

    passed = []
    for side in (0, 1):
        passed.append(move.send(gate_up_grad(others[2], side), gate_up_mid.at[side], plane[side]))
    for side in (0, 1):
        move.send(gate_up_grad(others[side], side), gate_up_in.at[side, 1], plane[side])
    handed = [gate_up_grad(others[1 - side], side) for side in (0, 1)]
    for side in (0, 1):
        move.keep(gate_up_grad(chip, side), gate_up_in.at[side, 0])

    move.arrive(*sums)
    gain_part[...] = jnp.zeros_like(gain_part)
    for row in range(2):

        def body2(part):
            total = from_partner[z, row, part].astype(full)
            for step in steps:
                total += came[ahead(z, step), row, part].astype(full)
            entries = hidden_in[row, part]
            scale = lax.rsqrt(jnp.mean(entries * entries, axis=-1, keepdims=True) + EPSILON)
            gain_part[...] += jnp.sum(total * entries * scale, axis=0, keepdims=True)
            total = total * gain_ffn[...]
            inner = jnp.mean(total * entries, axis=-1, keepdims=True) * (scale * scale * scale)
            grad = grad_out[row, part].astype(full) + total * scale - entries * inner
            d_hidden_in[row, part] = grad
            d_branch[row, part] = grad.astype(half)

        chunks(64, body2)
    branches = [move.send(d_branch, all_branch.at[me], peer) for peer in plane]
    move.send(d_branch, all_branch.at[me], partner)
    move.keep(d_branch, all_branch.at[me])

    move.sent(*to_partner)
    to_partner, sums = [], []
    for index, zb in enumerate(walk):

        @pl.loop(0, 4)
        def _(step, zb=zb):
            cols = wide(step * 512, 512)
            block = plain(hidden[zb], flat_wd[:, cols])
            partial[pl.ds(2 * zb, 2), :, :, cols] = block.reshape(2, 2, 64, 512).astype(half)

        to_partner.append(move.send(partial.at[2 * zb + other], all_tok.at[zb], partner))
        if index > 0:
            before = walk[index - 1]
            pair_sum(before, to_partner[index - 1], all_tok, 0)
            sums.append(move.send(all_tok.at[before], all_tok.at[4 + z], line[index - 1]))
    pair_sum(z, to_partner[3], all_tok, 0)

    @pl.loop(0, 4)
    def _(to):
        rows = wide(to * 256, 256)

        @pl.loop(0, 4)
        def _(step):
            cols = wide(step * 512, 512)
            flat_wd[rows, cols] = down(flat_hidden[:, rows], flat_grads[:, cols]).astype(half)

    move.keep(wd, down_part)
    loads = []
    for side in (0, 1):
        move.arrive(passed[side])
        rows = pl.ds(side * 512, 512)
        loads.append(move.keep(gate_up_mid.at[side], flat_d.at[rows, pl.ds(0, 1024)]))
    for side in (0, 1):
        move.arrive(loads[side])

        @pl.loop(0, 512 // CHUNK)
        def _(step, side=side):
            lanes = pl.ds(side * 1024, 1024)
            rows = wide(others[1 - side] * 512 + step * CHUNK, CHUNK)
            extra = flat_d[wide(side * 512 + step * CHUNK, CHUNK), pl.ds(0, 1024)]
            total = flat_wg[rows, lanes].astype(full) + extra.astype(full)
            flat_wg[rows, lanes] = total.astype(half)

        move.send(handed[side], gate_up_in.at[side, 2], plane[1 - side])
    for peer_chip, handle in zip(others, branches):
        move.arrive(handle)
        block = all_branch.at[2 * peer_chip + core]
        move.send(block, block, partner)
    move.arrive(*sums)
    for row in range(2):

        def body3(part):
            total = hidden_in[row, part] + all_tok[z, row, part].astype(full)
            for step in steps:
                total += all_tok[4 + ahead(z, step), row, part].astype(full)
            out_sum[row, part] = total.astype(half)

        chunks(64, body3)
    move.finish()


def backward_kernel(
    branch_in, wq_in, wo_in, tok_in, gate_up_in, down_part, projected, queries, keys_values, attended,
    cosines, sines, first, gain_heads,
    d_norm_came, gate_up_came, qkv_came, out_came, down_came, gain_qk,
    d_branch, wq, wo, all_tok, gate_up, d_attended, d_queries, d_keys_values, d_projected,
    qkv_part, out_part, partial, from_partner, gate_up_sum, qkv_in, qkv_sum, *sems,
):
    half, full = jnp.bfloat16, jnp.float32
    chip, core, z = here()
    others = flips(chip)
    other = 1 - core
    me = 2 * chip + core
    partner = at_place(chip, other, z)
    plane = [at_place(peer_chip, core, z) for peer_chip in others]
    plane_cross = [at_place(peer_chip, other, z) for peer_chip in others]
    everyone = [partner] + plane + plane_cross
    steps = (2, 1, 3)
    line = [at_place(chip, core, ahead(z, step)) for step in steps]
    cross = [at_place(chip, other, ahead(z, step)) for step in steps]
    move = Mover(*sems)
    load_gate_up = move.keep(gate_up_in, gate_up)
    loads = [move.keep(branch_in, d_branch), move.keep(wo_in, wo), move.keep(wq_in, wq)]
    load_tok = move.keep(tok_in, all_tok)
    greet(everyone + line + cross)
    for to, peer in zip(others, plane):
        move.send(down_part.at[to], down_came.at[chip], peer)
    move.keep(down_part.at[chip], down_came.at[chip])
    move.arrive(load_gate_up)

    @pl.loop(0, 8)
    def _(block):
        to_core, to_z = lax.div(block, 4), lax.rem(block, 4)

        @pl.loop(0, 64 // CHUNK)
        def _(step):
            rows = wide(block * 64 + step * CHUNK, CHUNK)
            for side in range(2):
                total = gate_up[side, 0, rows].astype(full)
                for slot in (1, 2):
                    total += gate_up[side, slot, rows].astype(full)
                part, lanes = wide(step * CHUNK, CHUNK), pl.ds(side * 1024, 1024)
                gate_up_sum[to_core, to_z, part, lanes] = total.astype(half)

    def turn_block(to_core, to_z):
        whole = gate_up_sum.at[to_core, to_z]
        pairs = [(whole.at[:, src], gate_up_came.at[:, dst]) for dst, src in segments(core, z)]
        return pairs, (whole, whole)

    for step, peer, peer_cross in zip(steps, line, cross):
        to = ahead(z, step)
        move.send_parts(*turn_block(core, to), peer)
        move.send_parts(*turn_block(other, to), peer_cross)
    move.send_parts(*turn_block(other, z), partner)
    move.keep_parts(*turn_block(core, z))

    move.arrive(*loads)
    flat_branch, flat_wo = d_branch.reshape(1024, D), wo.reshape(256, D)
    flat_d = d_attended.reshape(1024, 256)

    @pl.loop(0, 4)
    def _(step):
        rows = wide(step * 256, 256)
        flat_d[rows] = across(flat_branch[rows], flat_wo[...]).astype(half)

    d_keys_values[...] = jnp.zeros_like(d_keys_values)
    lower = lower_half((128, 128))

    @pl.loop(0, 2)
    def _(row):
        for tile in range(2):
            for part in range(4):
                own_places, upto = pl.ds(part * 128, 128), pl.ds(0, (part + 1) * 128)
                at = (pl.ds(2 * part, 2), row, slice(None), pl.ds(tile * 128, 128))
                d_heads = d_attended[at].reshape(128, 128)
                products = d_heads.astype(full) * attended[at].reshape(128, 128)
                query = queries[row, tile, own_places]
                total = jnp.zeros((128, 128), full)
                for side in range(2):
                    mask = lower if side == 0 else jnp.logical_not(lower)
                    delta = jnp.sum(jnp.where(mask, products, 0.0), axis=-1, keepdims=True)
                    keys = keys_values[row, side, upto]
                    probs = attention_probs(query, keys, first[row, own_places], part)
                    d_probs = across(d_heads, keys_values[row, 2 + side, upto])
                    d_scores = (probs * (d_probs - delta)).astype(half)
                    total += plain(d_scores, keys)
                    d_keys_values[row, side, upto] += down(d_scores, query)
                    d_keys_values[row, 2 + side, upto] += down(probs.astype(half), d_heads)
                d_queries[row, tile, own_places] = total

    low = lower_half((64, 128))
    gain_qk[...] = jnp.zeros_like(gain_qk)

    @pl.loop(0, 8)
    def _(block):
        for row in range(2):
            cosine, sine = cosines[block, row], sines[block, row]
            places = wide(block * 64, 64)
            for tile in range(3):
                lanes = pl.ds(tile * 128, 128)
                entries = projected[block, row, :, lanes]
                gain = gain_heads[min(tile, 2) // 2 : min(tile, 2) // 2 + 1]
                scale = lax.rsqrt(head_means(entries * entries) + EPSILON)
                if tile < 2:
                    grad = d_queries[row, tile, places] * HEAD_DIM ** (-0.5)
                else:
                    from_low, from_high = d_keys_values[row, 0, places], d_keys_values[row, 1, places]
                    grad = jnp.where(low, from_low + pltpu.roll(from_high, 64, 1), 0.0)
                grad = grad * cosine + swap_halves(grad * sine)
                for_gain = jnp.sum(grad * entries * scale, axis=0, keepdims=True)
                line_low = lower_half((1, 128))
                if tile < 2:
                    for_gain = jnp.where(line_low, for_gain + pltpu.roll(for_gain, 64, 1), 0.0)
                else:
                    for_gain = jnp.where(line_low, 0.0, pltpu.roll(for_gain, 64, 1))
                gain_qk[...] += for_gain
                grad = grad * gain
                inner = head_means(grad * entries) * (scale * scale * scale)
                grad = grad * scale - entries * inner
                if tile == 2:
                    values = pltpu.roll(d_keys_values[row, 2, places], 64, 1)
                    grad = jnp.where(low, grad, values + d_keys_values[row, 3, places])
                d_projected[block, row, :, lanes] = grad.astype(half)

    flat_p, flat_wq = d_projected.reshape(1024, 384), wq.reshape(D, 384)

    @pl.loop(0, 4)
    def _(step):
        rows = flat_p[wide(step * 256, 256)]

        @pl.loop(0, 4)
        def _(col):
            cols = wide(col * 512, 512)
            block = across(rows, flat_wq[cols])
            partial[wide(step * 2, 2), :, :, cols] = block.reshape(2, 2, 64, 512).astype(half)

    order = tuple(others) + (chip,)
    halves = [move.send(partial.at[2 * to + other], from_partner.at[to], partner) for to in order]
    move.arrive(load_tok)
    flat_tok = all_tok.reshape(1024, D)

    @pl.loop(0, 4)
    def _(step):
        block = down(flat_tok[:, wide(step * 512, 512)], flat_p[...])
        qkv_part[wide(step * 2, 2)] = block.reshape(2, 4, 64, 384).astype(half)

    qkv_pieces = [
        move.send(qkv_part.at[:, ahead(z, step)], qkv_in.at[z], peer)
        for step, peer in zip(steps, line)
    ]
    for to, arrived, peer in zip(others, halves, plane):
        move.arrive(arrived)
        add_blocks(partial.at[2 * to + core], from_partner.at[to], from_partner.at[to])
        move.send(from_partner.at[to], d_norm_came.at[chip], peer)
    move.arrive(halves[3])
    add_blocks(partial.at[me], from_partner.at[chip], from_partner.at[chip])
    move.keep(from_partner.at[chip], d_norm_came.at[chip])
    flat_attended = attended.reshape(1024, 256)

    @pl.loop(0, 4)
    def _(step):
        cols = wide(step * 512, 512)
        block = down(flat_attended[...].astype(half), flat_branch[:, cols])
        out_part[:, :, cols] = block.reshape(4, 64, 512).astype(half)

    for step, peer in zip(steps, line):
        move.send(out_part.at[ahead(z, step)], out_came.at[z], peer)
    move.keep(out_part.at[z], out_came.at[z])
    move.arrive(*qkv_pieces)

    @pl.loop(0, 8)
    def _(block):
        def body(part):
            total = qkv_part[block, z, part].astype(full)
            for step in steps:
                total += qkv_in[ahead(z, step), block, part].astype(full)
            qkv_sum[block, part] = total.astype(half)

        chunks(64, body)

    for peer in everyone:
        move.send(qkv_sum.at[peer[0]], qkv_came.at[me], peer)
    move.keep(qkv_sum.at[me], qkv_came.at[me])
    move.finish()


COL_ROWS, GAIN_ROWS = 184, 33
MATRICES = ((64, QKV, 0, 0), (64, D, 64, 24), (64, 2 * FF, 128, 40), (256, D, 192, 168))
ROW_TOTALS = (D, HEADS * HEAD_DIM, D, FF)
BETA = 1.0 - STEP ** (-0.8)


def lane_value(vector, lane):
    lanes = lax.broadcasted_iota(jnp.int32, (1, 128), 1)
    return jnp.sum(jnp.where(lanes == lane, vector, 0.0), axis=-1, keepdims=True)


def statistics_kernel(
    d_norm, tok, d_hidden_in, gain, gain_ffn, gain_qk, qkv, out, gate_up, down, rows,
    m_qkv, m_out, m_gate_up, m_down,
    grad_tok, g_qkv, g_out, g_gate_up, g_down, rows_new, packed,
    gain_part, sums, inverse,
):
    gain_part[...] = jnp.zeros_like(gain_part)

    @pl.loop(0, 128 // CHUNK)
    def _(step):
        part = pl.ds(pl.multiple_of(step * CHUNK, CHUNK), CHUNK)
        total = d_norm[0, part].astype(jnp.float32)
        for slot in range(1, 4):
            total += d_norm[slot, part].astype(jnp.float32)
        entries = tok[part].astype(jnp.float32)
        scale = lax.rsqrt(jnp.mean(entries * entries, axis=-1, keepdims=True) + EPSILON)
        gain_part[...] += jnp.sum(total * entries * scale, axis=0, keepdims=True)
        total = total * gain[...]
        inner = jnp.mean(total * entries, axis=-1, keepdims=True) * (scale * scale * scale)
        grad_tok[part] = (d_hidden_in[part] + total * scale - entries * inner).astype(jnp.bfloat16)

    first = 2 * COL_ROWS
    for slot in range(16):
        lanes = pl.ds(slot * 128, 128)
        packed[first + slot : first + slot + 1] = gain_part[:, lanes]
        packed[first + 16 + slot : first + 17 + slot] = gain_ffn[:, lanes]
    packed[first + 32 : first + 33] = gain_qk[...]
    lane = lax.broadcasted_iota(jnp.int32, (64, 128), 1)

    def wide(step):
        return pl.ds(pl.multiple_of(step * 128, 128), 128)

    def read_qkv(step):
        return g_qkv[:, wide(step)]

    for head in range(8):
        for half in range(2):
            g_qkv[:, pl.ds(head * 256 + half * 128, 128)] = qkv[
                head, :, pl.ds(half * 128, 128)
            ].astype(jnp.float32)
    for pair in range(4):
        low = qkv[2 * pair, :, pl.ds(256, 128)].astype(jnp.float32)
        high = qkv[2 * pair + 1, :, pl.ds(256, 128)].astype(jnp.float32)
        g_qkv[:, pl.ds(2048 + pair * 128, 128)] = jnp.where(lane < 64, low, pltpu.roll(high, 64, 1))
        g_qkv[:, pl.ds(2560 + pair * 128, 128)] = jnp.where(lane < 64, pltpu.roll(low, 64, 1), high)

    def read_out(step):
        total = out[0, :, wide(step)].astype(jnp.float32)
        for slot in range(1, 4):
            total += out[slot, :, wide(step)].astype(jnp.float32)
        return total

    def read_gate_up(step):
        return gate_up[:, wide(step)].astype(jnp.float32)

    def read_down(step):
        total = down[0, :, wide(step)].astype(jnp.float32)
        for slot in range(1, 4):
            total += down[slot, :, wide(step)].astype(jnp.float32)
        return total

    readers = (read_qkv, read_out, read_gate_up, read_down)
    grads = (g_qkv, g_out, g_gate_up, g_down)
    masters = (m_qkv, m_out, m_gate_up, m_down)
    stats = jnp.zeros((1, 128), jnp.float32)
    lanes = lax.broadcasted_iota(jnp.int32, (1, 128), 1)
    for slot, (count, width, row_at, col_at) in enumerate(MATRICES):
        own = pl.ds(0, count)
        sums[0, own] = jnp.zeros((count, 128), jnp.float32)
        sums[1, own] = jnp.zeros((count, 128), jnp.float32)

        @pl.loop(0, width // 128)
        def _(step, slot=slot, own=own):
            entries = readers[slot](step)
            if slot > 0:
                grads[slot][:, wide(step)] = entries
            sums[0, own] += entries * entries
            weight = masters[slot][:, wide(step)]
            sums[1, own] += weight * weight

        mean = jnp.sum(sums[0, own], axis=-1, keepdims=True) / width + SQUARE_EPSILON
        here_rows = pl.ds(row_at, count)
        new = BETA * rows[here_rows] + (1.0 - BETA) * mean
        rows_new[here_rows] = new
        inverse[own] = jnp.broadcast_to(1.0 / new, (count, 128))
        weight_sum = jnp.sum(jnp.sum(sums[1, own], axis=-1, keepdims=True), axis=0, keepdims=True)
        stats = jnp.where(lanes == slot, jnp.sum(new, axis=0, keepdims=True), stats)
        stats = jnp.where(lanes == 4 + slot, weight_sum, stats)

        @pl.loop(0, width // 128)
        def _(step, slot=slot, own=own, count=count, col_at=col_at):
            entries = grads[slot][:, wide(step)]
            square = entries * entries
            packed[pl.ds(col_at + step, 1)] = (
                jnp.sum(square, axis=0, keepdims=True) + count * SQUARE_EPSILON
            )
            packed[pl.ds(COL_ROWS + col_at + step, 1)] = jnp.sum(
                square * inverse[own], axis=0, keepdims=True
            )

    packed[first + 33 : first + 34] = stats
    packed[first + 34 : 512] = jnp.zeros((512 - first - 34, 128), jnp.float32)


def total_kernel(
    parts, col_moments, gain_moments, gains,
    cols_new, col_factors, moments_new, gains_new, grad_gains, spreads,
    totals, plane_came, line_came, plane_sum, line_sum, line_all, *sems,
):
    chip, core, z = here()
    me = 2 * chip + core
    other = 1 - core
    plane = [at_place(chip, other, z)]
    for peer_chip in flips(chip):
        plane += [at_place(peer_chip, core, z), at_place(peer_chip, other, z)]
    line = [at_place(chip, core, ahead(z, step)) for step in (2, 1, 3)]
    greet(plane + line)
    move = Mover(*sems)
    pieces = [move.send(parts.at[peer[0]], plane_came.at[me], peer) for peer in plane]
    plane_came[me] = parts[me]
    move.arrive(*pieces)
    total = plane_came[0]
    for slot in range(1, 8):
        total = total + plane_came[slot]
    plane_sum[...] = total
    pieces = [move.send(plane_sum.at[peer[1]], line_came.at[z], peer) for peer in line]
    line_came[z] = plane_sum[z]
    move.arrive(*pieces)
    line_sum[...] = line_came[0] + line_came[1] + line_came[2] + line_came[3]
    pieces = [move.send(line_sum, line_all.at[z], peer) for peer in line]
    line_all[z] = line_sum[...]
    move.arrive(*pieces)
    for peer in plane:
        move.send(line_all, totals.at[me], peer)
    totals[me] = line_all[...]
    move.finish()
    flat = totals.reshape(512, 128)
    first = 2 * COL_ROWS
    stats = flat[first + 33 : first + 34]
    lanes = lax.broadcasted_iota(jnp.int32, (1, 128), 1)
    out = jnp.zeros((1, 128), jnp.float32)
    for slot, (_, width, _, col_at) in enumerate(MATRICES):
        own = pl.ds(col_at, width // 128)
        entries_all = float(ROW_TOTALS[slot] * width)
        new = BETA * col_moments[own] + (1.0 - BETA) * (flat[own] / ROW_TOTALS[slot])
        cols_new[own] = new
        mean_rows = lane_value(stats, slot) / ROW_TOTALS[slot]
        ratio = flat[pl.ds(COL_ROWS + col_at, width // 128)] / new
        ratio = jnp.sum(jnp.sum(ratio, axis=-1, keepdims=True), axis=0, keepdims=True)
        spread = jnp.sqrt(mean_rows * ratio / entries_all)
        scale = STEP_RATE * jnp.maximum(
            SCALE_EPSILON, jnp.sqrt(lane_value(stats, 4 + slot) / entries_all)
        )
        factor = scale * jnp.sqrt(mean_rows) / jnp.maximum(1.0, spread / CLIP_LEVEL)
        col_factors[own] = lax.rsqrt(new) * factor
        out = jnp.where(lanes == slot, spread, out)
    gradient = flat[first : first + GAIN_ROWS]
    grad_gains[...] = gradient
    old = gains[...]
    new = BETA * gain_moments[...] + (1.0 - BETA) * (gradient * gradient + SQUARE_EPSILON)
    moments_new[...] = new
    unit = gradient * lax.rsqrt(new)
    row = lax.broadcasted_iota(jnp.int32, (GAIN_ROWS, 128), 0)
    lane = lax.broadcasted_iota(jnp.int32, (GAIN_ROWS, 128), 1)
    segment = jnp.where(row < 16, 0, jnp.where(row < 32, 1, jnp.where(lane < 64, 2, 3)))
    factors = jnp.zeros((GAIN_ROWS, 128), jnp.float32)

    def mean_of(square, mask, count):
        picked = jnp.where(mask, square, 0.0)
        return jnp.sum(jnp.sum(picked, axis=-1, keepdims=True), axis=0, keepdims=True) / count

    for slot, count in enumerate((D, D, HEAD_DIM, HEAD_DIM)):
        mask = segment == slot
        spread = jnp.sqrt(mean_of(unit * unit, mask, count))
        scale = STEP_RATE * jnp.maximum(SCALE_EPSILON, jnp.sqrt(mean_of(old * old, mask, count)))
        factors = jnp.where(mask, scale / jnp.maximum(1.0, spread / CLIP_LEVEL), factors)
        out = jnp.where(lanes == 4 + slot, spread, out)
    gains_new[...] = old - factors * unit
    spreads[...] = out


def split_local(
    tokens, doc_starts, grad_out, qkv_master, out_master, gate_up_master, down_master, gains,
    qkv_rows, out_rows, gate_up_rows, down_rows, col_moments, gain_moments,
):
    half, full = jnp.bfloat16, jnp.float32
    gain_attn, gain_ffn = gains[None, :D], gains[None, D : 2 * D]
    gain_query = gains[2 * D : 2 * D + HEAD_DIM]
    gain_key = gains[2 * D + HEAD_DIM :]
    gain_heads = jnp.stack(
        [jnp.concatenate([gain_query, gain_query]), jnp.concatenate([gain_key, gain_key])]
    )
    cosines, sines, first = head_tables(doc_starts, 512)

    def near(*shape, kind=half):
        return pltpu.VMEM(shape, kind)

    (
        all_branch, d_hidden_in, output, grad_gain_ffn, down_part, gate_up_in, _,
        all_tok, all_wq, all_wo, projected, queries, keys_values, attended,
    ) = exchange(
        forward_kernel, 0,
        [
            (tokens, True), (gain_attn, True), (gain_ffn, True), (gain_heads, True),
            (cosines, True), (sines, True), (first, True), (qkv_master, True),
            (out_master.astype(half), False), (down_master.astype(half), False),
            (gate_up_master.astype(half), False), (grad_out, True),
        ],
        [
            ((8, 2, 64, D), half, False), ((2, 64, D), full, True), ((2, 64, D), half, True),
            ((1, D), full, True), ((4, 256, D), half, False), ((2, 3, 512, 1024), half, False),
            ((2, 512, 1024), half, False), ((8, 2, 64, D), half, False), ((8, 4, 64, 384), half, False), ((4, 64, D), half, False),
            ((8, 2, 64, 384), full, True), ((2, 2, 512, 128), half, True),
            ((2, 4, 512, 128), half, True), ((8, 2, 64, 256), full, True),
        ],
        [
            near(8, 64, 384), near(2, 64, D), near(8, 2, 64, D), near(8, 4, 64, 384), near(4, 64, D),
            near(8, 2, 64, D), near(4, 2, 64, D), near(4, 2, 64, D), near(2, 64, D, kind=full),
            near(4, 2, 2, 64, D), near(4, 2, 2, 64, D), near(4, 2, 4, 64, 2048), near(4, 256, D),
            near(4, 256, 1024), near(4, 256, 2048), near(2, 64, D),
        ],
        (92, 18), 96 << 20, 42 << 30,
    )
    d_norm_came, gate_up_came, qkv_came, out_came, down_came, gain_qk = exchange(
        backward_kernel, 1,
        [
            (all_branch, False), (all_wq, False), (all_wo, False), (all_tok, False),
            (gate_up_in, False), (down_part, False), (projected, True), (queries, True),
            (keys_values, True), (attended, True), (cosines, True), (sines, True), (first, True),
            (gain_heads, True),
        ],
        [
            ((4, 2, 64, D), half, False), ((64, 2 * FF), half, False), ((8, 64, 384), half, False),
            ((4, 64, D), half, False), ((4, 256, D), half, False), ((1, 128), full, True),
        ],
        [
            near(8, 2, 64, D), near(8, 4, 64, 384), near(4, 64, D), near(8, 2, 64, D),
            near(2, 3, 512, 1024), near(8, 2, 64, 256), near(2, 2, 512, 128, kind=full),
            near(2, 4, 512, 128, kind=full), near(8, 2, 64, 384), near(8, 4, 64, 384),
            near(4, 64, D), near(8, 2, 64, D), near(4, 2, 64, D), near(2, 4, 64, 2048),
            near(4, 8, 64, 384), near(8, 64, 384),
        ],
        (34, 12), 64 << 20, 6 << 30,
    )
    row_states = jnp.concatenate([qkv_rows, out_rows, gate_up_rows, down_rows])[:, None]
    masters = (qkv_master, out_master, gate_up_master, down_master)
    grad_tokens, *grads, rows_new, packed = pl.pallas_call(
        statistics_kernel,
        out_shape=[
            jax.ShapeDtypeStruct((128, D), half),
            *[jax.ShapeDtypeStruct((count, width), full) for count, width, _, _ in MATRICES],
            jax.ShapeDtypeStruct((448, 1), full),
            jax.ShapeDtypeStruct((512, 128), full),
        ],
        scratch_shapes=[
            pltpu.VMEM((1, D), full), pltpu.VMEM((2, 256, 128), full), pltpu.VMEM((256, 128), full),
        ],
        compiler_params=pltpu.CompilerParams(vmem_limit_bytes=VMEM_BYTES),
    )(
        d_norm_came.reshape(4, 128, D), tokens.reshape(128, D), d_hidden_in.reshape(128, D), gain_attn,
        grad_gain_ffn, gain_qk,
        qkv_came, out_came, gate_up_came, down_came, row_states, *masters,
    )
    shape = (8, 4, 16, 128)
    cols_new, col_factors, moments_new, gains_new, grad_gains, spreads = exchange(
        total_kernel, 2,
        [
            (packed.reshape(shape), True), (col_moments.reshape(-1, 128), True),
            (gain_moments.reshape(-1, 128), True), (gains.reshape(-1, 128), True),
        ],
        [
            ((COL_ROWS, 128), full, True), ((COL_ROWS, 128), full, True),
            ((GAIN_ROWS, 128), full, True), ((GAIN_ROWS, 128), full, True),
            ((GAIN_ROWS, 128), full, True), ((1, 128), full, True),
        ],
        [
            pltpu.VMEM(shape, full), pltpu.VMEM(shape, full), pltpu.VMEM(shape[1:], full),
            pltpu.VMEM(shape[1:], full), pltpu.VMEM(shape[2:], full), pltpu.VMEM(shape[1:], full),
        ],
        (20, 0), 1 << 20,
    )
    col_factors = col_factors.reshape(-1)
    row_factors = lax.rsqrt(rows_new[:, 0])
    new_masters = []
    for slot, (count, width, row_at, col_at) in enumerate(MATRICES):
        row_factor = row_factors[row_at : row_at + count]
        col_factor = col_factors[col_at * 128 : col_at * 128 + width]
        new_masters.append(
            masters[slot] - grads[slot] * row_factor[:, None] * col_factor[None, :]
        )
    return (
        output,
        grad_tokens.reshape(2, 64, D),
        *grads,
        grad_gains.reshape(-1),
        *[rows_new[row_at : row_at + count, 0] for count, _, row_at, _ in MATRICES],
        cols_new.reshape(-1),
        moments_new.reshape(-1),
        *new_masters,
        *[master.astype(half) for master in new_masters],
        gains_new.reshape(-1),
        spreads[0, :8],
    )


def optimizer_step(
    grads, gain_local, masters, gains, row_states, col_moments, gain_moments, total_fn
):
    beta = 1.0 - STEP ** (-0.8)
    col_widths = (QKV, D, 2 * FF, D)
    row_totals = (D, HEADS * HEAD_DIM, D, FF)
    squares = [gradient * gradient + SQUARE_EPSILON for gradient in grads]
    rows_new = [
        beta * row_state + (1.0 - beta) * jnp.mean(square, axis=1)
        for row_state, square in zip(row_states, squares)
    ]
    col_local = [jnp.sum(square, axis=0) for square in squares]
    weighted_local = [
        jnp.sum(gradient * gradient / row_new[:, None], axis=0)
        for gradient, row_new in zip(grads, rows_new)
    ]
    stats_local = jnp.stack(
        [jnp.sum(row_new) for row_new in rows_new]
        + [jnp.sum(master * master) for master in masters]
    )
    totals = total_fn(jnp.concatenate(col_local + weighted_local + [stats_local, gain_local]))
    cols = sum(col_widths)
    col_sums, weighted = totals[:cols], totals[cols : 2 * cols]
    stats, grad_gains = totals[2 * cols : 2 * cols + 8], totals[2 * cols + 8 :]
    col_divisor = jnp.concatenate(
        [
            jnp.full((col_width,), float(row_total), jnp.float32)
            for col_width, row_total in zip(col_widths, row_totals)
        ]
    )
    cols_new = beta * col_moments + (1.0 - beta) * col_sums / col_divisor
    new_masters = []
    spreads = []
    begin_at = 0
    for slot in range(4):
        col_part = cols_new[begin_at : begin_at + col_widths[slot]]
        weighted_part = weighted[begin_at : begin_at + col_widths[slot]]
        begin_at = begin_at + col_widths[slot]
        mean_rows = stats[slot] / row_totals[slot]
        unit = (
            grads[slot]
            * lax.rsqrt(rows_new[slot] / mean_rows)[:, None]
            * lax.rsqrt(col_part)[None, :]
        )
        entries_all = float(row_totals[slot] * col_widths[slot])
        spread = jnp.sqrt(mean_rows * jnp.sum(weighted_part / col_part) / entries_all)
        scale = STEP_RATE * jnp.maximum(SCALE_EPSILON, jnp.sqrt(stats[4 + slot] / entries_all))
        new_masters.append(masters[slot] - scale * unit / jnp.maximum(1.0, spread / CLIP_LEVEL))
        spreads.append(spread)
    bounds = (0, D, 2 * D, 2 * D + HEAD_DIM, 2 * D + 2 * HEAD_DIM)
    moment_parts, gain_parts = ([], [])
    for segment in range(4):
        gradient = grad_gains[bounds[segment] : bounds[segment + 1]]
        gain_old = gains[bounds[segment] : bounds[segment + 1]]
        moment_new = beta * gain_moments[bounds[segment] : bounds[segment + 1]] + (1.0 - beta) * (
            gradient * gradient + SQUARE_EPSILON
        )
        unit = gradient * lax.rsqrt(moment_new)
        spread = jnp.sqrt(jnp.mean(unit * unit))
        scale = STEP_RATE * jnp.maximum(SCALE_EPSILON, jnp.sqrt(jnp.mean(gain_old * gain_old)))
        moment_parts.append(moment_new)
        gain_parts.append(gain_old - scale * unit / jnp.maximum(1.0, spread / CLIP_LEVEL))
        spreads.append(spread)
    return (
        grad_gains,
        *rows_new,
        cols_new,
        jnp.concatenate(moment_parts),
        *new_masters,
        *[master.astype(jnp.bfloat16) for master in new_masters],
        jnp.concatenate(gain_parts),
        jnp.stack(spreads),
    )


def solution(mesh):
    split = mesh.shape["seq"] == 8 and mesh.shape["rows"] == 4
    return jax.shard_map(
        split_local if split else gathered_local,
        mesh=mesh,
        in_specs=(
            P("rows", "seq", None),
            P("rows", None),
            P("rows", "seq", None),
            P(("seq", "rows"), None),
            P(("seq", "rows"), None),
            P(("seq", "rows"), None),
            P(("seq", "rows"), None),
            P(),
            P(("seq", "rows")),
            P(("seq", "rows")),
            P(("seq", "rows")),
            P(("seq", "rows")),
            P(),
            P(),
        ),
        out_specs=(
            P("rows", "seq", None),
            P("rows", "seq", None),
            P(("seq", "rows"), None),
            P(("seq", "rows"), None),
            P(("seq", "rows"), None),
            P(("seq", "rows"), None),
            P(),
            P(("seq", "rows")),
            P(("seq", "rows")),
            P(("seq", "rows")),
            P(("seq", "rows")),
            P(),
            P(),
            P(("seq", "rows"), None),
            P(("seq", "rows"), None),
            P(("seq", "rows"), None),
            P(("seq", "rows"), None),
            P(("seq", "rows"), None),
            P(("seq", "rows"), None),
            P(("seq", "rows"), None),
            P(("seq", "rows"), None),
            P(),
            P(),
        ),
        check_vma=False,
    )
```

```python
from functools import partial

import jax
import jax.numpy as jnp
from jax import lax
from jax.experimental import pallas as pl
from jax.experimental.pallas import tpu as pltpu
from jax.sharding import PartitionSpec as P

D = 2048
HEADS = 32
KV_HEADS = 8
HEAD_DIM = 64
FF = 8192
STEP = 10
QKV = 3072


EPSILON = 1e-06
ROPE_BASE = 10000.0
MASKED_SCORE = -1e30
STEP_RATE = 0.3
CLIP_LEVEL = 1.0
SQUARE_EPSILON = 1e-30
SCALE_EPSILON = 0.001


def from_behind(value, axis, steps):
    count = lax.axis_size(axis)
    pairs = [(source, (source + steps) % count) for source in range(count)]
    return lax.ppermute(value, axis, pairs)


def norm_rows(entries, gain):
    return entries * lax.rsqrt(jnp.mean(entries * entries, axis=-1, keepdims=True) + EPSILON) * gain


def turn(entries, cos_wide, sin_wide):
    half_width = entries.shape[-1] // 2
    turned = jnp.concatenate([-entries[..., half_width:], entries[..., :half_width]], axis=-1)
    return entries * cos_wide + turned * sin_wide


def doc_tables(doc_starts, places):
    before = doc_starts[:, None, :] <= places[None, :, None]
    doc_ids = jnp.sum(before.astype(jnp.int32), axis=-1)
    doc_first = jnp.max(jnp.where(before, doc_starts[:, None, :], 0), axis=-1)
    return (doc_ids, places[None, :] - doc_first)


def rotary(offsets):
    frequency = ROPE_BASE ** (-(jnp.arange(HEAD_DIM // 2, dtype=jnp.float32) * 2.0 / HEAD_DIM))
    angles = offsets.astype(jnp.float32)[..., None] * frequency
    cos_table = jnp.concatenate([jnp.cos(angles), jnp.cos(angles)], axis=-1)
    sin_table = jnp.concatenate([jnp.sin(angles), jnp.sin(angles)], axis=-1)
    return (cos_table, sin_table)


def queries_keys(
    cos_table, sin_table, projected, gain_query, gain_key, heads=HEADS, kv_heads=KV_HEADS
):
    rows_here, seq_here = (projected.shape[0], projected.shape[1])
    att_width = heads * HEAD_DIM
    queries = projected[..., :att_width].reshape(rows_here, seq_here, heads, HEAD_DIM)
    keys_rot = projected[..., att_width : att_width + kv_heads * HEAD_DIM].reshape(
        rows_here, seq_here, kv_heads, HEAD_DIM
    )
    cos_wide = cos_table[:, :, None, :]
    sin_wide = sin_table[:, :, None, :]
    queries = turn(norm_rows(queries, gain_query), cos_wide, sin_wide) * HEAD_DIM ** (-0.5)
    keys_rot = turn(norm_rows(keys_rot, gain_key), cos_wide, sin_wide)
    return (queries, keys_rot)


def mask_of(query_docs, query_places, key_docs, key_places):
    same_doc = query_docs[:, :, None] == key_docs[:, None, :]
    causal = query_places[None, :, None] >= key_places[None, None, :]
    return (same_doc & causal)[:, None, None, :, :]


def gathered_local(
    tokens,
    doc_starts,
    grad_out,
    qkv_master,
    out_master,
    gate_up_master,
    down_master,
    gains,
    qkv_rows,
    out_rows,
    gate_up_rows,
    down_rows,
    col_moments,
    gain_moments,
):
    cycle_size = lax.axis_size("seq")
    seq_index = lax.axis_index("seq")
    rows_dev, seq_dev = (tokens.shape[0], tokens.shape[1])
    group_size = HEADS // KV_HEADS
    att_width = HEADS * HEAD_DIM
    kv_width = KV_HEADS * HEAD_DIM
    gain_attn = gains[:D]
    gain_ffn = gains[D : 2 * D]
    gain_query = gains[2 * D : 2 * D + HEAD_DIM]
    gain_key = gains[2 * D + HEAD_DIM :]
    local_places = jnp.arange(seq_dev, dtype=jnp.int32)
    places = seq_index * seq_dev + local_places
    query_docs, offsets = doc_tables(doc_starts, places)
    cos_table, sin_table = rotary(offsets)
    copies = (
        qkv_master.astype(jnp.bfloat16),
        out_master.astype(jnp.bfloat16),
        gate_up_master.astype(jnp.bfloat16),
        down_master.astype(jnp.bfloat16),
    )
    w_qkv, w_out, w_gate_up, w_down = (
        lax.all_gather(copies[0], ("seq", "rows"), axis=0, tiled=True),
        lax.all_gather(copies[1], ("seq", "rows"), axis=0, tiled=True),
        lax.all_gather(copies[2], ("seq", "rows"), axis=0, tiled=True),
        lax.all_gather(copies[3], ("seq", "rows"), axis=0, tiled=True),
    )
    tokens_wide = tokens.astype(jnp.float32)
    normed = norm_rows(tokens_wide, gain_attn).astype(jnp.bfloat16)
    projected = jnp.einsum("rtd,de->rte", normed, w_qkv, preferred_element_type=jnp.float32)
    head_fn = partial(queries_keys, cos_table, sin_table)
    queries, keys_rot = head_fn(projected, gain_query, gain_key)
    query16 = queries.astype(jnp.bfloat16).reshape(
        rows_dev, seq_dev, KV_HEADS, group_size, HEAD_DIM
    )
    keys16 = keys_rot.astype(jnp.bfloat16).reshape(rows_dev, seq_dev, kv_width)
    values16 = projected[..., att_width + kv_width :].astype(jnp.bfloat16)
    stat_shape = (rows_dev, KV_HEADS, group_size, seq_dev)
    initial = (
        jnp.full(stat_shape, MASKED_SCORE, jnp.float32),
        jnp.zeros(stat_shape, jnp.float32),
        jnp.zeros(stat_shape + (HEAD_DIM,), jnp.float32),
    )
    carry = initial
    key_piece = lax.all_gather(keys16, "seq", axis=1, tiled=True)
    value_piece = lax.all_gather(values16, "seq", axis=1, tiled=True)
    key_count = key_piece.shape[1]

    def absorb_block(state, block_index):
        best, total, summed = state
        block_begin = block_index * seq_dev
        key_block = lax.dynamic_slice_in_dim(key_piece, block_begin, seq_dev, 1).reshape(
            rows_dev, seq_dev, KV_HEADS, HEAD_DIM
        )
        value_block = lax.dynamic_slice_in_dim(value_piece, block_begin, seq_dev, 1).reshape(
            rows_dev, seq_dev, KV_HEADS, HEAD_DIM
        )
        key_places = block_begin + jnp.arange(seq_dev, dtype=jnp.int32)
        key_docs, _ = doc_tables(doc_starts, key_places)
        allowed = mask_of(query_docs, places, key_docs, key_places)
        scores = jnp.einsum(
            "rqkgh,rtkh->rkgqt", query16, key_block, preferred_element_type=jnp.float32
        )
        scores = jnp.where(allowed, scores, MASKED_SCORE)
        best_new = jnp.maximum(best, jnp.max(scores, axis=-1))
        weights = jnp.where(allowed, jnp.exp(scores - best_new[..., None]), 0.0)
        factor = jnp.exp(best - best_new)
        total = total * factor + jnp.sum(weights, axis=-1)
        summed = summed * factor[..., None] + jnp.einsum(
            "rkgqt,rtkh->rkgqh",
            weights.astype(jnp.bfloat16),
            value_block,
            preferred_element_type=jnp.float32,
        )
        return ((best_new, total, summed), None)

    carry, _ = lax.scan(absorb_block, carry, jnp.arange(key_count // seq_dev, dtype=jnp.int32))
    best, total, summed = carry
    log_total = best + jnp.log(total)
    attended = summed / total[..., None]
    attended16 = (
        attended.transpose(0, 3, 1, 2, 4).reshape(rows_dev, seq_dev, att_width).astype(jnp.bfloat16)
    )
    branch = jnp.einsum("rtc,cd->rtd", attended16, w_out, preferred_element_type=jnp.float32)
    hidden_in = tokens_wide + branch
    normed2 = norm_rows(hidden_in, gain_ffn).astype(jnp.bfloat16)
    gate_up = jnp.einsum("rtd,df->rtf", normed2, w_gate_up, preferred_element_type=jnp.float32)
    gate_part, up_part = (gate_up[..., :FF], gate_up[..., FF:])
    hidden = (jax.nn.silu(gate_part) * up_part).astype(jnp.bfloat16)
    output = hidden_in + jnp.einsum(
        "rtf,fd->rtd", hidden, w_down, preferred_element_type=jnp.float32
    )
    d_hidden = jnp.einsum("rtd,fd->rtf", grad_out, w_down, preferred_element_type=jnp.float32)
    silu_value, silu_back = jax.vjp(jax.nn.silu, gate_part)
    d_gate = silu_back(d_hidden * up_part)[0]
    d_gate_up = jnp.concatenate([d_gate, d_hidden * silu_value], axis=-1).astype(jnp.bfloat16)
    d_normed2 = jnp.einsum("rtf,df->rtd", d_gate_up, w_gate_up, preferred_element_type=jnp.float32)
    _, ffn_norm_back = jax.vjp(norm_rows, hidden_in, gain_ffn)
    d_inner, grad_gain_ffn = ffn_norm_back(d_normed2)
    d_hidden_in = grad_out.astype(jnp.float32) + d_inner
    term_down = jnp.einsum("rtf,rtd->fd", hidden, grad_out, preferred_element_type=jnp.float32)
    grad_down = lax.psum_scatter(term_down, ("seq", "rows"), scatter_dimension=0, tiled=True)
    term_gate_up = jnp.einsum("rtd,rtf->df", normed2, d_gate_up, preferred_element_type=jnp.float32)
    grad_gate_up = lax.psum_scatter(term_gate_up, ("seq", "rows"), scatter_dimension=0, tiled=True)
    d_branch = d_hidden_in.astype(jnp.bfloat16)
    term_out = jnp.einsum("rtc,rtd->cd", attended16, d_branch, preferred_element_type=jnp.float32)
    d_attended = jnp.einsum(
        "rtd,cd->rtc", d_branch, w_out, preferred_element_type=jnp.float32
    ).astype(jnp.bfloat16)
    d_heads = d_attended.reshape(rows_dev, seq_dev, KV_HEADS, group_size, HEAD_DIM).transpose(
        0, 2, 3, 1, 4
    )
    delta = jnp.sum(d_heads.astype(jnp.float32) * attended, axis=-1)

    def cycle_turn(turn_index, carry):
        pair16, grad_pair, d_queries = carry
        source = (seq_index + turn_index) % cycle_size
        key_places = source * seq_dev + local_places
        key_docs, _ = doc_tables(doc_starts, key_places)
        allowed = mask_of(query_docs, places, key_docs, key_places)
        key_block = pair16[0].reshape(rows_dev, seq_dev, KV_HEADS, HEAD_DIM)
        value_block = pair16[1].reshape(rows_dev, seq_dev, KV_HEADS, HEAD_DIM)
        scores = jnp.einsum(
            "rqkgh,rtkh->rkgqt", query16, key_block, preferred_element_type=jnp.float32
        )
        scores = jnp.where(allowed, scores, MASKED_SCORE)
        probs = jnp.where(allowed, jnp.exp(scores - log_total[..., None]), 0.0)
        d_values = jnp.einsum(
            "rkgqt,rkgqh->rtkh",
            probs.astype(jnp.bfloat16),
            d_heads,
            preferred_element_type=jnp.float32,
        )
        d_probs = jnp.einsum(
            "rkgqh,rtkh->rkgqt", d_heads, value_block, preferred_element_type=jnp.float32
        )
        d_scores = (probs * (d_probs - delta[..., None])).astype(jnp.bfloat16)
        d_queries = d_queries + jnp.einsum(
            "rkgqt,rtkh->rkgqh", d_scores, key_block, preferred_element_type=jnp.float32
        )
        d_keys = jnp.einsum(
            "rkgqt,rqkgh->rtkh", d_scores, query16, preferred_element_type=jnp.float32
        )
        grad_pair = grad_pair + jnp.stack(
            [
                d_keys.reshape(rows_dev, seq_dev, kv_width),
                d_values.reshape(rows_dev, seq_dev, kv_width),
            ]
        )
        grad_pair = from_behind(grad_pair.astype(jnp.bfloat16), "seq", -1).astype(grad_pair.dtype)
        pair16 = from_behind(pair16, "seq", -1)
        return (pair16, grad_pair, d_queries)

    start_pair = jnp.stack([keys16, values16])
    start_grads = jnp.zeros((2, rows_dev, seq_dev, kv_width), jnp.float32)
    start_queries = jnp.zeros(stat_shape + (HEAD_DIM,), jnp.float32)
    _, grad_pair, d_queries = lax.fori_loop(
        0, cycle_size, cycle_turn, (start_pair, start_grads, start_queries)
    )
    d_queries = d_queries.transpose(0, 3, 1, 2, 4).reshape(rows_dev, seq_dev, HEADS, HEAD_DIM)
    d_keys_home = grad_pair[0].reshape(rows_dev, seq_dev, KV_HEADS, HEAD_DIM)
    _, heads_back = jax.vjp(head_fn, projected, gain_query, gain_key)
    d_projected, grad_gain_query, grad_gain_key = heads_back((d_queries, d_keys_home))
    d_projected = jnp.concatenate(
        [d_projected[..., : att_width + kv_width], grad_pair[1]], axis=-1
    ).astype(jnp.bfloat16)
    term_qkv = jnp.einsum("rtd,rte->de", normed, d_projected, preferred_element_type=jnp.float32)
    d_normed = jnp.einsum("rte,de->rtd", d_projected, w_qkv, preferred_element_type=jnp.float32)
    _, attn_norm_back = jax.vjp(norm_rows, tokens_wide, gain_attn)
    d_tokens_part, grad_gain_attn = attn_norm_back(d_normed)
    grad_tokens = (d_hidden_in + d_tokens_part).astype(jnp.bfloat16)
    grad_qkv, grad_out_proj = (
        lax.psum_scatter(term_qkv, ("seq", "rows"), scatter_dimension=0, tiled=True),
        lax.psum_scatter(term_out, ("seq", "rows"), scatter_dimension=0, tiled=True),
    )
    gain_local = jnp.concatenate([grad_gain_attn, grad_gain_ffn, grad_gain_query, grad_gain_key])
    grads = (grad_qkv, grad_out_proj, grad_gate_up, grad_down)
    updated = optimizer_step(
        grads, gain_local, (qkv_master, out_master, gate_up_master, down_master), gains,
        (qkv_rows, out_rows, gate_up_rows, down_rows), col_moments, gain_moments,
        lambda vector: lax.psum(vector, ("seq", "rows")),
    )
    return (output.astype(jnp.bfloat16), grad_tokens, *grads, *updated)


MESH = pl.DeviceIdType.MESH
PLACES = 32
VMEM_BYTES = 61 * 1024 * 1024
CHUNK = 16


def here():
    seq = lax.axis_index("seq")
    return lax.div(seq, 2), lax.rem(seq, 2), lax.axis_index("rows")


def flips(chip):
    return (chip + 1 - 2 * lax.rem(chip, 2), lax.rem(chip + 2, 4), 3 - chip)


def ahead(z, step):
    return lax.rem(z + step, 4)


def at_place(chip, core, z):
    return (2 * chip + core, z)


def greet(peers):
    barrier = pltpu.get_barrier_semaphore()
    for peer in peers:
        pl.semaphore_signal(barrier, inc=1, device_id=peer, device_id_type=MESH)
    pl.semaphore_wait(barrier, len(peers))


class Mover:
    def __init__(self, send_sem, recv_sem, local_sem):
        self.send_sem, self.recv_sem, self.local_sem = send_sem, recv_sem, local_sem
        self.remote, self.own, self.lines, self.scattered = [], [], [], []
        self.used = 0

    def copy_of(self, src, dst, peer, send_slot, recv_slot):
        return pltpu.make_async_remote_copy(
            src_ref=src,
            dst_ref=dst,
            send_sem=self.send_sem.at[send_slot],
            recv_sem=self.recv_sem.at[recv_slot],
            device_id=peer,
            device_id_type=MESH,
        )

    def send_parts(self, pairs, whole, peer):
        slot = self.used
        self.used += 1
        for src, dst in pairs:
            self.copy_of(src, dst, peer, slot, slot).start()
        copy = self.copy_of(whole[0], whole[1], peer, slot, slot)
        handle = [copy, False, copy.wait_recv, False]
        self.remote.append(handle)
        return handle

    def send(self, src, dst, peer):
        return self.send_parts([(src, dst)], (src, dst), peer)

    def keep_parts(self, pairs, whole):
        sem = self.local_sem.at[len(self.own)]
        for src, dst in pairs:
            pltpu.make_async_copy(src, dst, sem).start()
        copy = pltpu.make_async_copy(whole[0], whole[1], sem)
        handle = [copy, False, copy.wait]
        self.own.append(handle)
        return handle

    def keep(self, src, dst):
        return self.keep_parts([(src, dst)], (src, dst))

    def line(self, source, block_of, chip, core, z):
        line = (self.used, block_of, chip, core, z)
        self.used += 5
        base = line[0]
        up, low = at_place(chip, core, z + 1), at_place(chip, core, z - 1)
        rising = self.copy_of(source, block_of(z), up, base, base + 3)
        falling = self.copy_of(source, block_of(z), low, base + 4, base + 1)
        pl.when(z < 3)(rising.start)
        pl.when(z > 0)(falling.start)
        self.lines += [(z < 3, rising), (z > 0, falling)]
        return line

    def wait_line(self, line, step, when=None):
        base, block_of, chip, core, z = line
        block = block_of(ahead(z, step))
        peer = at_place(chip, core, ahead(z, step))
        copy = self.copy_of(block, block, peer, base + step, base + step)
        if when is None:
            copy.wait_recv()
        else:
            pl.when(when)(copy.wait_recv)
        return block

    def arrive_line(self, line, step, when=None):
        base, _, chip, core, z = line
        block = self.wait_line(line, step, when)
        rises, falls = (z + step >= 4) & (z < 3), (z + step < 4) & (z > 0)
        up, low = at_place(chip, core, z + 1), at_place(chip, core, z - 1)
        rising = self.copy_of(block, block, up, base + step, base + step - 1)
        falling = self.copy_of(block, block, low, base + step, base + step + 1)
        for moves, copy in ((rises, rising), (falls, falling)):
            moves = moves if when is None else moves & when
            pl.when(moves)(copy.start)
            self.lines.append((moves, copy))
        return block

    def scatter(self, source, target, steps, chip, core, z):
        base = self.used
        self.used += 3

        def start(index):
            at = ahead(z, steps[index])
            copy = self.copy_of(
                source(at), target(z), at_place(chip, core, at), base + index, base + 3 - steps[index]
            )
            copy.start()
            self.scattered.append(copy)

        def wait():
            for step in (1, 2, 3):
                at = ahead(z, step)
                peer = at_place(chip, core, at)
                self.copy_of(source(at), target(at), peer, base, base + step - 1).wait_recv()

        return start, wait

    def arrive(self, *handles):
        for handle in handles:
            if not handle[1]:
                handle[1] = True
                handle[2]()

    def sent(self, *handles):
        for handle in handles:
            if not handle[3]:
                handle[3] = True
                handle[0].wait_send()

    def sent_lines(self):
        for when, copy in self.lines:
            pl.when(when)(copy.wait_send)
        self.lines = []

    def sent_sums(self):
        for copy in self.scattered:
            copy.wait_send()
        self.scattered = []

    def finish(self):
        self.arrive(*self.own, *self.remote)
        self.sent(*self.remote)
        self.sent_lines()
        self.sent_sums()


def semaphores(remote, own):
    return [
        pltpu.SemaphoreType.DMA((remote,)),
        pltpu.SemaphoreType.DMA((remote,)),
        pltpu.SemaphoreType.DMA((max(own, 1),)),
    ]


def exchange(kernel, ident, inputs, outputs, scratch, copies, moved, flops=0):
    vmem, anywhere = pl.BlockSpec(memory_space=pltpu.VMEM), pl.BlockSpec(memory_space=pl.ANY)
    return pl.pallas_call(
        kernel,
        out_shape=[jax.ShapeDtypeStruct(shape, kind) for shape, kind, _ in outputs],
        in_specs=[vmem if near else anywhere for _, near in inputs],
        out_specs=[vmem if near else anywhere for _, _, near in outputs],
        scratch_shapes=scratch + semaphores(*copies),
        compiler_params=pltpu.CompilerParams(
            collective_id=ident, has_side_effects=True, vmem_limit_bytes=VMEM_BYTES
        ),
        cost_estimate=pl.CostEstimate(flops=flops, bytes_accessed=moved, transcendentals=0),
    )(*[array for array, _ in inputs])


def chunks(length, body):
    @pl.loop(0, length // CHUNK)
    def _(step):
        body(pl.ds(pl.multiple_of(step * CHUNK, CHUNK), CHUNK))


def segments(core, z):
    for part in range(2):
        for chip in range(4):
            start = part * FF + ((2 * chip + core) * 4 + z) * 256
            yield pl.ds(pl.multiple_of(start, 256), 256), pl.ds(part * 1024 + chip * 256, 256)


def add_blocks(first, second, result):
    for row in range(2):

        def body(part):
            total = first[row, part].astype(jnp.float32) + second[row, part].astype(jnp.float32)
            result[row, part] = total.astype(result.dtype)

        chunks(64, body)


def head_tables(doc_starts, length):
    places = jnp.arange(length, dtype=jnp.int32)
    _, offsets = doc_tables(doc_starts, places)
    cos_table, sin_table = rotary(offsets)
    signs = jnp.where(jnp.arange(HEAD_DIM) < HEAD_DIM // 2, -1.0, 1.0)
    tables = []
    for table in (cos_table, sin_table * signs):
        wide = jnp.concatenate([table, table], axis=-1)
        tables.append(wide.reshape(2, 8, 64, 128).transpose(1, 0, 2, 3))
    return (*tables, (places[None, :] - offsets)[..., None])


def lower_half(shape):
    return lax.broadcasted_iota(jnp.int32, shape, len(shape) - 1) < 64


def swap_halves(entries):
    lane = lax.broadcasted_iota(jnp.int32, entries.shape, 1)
    return jnp.where(lax.rem(lane, 64) < 32, pltpu.roll(entries, 96, 1), pltpu.roll(entries, 32, 1))


def head_means(entries):
    lower = lower_half(entries.shape)
    low = jnp.sum(jnp.where(lower, entries, 0.0), axis=-1, keepdims=True)
    high = jnp.sum(jnp.where(lower, 0.0, entries), axis=-1, keepdims=True)
    return jnp.where(lower, low, high) * (1.0 / HEAD_DIM)


def wide(start, size):
    return pl.ds(pl.multiple_of(start, size), size)


def plain(left, right):
    return jnp.dot(left, right, preferred_element_type=jnp.float32)


def across(left, right):
    return lax.dot_general(
        left, right, (((1,), (1,)), ((), ())), preferred_element_type=jnp.float32
    )


def down(left, right):
    return lax.dot_general(
        left, right, (((0,), (0,)), ((), ())), preferred_element_type=jnp.float32
    )


def attention_probs(queries, keys, first, part):
    scores = across(queries, keys)
    place = lax.broadcasted_iota(jnp.int32, scores.shape, 1)
    query = lax.broadcasted_iota(jnp.int32, scores.shape, 0) + part * 128
    allowed = (place >= first) & (place <= query)
    scores = jnp.where(allowed, scores, MASKED_SCORE)
    best = jnp.max(scores, axis=-1, keepdims=True)
    weights = jnp.where(allowed, jnp.exp(scores - best), 0.0)
    return weights / jnp.sum(weights, axis=-1, keepdims=True)


def layer_kernel(
    tok, gain_attn, gain_ffn, gain_heads, cosines, sines, first, qkv_master, wo, wd_own, wg, grad_out,
    d_hidden_in, out_sum, gain_part, gain_qk,
    d_norm_came, gate_up_came, qkv_came, out_came, down_came, gate_up_in, gate_up_mid, kept_tok,
    projected, queries, keys_values, attended,
    wq_send, normed, all_tok, all_wq, all_wo, partial, from_partner, came,
    hidden_in, all_norm, all_out, all_wg, wd, hidden, d_gate_up, d_branch,
    d_queries, d_keys_values, qkv_in, credit, *sems,
):
    half, full = jnp.bfloat16, jnp.float32
    chip, core, z = here()
    others = flips(chip)
    other = 1 - core
    me = 2 * chip + core
    partner = at_place(chip, other, z)
    plane = [at_place(peer_chip, core, z) for peer_chip in others]
    plane_cross = [at_place(peer_chip, other, z) for peer_chip in others]
    steps = (2, 1, 3)
    line = [at_place(chip, core, ahead(z, step)) for step in steps]
    cross = [at_place(chip, other, ahead(z, step)) for step in steps]
    everyone = [partner] + plane + plane_cross
    greet(everyone + line + cross)
    move = Mover(*sems)

    for head in range(8):
        wq_send[head, :, pl.ds(0, 256)] = qkv_master[:, pl.ds(head * 256, 256)].astype(half)
    low = lower_half((64, 128))
    for pair in range(4):
        keys = qkv_master[:, pl.ds(2048 + pair * 128, 128)]
        values = qkv_master[:, pl.ds(2560 + pair * 128, 128)]
        tail = pl.ds(256, 128)
        wq_send[2 * pair, :, tail] = jnp.where(low, keys, pltpu.roll(values, 64, 1)).astype(half)
        wq_send[2 * pair + 1, :, tail] = jnp.where(low, pltpu.roll(keys, 64, 1), values).astype(half)
    heads = [move.keep(wq_send.at[me], all_wq.at[me, z])]
    for peer in everyone:
        heads.append(move.send(wq_send.at[peer[0]], all_wq.at[me, z], peer))

    for row in range(2):

        def body0(part):
            total = tok[row, part].astype(full)
            scale = lax.rsqrt(jnp.mean(total * total, axis=-1, keepdims=True) + EPSILON)
            normed[row, part] = (total * scale * gain_attn[...]).astype(half)

        chunks(64, body0)
    token_copies = [move.send(normed, all_tok.at[me], peer) for peer in plane]
    token_copies.append(move.send(normed, all_tok.at[me], partner))
    tokens_here = move.keep(normed, all_tok.at[me])
    move.arrive(*heads)
    hops = (3, 1, 2)
    line_wq = move.line(all_wq.at[:, z], lambda at: all_wq.at[:, at], chip, core, z)
    weights = [move.send(wo, all_wo.at[z], peer) for peer in line]
    weights.append(move.keep(wo, all_wo.at[z]))

    def turn_block(to_core, to_z):
        whole = all_wg.at[chip, core, z]
        pairs = [(wg.at[:, src], whole.at[:, dst]) for src, dst in segments(to_core, to_z)]
        return pairs, (whole, whole)

    own = [
        move.keep(wd_own, wd.at[chip]),
        move.keep(grad_out, all_out.at[z, core]),
        move.send(grad_out, all_out.at[z, core], partner),
    ]
    own += [move.send(wd_own, wd.at[chip], peer) for peer in plane]
    for peer_chip, handle in zip(others, tuple(token_copies)):
        move.arrive(handle)
        block = all_tok.at[2 * peer_chip + core]
        token_copies.append(move.send(block, block, partner))
    for step in hops:
        move.arrive_line(line_wq, step)
    turned = []
    for step, peer, peer_cross in zip(steps, line, cross):
        to = ahead(z, step)
        turned.append(move.send_parts(*turn_block(core, to), peer))
        turned.append(move.send_parts(*turn_block(other, to), peer_cross))
    turned += [move.keep_parts(*turn_block(core, z)), move.send_parts(*turn_block(other, z), partner)]
    line_grads = move.line(grad_out, lambda at: all_out.at[at, core], chip, core, z)
    move.arrive(tokens_here, *token_copies, *weights)
    saved = [move.keep(all_tok, kept_tok)]

    flat_tok, flat_wq = all_tok.reshape(1024, D), all_wq.reshape(D, 384)
    flat_wo = all_wo.reshape(256, D)

    @pl.loop(0, 4)
    def _(step):
        block = plain(flat_tok[wide(step * 256, 256)], flat_wq[...])
        projected[wide(step * 2, 2)] = block.reshape(2, 2, 64, 384)

    @pl.loop(0, 8)
    def _(block):
        for row in range(2):
            cosine, sine = cosines[block, row], sines[block, row]
            places = wide(block * 64, 64)
            for tile in range(3):
                entries = projected[block, row, :, pl.ds(tile * 128, 128)]
                gain = gain_heads[min(tile, 2) // 2 : min(tile, 2) // 2 + 1]
                scale = lax.rsqrt(head_means(entries * entries) + EPSILON)
                turned_entries = entries * scale * gain
                turned_entries = turned_entries * cosine + swap_halves(turned_entries) * sine
                if tile < 2:
                    queries[row, tile, places] = (turned_entries * HEAD_DIM ** (-0.5)).astype(half)
                else:
                    zero = jnp.zeros_like(entries)
                    rolled = pltpu.roll(turned_entries, 64, 1)
                    values = pltpu.roll(entries, 64, 1)
                    keys_values[row, 0, places] = jnp.where(low, turned_entries, zero).astype(half)
                    keys_values[row, 1, places] = jnp.where(low, zero, rolled).astype(half)
                    keys_values[row, 2, places] = jnp.where(low, values, zero).astype(half)
                    keys_values[row, 3, places] = jnp.where(low, zero, entries).astype(half)

    @pl.loop(0, 2)
    def _(row):
        for tile in range(2):
            for part in range(4):
                own_places, upto = pl.ds(part * 128, 128), pl.ds(0, (part + 1) * 128)
                total = jnp.zeros((128, 128), full)
                for side in range(2):
                    probs = attention_probs(
                        queries[row, tile, own_places], keys_values[row, side, upto],
                        first[row, own_places], part,
                    )
                    total += plain(probs.astype(half), keys_values[row, 2 + side, upto])
                attended[pl.ds(2 * part, 2), row, :, pl.ds(tile * 128, 128)] = total.reshape(2, 64, 128)

    flat_attended = attended.reshape(1024, 256)

    @pl.loop(0, 4)
    def _(step):
        rows = flat_attended[wide(step * 256, 256)].astype(half)

        @pl.loop(0, 4)
        def _(col):
            cols = wide(col * 512, 512)
            block = plain(rows, flat_wo[:, cols])
            partial[wide(step * 2, 2), :, :, cols] = block.reshape(2, 2, 64, 512).astype(half)

    order = tuple(others) + (chip,)
    halves = [move.send(partial.at[2 * to + other], from_partner.at[to], partner) for to in order]
    sums = []
    for to, arrived, peer in zip(others, halves, plane):
        move.arrive(arrived)
        add_blocks(partial.at[2 * to + core], from_partner.at[to], from_partner.at[to])
        sums.append(move.send(from_partner.at[to], came.at[chip], peer))
    move.sent(*token_copies)
    move.arrive(halves[3], *sums)
    for row in range(2):

        def body(part):
            total = tok[row, part].astype(full)
            total += partial[me, row, part].astype(full)
            total += from_partner[chip, row, part].astype(full)
            for peer_chip in others:
                total += came[peer_chip, row, part].astype(full)
            hidden_in[row, part] = total
            scale = lax.rsqrt(jnp.mean(total * total, axis=-1, keepdims=True) + EPSILON)
            normed[row, part] = (total * scale * gain_ffn[...]).astype(half)

        chunks(64, body)
    move.sent(*sums, *halves)
    move.arrive(*saved)
    line_norms = move.line(normed, lambda at: all_norm.at[at, core], chip, core, z)
    own.append(move.send(normed, all_norm.at[z, core], partner))
    own.append(move.keep(normed, all_norm.at[z, core]))

    move.arrive(*turned)
    by_x, by_y = plane[0], plane[1]
    front, back = all_wg.at[chip, 0], all_wg.at[chip, 1]
    from_x = move.send(front, front, by_x)
    from_y = move.send(back, back, by_y)
    weights = [from_x, from_y, move.send(back, back, by_x), move.send(front, front, by_y)]

    at_first, at_last = lax.div(3 - z, 3), lax.div(z, 3)
    arrivals = (3 - 2 * at_first, 1 + at_first + at_last, 2 + at_first - at_last)
    inner = (z > 0) & (z < 3)
    shared = []

    def share(step, wait_only=False):
        for line_of in (line_grads, line_norms):
            if wait_only:
                block = move.wait_line(line_of, step, jnp.logical_not(inner))
            else:
                block = move.arrive_line(line_of, step)
            shared.append(move.send(block, block, partner))

    share(arrivals[0])
    share(arrivals[1])
    move.arrive(from_x, from_y)
    front, back = all_wg.at[others[0], 0], all_wg.at[others[1], 1]
    weights += [move.send(front, front, by_y), move.send(back, back, by_x)]
    for line_of in (line_grads, line_norms):
        move.arrive_line(line_of, arrivals[2], inner)
    move.arrive(*weights, *own)

    flat_wg, flat_wd = all_wg.reshape(D, 2048), wd.reshape(1024, D)

    def block_of(zb):
        @pl.loop(0, 4)
        def _(step):
            cols, ups = wide(step * 256, 256), wide(1024 + step * 256, 256)
            rows = all_norm[zb].reshape(256, D)
            gate = plain(rows, flat_wg[:, cols])
            up = plain(rows, flat_wg[:, ups])
            d_hidden = across(all_out[zb].reshape(256, D), flat_wd[cols])
            sigmoid = 1.0 / (1.0 + jnp.exp(-gate))
            silu = gate * sigmoid
            hidden[zb, :, cols] = (silu * up).astype(half)
            d_gate = d_hidden * up * (sigmoid * (1.0 + gate * (1.0 - sigmoid)))
            d_gate_up[zb, :, cols] = d_gate.astype(half)
            d_gate_up[zb, :, ups] = (d_hidden * silu).astype(half)

        @pl.loop(0, 8)
        def _(step):
            cols = wide(step * 256, 256)
            block = across(d_gate_up[zb], flat_wg[cols])
            partial[pl.ds(2 * zb, 2), :, :, cols] = block.reshape(2, 2, 64, 256).astype(half)

    def pair_sum(zb, handle, into, base):
        move.arrive(handle)
        add_blocks(partial.at[2 * zb + core], into.at[base + zb], into.at[base + zb])

    start_sum, wait_sums = move.scatter(
        lambda at: from_partner.at[at], lambda at: came.at[at], arrivals, chip, core, z
    )
    to_partner = []
    walk = [z] + [ahead(z, step) for step in arrivals]
    for index, zb in enumerate(walk):
        if index > 0:
            move.arrive(*shared[2 * index - 2 : 2 * index])
        block_of(zb)
        to_partner.append(move.send(partial.at[2 * zb + other], from_partner.at[zb], partner))
        if index == 0:
            share(arrivals[2], True)
        if index > 0:
            pair_sum(walk[index - 1], to_partner[index - 1], from_partner, 0)
        if index > 1:
            start_sum(index - 2)
    pair_sum(walk[3], to_partner[3], from_partner, 0)
    start_sum(2)

    flat_norm, flat_grads = all_norm.reshape(1024, D), all_out.reshape(1024, D)
    flat_hidden, flat_d = hidden.reshape(1024, 1024), d_gate_up.reshape(1024, 2048)
    move.sent(*weights)

    def gate_up_grad(to, side):
        rows, lanes = wide(to * 512, 512), pl.ds(side * 1024, 1024)

        @pl.loop(0, 2)
        def _(step):
            cols = wide(side * 1024 + step * 512, 512)
            flat_wg[rows, cols] = down(flat_norm[:, rows], flat_d[:, cols]).astype(half)

        return flat_wg.at[rows, lanes]

    passed = []
    for side in (0, 1):
        passed.append(move.send(gate_up_grad(others[2], side), gate_up_mid.at[side], plane[side]))
    direct = [gate_up_grad(others[side], side) for side in (0, 1)]
    handed = [gate_up_grad(others[1 - side], side) for side in (0, 1)]
    for side in (0, 1):
        gate_up_grad(chip, side)
    move.sent(*shared)
    move.sent_lines()
    for peer in [partner] + plane:
        pl.semaphore_signal(credit, inc=1, device_id=peer, device_id_type=MESH)

    wait_sums()
    gain_part[...] = jnp.zeros_like(gain_part)
    for row in range(2):

        def body2(part):
            total = from_partner[z, row, part].astype(full)
            for step in steps:
                total += came[ahead(z, step), row, part].astype(full)
            entries = hidden_in[row, part]
            scale = lax.rsqrt(jnp.mean(entries * entries, axis=-1, keepdims=True) + EPSILON)
            gain_part[...] += jnp.sum(total * entries * scale, axis=0, keepdims=True)
            total = total * gain_ffn[...]
            inside = jnp.mean(total * entries, axis=-1, keepdims=True) * (scale * scale * scale)
            grad = grad_out[row, part].astype(full) + total * scale - entries * inside
            d_hidden_in[row, part] = grad
            d_branch[row, part] = grad.astype(half)

        chunks(64, body2)
    pl.semaphore_wait(credit, 4)
    move.sent_sums()
    all_branch = all_norm.reshape(8, 2, 64, D)
    branches = [move.send(d_branch, all_branch.at[me], peer) for peer in plane]
    branch_copies = [
        move.send(d_branch, all_branch.at[me], partner), move.keep(d_branch, all_branch.at[me])
    ]
    pieces = [
        move.send(direct[side], gate_up_in.at[side, 0], plane[side]) for side in (0, 1)
    ]

    move.sent(*to_partner)
    to_partner, sums = [], []
    walk = [ahead(z, step) for step in steps] + [z]
    for index, zb in enumerate(walk):

        @pl.loop(0, 4)
        def _(step, zb=zb):
            cols = wide(step * 512, 512)
            block = plain(hidden[zb], flat_wd[:, cols])
            partial[pl.ds(2 * zb, 2), :, :, cols] = block.reshape(2, 2, 64, 512).astype(half)

        to_partner.append(move.send(partial.at[2 * zb + other], all_tok.at[zb], partner))
        if index > 0:
            before = walk[index - 1]
            pair_sum(before, to_partner[index - 1], all_tok, 0)
            sums.append(move.send(all_tok.at[before], all_tok.at[4 + z], line[index - 1]))
    pair_sum(z, to_partner[3], all_tok, 0)

    @pl.loop(0, 4)
    def _(to):
        rows = wide(to * 256, 256)

        @pl.loop(0, 4)
        def _(step):
            cols = wide(step * 512, 512)
            flat_wd[rows, cols] = down(flat_hidden[:, rows], flat_grads[:, cols]).astype(half)

    load_tok = move.keep(kept_tok, all_out.reshape(8, 2, 64, D))

    def load(source):
        return [
            move.keep(source(side), flat_d.at[pl.ds(side * 512, 512), pl.ds(0, 1024)])
            for side in (0, 1)
        ]

    def add_loaded(side, chunk):
        @pl.loop(0, 512 // CHUNK)
        def _(step):
            lanes = pl.ds(side * 1024, 1024)
            rows = wide(chunk * 512 + step * CHUNK, CHUNK)
            extra = flat_d[wide(side * 512 + step * CHUNK, CHUNK), pl.ds(0, 1024)]
            total = flat_wg[rows, lanes].astype(full) + extra.astype(full)
            flat_wg[rows, lanes] = total.astype(half)

    move.arrive(*passed)
    loads = load(lambda side: gate_up_mid.at[side])
    later = []
    for side in (0, 1):
        move.arrive(loads[side])
        add_loaded(side, others[1 - side])
        later.append(move.send(handed[side], gate_up_in.at[side, 1], plane[1 - side]))
    for peer_chip, handle in zip(others, branches):
        move.arrive(handle)
        block = all_branch.at[2 * peer_chip + core]
        branch_copies.append(move.send(block, block, partner))
    move.arrive(*branch_copies)

    flat_branch = all_branch.reshape(1024, D)
    flat_wo = all_wo.reshape(256, D)
    d_heads_at, d_projected_at = pl.ds(0, 256), pl.ds(256, 384)

    @pl.loop(0, 4)
    def _(step):
        rows = wide(step * 256, 256)
        flat_hidden[rows, d_heads_at] = across(flat_branch[rows], flat_wo[...]).astype(half)

    @pl.loop(0, 4)
    def _(step):
        cols = wide(step * 512, 512)
        block = down(flat_attended[...].astype(half), flat_branch[:, cols])
        flat_wo[:, cols] = block.astype(half)

    for step, peer in zip(steps, line):
        move.send(all_wo.at[ahead(z, step)], out_came.at[z], peer)
    move.keep(all_wo.at[z], out_came.at[z])
    lower = lower_half((128, 128))
    line_low = lower_half((1, 128))
    gain_qk[...] = jnp.zeros_like(gain_qk)

    @pl.loop(0, 2)
    def _(row):
        d_keys_values[...] = jnp.zeros_like(d_keys_values)

        def token_rows(block):
            return wide((2 * block + row) * 64, 64)

        for tile in range(2):
            lanes = pl.ds(tile * 128, 128)
            for part in range(4):
                own_places, upto = pl.ds(part * 128, 128), pl.ds(0, (part + 1) * 128)
                d_heads = jnp.concatenate(
                    [flat_hidden[token_rows(2 * part + index), lanes] for index in range(2)], axis=0
                )
                products = d_heads.astype(full) * attended[pl.ds(2 * part, 2), row, :, lanes].reshape(128, 128)
                query = queries[row, tile, own_places]
                total = jnp.zeros((128, 128), full)
                for side in range(2):
                    mask = lower if side == 0 else jnp.logical_not(lower)
                    delta = jnp.sum(jnp.where(mask, products, 0.0), axis=-1, keepdims=True)
                    keys = keys_values[row, side, upto]
                    probs = attention_probs(query, keys, first[row, own_places], part)
                    d_probs = across(d_heads, keys_values[row, 2 + side, upto])
                    d_scores = (probs * (d_probs - delta)).astype(half)
                    total += plain(d_scores, keys)
                    d_keys_values[side, upto] += down(d_scores, query)
                    d_keys_values[2 + side, upto] += down(probs.astype(half), d_heads)
                d_queries[tile, own_places] = total

        @pl.loop(0, 8)
        def _(block):
            cosine, sine = cosines[block, row], sines[block, row]
            places = wide(block * 64, 64)
            for tile in range(3):
                entries = projected[block, row, :, pl.ds(tile * 128, 128)]
                gain = gain_heads[tile // 2 : tile // 2 + 1]
                scale = lax.rsqrt(head_means(entries * entries) + EPSILON)
                if tile < 2:
                    grad = d_queries[tile, places] * HEAD_DIM ** (-0.5)
                else:
                    from_low, from_high = d_keys_values[0, places], d_keys_values[1, places]
                    grad = jnp.where(low, from_low + pltpu.roll(from_high, 64, 1), 0.0)
                grad = grad * cosine + swap_halves(grad * sine)
                for_gain = jnp.sum(grad * entries * scale, axis=0, keepdims=True)
                if tile < 2:
                    for_gain = jnp.where(line_low, for_gain + pltpu.roll(for_gain, 64, 1), 0.0)
                else:
                    for_gain = jnp.where(line_low, 0.0, pltpu.roll(for_gain, 64, 1))
                gain_qk[...] += for_gain
                grad = grad * gain
                inside = head_means(grad * entries) * (scale * scale * scale)
                grad = grad * scale - entries * inside
                if tile == 2:
                    values = pltpu.roll(d_keys_values[2, places], 64, 1)
                    grad = jnp.where(low, grad, values + d_keys_values[3, places])
                flat_hidden[token_rows(block), pl.ds(256 + tile * 128, 128)] = grad.astype(half)

    move.sent(*to_partner)

    @pl.loop(0, 4)
    def _(step):
        rows = flat_hidden[wide(step * 256, 256), d_projected_at]

        @pl.loop(0, 4)
        def _(col):
            cols = wide(col * 512, 512)
            block = across(rows, flat_wq[cols])
            partial[wide(step * 2, 2), :, :, cols] = block.reshape(2, 2, 64, 512).astype(half)

    halves = [move.send(partial.at[2 * to + other], from_partner.at[to], partner) for to in order]
    move.arrive(load_tok)

    for block in range(4):
        strip = pl.ds(1024 + 384 * (block // 2), 384)
        product = down(
            flat_grads[:, pl.ds(block * 512, 512)], flat_hidden[:, d_projected_at]
        )
        flat_d[pl.ds(512 * (block % 2), 512), strip] = product.astype(half)

    def head_block(head, at):
        rows = wide(((head % 4) * 4 + at) * 64, 64)
        return flat_d.at[rows, pl.ds(1024 + 384 * (head // 4), 384)]

    qkv_pieces = []
    for step, peer in zip(steps, line):
        pairs = [(head_block(head, ahead(z, step)), qkv_in.at[z, head]) for head in range(8)]
        qkv_pieces.append(move.send_parts(pairs, (qkv_in.at[z], qkv_in.at[z]), peer))
    for to, arrived, peer in zip(others, halves, plane):
        move.arrive(arrived)
        add_blocks(partial.at[2 * to + core], from_partner.at[to], from_partner.at[to])
        move.send(from_partner.at[to], d_norm_came.at[chip], peer)
    for to, peer in zip(others, plane):
        move.send(wd.at[to], down_came.at[chip], peer)
    move.keep(wd.at[chip], down_came.at[chip])
    move.arrive(halves[3])
    add_blocks(partial.at[me], from_partner.at[chip], from_partner.at[chip])
    move.keep(from_partner.at[chip], d_norm_came.at[chip])

    for slot, handles in ((0, pieces), (1, later)):
        move.arrive(*handles)
        loads = load(lambda side, slot=slot: gate_up_in.at[side, slot])
        for side in (0, 1):
            move.arrive(loads[side])
            add_loaded(side, chip)

    def back_block(to_core, to_z):
        whole = all_wg.at[chip, to_core, to_z]
        pairs = [(whole.at[:, src], gate_up_came.at[:, dst]) for dst, src in segments(core, z)]
        return pairs, (whole, whole)

    for step, peer, peer_cross in zip(steps, line, cross):
        to = ahead(z, step)
        move.send_parts(*back_block(core, to), peer)
        move.send_parts(*back_block(other, to), peer_cross)
    move.send_parts(*back_block(other, z), partner)
    move.keep_parts(*back_block(core, z))

    move.arrive(*qkv_pieces)
    move.sent(*heads[1:])
    for head in range(8):
        total = head_block(head, z)[...].astype(full)
        for step in steps:
            total += qkv_in[ahead(z, step), head].astype(full)
        wq_send[head] = total.astype(half)
    for peer in everyone:
        move.send(wq_send.at[peer[0]], qkv_came.at[me], peer)
    move.keep(wq_send.at[me], qkv_came.at[me])
    move.arrive(*sums)
    for row in range(2):

        def body3(part):
            total = hidden_in[row, part] + all_tok[z, row, part].astype(full)
            for step in steps:
                total += all_tok[4 + ahead(z, step), row, part].astype(full)
            out_sum[row, part] = total.astype(half)

        chunks(64, body3)
    move.finish()


COL_ROWS, GAIN_ROWS = 184, 33
MATRICES = ((64, QKV, 0, 0), (64, D, 64, 24), (64, 2 * FF, 128, 40), (256, D, 192, 168))
ROW_TOTALS = (D, HEADS * HEAD_DIM, D, FF)
BETA = 1.0 - STEP ** (-0.8)


def lane_value(vector, lane):
    lanes = lax.broadcasted_iota(jnp.int32, (1, 128), 1)
    return jnp.sum(jnp.where(lanes == lane, vector, 0.0), axis=-1, keepdims=True)


def statistics_kernel(
    d_norm, tok, d_hidden_in, gain, gain_ffn, gain_qk, qkv, out, gate_up, down, rows,
    m_qkv, m_out, m_gate_up, m_down,
    grad_tok, g_qkv, g_out, g_gate_up, g_down, rows_new, packed,
    gain_part, sums, inverse,
):
    gain_part[...] = jnp.zeros_like(gain_part)

    @pl.loop(0, 128 // CHUNK)
    def _(step):
        part = pl.ds(pl.multiple_of(step * CHUNK, CHUNK), CHUNK)
        total = d_norm[0, part].astype(jnp.float32)
        for slot in range(1, 4):
            total += d_norm[slot, part].astype(jnp.float32)
        entries = tok[part].astype(jnp.float32)
        scale = lax.rsqrt(jnp.mean(entries * entries, axis=-1, keepdims=True) + EPSILON)
        gain_part[...] += jnp.sum(total * entries * scale, axis=0, keepdims=True)
        total = total * gain[...]
        inner = jnp.mean(total * entries, axis=-1, keepdims=True) * (scale * scale * scale)
        grad_tok[part] = (d_hidden_in[part] + total * scale - entries * inner).astype(jnp.bfloat16)

    first = 2 * COL_ROWS
    for slot in range(16):
        lanes = pl.ds(slot * 128, 128)
        packed[first + slot : first + slot + 1] = gain_part[:, lanes]
        packed[first + 16 + slot : first + 17 + slot] = gain_ffn[:, lanes]
    packed[first + 32 : first + 33] = gain_qk[...]
    lane = lax.broadcasted_iota(jnp.int32, (64, 128), 1)

    def wide(step):
        return pl.ds(pl.multiple_of(step * 128, 128), 128)

    def read_qkv(step):
        return g_qkv[:, wide(step)]

    for head in range(8):
        for half in range(2):
            g_qkv[:, pl.ds(head * 256 + half * 128, 128)] = qkv[
                head, :, pl.ds(half * 128, 128)
            ].astype(jnp.float32)
    for pair in range(4):
        low = qkv[2 * pair, :, pl.ds(256, 128)].astype(jnp.float32)
        high = qkv[2 * pair + 1, :, pl.ds(256, 128)].astype(jnp.float32)
        g_qkv[:, pl.ds(2048 + pair * 128, 128)] = jnp.where(lane < 64, low, pltpu.roll(high, 64, 1))
        g_qkv[:, pl.ds(2560 + pair * 128, 128)] = jnp.where(lane < 64, pltpu.roll(low, 64, 1), high)

    def read_out(step):
        total = out[0, :, wide(step)].astype(jnp.float32)
        for slot in range(1, 4):
            total += out[slot, :, wide(step)].astype(jnp.float32)
        return total

    def read_gate_up(step):
        return gate_up[:, wide(step)].astype(jnp.float32)

    def read_down(step):
        total = down[0, :, wide(step)].astype(jnp.float32)
        for slot in range(1, 4):
            total += down[slot, :, wide(step)].astype(jnp.float32)
        return total

    readers = (read_qkv, read_out, read_gate_up, read_down)
    grads = (g_qkv, g_out, g_gate_up, g_down)
    masters = (m_qkv, m_out, m_gate_up, m_down)
    stats = jnp.zeros((1, 128), jnp.float32)
    lanes = lax.broadcasted_iota(jnp.int32, (1, 128), 1)
    for slot, (count, width, row_at, col_at) in enumerate(MATRICES):
        own = pl.ds(0, count)
        sums[0, own] = jnp.zeros((count, 128), jnp.float32)
        sums[1, own] = jnp.zeros((count, 128), jnp.float32)

        @pl.loop(0, width // 128)
        def _(step, slot=slot, own=own):
            entries = readers[slot](step)
            if slot > 0:
                grads[slot][:, wide(step)] = entries
            sums[0, own] += entries * entries
            weight = masters[slot][:, wide(step)]
            sums[1, own] += weight * weight

        mean = jnp.sum(sums[0, own], axis=-1, keepdims=True) / width + SQUARE_EPSILON
        here_rows = pl.ds(row_at, count)
        new = BETA * rows[here_rows] + (1.0 - BETA) * mean
        rows_new[here_rows] = new
        inverse[own] = jnp.broadcast_to(1.0 / new, (count, 128))
        weight_sum = jnp.sum(jnp.sum(sums[1, own], axis=-1, keepdims=True), axis=0, keepdims=True)
        stats = jnp.where(lanes == slot, jnp.sum(new, axis=0, keepdims=True), stats)
        stats = jnp.where(lanes == 4 + slot, weight_sum, stats)

        @pl.loop(0, width // 128)
        def _(step, slot=slot, own=own, count=count, col_at=col_at):
            entries = grads[slot][:, wide(step)]
            square = entries * entries
            packed[pl.ds(col_at + step, 1)] = (
                jnp.sum(square, axis=0, keepdims=True) + count * SQUARE_EPSILON
            )
            packed[pl.ds(COL_ROWS + col_at + step, 1)] = jnp.sum(
                square * inverse[own], axis=0, keepdims=True
            )

    packed[first + 33 : first + 34] = stats
    packed[first + 34 : 512] = jnp.zeros((512 - first - 34, 128), jnp.float32)


def total_kernel(
    parts, col_moments, gain_moments, gains,
    cols_new, col_factors, moments_new, gains_new, grad_gains, spreads,
    totals, plane_came, line_came, plane_sum, line_sum, line_all, *sems,
):
    chip, core, z = here()
    me = 2 * chip + core
    other = 1 - core
    plane = [at_place(chip, other, z)]
    for peer_chip in flips(chip):
        plane += [at_place(peer_chip, core, z), at_place(peer_chip, other, z)]
    line = [at_place(chip, core, ahead(z, step)) for step in (2, 1, 3)]
    greet(plane + line)
    move = Mover(*sems)
    pieces = [move.send(parts.at[peer[0]], plane_came.at[me], peer) for peer in plane]
    plane_came[me] = parts[me]
    move.arrive(*pieces)
    total = plane_came[0]
    for slot in range(1, 8):
        total = total + plane_came[slot]
    plane_sum[...] = total
    pieces = [move.send(plane_sum.at[peer[1]], line_came.at[z], peer) for peer in line]
    line_came[z] = plane_sum[z]
    move.arrive(*pieces)
    line_sum[...] = line_came[0] + line_came[1] + line_came[2] + line_came[3]
    pieces = [move.send(line_sum, line_all.at[z], peer) for peer in line]
    line_all[z] = line_sum[...]
    move.arrive(*pieces)
    for peer in plane:
        move.send(line_all, totals.at[me], peer)
    totals[me] = line_all[...]
    move.finish()
    flat = totals.reshape(512, 128)
    first = 2 * COL_ROWS
    stats = flat[first + 33 : first + 34]
    lanes = lax.broadcasted_iota(jnp.int32, (1, 128), 1)
    out = jnp.zeros((1, 128), jnp.float32)
    for slot, (_, width, _, col_at) in enumerate(MATRICES):
        own = pl.ds(col_at, width // 128)
        entries_all = float(ROW_TOTALS[slot] * width)
        new = BETA * col_moments[own] + (1.0 - BETA) * (flat[own] / ROW_TOTALS[slot])
        cols_new[own] = new
        mean_rows = lane_value(stats, slot) / ROW_TOTALS[slot]
        ratio = flat[pl.ds(COL_ROWS + col_at, width // 128)] / new
        ratio = jnp.sum(jnp.sum(ratio, axis=-1, keepdims=True), axis=0, keepdims=True)
        spread = jnp.sqrt(mean_rows * ratio / entries_all)
        scale = STEP_RATE * jnp.maximum(
            SCALE_EPSILON, jnp.sqrt(lane_value(stats, 4 + slot) / entries_all)
        )
        factor = scale * jnp.sqrt(mean_rows) / jnp.maximum(1.0, spread / CLIP_LEVEL)
        col_factors[own] = lax.rsqrt(new) * factor
        out = jnp.where(lanes == slot, spread, out)
    gradient = flat[first : first + GAIN_ROWS]
    grad_gains[...] = gradient
    old = gains[...]
    new = BETA * gain_moments[...] + (1.0 - BETA) * (gradient * gradient + SQUARE_EPSILON)
    moments_new[...] = new
    unit = gradient * lax.rsqrt(new)
    row = lax.broadcasted_iota(jnp.int32, (GAIN_ROWS, 128), 0)
    lane = lax.broadcasted_iota(jnp.int32, (GAIN_ROWS, 128), 1)
    segment = jnp.where(row < 16, 0, jnp.where(row < 32, 1, jnp.where(lane < 64, 2, 3)))
    factors = jnp.zeros((GAIN_ROWS, 128), jnp.float32)

    def mean_of(square, mask, count):
        picked = jnp.where(mask, square, 0.0)
        return jnp.sum(jnp.sum(picked, axis=-1, keepdims=True), axis=0, keepdims=True) / count

    for slot, count in enumerate((D, D, HEAD_DIM, HEAD_DIM)):
        mask = segment == slot
        spread = jnp.sqrt(mean_of(unit * unit, mask, count))
        scale = STEP_RATE * jnp.maximum(SCALE_EPSILON, jnp.sqrt(mean_of(old * old, mask, count)))
        factors = jnp.where(mask, scale / jnp.maximum(1.0, spread / CLIP_LEVEL), factors)
        out = jnp.where(lanes == 4 + slot, spread, out)
    gains_new[...] = old - factors * unit
    spreads[...] = out


def split_local(
    tokens, doc_starts, grad_out, qkv_master, out_master, gate_up_master, down_master, gains,
    qkv_rows, out_rows, gate_up_rows, down_rows, col_moments, gain_moments,
):
    half, full = jnp.bfloat16, jnp.float32
    gain_attn, gain_ffn = gains[None, :D], gains[None, D : 2 * D]
    gain_query = gains[2 * D : 2 * D + HEAD_DIM]
    gain_key = gains[2 * D + HEAD_DIM :]
    gain_heads = jnp.stack(
        [jnp.concatenate([gain_query, gain_query]), jnp.concatenate([gain_key, gain_key])]
    )
    cosines, sines, first = head_tables(doc_starts, 512)

    def near(*shape, kind=half):
        return pltpu.VMEM(shape, kind)

    (
        d_hidden_in, output, grad_gain_ffn, gain_qk,
        d_norm_came, gate_up_came, qkv_came, out_came, down_came, *_,
    ) = exchange(
        layer_kernel, 0,
        [
            (tokens, True), (gain_attn, True), (gain_ffn, True), (gain_heads, True),
            (cosines, True), (sines, True), (first, True), (qkv_master, True),
            (out_master.astype(half), False), (down_master.astype(half), False),
            (gate_up_master.astype(half), False), (grad_out, True),
        ],
        [
            ((2, 64, D), full, True), ((2, 64, D), half, True), ((1, D), full, True),
            ((1, 128), full, True), ((4, 2, 64, D), half, False), ((64, 2 * FF), half, False),
            ((8, 64, 384), half, False), ((4, 64, D), half, False), ((4, 256, D), half, False),
            ((2, 2, 512, 1024), half, False), ((2, 512, 1024), half, False),
            ((8, 2, 64, D), half, False),
        ],
        [
            near(8, 2, 64, 384, kind=full), near(2, 2, 512, 128), near(2, 4, 512, 128),
            near(8, 2, 64, 256, kind=full),
            near(8, 64, 384), near(2, 64, D), near(8, 2, 64, D), near(8, 4, 64, 384), near(4, 64, D),
            near(8, 2, 64, D), near(4, 2, 64, D), near(4, 2, 64, D), near(2, 64, D, kind=full),
            near(4, 2, 2, 64, D), near(4, 2, 2, 64, D), near(4, 2, 4, 64, 2048), near(4, 256, D),
            near(4, 256, 1024), near(4, 256, 2048), near(2, 64, D),
            near(2, 512, 128, kind=full), near(4, 512, 128, kind=full), near(4, 8, 64, 384),
            pltpu.SemaphoreType.REGULAR,
        ],
        (130, 24), 160 << 20, 48 << 30,
    )
    row_states = jnp.concatenate([qkv_rows, out_rows, gate_up_rows, down_rows])[:, None]
    masters = (qkv_master, out_master, gate_up_master, down_master)
    grad_tokens, *grads, rows_new, packed = pl.pallas_call(
        statistics_kernel,
        out_shape=[
            jax.ShapeDtypeStruct((128, D), half),
            *[jax.ShapeDtypeStruct((count, width), full) for count, width, _, _ in MATRICES],
            jax.ShapeDtypeStruct((448, 1), full),
            jax.ShapeDtypeStruct((512, 128), full),
        ],
        scratch_shapes=[
            pltpu.VMEM((1, D), full), pltpu.VMEM((2, 256, 128), full), pltpu.VMEM((256, 128), full),
        ],
        compiler_params=pltpu.CompilerParams(vmem_limit_bytes=VMEM_BYTES),
    )(
        d_norm_came.reshape(4, 128, D), tokens.reshape(128, D), d_hidden_in.reshape(128, D), gain_attn,
        grad_gain_ffn, gain_qk,
        qkv_came, out_came, gate_up_came, down_came, row_states, *masters,
    )
    shape = (8, 4, 16, 128)
    cols_new, col_factors, moments_new, gains_new, grad_gains, spreads = exchange(
        total_kernel, 1,
        [
            (packed.reshape(shape), True), (col_moments.reshape(-1, 128), True),
            (gain_moments.reshape(-1, 128), True), (gains.reshape(-1, 128), True),
        ],
        [
            ((COL_ROWS, 128), full, True), ((COL_ROWS, 128), full, True),
            ((GAIN_ROWS, 128), full, True), ((GAIN_ROWS, 128), full, True),
            ((GAIN_ROWS, 128), full, True), ((1, 128), full, True),
        ],
        [
            pltpu.VMEM(shape, full), pltpu.VMEM(shape, full), pltpu.VMEM(shape[1:], full),
            pltpu.VMEM(shape[1:], full), pltpu.VMEM(shape[2:], full), pltpu.VMEM(shape[1:], full),
        ],
        (20, 0), 1 << 20,
    )
    col_factors = col_factors.reshape(-1)
    row_factors = lax.rsqrt(rows_new[:, 0])
    new_masters = []
    for slot, (count, width, row_at, col_at) in enumerate(MATRICES):
        row_factor = row_factors[row_at : row_at + count]
        col_factor = col_factors[col_at * 128 : col_at * 128 + width]
        new_masters.append(
            masters[slot] - grads[slot] * row_factor[:, None] * col_factor[None, :]
        )
    return (
        output,
        grad_tokens.reshape(2, 64, D),
        *grads,
        grad_gains.reshape(-1),
        *[rows_new[row_at : row_at + count, 0] for count, _, row_at, _ in MATRICES],
        cols_new.reshape(-1),
        moments_new.reshape(-1),
        *new_masters,
        *[master.astype(half) for master in new_masters],
        gains_new.reshape(-1),
        spreads[0, :8],
    )


def optimizer_step(
    grads, gain_local, masters, gains, row_states, col_moments, gain_moments, total_fn
):
    beta = 1.0 - STEP ** (-0.8)
    col_widths = (QKV, D, 2 * FF, D)
    row_totals = (D, HEADS * HEAD_DIM, D, FF)
    squares = [gradient * gradient + SQUARE_EPSILON for gradient in grads]
    rows_new = [
        beta * row_state + (1.0 - beta) * jnp.mean(square, axis=1)
        for row_state, square in zip(row_states, squares)
    ]
    col_local = [jnp.sum(square, axis=0) for square in squares]
    weighted_local = [
        jnp.sum(gradient * gradient / row_new[:, None], axis=0)
        for gradient, row_new in zip(grads, rows_new)
    ]
    stats_local = jnp.stack(
        [jnp.sum(row_new) for row_new in rows_new]
        + [jnp.sum(master * master) for master in masters]
    )
    totals = total_fn(jnp.concatenate(col_local + weighted_local + [stats_local, gain_local]))
    cols = sum(col_widths)
    col_sums, weighted = totals[:cols], totals[cols : 2 * cols]
    stats, grad_gains = totals[2 * cols : 2 * cols + 8], totals[2 * cols + 8 :]
    col_divisor = jnp.concatenate(
        [
            jnp.full((col_width,), float(row_total), jnp.float32)
            for col_width, row_total in zip(col_widths, row_totals)
        ]
    )
    cols_new = beta * col_moments + (1.0 - beta) * col_sums / col_divisor
    new_masters = []
    spreads = []
    begin_at = 0
    for slot in range(4):
        col_part = cols_new[begin_at : begin_at + col_widths[slot]]
        weighted_part = weighted[begin_at : begin_at + col_widths[slot]]
        begin_at = begin_at + col_widths[slot]
        mean_rows = stats[slot] / row_totals[slot]
        unit = (
            grads[slot]
            * lax.rsqrt(rows_new[slot] / mean_rows)[:, None]
            * lax.rsqrt(col_part)[None, :]
        )
        entries_all = float(row_totals[slot] * col_widths[slot])
        spread = jnp.sqrt(mean_rows * jnp.sum(weighted_part / col_part) / entries_all)
        scale = STEP_RATE * jnp.maximum(SCALE_EPSILON, jnp.sqrt(stats[4 + slot] / entries_all))
        new_masters.append(masters[slot] - scale * unit / jnp.maximum(1.0, spread / CLIP_LEVEL))
        spreads.append(spread)
    bounds = (0, D, 2 * D, 2 * D + HEAD_DIM, 2 * D + 2 * HEAD_DIM)
    moment_parts, gain_parts = ([], [])
    for segment in range(4):
        gradient = grad_gains[bounds[segment] : bounds[segment + 1]]
        gain_old = gains[bounds[segment] : bounds[segment + 1]]
        moment_new = beta * gain_moments[bounds[segment] : bounds[segment + 1]] + (1.0 - beta) * (
            gradient * gradient + SQUARE_EPSILON
        )
        unit = gradient * lax.rsqrt(moment_new)
        spread = jnp.sqrt(jnp.mean(unit * unit))
        scale = STEP_RATE * jnp.maximum(SCALE_EPSILON, jnp.sqrt(jnp.mean(gain_old * gain_old)))
        moment_parts.append(moment_new)
        gain_parts.append(gain_old - scale * unit / jnp.maximum(1.0, spread / CLIP_LEVEL))
        spreads.append(spread)
    return (
        grad_gains,
        *rows_new,
        cols_new,
        jnp.concatenate(moment_parts),
        *new_masters,
        *[master.astype(jnp.bfloat16) for master in new_masters],
        jnp.concatenate(gain_parts),
        jnp.stack(spreads),
    )


def solution(mesh):
    split = mesh.shape["seq"] == 8 and mesh.shape["rows"] == 4
    return jax.shard_map(
        split_local if split else gathered_local,
        mesh=mesh,
        in_specs=(
            P("rows", "seq", None),
            P("rows", None),
            P("rows", "seq", None),
            P(("seq", "rows"), None),
            P(("seq", "rows"), None),
            P(("seq", "rows"), None),
            P(("seq", "rows"), None),
            P(),
            P(("seq", "rows")),
            P(("seq", "rows")),
            P(("seq", "rows")),
            P(("seq", "rows")),
            P(),
            P(),
        ),
        out_specs=(
            P("rows", "seq", None),
            P("rows", "seq", None),
            P(("seq", "rows"), None),
            P(("seq", "rows"), None),
            P(("seq", "rows"), None),
            P(("seq", "rows"), None),
            P(),
            P(("seq", "rows")),
            P(("seq", "rows")),
            P(("seq", "rows")),
            P(("seq", "rows")),
            P(),
            P(),
            P(("seq", "rows"), None),
            P(("seq", "rows"), None),
            P(("seq", "rows"), None),
            P(("seq", "rows"), None),
            P(("seq", "rows"), None),
            P(("seq", "rows"), None),
            P(("seq", "rows"), None),
            P(("seq", "rows"), None),
            P(),
            P(),
        ),
        check_vma=False,
    )
```

```python
from functools import partial

import jax
import jax.numpy as jnp
from jax import lax
from jax.experimental import pallas as pl
from jax.experimental.pallas import tpu as pltpu
from jax.sharding import PartitionSpec as P

D = 2048
HEADS = 32
KV_HEADS = 8
HEAD_DIM = 64
FF = 8192
STEP = 10
QKV = 3072


EPSILON = 1e-06
ROPE_BASE = 10000.0
MASKED_SCORE = -1e30
STEP_RATE = 0.3
CLIP_LEVEL = 1.0
SQUARE_EPSILON = 1e-30
SCALE_EPSILON = 0.001


def from_behind(value, axis, steps):
    count = lax.axis_size(axis)
    pairs = [(source, (source + steps) % count) for source in range(count)]
    return lax.ppermute(value, axis, pairs)


def norm_rows(entries, gain):
    return entries * lax.rsqrt(jnp.mean(entries * entries, axis=-1, keepdims=True) + EPSILON) * gain


def turn(entries, cos_wide, sin_wide):
    half_width = entries.shape[-1] // 2
    turned = jnp.concatenate([-entries[..., half_width:], entries[..., :half_width]], axis=-1)
    return entries * cos_wide + turned * sin_wide


def doc_tables(doc_starts, places):
    before = doc_starts[:, None, :] <= places[None, :, None]
    doc_ids = jnp.sum(before.astype(jnp.int32), axis=-1)
    doc_first = jnp.max(jnp.where(before, doc_starts[:, None, :], 0), axis=-1)
    return (doc_ids, places[None, :] - doc_first)


def rotary(offsets):
    frequency = ROPE_BASE ** (-(jnp.arange(HEAD_DIM // 2, dtype=jnp.float32) * 2.0 / HEAD_DIM))
    angles = offsets.astype(jnp.float32)[..., None] * frequency
    cos_table = jnp.concatenate([jnp.cos(angles), jnp.cos(angles)], axis=-1)
    sin_table = jnp.concatenate([jnp.sin(angles), jnp.sin(angles)], axis=-1)
    return (cos_table, sin_table)


def queries_keys(
    cos_table, sin_table, projected, gain_query, gain_key, heads=HEADS, kv_heads=KV_HEADS
):
    rows_here, seq_here = (projected.shape[0], projected.shape[1])
    att_width = heads * HEAD_DIM
    queries = projected[..., :att_width].reshape(rows_here, seq_here, heads, HEAD_DIM)
    keys_rot = projected[..., att_width : att_width + kv_heads * HEAD_DIM].reshape(
        rows_here, seq_here, kv_heads, HEAD_DIM
    )
    cos_wide = cos_table[:, :, None, :]
    sin_wide = sin_table[:, :, None, :]
    queries = turn(norm_rows(queries, gain_query), cos_wide, sin_wide) * HEAD_DIM ** (-0.5)
    keys_rot = turn(norm_rows(keys_rot, gain_key), cos_wide, sin_wide)
    return (queries, keys_rot)


def mask_of(query_docs, query_places, key_docs, key_places):
    same_doc = query_docs[:, :, None] == key_docs[:, None, :]
    causal = query_places[None, :, None] >= key_places[None, None, :]
    return (same_doc & causal)[:, None, None, :, :]


def gathered_local(
    tokens,
    doc_starts,
    grad_out,
    qkv_master,
    out_master,
    gate_up_master,
    down_master,
    gains,
    qkv_rows,
    out_rows,
    gate_up_rows,
    down_rows,
    col_moments,
    gain_moments,
):
    cycle_size = lax.axis_size("seq")
    seq_index = lax.axis_index("seq")
    rows_dev, seq_dev = (tokens.shape[0], tokens.shape[1])
    group_size = HEADS // KV_HEADS
    att_width = HEADS * HEAD_DIM
    kv_width = KV_HEADS * HEAD_DIM
    gain_attn = gains[:D]
    gain_ffn = gains[D : 2 * D]
    gain_query = gains[2 * D : 2 * D + HEAD_DIM]
    gain_key = gains[2 * D + HEAD_DIM :]
    local_places = jnp.arange(seq_dev, dtype=jnp.int32)
    places = seq_index * seq_dev + local_places
    query_docs, offsets = doc_tables(doc_starts, places)
    cos_table, sin_table = rotary(offsets)
    copies = (
        qkv_master.astype(jnp.bfloat16),
        out_master.astype(jnp.bfloat16),
        gate_up_master.astype(jnp.bfloat16),
        down_master.astype(jnp.bfloat16),
    )
    w_qkv, w_out, w_gate_up, w_down = (
        lax.all_gather(copies[0], ("seq", "rows"), axis=0, tiled=True),
        lax.all_gather(copies[1], ("seq", "rows"), axis=0, tiled=True),
        lax.all_gather(copies[2], ("seq", "rows"), axis=0, tiled=True),
        lax.all_gather(copies[3], ("seq", "rows"), axis=0, tiled=True),
    )
    tokens_wide = tokens.astype(jnp.float32)
    normed = norm_rows(tokens_wide, gain_attn).astype(jnp.bfloat16)
    projected = jnp.einsum("rtd,de->rte", normed, w_qkv, preferred_element_type=jnp.float32)
    head_fn = partial(queries_keys, cos_table, sin_table)
    queries, keys_rot = head_fn(projected, gain_query, gain_key)
    query16 = queries.astype(jnp.bfloat16).reshape(
        rows_dev, seq_dev, KV_HEADS, group_size, HEAD_DIM
    )
    keys16 = keys_rot.astype(jnp.bfloat16).reshape(rows_dev, seq_dev, kv_width)
    values16 = projected[..., att_width + kv_width :].astype(jnp.bfloat16)
    stat_shape = (rows_dev, KV_HEADS, group_size, seq_dev)
    initial = (
        jnp.full(stat_shape, MASKED_SCORE, jnp.float32),
        jnp.zeros(stat_shape, jnp.float32),
        jnp.zeros(stat_shape + (HEAD_DIM,), jnp.float32),
    )
    carry = initial
    key_piece = lax.all_gather(keys16, "seq", axis=1, tiled=True)
    value_piece = lax.all_gather(values16, "seq", axis=1, tiled=True)
    key_count = key_piece.shape[1]

    def absorb_block(state, block_index):
        best, total, summed = state
        block_begin = block_index * seq_dev
        key_block = lax.dynamic_slice_in_dim(key_piece, block_begin, seq_dev, 1).reshape(
            rows_dev, seq_dev, KV_HEADS, HEAD_DIM
        )
        value_block = lax.dynamic_slice_in_dim(value_piece, block_begin, seq_dev, 1).reshape(
            rows_dev, seq_dev, KV_HEADS, HEAD_DIM
        )
        key_places = block_begin + jnp.arange(seq_dev, dtype=jnp.int32)
        key_docs, _ = doc_tables(doc_starts, key_places)
        allowed = mask_of(query_docs, places, key_docs, key_places)
        scores = jnp.einsum(
            "rqkgh,rtkh->rkgqt", query16, key_block, preferred_element_type=jnp.float32
        )
        scores = jnp.where(allowed, scores, MASKED_SCORE)
        best_new = jnp.maximum(best, jnp.max(scores, axis=-1))
        weights = jnp.where(allowed, jnp.exp(scores - best_new[..., None]), 0.0)
        factor = jnp.exp(best - best_new)
        total = total * factor + jnp.sum(weights, axis=-1)
        summed = summed * factor[..., None] + jnp.einsum(
            "rkgqt,rtkh->rkgqh",
            weights.astype(jnp.bfloat16),
            value_block,
            preferred_element_type=jnp.float32,
        )
        return ((best_new, total, summed), None)

    carry, _ = lax.scan(absorb_block, carry, jnp.arange(key_count // seq_dev, dtype=jnp.int32))
    best, total, summed = carry
    log_total = best + jnp.log(total)
    attended = summed / total[..., None]
    attended16 = (
        attended.transpose(0, 3, 1, 2, 4).reshape(rows_dev, seq_dev, att_width).astype(jnp.bfloat16)
    )
    branch = jnp.einsum("rtc,cd->rtd", attended16, w_out, preferred_element_type=jnp.float32)
    hidden_in = tokens_wide + branch
    normed2 = norm_rows(hidden_in, gain_ffn).astype(jnp.bfloat16)
    gate_up = jnp.einsum("rtd,df->rtf", normed2, w_gate_up, preferred_element_type=jnp.float32)
    gate_part, up_part = (gate_up[..., :FF], gate_up[..., FF:])
    hidden = (jax.nn.silu(gate_part) * up_part).astype(jnp.bfloat16)
    output = hidden_in + jnp.einsum(
        "rtf,fd->rtd", hidden, w_down, preferred_element_type=jnp.float32
    )
    d_hidden = jnp.einsum("rtd,fd->rtf", grad_out, w_down, preferred_element_type=jnp.float32)
    silu_value, silu_back = jax.vjp(jax.nn.silu, gate_part)
    d_gate = silu_back(d_hidden * up_part)[0]
    d_gate_up = jnp.concatenate([d_gate, d_hidden * silu_value], axis=-1).astype(jnp.bfloat16)
    d_normed2 = jnp.einsum("rtf,df->rtd", d_gate_up, w_gate_up, preferred_element_type=jnp.float32)
    _, ffn_norm_back = jax.vjp(norm_rows, hidden_in, gain_ffn)
    d_inner, grad_gain_ffn = ffn_norm_back(d_normed2)
    d_hidden_in = grad_out.astype(jnp.float32) + d_inner
    term_down = jnp.einsum("rtf,rtd->fd", hidden, grad_out, preferred_element_type=jnp.float32)
    grad_down = lax.psum_scatter(term_down, ("seq", "rows"), scatter_dimension=0, tiled=True)
    term_gate_up = jnp.einsum("rtd,rtf->df", normed2, d_gate_up, preferred_element_type=jnp.float32)
    grad_gate_up = lax.psum_scatter(term_gate_up, ("seq", "rows"), scatter_dimension=0, tiled=True)
    d_branch = d_hidden_in.astype(jnp.bfloat16)
    term_out = jnp.einsum("rtc,rtd->cd", attended16, d_branch, preferred_element_type=jnp.float32)
    d_attended = jnp.einsum(
        "rtd,cd->rtc", d_branch, w_out, preferred_element_type=jnp.float32
    ).astype(jnp.bfloat16)
    d_heads = d_attended.reshape(rows_dev, seq_dev, KV_HEADS, group_size, HEAD_DIM).transpose(
        0, 2, 3, 1, 4
    )
    delta = jnp.sum(d_heads.astype(jnp.float32) * attended, axis=-1)

    def cycle_turn(turn_index, carry):
        pair16, grad_pair, d_queries = carry
        source = (seq_index + turn_index) % cycle_size
        key_places = source * seq_dev + local_places
        key_docs, _ = doc_tables(doc_starts, key_places)
        allowed = mask_of(query_docs, places, key_docs, key_places)
        key_block = pair16[0].reshape(rows_dev, seq_dev, KV_HEADS, HEAD_DIM)
        value_block = pair16[1].reshape(rows_dev, seq_dev, KV_HEADS, HEAD_DIM)
        scores = jnp.einsum(
            "rqkgh,rtkh->rkgqt", query16, key_block, preferred_element_type=jnp.float32
        )
        scores = jnp.where(allowed, scores, MASKED_SCORE)
        probs = jnp.where(allowed, jnp.exp(scores - log_total[..., None]), 0.0)
        d_values = jnp.einsum(
            "rkgqt,rkgqh->rtkh",
            probs.astype(jnp.bfloat16),
            d_heads,
            preferred_element_type=jnp.float32,
        )
        d_probs = jnp.einsum(
            "rkgqh,rtkh->rkgqt", d_heads, value_block, preferred_element_type=jnp.float32
        )
        d_scores = (probs * (d_probs - delta[..., None])).astype(jnp.bfloat16)
        d_queries = d_queries + jnp.einsum(
            "rkgqt,rtkh->rkgqh", d_scores, key_block, preferred_element_type=jnp.float32
        )
        d_keys = jnp.einsum(
            "rkgqt,rqkgh->rtkh", d_scores, query16, preferred_element_type=jnp.float32
        )
        grad_pair = grad_pair + jnp.stack(
            [
                d_keys.reshape(rows_dev, seq_dev, kv_width),
                d_values.reshape(rows_dev, seq_dev, kv_width),
            ]
        )
        grad_pair = from_behind(grad_pair.astype(jnp.bfloat16), "seq", -1).astype(grad_pair.dtype)
        pair16 = from_behind(pair16, "seq", -1)
        return (pair16, grad_pair, d_queries)

    start_pair = jnp.stack([keys16, values16])
    start_grads = jnp.zeros((2, rows_dev, seq_dev, kv_width), jnp.float32)
    start_queries = jnp.zeros(stat_shape + (HEAD_DIM,), jnp.float32)
    _, grad_pair, d_queries = lax.fori_loop(
        0, cycle_size, cycle_turn, (start_pair, start_grads, start_queries)
    )
    d_queries = d_queries.transpose(0, 3, 1, 2, 4).reshape(rows_dev, seq_dev, HEADS, HEAD_DIM)
    d_keys_home = grad_pair[0].reshape(rows_dev, seq_dev, KV_HEADS, HEAD_DIM)
    _, heads_back = jax.vjp(head_fn, projected, gain_query, gain_key)
    d_projected, grad_gain_query, grad_gain_key = heads_back((d_queries, d_keys_home))
    d_projected = jnp.concatenate(
        [d_projected[..., : att_width + kv_width], grad_pair[1]], axis=-1
    ).astype(jnp.bfloat16)
    term_qkv = jnp.einsum("rtd,rte->de", normed, d_projected, preferred_element_type=jnp.float32)
    d_normed = jnp.einsum("rte,de->rtd", d_projected, w_qkv, preferred_element_type=jnp.float32)
    _, attn_norm_back = jax.vjp(norm_rows, tokens_wide, gain_attn)
    d_tokens_part, grad_gain_attn = attn_norm_back(d_normed)
    grad_tokens = (d_hidden_in + d_tokens_part).astype(jnp.bfloat16)
    grad_qkv, grad_out_proj = (
        lax.psum_scatter(term_qkv, ("seq", "rows"), scatter_dimension=0, tiled=True),
        lax.psum_scatter(term_out, ("seq", "rows"), scatter_dimension=0, tiled=True),
    )
    gain_local = jnp.concatenate([grad_gain_attn, grad_gain_ffn, grad_gain_query, grad_gain_key])
    grads = (grad_qkv, grad_out_proj, grad_gate_up, grad_down)
    updated = optimizer_step(
        grads, gain_local, (qkv_master, out_master, gate_up_master, down_master), gains,
        (qkv_rows, out_rows, gate_up_rows, down_rows), col_moments, gain_moments,
        lambda vector: lax.psum(vector, ("seq", "rows")),
    )
    return (output.astype(jnp.bfloat16), grad_tokens, *grads, *updated)


MESH = pl.DeviceIdType.MESH
PLACES = 32
VMEM_BYTES = 61 * 1024 * 1024
CHUNK = 16


def here():
    seq = lax.axis_index("seq")
    return lax.div(seq, 2), lax.rem(seq, 2), lax.axis_index("rows")


def flips(chip):
    return (chip + 1 - 2 * lax.rem(chip, 2), lax.rem(chip + 2, 4), 3 - chip)


def ahead(z, step):
    return lax.rem(z + step, 4)


def at_place(chip, core, z):
    return (2 * chip + core, z)


def greet(peers):
    barrier = pltpu.get_barrier_semaphore()
    for peer in peers:
        pl.semaphore_signal(barrier, inc=1, device_id=peer, device_id_type=MESH)
    pl.semaphore_wait(barrier, len(peers))


class Mover:
    def __init__(self, send_sem, recv_sem, local_sem):
        self.send_sem, self.recv_sem, self.local_sem = send_sem, recv_sem, local_sem
        self.remote, self.own, self.lines, self.scattered = [], [], [], []
        self.used = 0

    def copy_of(self, src, dst, peer, send_slot, recv_slot):
        return pltpu.make_async_remote_copy(
            src_ref=src,
            dst_ref=dst,
            send_sem=self.send_sem.at[send_slot],
            recv_sem=self.recv_sem.at[recv_slot],
            device_id=peer,
            device_id_type=MESH,
        )

    def send_parts(self, pairs, whole, peer):
        slot = self.used
        self.used += 1
        for src, dst in pairs:
            self.copy_of(src, dst, peer, slot, slot).start()
        copy = self.copy_of(whole[0], whole[1], peer, slot, slot)
        handle = [copy, False, copy.wait_recv, False]
        self.remote.append(handle)
        return handle

    def send(self, src, dst, peer):
        return self.send_parts([(src, dst)], (src, dst), peer)

    def keep_parts(self, pairs, whole):
        sem = self.local_sem.at[len(self.own)]
        for src, dst in pairs:
            pltpu.make_async_copy(src, dst, sem).start()
        copy = pltpu.make_async_copy(whole[0], whole[1], sem)
        handle = [copy, False, copy.wait]
        self.own.append(handle)
        return handle

    def keep(self, src, dst):
        return self.keep_parts([(src, dst)], (src, dst))

    def line(self, source, block_of, chip, core, z):
        line = (self.used, block_of, chip, core, z)
        self.used += 5
        base = line[0]
        up, low = at_place(chip, core, z + 1), at_place(chip, core, z - 1)
        rising = self.copy_of(source, block_of(z), up, base, base + 3)
        falling = self.copy_of(source, block_of(z), low, base + 4, base + 1)
        pl.when(z < 3)(rising.start)
        pl.when(z > 0)(falling.start)
        self.lines += [(z < 3, rising), (z > 0, falling)]
        return line

    def wait_line(self, line, step, when=None):
        base, block_of, chip, core, z = line
        block = block_of(ahead(z, step))
        peer = at_place(chip, core, ahead(z, step))
        copy = self.copy_of(block, block, peer, base + step, base + step)
        if when is None:
            copy.wait_recv()
        else:
            pl.when(when)(copy.wait_recv)
        return block

    def arrive_line(self, line, step, when=None):
        base, _, chip, core, z = line
        block = self.wait_line(line, step, when)
        rises, falls = (z + step >= 4) & (z < 3), (z + step < 4) & (z > 0)
        up, low = at_place(chip, core, z + 1), at_place(chip, core, z - 1)
        rising = self.copy_of(block, block, up, base + step, base + step - 1)
        falling = self.copy_of(block, block, low, base + step, base + step + 1)
        for moves, copy in ((rises, rising), (falls, falling)):
            moves = moves if when is None else moves & when
            pl.when(moves)(copy.start)
            self.lines.append((moves, copy))
        return block

    def scatter(self, source, target, steps, chip, core, z):
        base = self.used
        self.used += 3

        def start(index):
            at = ahead(z, steps[index])
            copy = self.copy_of(
                source(at), target(z), at_place(chip, core, at), base + index, base + 3 - steps[index]
            )
            copy.start()
            self.scattered.append(copy)

        def wait():
            for step in (1, 2, 3):
                at = ahead(z, step)
                peer = at_place(chip, core, at)
                self.copy_of(source(at), target(at), peer, base, base + step - 1).wait_recv()

        return start, wait

    def arrive(self, *handles):
        for handle in handles:
            if not handle[1]:
                handle[1] = True
                handle[2]()

    def sent(self, *handles):
        for handle in handles:
            if not handle[3]:
                handle[3] = True
                handle[0].wait_send()

    def sent_lines(self):
        for when, copy in self.lines:
            pl.when(when)(copy.wait_send)
        self.lines = []

    def sent_sums(self):
        for copy in self.scattered:
            copy.wait_send()
        self.scattered = []

    def finish(self):
        self.arrive(*self.own, *self.remote)
        self.sent(*self.remote)
        self.sent_lines()
        self.sent_sums()


def semaphores(remote, own):
    return [
        pltpu.SemaphoreType.DMA((remote,)),
        pltpu.SemaphoreType.DMA((remote,)),
        pltpu.SemaphoreType.DMA((max(own, 1),)),
    ]


def exchange(kernel, ident, inputs, outputs, scratch, copies, moved, flops=0):
    spaces = {True: pltpu.VMEM, False: pl.ANY, None: pltpu.SMEM}
    specs = {near: pl.BlockSpec(memory_space=space) for near, space in spaces.items()}
    return pl.pallas_call(
        kernel,
        out_shape=[jax.ShapeDtypeStruct(shape, kind) for shape, kind, _ in outputs],
        in_specs=[specs[near] for _, near in inputs],
        out_specs=[specs[near] for _, _, near in outputs],
        scratch_shapes=scratch + semaphores(*copies),
        compiler_params=pltpu.CompilerParams(
            collective_id=ident, has_side_effects=True, vmem_limit_bytes=VMEM_BYTES
        ),
        cost_estimate=pl.CostEstimate(flops=flops, bytes_accessed=moved, transcendentals=0),
    )(*[array for array, _ in inputs])


def chunks(length, body):
    @pl.loop(0, length // CHUNK)
    def _(step):
        body(pl.ds(pl.multiple_of(step * CHUNK, CHUNK), CHUNK))


def segments(core, z):
    for part in range(2):
        for chip in range(4):
            start = part * FF + ((2 * chip + core) * 4 + z) * 256
            yield pl.ds(pl.multiple_of(start, 256), 256), pl.ds(part * 1024 + chip * 256, 256)


def add_blocks(first, second, result):
    for row in range(2):

        def body(part):
            total = first[row, part].astype(jnp.float32) + second[row, part].astype(jnp.float32)
            result[row, part] = total.astype(result.dtype)

        chunks(64, body)


def lower_half(shape):
    return lax.broadcasted_iota(jnp.int32, shape, len(shape) - 1) < 64


def swap_halves(entries):
    lane = lax.broadcasted_iota(jnp.int32, entries.shape, 1)
    return jnp.where(lax.rem(lane, 64) < 32, pltpu.roll(entries, 96, 1), pltpu.roll(entries, 32, 1))


def head_means(entries):
    lower = lower_half(entries.shape)
    low = jnp.sum(jnp.where(lower, entries, 0.0), axis=-1, keepdims=True)
    high = jnp.sum(jnp.where(lower, 0.0, entries), axis=-1, keepdims=True)
    return jnp.where(lower, low, high) * (1.0 / HEAD_DIM)


def wide(start, size):
    return pl.ds(pl.multiple_of(start, size), size)


def plain(left, right):
    return jnp.dot(left, right, preferred_element_type=jnp.float32)


def across(left, right):
    return lax.dot_general(
        left, right, (((1,), (1,)), ((), ())), preferred_element_type=jnp.float32
    )


def down(left, right):
    return lax.dot_general(
        left, right, (((0,), (0,)), ((), ())), preferred_element_type=jnp.float32
    )


def attention_probs(queries, keys, first, part):
    scores = across(queries, keys)
    place = lax.broadcasted_iota(jnp.int32, scores.shape, 1)
    query = lax.broadcasted_iota(jnp.int32, scores.shape, 0) + part * 128
    allowed = (place >= first) & (place <= query)
    scores = jnp.where(allowed, scores, MASKED_SCORE)
    best = jnp.max(scores, axis=-1, keepdims=True)
    weights = jnp.where(allowed, jnp.exp(scores - best), 0.0)
    return weights / jnp.sum(weights, axis=-1, keepdims=True)


COL_ROWS, GAIN_ROWS = 184, 33
COLS = COL_ROWS * 128
MATRICES = ((64, QKV, 0, 0), (64, D, 64, 24), (64, 2 * FF, 128, 40), (256, D, 192, 168))
ROW_TOTALS = (D, HEADS * HEAD_DIM, D, FF)
BETA = 1.0 - STEP ** (-0.8)


def lane_value(vector, lane):
    lanes = lax.broadcasted_iota(jnp.int32, (1, 128), 1)
    return jnp.sum(jnp.where(lanes == lane, vector, 0.0), axis=-1, keepdims=True)


def total(entries):
    return jnp.sum(jnp.sum(entries, axis=-1, keepdims=True), axis=0, keepdims=True)


def document_start(starts, row, place):
    start = jnp.zeros_like(place)
    for document in range(starts.shape[1]):
        begin = starts[row, document]
        start = jnp.maximum(start, jnp.where(place >= begin, begin, 0))
    return start


def derive_updates(
    flat, col_moments, gain_moments, gains,
    cols_new, col_factors, moments_new, gains_new, grad_gains, spreads,
):
    first = 2 * COL_ROWS
    stats = flat[first + 33 : first + 34]
    lanes = lax.broadcasted_iota(jnp.int32, (1, 128), 1)
    out = jnp.zeros((1, 128), jnp.float32)
    for slot, (_, width, _, col_at) in enumerate(MATRICES):
        own = pl.ds(col_at, width // 128)
        entries_all = float(ROW_TOTALS[slot] * width)
        new = BETA * col_moments[own] + (1.0 - BETA) * (flat[own] / ROW_TOTALS[slot])
        cols_new[own] = new
        mean_rows = lane_value(stats, slot) / ROW_TOTALS[slot]
        ratio = total(flat[pl.ds(COL_ROWS + col_at, width // 128)] / new)
        spread = jnp.sqrt(mean_rows * ratio / entries_all)
        scale = STEP_RATE * jnp.maximum(
            SCALE_EPSILON, jnp.sqrt(lane_value(stats, 4 + slot) / entries_all)
        )
        factor = scale * jnp.sqrt(mean_rows) / jnp.maximum(1.0, spread / CLIP_LEVEL)
        factors = lax.rsqrt(new) * factor
        for row in range(width // 128):
            col_factors[:, pl.ds((col_at + row) * 128, 128)] = factors[row : row + 1]
        out = jnp.where(lanes == slot, spread, out)
    gradient = flat[first : first + GAIN_ROWS]
    grad_gains[...] = gradient
    old = gains[...]
    new = BETA * gain_moments[...] + (1.0 - BETA) * (gradient * gradient + SQUARE_EPSILON)
    moments_new[...] = new
    unit = gradient * lax.rsqrt(new)
    row = lax.broadcasted_iota(jnp.int32, (GAIN_ROWS, 128), 0)
    lane = lax.broadcasted_iota(jnp.int32, (GAIN_ROWS, 128), 1)
    segment = jnp.where(row < 16, 0, jnp.where(row < 32, 1, jnp.where(lane < 64, 2, 3)))
    factors = jnp.zeros((GAIN_ROWS, 128), jnp.float32)
    for slot, count in enumerate((D, D, HEAD_DIM, HEAD_DIM)):
        mask = segment == slot
        spread = jnp.sqrt(total(jnp.where(mask, unit * unit, 0.0)) / count)
        mean = total(jnp.where(mask, old * old, 0.0)) / count
        scale = STEP_RATE * jnp.maximum(SCALE_EPSILON, jnp.sqrt(mean))
        factors = jnp.where(mask, scale / jnp.maximum(1.0, spread / CLIP_LEVEL), factors)
        out = jnp.where(lanes == 4 + slot, spread, out)
    gains_new[...] = old - factors * unit
    spreads[...] = out


def layer_kernel(
    tok, starts, rates, gain_attn, gain_ffn, gain_heads, gains, grad_out,
    m_qkv, m_out, m_down, m_gate_up, rows, col_moments, gain_moments,
    out_sum, grad_tok, g_qkv, gate_up_came, out_came, down_came, rows_new, row_factors,
    cols_new, col_factors, moments_new, gains_new, grad_gains, spreads,
    gate_up_in, gate_up_mid, kept_tok,
    projected, queries, keys_values, attended, cosines, sines,
    wq_send, normed, all_tok, all_wq, all_wo, partial, from_partner, came,
    hidden_in, all_norm, all_out, all_wg, wd, hidden, d_gate_up,
    d_queries, d_keys_values, qkv_in, d_hidden_in, gain_part, gain_part2, gain_qk, weight_sums, qkv_came,
    packed, plane_came, plane_sum, line_came, line_sum, line_all, totals, credit, *sems,
):
    half, full = jnp.bfloat16, jnp.float32
    chip, core, z = here()
    others = flips(chip)
    other = 1 - core
    me = 2 * chip + core
    partner = at_place(chip, other, z)
    plane = [at_place(peer_chip, core, z) for peer_chip in others]
    plane_cross = [at_place(peer_chip, other, z) for peer_chip in others]
    steps = (2, 1, 3)
    line = [at_place(chip, core, ahead(z, step)) for step in steps]
    cross = [at_place(chip, other, ahead(z, step)) for step in steps]
    everyone = [partner] + plane + plane_cross
    greet(everyone + line + cross)
    move = Mover(*sems)

    for head in range(8):
        wq_send[head, :, pl.ds(0, 256)] = m_qkv[:, pl.ds(head * 256, 256)].astype(half)
    low = lower_half((64, 128))
    for pair in range(4):
        keys = m_qkv[:, pl.ds(2048 + pair * 128, 128)]
        values = m_qkv[:, pl.ds(2560 + pair * 128, 128)]
        tail = pl.ds(256, 128)
        wq_send[2 * pair, :, tail] = jnp.where(low, keys, pltpu.roll(values, 64, 1)).astype(half)
        wq_send[2 * pair + 1, :, tail] = jnp.where(low, pltpu.roll(keys, 64, 1), values).astype(half)
    heads = [move.keep(wq_send.at[me], all_wq.at[me, z])]
    for peer in everyone:
        heads.append(move.send(wq_send.at[peer[0]], all_wq.at[me, z], peer))

    for row in range(2):

        def body0(part):
            result = tok[row, part].astype(full)
            scale = lax.rsqrt(jnp.mean(result * result, axis=-1, keepdims=True) + EPSILON)
            normed[row, part] = (result * scale * gain_attn[...]).astype(half)

        chunks(64, body0)
    token_copies = [move.send(normed, all_tok.at[me], peer) for peer in plane]
    token_copies.append(move.send(normed, all_tok.at[me], partner))
    tokens_here = move.keep(normed, all_tok.at[me])
    move.arrive(*heads)
    line_wq = move.line(all_wq.at[:, z], lambda at: all_wq.at[:, at], chip, core, z)
    flat_d = d_gate_up.reshape(1024, 2048)
    weight_sums[...] = jnp.zeros_like(weight_sums)

    def cast_all(slot, blocks):
        loads = [move.keep(blocks[0][0], hidden_in.at[0])]
        for index, (_, target) in enumerate(blocks):
            if index + 1 < len(blocks):
                loads.append(move.keep(blocks[index + 1][0], hidden_in.at[(index + 1) % 2]))
            move.arrive(loads[index])

            def body(part, index=index, target=target):
                entries = hidden_in[index % 2, part]
                weight_sums[slot] += jnp.sum(entries * entries, axis=0, keepdims=True)
                target[part] = entries.astype(half)

            chunks(64, body)

    cast_all(1, [(m_out, all_wo.at[z])])
    wo_copies = [move.send(all_wo.at[z], all_wo.at[z], peer) for peer in line]
    cast_all(
        3, [(m_down.at[pl.ds(64 * block, 64)], wd.at[chip, pl.ds(64 * block, 64)]) for block in range(4)]
    )
    down_copies = [move.send(wd.at[chip], wd.at[chip], peer) for peer in plane]
    move.arrive_line(line_wq, 3)
    move.arrive_line(line_wq, 1)
    cast_all(
        2,
        [
            (m_gate_up.at[:, pl.ds(2048 * block, 2048)], flat_d.at[pl.ds(64 * block, 64)])
            for block in range(8)
        ],
    )
    move.arrive_line(line_wq, 2)

    def turn_block(to_core, to_z):
        whole = all_wg.at[chip, core, z]
        pairs = []
        for index, (_, dst) in enumerate(segments(to_core, to_z)):
            begin = (((index % 4) * 2 + to_core) * 4 + to_z) * 256
            strip = 4 * (index // 4) + lax.div(begin, 2048)
            src = flat_d.at[wide(strip * 64, 64), wide(lax.rem(begin, 2048), 256)]
            pairs.append((src, whole.at[:, dst]))
        return pairs, (whole, whole)

    turned = []
    for step, peer, peer_cross in zip(steps, line, cross):
        to = ahead(z, step)
        turned.append(move.send_parts(*turn_block(core, to), peer))
        turned.append(move.send_parts(*turn_block(other, to), peer_cross))
    turned.append(move.send_parts(*turn_block(other, z), partner))
    turned_own = move.keep_parts(*turn_block(core, z))
    line_grads = move.line(grad_out, lambda at: all_out.at[at, core], chip, core, z)
    own = [
        move.keep(grad_out, all_out.at[z, core]),
        move.send(grad_out, all_out.at[z, core], partner),
    ]

    @pl.loop(0, 8)
    def _(block):
        for row in range(2):
            place = lax.broadcasted_iota(jnp.int32, (64, 1), 0) + block * 64
            offset = (place - document_start(starts, row, place)).astype(full)
            angle = offset * rates[0:1]
            cosines[block, row] = jnp.cos(angle)
            sines[block, row] = jnp.sin(angle) * rates[1:2]

    for peer_chip, handle in zip(others, tuple(token_copies)):
        move.arrive(handle)
        block = all_tok.at[2 * peer_chip + core]
        token_copies.append(move.send(block, block, partner))
    move.arrive(tokens_here, *token_copies, *wo_copies)
    saved = [move.keep(all_tok, kept_tok)]

    flat_tok, flat_wq = all_tok.reshape(1024, D), all_wq.reshape(D, 384)
    flat_wo = all_wo.reshape(256, D)

    @pl.loop(0, 4)
    def _(step):
        block = plain(flat_tok[wide(step * 256, 256)], flat_wq[...])
        projected[wide(step * 2, 2)] = block.reshape(2, 2, 64, 384)

    @pl.loop(0, 8)
    def _(block):
        for row in range(2):
            cosine, sine = cosines[block, row], sines[block, row]
            places = wide(block * 64, 64)
            for tile in range(3):
                entries = projected[block, row, :, pl.ds(tile * 128, 128)]
                gain = gain_heads[min(tile, 2) // 2 : min(tile, 2) // 2 + 1]
                scale = lax.rsqrt(head_means(entries * entries) + EPSILON)
                turned_entries = entries * scale * gain
                turned_entries = turned_entries * cosine + swap_halves(turned_entries) * sine
                if tile < 2:
                    queries[row, tile, places] = (turned_entries * HEAD_DIM ** (-0.5)).astype(half)
                else:
                    zero = jnp.zeros_like(entries)
                    rolled = pltpu.roll(turned_entries, 64, 1)
                    values = pltpu.roll(entries, 64, 1)
                    keys_values[row, 0, places] = jnp.where(low, turned_entries, zero).astype(half)
                    keys_values[row, 1, places] = jnp.where(low, zero, rolled).astype(half)
                    keys_values[row, 2, places] = jnp.where(low, values, zero).astype(half)
                    keys_values[row, 3, places] = jnp.where(low, zero, entries).astype(half)

    def first_of(row, part):
        place = lax.broadcasted_iota(jnp.int32, (128, 1), 0) + part * 128
        return document_start(starts, row, place)

    @pl.loop(0, 2)
    def _(row):
        for tile in range(2):
            for part in range(4):
                own_places, upto = pl.ds(part * 128, 128), pl.ds(0, (part + 1) * 128)
                result = jnp.zeros((128, 128), full)
                for side in range(2):
                    probs = attention_probs(
                        queries[row, tile, own_places], keys_values[row, side, upto],
                        first_of(row, part), part,
                    )
                    result += plain(probs.astype(half), keys_values[row, 2 + side, upto])
                attended[pl.ds(2 * part, 2), row, :, pl.ds(tile * 128, 128)] = result.reshape(2, 64, 128)

    flat_attended = attended.reshape(1024, 256)

    @pl.loop(0, 4)
    def _(step):
        rows = flat_attended[wide(step * 256, 256)].astype(half)

        @pl.loop(0, 4)
        def _(col):
            cols = wide(col * 512, 512)
            block = plain(rows, flat_wo[:, cols])
            partial[wide(step * 2, 2), :, :, cols] = block.reshape(2, 2, 64, 512).astype(half)

    order = tuple(others) + (chip,)
    halves = [move.send(partial.at[2 * to + other], from_partner.at[to], partner) for to in order]
    sums = []
    for to, arrived, peer in zip(others, halves, plane):
        move.arrive(arrived)
        add_blocks(partial.at[2 * to + core], from_partner.at[to], from_partner.at[to])
        sums.append(move.send(from_partner.at[to], came.at[chip], peer))
    move.sent(*token_copies)
    move.arrive(halves[3], *sums)
    for row in range(2):

        def body(part):
            result = tok[row, part].astype(full)
            result += partial[me, row, part].astype(full)
            result += from_partner[chip, row, part].astype(full)
            for peer_chip in others:
                result += came[peer_chip, row, part].astype(full)
            hidden_in[row, part] = result
            scale = lax.rsqrt(jnp.mean(result * result, axis=-1, keepdims=True) + EPSILON)
            normed[row, part] = (result * scale * gain_ffn[...]).astype(half)

        chunks(64, body)
    move.sent(*sums, *halves)
    move.arrive(*saved)
    line_norms = move.line(normed, lambda at: all_norm.at[at, core], chip, core, z)
    own.append(move.send(normed, all_norm.at[z, core], partner))
    own.append(move.keep(normed, all_norm.at[z, core]))

    move.arrive(turned_own, *turned)
    by_x, by_y = plane[0], plane[1]
    front, back = all_wg.at[chip, 0], all_wg.at[chip, 1]
    from_x = move.send(front, front, by_x)
    from_y = move.send(back, back, by_y)
    weights = [from_x, from_y, move.send(back, back, by_x), move.send(front, front, by_y)]

    at_first, at_last = lax.div(3 - z, 3), lax.div(z, 3)
    arrivals = (3 - 2 * at_first, 1 + at_first + at_last, 2 + at_first - at_last)
    inner = (z > 0) & (z < 3)
    shared = []

    def share(step, wait_only=False):
        for line_of in (line_grads, line_norms):
            if wait_only:
                block = move.wait_line(line_of, step, jnp.logical_not(inner))
            else:
                block = move.arrive_line(line_of, step)
            shared.append(move.send(block, block, partner))

    share(arrivals[0])
    share(arrivals[1])
    move.arrive(from_x, from_y)
    front, back = all_wg.at[others[0], 0], all_wg.at[others[1], 1]
    weights += [move.send(front, front, by_y), move.send(back, back, by_x)]
    for line_of in (line_grads, line_norms):
        move.arrive_line(line_of, arrivals[2], inner)
    move.arrive(*weights, *own, *down_copies)
    move.sent(*turned)

    flat_wg, flat_wd = all_wg.reshape(D, 2048), wd.reshape(1024, D)

    def block_of(zb):
        @pl.loop(0, 4)
        def _(step):
            cols, ups = wide(step * 256, 256), wide(1024 + step * 256, 256)
            rows = all_norm[zb].reshape(256, D)
            gate = plain(rows, flat_wg[:, cols])
            up = plain(rows, flat_wg[:, ups])
            d_hidden = across(all_out[zb].reshape(256, D), flat_wd[cols])
            sigmoid = 1.0 / (1.0 + jnp.exp(-gate))
            silu = gate * sigmoid
            hidden[zb, :, cols] = (silu * up).astype(half)
            d_gate = d_hidden * up * (sigmoid * (1.0 + gate * (1.0 - sigmoid)))
            d_gate_up[zb, :, cols] = d_gate.astype(half)
            d_gate_up[zb, :, ups] = (d_hidden * silu).astype(half)

        @pl.loop(0, 8)
        def _(step):
            cols = wide(step * 256, 256)
            block = across(d_gate_up[zb], flat_wg[cols])
            partial[pl.ds(2 * zb, 2), :, :, cols] = block.reshape(2, 2, 64, 256).astype(half)

    def pair_sum(zb, handle, into, base):
        move.arrive(handle)
        add_blocks(partial.at[2 * zb + core], into.at[base + zb], into.at[base + zb])

    start_sum, wait_sums = move.scatter(
        lambda at: from_partner.at[at], lambda at: came.at[at], arrivals, chip, core, z
    )
    to_partner = []
    walk = [z] + [ahead(z, step) for step in arrivals]
    for index, zb in enumerate(walk):
        if index > 0:
            move.arrive(*shared[2 * index - 2 : 2 * index])
        block_of(zb)
        to_partner.append(move.send(partial.at[2 * zb + other], from_partner.at[zb], partner))
        if index == 0:
            share(arrivals[2], True)
        if index > 0:
            pair_sum(walk[index - 1], to_partner[index - 1], from_partner, 0)
        if index > 1:
            start_sum(index - 2)
    pair_sum(walk[3], to_partner[3], from_partner, 0)
    start_sum(2)

    flat_norm, flat_grads = all_norm.reshape(1024, D), all_out.reshape(1024, D)
    flat_hidden = hidden.reshape(1024, 1024)
    move.sent(*weights)

    def gate_up_grad(to, side):
        rows, lanes = wide(to * 512, 512), pl.ds(side * 1024, 1024)

        @pl.loop(0, 2)
        def _(step):
            cols = wide(side * 1024 + step * 512, 512)
            flat_wg[rows, cols] = down(flat_norm[:, rows], flat_d[:, cols]).astype(half)

        return flat_wg.at[rows, lanes]

    passed = []
    for side in (0, 1):
        passed.append(move.send(gate_up_grad(others[2], side), gate_up_mid.at[side], plane[side]))
    direct = [gate_up_grad(others[side], side) for side in (0, 1)]
    handed = [gate_up_grad(others[1 - side], side) for side in (0, 1)]
    for side in (0, 1):
        gate_up_grad(chip, side)
    move.sent(*shared, own[2])
    move.sent_lines()
    for peer in [partner] + plane:
        pl.semaphore_signal(credit, inc=1, device_id=peer, device_id_type=MESH)

    wait_sums()
    gain_part[...] = jnp.zeros_like(gain_part)
    for row in range(2):

        def body2(part):
            result = from_partner[z, row, part].astype(full)
            for step in steps:
                result += came[ahead(z, step), row, part].astype(full)
            entries = hidden_in[row, part]
            scale = lax.rsqrt(jnp.mean(entries * entries, axis=-1, keepdims=True) + EPSILON)
            gain_part[...] += jnp.sum(result * entries * scale, axis=0, keepdims=True)
            result = result * gain_ffn[...]
            inside = jnp.mean(result * entries, axis=-1, keepdims=True) * (scale * scale * scale)
            grad = grad_out[row, part].astype(full) + result * scale - entries * inside
            d_hidden_in[row, part] = grad
            normed[row, part] = grad.astype(half)

        chunks(64, body2)
    pl.semaphore_wait(credit, 4)
    move.sent_sums()
    all_branch = all_norm.reshape(8, 2, 64, D)
    branches = [move.send(normed, all_branch.at[me], peer) for peer in plane]
    branch_copies = [
        move.send(normed, all_branch.at[me], partner), move.keep(normed, all_branch.at[me])
    ]
    pieces = [
        move.send(direct[side], gate_up_in.at[side, 0], plane[side]) for side in (0, 1)
    ]

    move.sent(*to_partner)
    to_partner, sums = [], []
    walk = [ahead(z, step) for step in steps] + [z]
    for index, zb in enumerate(walk):

        @pl.loop(0, 4)
        def _(step, zb=zb):
            cols = wide(step * 512, 512)
            block = plain(hidden[zb], flat_wd[:, cols])
            partial[pl.ds(2 * zb, 2), :, :, cols] = block.reshape(2, 2, 64, 512).astype(half)

        to_partner.append(move.send(partial.at[2 * zb + other], all_tok.at[zb], partner))
        if index > 0:
            before = walk[index - 1]
            pair_sum(before, to_partner[index - 1], all_tok, 0)
            sums.append(move.send(all_tok.at[before], all_tok.at[4 + z], line[index - 1]))
    pair_sum(z, to_partner[3], all_tok, 0)

    move.sent(*down_copies, *wo_copies)

    @pl.loop(0, 4)
    def _(to):
        rows_at = wide(to * 256, 256)

        @pl.loop(0, 4)
        def _(step):
            cols = wide(step * 512, 512)
            flat_wd[rows_at, cols] = down(flat_hidden[:, rows_at], flat_grads[:, cols]).astype(half)

    load_tok = move.keep(kept_tok, all_out.reshape(8, 2, 64, D))

    def load(source):
        return [
            move.keep(source(side), flat_d.at[pl.ds(side * 512, 512), pl.ds(0, 1024)])
            for side in (0, 1)
        ]

    def add_loaded(side, chunk):
        @pl.loop(0, 512 // CHUNK)
        def _(step):
            lanes = pl.ds(side * 1024, 1024)
            rows = wide(chunk * 512 + step * CHUNK, CHUNK)
            extra = flat_d[wide(side * 512 + step * CHUNK, CHUNK), pl.ds(0, 1024)]
            result = flat_wg[rows, lanes].astype(full) + extra.astype(full)
            flat_wg[rows, lanes] = result.astype(half)

    move.arrive(*passed)
    loads = load(lambda side: gate_up_mid.at[side])
    later = []
    for side in (0, 1):
        move.arrive(loads[side])
        add_loaded(side, others[1 - side])
        later.append(move.send(handed[side], gate_up_in.at[side, 1], plane[1 - side]))
    for peer_chip, handle in zip(others, branches):
        move.arrive(handle)
        block = all_branch.at[2 * peer_chip + core]
        branch_copies.append(move.send(block, block, partner))
    move.arrive(*branch_copies)

    flat_branch = all_branch.reshape(1024, D)
    flat_wo = all_wo.reshape(256, D)
    d_heads_at, d_projected_at = pl.ds(0, 256), pl.ds(256, 384)

    @pl.loop(0, 4)
    def _(step):
        rows = wide(step * 256, 256)
        flat_hidden[rows, d_heads_at] = across(flat_branch[rows], flat_wo[...]).astype(half)

    @pl.loop(0, 4)
    def _(step):
        cols = wide(step * 512, 512)
        block = down(flat_attended[...].astype(half), flat_branch[:, cols])
        flat_wo[:, cols] = block.astype(half)

    outs = [
        move.send(all_wo.at[ahead(z, step)], out_came.at[z], peer) for step, peer in zip(steps, line)
    ]
    outs.append(move.keep(all_wo.at[z], out_came.at[z]))
    lower = lower_half((128, 128))
    line_low = lower_half((1, 128))
    gain_qk[...] = jnp.zeros_like(gain_qk)

    @pl.loop(0, 2)
    def _(row):
        d_keys_values[...] = jnp.zeros_like(d_keys_values)

        def token_rows(block):
            return wide((2 * block + row) * 64, 64)

        for tile in range(2):
            lanes = pl.ds(tile * 128, 128)
            for part in range(4):
                own_places, upto = pl.ds(part * 128, 128), pl.ds(0, (part + 1) * 128)
                d_heads = jnp.concatenate(
                    [flat_hidden[token_rows(2 * part + index), lanes] for index in range(2)], axis=0
                )
                products = d_heads.astype(full) * attended[pl.ds(2 * part, 2), row, :, lanes].reshape(128, 128)
                query = queries[row, tile, own_places]
                result = jnp.zeros((128, 128), full)
                for side in range(2):
                    mask = lower if side == 0 else jnp.logical_not(lower)
                    delta = jnp.sum(jnp.where(mask, products, 0.0), axis=-1, keepdims=True)
                    keys = keys_values[row, side, upto]
                    probs = attention_probs(query, keys, first_of(row, part), part)
                    d_probs = across(d_heads, keys_values[row, 2 + side, upto])
                    d_scores = (probs * (d_probs - delta)).astype(half)
                    result += plain(d_scores, keys)
                    d_keys_values[side, upto] += down(d_scores, query)
                    d_keys_values[2 + side, upto] += down(probs.astype(half), d_heads)
                d_queries[tile, own_places] = result

        @pl.loop(0, 8)
        def _(block):
            cosine, sine = cosines[block, row], sines[block, row]
            places = wide(block * 64, 64)
            for tile in range(3):
                entries = projected[block, row, :, pl.ds(tile * 128, 128)]
                gain = gain_heads[tile // 2 : tile // 2 + 1]
                scale = lax.rsqrt(head_means(entries * entries) + EPSILON)
                if tile < 2:
                    grad = d_queries[tile, places] * HEAD_DIM ** (-0.5)
                else:
                    from_low, from_high = d_keys_values[0, places], d_keys_values[1, places]
                    grad = jnp.where(low, from_low + pltpu.roll(from_high, 64, 1), 0.0)
                grad = grad * cosine + swap_halves(grad * sine)
                for_gain = jnp.sum(grad * entries * scale, axis=0, keepdims=True)
                if tile < 2:
                    for_gain = jnp.where(line_low, for_gain + pltpu.roll(for_gain, 64, 1), 0.0)
                else:
                    for_gain = jnp.where(line_low, 0.0, pltpu.roll(for_gain, 64, 1))
                gain_qk[...] += for_gain
                grad = grad * gain
                inside = head_means(grad * entries) * (scale * scale * scale)
                grad = grad * scale - entries * inside
                if tile == 2:
                    values = pltpu.roll(d_keys_values[2, places], 64, 1)
                    grad = jnp.where(low, grad, values + d_keys_values[3, places])
                flat_hidden[token_rows(block), pl.ds(256 + tile * 128, 128)] = grad.astype(half)

    move.sent(*to_partner)

    @pl.loop(0, 4)
    def _(step):
        rows = flat_hidden[wide(step * 256, 256), d_projected_at]

        @pl.loop(0, 4)
        def _(col):
            cols = wide(col * 512, 512)
            block = across(rows, flat_wq[cols])
            partial[wide(step * 2, 2), :, :, cols] = block.reshape(2, 2, 64, 512).astype(half)

    halves = [move.send(partial.at[2 * to + other], from_partner.at[to], partner) for to in order]
    move.arrive(load_tok)

    for block in range(4):
        strip = pl.ds(1024 + 384 * (block // 2), 384)
        product = down(
            flat_grads[:, pl.ds(block * 512, 512)], flat_hidden[:, d_projected_at]
        )
        flat_d[pl.ds(512 * (block % 2), 512), strip] = product.astype(half)

    def head_block(head, at):
        rows = wide(((head % 4) * 4 + at) * 64, 64)
        return flat_d.at[rows, pl.ds(1024 + 384 * (head // 4), 384)]

    qkv_pieces = []
    for step, peer in zip(steps, line):
        pairs = [(head_block(head, ahead(z, step)), qkv_in.at[z, head]) for head in range(8)]
        qkv_pieces.append(move.send_parts(pairs, (qkv_in.at[z], qkv_in.at[z]), peer))
    d_norms = []
    for to, arrived, peer in zip(others, halves, plane):
        move.arrive(arrived)
        add_blocks(partial.at[2 * to + core], from_partner.at[to], from_partner.at[to])
        d_norms.append(move.send(from_partner.at[to], came.at[chip], peer))
    downs = [move.send(wd.at[to], down_came.at[chip], peer) for to, peer in zip(others, plane)]
    downs.append(move.keep(wd.at[chip], down_came.at[chip]))
    move.arrive(halves[3])
    add_blocks(partial.at[me], from_partner.at[chip], from_partner.at[chip])

    for slot, handles in ((0, pieces), (1, later)):
        move.arrive(*handles)
        loads = load(lambda side, slot=slot: gate_up_in.at[side, slot])
        for side in (0, 1):
            move.arrive(loads[side])
            add_loaded(side, chip)

    def back_block(to_core, to_z):
        whole = all_wg.at[chip, to_core, to_z]
        pairs = [(whole.at[:, src], gate_up_came.at[:, dst]) for dst, src in segments(core, z)]
        return pairs, (whole, whole)

    gate_ups = []
    for step, peer, peer_cross in zip(steps, line, cross):
        to = ahead(z, step)
        gate_ups.append(move.send_parts(*back_block(core, to), peer))
        gate_ups.append(move.send_parts(*back_block(other, to), peer_cross))
    gate_ups.append(move.send_parts(*back_block(other, z), partner))
    gate_ups.append(move.keep_parts(*back_block(core, z)))

    move.arrive(*sums)
    for row in range(2):

        def body3(part):
            result = hidden_in[row, part] + all_tok[z, row, part].astype(full)
            for step in steps:
                result += all_tok[4 + ahead(z, step), row, part].astype(full)
            out_sum[row, part] = result.astype(half)

        chunks(64, body3)

    move.arrive(*d_norms)
    gain_part2[...] = jnp.zeros_like(gain_part2)
    for row in range(2):

        def body4(part):
            result = from_partner[chip, row, part].astype(full)
            for peer_chip in others:
                result += came[peer_chip, row, part].astype(full)
            entries = tok[row, part].astype(full)
            scale = lax.rsqrt(jnp.mean(entries * entries, axis=-1, keepdims=True) + EPSILON)
            gain_part2[...] += jnp.sum(result * entries * scale, axis=0, keepdims=True)
            result = result * gain_attn[...]
            inside = jnp.mean(result * entries, axis=-1, keepdims=True) * (scale * scale * scale)
            result = d_hidden_in[row, part] + result * scale - entries * inside
            grad_tok[row, part] = result.astype(half)

        chunks(64, body4)

    def send_heads():
        move.arrive(*qkv_pieces)
        move.sent(*heads[1:])
        for head in range(8):
            result = head_block(head, z)[...].astype(full)
            for step in steps:
                result += qkv_in[ahead(z, step), head].astype(full)
            wq_send[head] = result.astype(half)
        copies = [move.send(wq_send.at[peer[0]], qkv_came.at[me], peer) for peer in everyone]
        return copies + [move.keep(wq_send.at[me], qkv_came.at[me])]

    flat_packed = packed.reshape(512, 128)
    first = 2 * COL_ROWS
    line_lanes = lax.broadcasted_iota(jnp.int32, (1, 128), 1)
    flat_packed[pl.ds(first + 33, 512 - first - 33)] = jnp.zeros((512 - first - 33, 128), full)

    def statistics(slot, read):
        count, width, row_at, col_at = MATRICES[slot]
        own_rows, some = pl.ds(row_at, count), pl.ds(0, count)
        d_queries[0, some] = jnp.zeros((count, 128), full)

        @pl.loop(0, width // 128)
        def _(step):
            entries = read(step)
            d_queries[0, some] += entries * entries

        mean = jnp.sum(d_queries[0, some], axis=-1, keepdims=True) / width + SQUARE_EPSILON
        new = BETA * rows[own_rows] + (1.0 - BETA) * mean
        rows_new[own_rows] = new
        row_factors[own_rows] = lax.rsqrt(new)
        d_keys_values[0, some] = jnp.broadcast_to(1.0 / new, (count, 128))

        @pl.loop(0, width // 128)
        def _(step):
            entries = read(step)
            square = entries * entries
            flat_packed[pl.ds(col_at + step, 1)] = (
                jnp.sum(square, axis=0, keepdims=True) + count * SQUARE_EPSILON
            )
            flat_packed[pl.ds(COL_ROWS + col_at + step, 1)] = jnp.sum(
                square * d_keys_values[0, some], axis=0, keepdims=True
            )

        stats = flat_packed[pl.ds(first + 33, 1)]
        stats = jnp.where(line_lanes == slot, jnp.sum(new, axis=0, keepdims=True), stats)
        stats = jnp.where(line_lanes == 4 + slot, total(weight_sums[slot]), stats)
        flat_packed[pl.ds(first + 33, 1)] = stats

    def lanes_of(step):
        return wide(step * 128, 128)

    def four(buffer):
        def read(step):
            result = buffer[0, :, lanes_of(step)].astype(full)
            for slot in range(1, 4):
                result += buffer[slot, :, lanes_of(step)].astype(full)
            return result

        return read

    out_here, down_here = all_out.reshape(16, 64, D), all_norm.reshape(4, 256, D)
    move.arrive(*outs)
    out_load = move.keep(out_came, out_here.at[pl.ds(0, 4)])
    qkv_copies = send_heads()
    move.arrive(*downs)
    move.sent(*branch_copies[2:])
    down_load = move.keep(down_came, down_here)
    move.arrive(out_load)
    statistics(1, four(out_here))
    move.arrive(down_load)
    statistics(3, four(down_here))

    move.arrive(*qkv_copies)
    for head in range(8):
        for part in range(2):
            strip = qkv_came[head, :, pl.ds(part * 128, 128)]
            g_qkv[:, pl.ds(head * 256 + part * 128, 128)] = strip.astype(full)
    for pair in range(4):
        keys = qkv_came[2 * pair, :, pl.ds(256, 128)].astype(full)
        values = qkv_came[2 * pair + 1, :, pl.ds(256, 128)].astype(full)
        g_qkv[:, pl.ds(2048 + pair * 128, 128)] = jnp.where(low, keys, pltpu.roll(values, 64, 1))
        g_qkv[:, pl.ds(2560 + pair * 128, 128)] = jnp.where(low, pltpu.roll(keys, 64, 1), values)

    @pl.loop(0, QKV // 128)
    def _(step):
        entries = m_qkv[:, lanes_of(step)]
        weight_sums[0, :, pl.ds(0, 128)] += jnp.sum(entries * entries, axis=0, keepdims=True)

    statistics(0, lambda step: g_qkv[:, lanes_of(step)])
    for slot in range(16):
        strip = pl.ds(slot * 128, 128)
        flat_packed[pl.ds(first + slot, 1)] = gain_part2[:, strip]
        flat_packed[pl.ds(first + 16 + slot, 1)] = gain_part[:, strip]
    flat_packed[pl.ds(first + 32, 1)] = gain_qk[...]

    move.arrive(*gate_ups)
    move.sent(*qkv_pieces)
    gate_up_load = move.keep_parts(
        [
            (gate_up_came.at[:, pl.ds(2048 * block, 2048)], flat_d.at[pl.ds(64 * block, 64)])
            for block in range(8)
        ],
        (flat_d.at[pl.ds(0, 512)], flat_d.at[pl.ds(0, 512)]),
    )
    move.arrive(gate_up_load)

    def read_gate_up(step):
        return flat_d[wide(lax.div(step, 16) * 64, 64), lanes_of(lax.rem(step, 16))].astype(full)

    statistics(2, read_gate_up)

    copies = [move.send(packed.at[peer[0]], plane_came.at[me], peer) for peer in everyone]
    plane_came[me] = packed[me]
    move.arrive(*copies)
    result = plane_came[0]
    for slot in range(1, 8):
        result = result + plane_came[slot]
    plane_sum[...] = result
    copies = [move.send(plane_sum.at[peer[1]], line_came.at[z], peer) for peer in line]
    line_came[z] = plane_sum[z]
    move.arrive(*copies)
    line_sum[...] = line_came[0] + line_came[1] + line_came[2] + line_came[3]
    copies = [move.send(line_sum, line_all.at[z], peer) for peer in line]
    line_all[z] = line_sum[...]
    move.arrive(*copies)
    copies = [move.send(line_all, totals.at[me], peer) for peer in everyone]
    totals[me] = line_all[...]
    move.arrive(*copies)
    derive_updates(
        totals.reshape(512, 128), col_moments, gain_moments, gains,
        cols_new, col_factors, moments_new, gains_new, grad_gains, spreads,
    )
    move.finish()


def split_local(
    tokens, doc_starts, grad_out, qkv_master, out_master, gate_up_master, down_master, gains,
    qkv_rows, out_rows, gate_up_rows, down_rows, col_moments, gain_moments,
):
    half, full = jnp.bfloat16, jnp.float32
    gain_query, gain_key = gains[2 * D : 2 * D + HEAD_DIM], gains[2 * D + HEAD_DIM :]
    gain_heads = jnp.stack(
        [jnp.concatenate([gain_query, gain_query]), jnp.concatenate([gain_key, gain_key])]
    )
    lane = jnp.arange(128)
    rates = ROPE_BASE ** (-((lane % 32).astype(full) * 2.0 / HEAD_DIM))
    rates = jnp.stack([rates, jnp.where(lane % 64 < 32, -1.0, 1.0)])

    def near(*shape, kind=half):
        return pltpu.VMEM(shape, kind)

    masters = (qkv_master, out_master, gate_up_master, down_master)
    stats_shape = (8, 4, 16, 128)
    (
        output, grad_tokens, grad_qkv, gate_up_came, out_came, down_came, rows_new, row_factors,
        cols_new, col_factors, moments_new, gains_new, grad_gains, spreads, *_,
    ) = exchange(
        layer_kernel, 0,
        [
            (tokens, True), (doc_starts, None), (rates, True), (gains[None, :D], True),
            (gains[None, D : 2 * D], True), (gain_heads, True), (gains.reshape(-1, 128), True),
            (grad_out, True), (qkv_master, True), (out_master, False), (down_master, False),
            (gate_up_master, False),
            (jnp.concatenate([qkv_rows, out_rows, gate_up_rows, down_rows])[:, None], True),
            (col_moments.reshape(-1, 128), True), (gain_moments.reshape(-1, 128), True),
        ],
        [
            ((2, 64, D), half, True), ((2, 64, D), half, True), ((64, QKV), full, True),
            ((64, 2 * FF), half, False), ((4, 64, D), half, False), ((4, 256, D), half, False),
            ((448, 1), full, True), ((448, 1), full, True),
            ((COL_ROWS, 128), full, True), ((1, COLS), full, True),
            ((GAIN_ROWS, 128), full, True), ((GAIN_ROWS, 128), full, True),
            ((GAIN_ROWS, 128), full, True), ((1, 128), full, True),
            ((2, 2, 512, 1024), half, False), ((2, 512, 1024), half, False),
            ((8, 2, 64, D), half, False),
        ],
        [
            near(8, 2, 64, 384, kind=full), near(2, 2, 512, 128), near(2, 4, 512, 128),
            near(8, 2, 64, 256, kind=full), near(8, 2, 64, 128, kind=full),
            near(8, 2, 64, 128, kind=full),
            near(8, 64, 384), near(2, 64, D), near(8, 2, 64, D), near(8, 4, 64, 384), near(4, 64, D),
            near(8, 2, 64, D), near(4, 2, 64, D), near(4, 2, 64, D), near(2, 64, D, kind=full),
            near(4, 2, 2, 64, D), near(4, 2, 2, 64, D), near(4, 2, 4, 64, 2048), near(4, 256, D),
            near(4, 256, 1024), near(4, 256, 2048),
            near(2, 512, 128, kind=full), near(4, 512, 128, kind=full), near(4, 8, 64, 384),
            near(2, 64, D, kind=full), near(1, D, kind=full), near(1, D, kind=full),
            near(1, 128, kind=full), near(4, 1, D, kind=full), near(8, 64, 384),
            near(*stats_shape, kind=full), near(*stats_shape, kind=full),
            near(*stats_shape[1:], kind=full), near(*stats_shape[1:], kind=full),
            near(*stats_shape[2:], kind=full), near(*stats_shape[1:], kind=full),
            near(*stats_shape, kind=full),
            pltpu.SemaphoreType.REGULAR,
        ],
        (150, 48), 170 << 20, 48 << 30,
    )
    grads = (
        grad_qkv, jnp.sum(out_came.astype(full), axis=0), gate_up_came.astype(full),
        jnp.sum(down_came.astype(full), axis=0),
    )
    new_masters = []
    for slot, (count, width, row_at, col_at) in enumerate(MATRICES):
        row_factor = row_factors[row_at : row_at + count]
        col_factor = col_factors[:, col_at * 128 : col_at * 128 + width]
        new_masters.append(masters[slot] - grads[slot] * row_factor * col_factor)
    return (
        output,
        grad_tokens,
        *grads,
        grad_gains.reshape(-1),
        *[rows_new[row_at : row_at + count, 0] for count, _, row_at, _ in MATRICES],
        cols_new.reshape(-1),
        moments_new.reshape(-1),
        *new_masters,
        *[master.astype(half) for master in new_masters],
        gains_new.reshape(-1),
        spreads[0, :8],
    )


def optimizer_step(
    grads, gain_local, masters, gains, row_states, col_moments, gain_moments, total_fn
):
    beta = 1.0 - STEP ** (-0.8)
    col_widths = (QKV, D, 2 * FF, D)
    row_totals = (D, HEADS * HEAD_DIM, D, FF)
    squares = [gradient * gradient + SQUARE_EPSILON for gradient in grads]
    rows_new = [
        beta * row_state + (1.0 - beta) * jnp.mean(square, axis=1)
        for row_state, square in zip(row_states, squares)
    ]
    col_local = [jnp.sum(square, axis=0) for square in squares]
    weighted_local = [
        jnp.sum(gradient * gradient / row_new[:, None], axis=0)
        for gradient, row_new in zip(grads, rows_new)
    ]
    stats_local = jnp.stack(
        [jnp.sum(row_new) for row_new in rows_new]
        + [jnp.sum(master * master) for master in masters]
    )
    totals = total_fn(jnp.concatenate(col_local + weighted_local + [stats_local, gain_local]))
    cols = sum(col_widths)
    col_sums, weighted = totals[:cols], totals[cols : 2 * cols]
    stats, grad_gains = totals[2 * cols : 2 * cols + 8], totals[2 * cols + 8 :]
    col_divisor = jnp.concatenate(
        [
            jnp.full((col_width,), float(row_total), jnp.float32)
            for col_width, row_total in zip(col_widths, row_totals)
        ]
    )
    cols_new = beta * col_moments + (1.0 - beta) * col_sums / col_divisor
    new_masters = []
    spreads = []
    begin_at = 0
    for slot in range(4):
        col_part = cols_new[begin_at : begin_at + col_widths[slot]]
        weighted_part = weighted[begin_at : begin_at + col_widths[slot]]
        begin_at = begin_at + col_widths[slot]
        mean_rows = stats[slot] / row_totals[slot]
        unit = (
            grads[slot]
            * lax.rsqrt(rows_new[slot] / mean_rows)[:, None]
            * lax.rsqrt(col_part)[None, :]
        )
        entries_all = float(row_totals[slot] * col_widths[slot])
        spread = jnp.sqrt(mean_rows * jnp.sum(weighted_part / col_part) / entries_all)
        scale = STEP_RATE * jnp.maximum(SCALE_EPSILON, jnp.sqrt(stats[4 + slot] / entries_all))
        new_masters.append(masters[slot] - scale * unit / jnp.maximum(1.0, spread / CLIP_LEVEL))
        spreads.append(spread)
    bounds = (0, D, 2 * D, 2 * D + HEAD_DIM, 2 * D + 2 * HEAD_DIM)
    moment_parts, gain_parts = ([], [])
    for segment in range(4):
        gradient = grad_gains[bounds[segment] : bounds[segment + 1]]
        gain_old = gains[bounds[segment] : bounds[segment + 1]]
        moment_new = beta * gain_moments[bounds[segment] : bounds[segment + 1]] + (1.0 - beta) * (
            gradient * gradient + SQUARE_EPSILON
        )
        unit = gradient * lax.rsqrt(moment_new)
        spread = jnp.sqrt(jnp.mean(unit * unit))
        scale = STEP_RATE * jnp.maximum(SCALE_EPSILON, jnp.sqrt(jnp.mean(gain_old * gain_old)))
        moment_parts.append(moment_new)
        gain_parts.append(gain_old - scale * unit / jnp.maximum(1.0, spread / CLIP_LEVEL))
        spreads.append(spread)
    return (
        grad_gains,
        *rows_new,
        cols_new,
        jnp.concatenate(moment_parts),
        *new_masters,
        *[master.astype(jnp.bfloat16) for master in new_masters],
        jnp.concatenate(gain_parts),
        jnp.stack(spreads),
    )


def solution(mesh):
    split = mesh.shape["seq"] == 8 and mesh.shape["rows"] == 4
    return jax.shard_map(
        split_local if split else gathered_local,
        mesh=mesh,
        in_specs=(
            P("rows", "seq", None),
            P("rows", None),
            P("rows", "seq", None),
            P(("seq", "rows"), None),
            P(("seq", "rows"), None),
            P(("seq", "rows"), None),
            P(("seq", "rows"), None),
            P(),
            P(("seq", "rows")),
            P(("seq", "rows")),
            P(("seq", "rows")),
            P(("seq", "rows")),
            P(),
            P(),
        ),
        out_specs=(
            P("rows", "seq", None),
            P("rows", "seq", None),
            P(("seq", "rows"), None),
            P(("seq", "rows"), None),
            P(("seq", "rows"), None),
            P(("seq", "rows"), None),
            P(),
            P(("seq", "rows")),
            P(("seq", "rows")),
            P(("seq", "rows")),
            P(("seq", "rows")),
            P(),
            P(),
            P(("seq", "rows"), None),
            P(("seq", "rows"), None),
            P(("seq", "rows"), None),
            P(("seq", "rows"), None),
            P(("seq", "rows"), None),
            P(("seq", "rows"), None),
            P(("seq", "rows"), None),
            P(("seq", "rows"), None),
            P(),
            P(),
        ),
        check_vma=False,
    )
```

```python
from functools import partial

import jax
import jax.numpy as jnp
import numpy as np
from jax import lax
from jax.experimental import pallas as pl
from jax.experimental.pallas import tpu as pltpu
from jax.sharding import PartitionSpec as P

D = 2048
HEADS = 32
KV_HEADS = 8
HEAD_DIM = 64
FF = 8192
STEP = 10
QKV = 3072


EPSILON = 1e-06
ROPE_BASE = 10000.0
MASKED_SCORE = -1e30
STEP_RATE = 0.3
CLIP_LEVEL = 1.0
SQUARE_EPSILON = 1e-30
SCALE_EPSILON = 0.001


def from_behind(value, axis, steps):
    count = lax.axis_size(axis)
    pairs = [(source, (source + steps) % count) for source in range(count)]
    return lax.ppermute(value, axis, pairs)


def norm_rows(entries, gain):
    return entries * lax.rsqrt(jnp.mean(entries * entries, axis=-1, keepdims=True) + EPSILON) * gain


def turn(entries, cos_wide, sin_wide):
    half_width = entries.shape[-1] // 2
    turned = jnp.concatenate([-entries[..., half_width:], entries[..., :half_width]], axis=-1)
    return entries * cos_wide + turned * sin_wide


def doc_tables(doc_starts, places):
    before = doc_starts[:, None, :] <= places[None, :, None]
    doc_ids = jnp.sum(before.astype(jnp.int32), axis=-1)
    doc_first = jnp.max(jnp.where(before, doc_starts[:, None, :], 0), axis=-1)
    return (doc_ids, places[None, :] - doc_first)


def rotary(offsets):
    frequency = ROPE_BASE ** (-(jnp.arange(HEAD_DIM // 2, dtype=jnp.float32) * 2.0 / HEAD_DIM))
    angles = offsets.astype(jnp.float32)[..., None] * frequency
    cos_table = jnp.concatenate([jnp.cos(angles), jnp.cos(angles)], axis=-1)
    sin_table = jnp.concatenate([jnp.sin(angles), jnp.sin(angles)], axis=-1)
    return (cos_table, sin_table)


def queries_keys(
    cos_table, sin_table, projected, gain_query, gain_key, heads=HEADS, kv_heads=KV_HEADS
):
    rows_here, seq_here = (projected.shape[0], projected.shape[1])
    att_width = heads * HEAD_DIM
    queries = projected[..., :att_width].reshape(rows_here, seq_here, heads, HEAD_DIM)
    keys_rot = projected[..., att_width : att_width + kv_heads * HEAD_DIM].reshape(
        rows_here, seq_here, kv_heads, HEAD_DIM
    )
    cos_wide = cos_table[:, :, None, :]
    sin_wide = sin_table[:, :, None, :]
    queries = turn(norm_rows(queries, gain_query), cos_wide, sin_wide) * HEAD_DIM ** (-0.5)
    keys_rot = turn(norm_rows(keys_rot, gain_key), cos_wide, sin_wide)
    return (queries, keys_rot)


def mask_of(query_docs, query_places, key_docs, key_places):
    same_doc = query_docs[:, :, None] == key_docs[:, None, :]
    causal = query_places[None, :, None] >= key_places[None, None, :]
    return (same_doc & causal)[:, None, None, :, :]


def gathered_local(
    tokens,
    doc_starts,
    grad_out,
    qkv_master,
    out_master,
    gate_up_master,
    down_master,
    gains,
    qkv_rows,
    out_rows,
    gate_up_rows,
    down_rows,
    col_moments,
    gain_moments,
):
    cycle_size = lax.axis_size("seq")
    seq_index = lax.axis_index("seq")
    rows_dev, seq_dev = (tokens.shape[0], tokens.shape[1])
    group_size = HEADS // KV_HEADS
    att_width = HEADS * HEAD_DIM
    kv_width = KV_HEADS * HEAD_DIM
    gain_attn = gains[:D]
    gain_ffn = gains[D : 2 * D]
    gain_query = gains[2 * D : 2 * D + HEAD_DIM]
    gain_key = gains[2 * D + HEAD_DIM :]
    local_places = jnp.arange(seq_dev, dtype=jnp.int32)
    places = seq_index * seq_dev + local_places
    query_docs, offsets = doc_tables(doc_starts, places)
    cos_table, sin_table = rotary(offsets)
    copies = (
        qkv_master.astype(jnp.bfloat16),
        out_master.astype(jnp.bfloat16),
        gate_up_master.astype(jnp.bfloat16),
        down_master.astype(jnp.bfloat16),
    )
    w_qkv, w_out, w_gate_up, w_down = (
        lax.all_gather(copies[0], ("seq", "rows"), axis=0, tiled=True),
        lax.all_gather(copies[1], ("seq", "rows"), axis=0, tiled=True),
        lax.all_gather(copies[2], ("seq", "rows"), axis=0, tiled=True),
        lax.all_gather(copies[3], ("seq", "rows"), axis=0, tiled=True),
    )
    tokens_wide = tokens.astype(jnp.float32)
    normed = norm_rows(tokens_wide, gain_attn).astype(jnp.bfloat16)
    projected = jnp.einsum("rtd,de->rte", normed, w_qkv, preferred_element_type=jnp.float32)
    head_fn = partial(queries_keys, cos_table, sin_table)
    queries, keys_rot = head_fn(projected, gain_query, gain_key)
    query16 = queries.astype(jnp.bfloat16).reshape(
        rows_dev, seq_dev, KV_HEADS, group_size, HEAD_DIM
    )
    keys16 = keys_rot.astype(jnp.bfloat16).reshape(rows_dev, seq_dev, kv_width)
    values16 = projected[..., att_width + kv_width :].astype(jnp.bfloat16)
    stat_shape = (rows_dev, KV_HEADS, group_size, seq_dev)
    initial = (
        jnp.full(stat_shape, MASKED_SCORE, jnp.float32),
        jnp.zeros(stat_shape, jnp.float32),
        jnp.zeros(stat_shape + (HEAD_DIM,), jnp.float32),
    )
    carry = initial
    key_piece = lax.all_gather(keys16, "seq", axis=1, tiled=True)
    value_piece = lax.all_gather(values16, "seq", axis=1, tiled=True)
    key_count = key_piece.shape[1]

    def absorb_block(state, block_index):
        best, total, summed = state
        block_begin = block_index * seq_dev
        key_block = lax.dynamic_slice_in_dim(key_piece, block_begin, seq_dev, 1).reshape(
            rows_dev, seq_dev, KV_HEADS, HEAD_DIM
        )
        value_block = lax.dynamic_slice_in_dim(value_piece, block_begin, seq_dev, 1).reshape(
            rows_dev, seq_dev, KV_HEADS, HEAD_DIM
        )
        key_places = block_begin + jnp.arange(seq_dev, dtype=jnp.int32)
        key_docs, _ = doc_tables(doc_starts, key_places)
        allowed = mask_of(query_docs, places, key_docs, key_places)
        scores = jnp.einsum(
            "rqkgh,rtkh->rkgqt", query16, key_block, preferred_element_type=jnp.float32
        )
        scores = jnp.where(allowed, scores, MASKED_SCORE)
        best_new = jnp.maximum(best, jnp.max(scores, axis=-1))
        weights = jnp.where(allowed, jnp.exp(scores - best_new[..., None]), 0.0)
        factor = jnp.exp(best - best_new)
        total = total * factor + jnp.sum(weights, axis=-1)
        summed = summed * factor[..., None] + jnp.einsum(
            "rkgqt,rtkh->rkgqh",
            weights.astype(jnp.bfloat16),
            value_block,
            preferred_element_type=jnp.float32,
        )
        return ((best_new, total, summed), None)

    carry, _ = lax.scan(absorb_block, carry, jnp.arange(key_count // seq_dev, dtype=jnp.int32))
    best, total, summed = carry
    log_total = best + jnp.log(total)
    attended = summed / total[..., None]
    attended16 = (
        attended.transpose(0, 3, 1, 2, 4).reshape(rows_dev, seq_dev, att_width).astype(jnp.bfloat16)
    )
    branch = jnp.einsum("rtc,cd->rtd", attended16, w_out, preferred_element_type=jnp.float32)
    hidden_in = tokens_wide + branch
    normed2 = norm_rows(hidden_in, gain_ffn).astype(jnp.bfloat16)
    gate_up = jnp.einsum("rtd,df->rtf", normed2, w_gate_up, preferred_element_type=jnp.float32)
    gate_part, up_part = (gate_up[..., :FF], gate_up[..., FF:])
    hidden = (jax.nn.silu(gate_part) * up_part).astype(jnp.bfloat16)
    output = hidden_in + jnp.einsum(
        "rtf,fd->rtd", hidden, w_down, preferred_element_type=jnp.float32
    )
    d_hidden = jnp.einsum("rtd,fd->rtf", grad_out, w_down, preferred_element_type=jnp.float32)
    silu_value, silu_back = jax.vjp(jax.nn.silu, gate_part)
    d_gate = silu_back(d_hidden * up_part)[0]
    d_gate_up = jnp.concatenate([d_gate, d_hidden * silu_value], axis=-1).astype(jnp.bfloat16)
    d_normed2 = jnp.einsum("rtf,df->rtd", d_gate_up, w_gate_up, preferred_element_type=jnp.float32)
    _, ffn_norm_back = jax.vjp(norm_rows, hidden_in, gain_ffn)
    d_inner, grad_gain_ffn = ffn_norm_back(d_normed2)
    d_hidden_in = grad_out.astype(jnp.float32) + d_inner
    term_down = jnp.einsum("rtf,rtd->fd", hidden, grad_out, preferred_element_type=jnp.float32)
    grad_down = lax.psum_scatter(term_down, ("seq", "rows"), scatter_dimension=0, tiled=True)
    term_gate_up = jnp.einsum("rtd,rtf->df", normed2, d_gate_up, preferred_element_type=jnp.float32)
    grad_gate_up = lax.psum_scatter(term_gate_up, ("seq", "rows"), scatter_dimension=0, tiled=True)
    d_branch = d_hidden_in.astype(jnp.bfloat16)
    term_out = jnp.einsum("rtc,rtd->cd", attended16, d_branch, preferred_element_type=jnp.float32)
    d_attended = jnp.einsum(
        "rtd,cd->rtc", d_branch, w_out, preferred_element_type=jnp.float32
    ).astype(jnp.bfloat16)
    d_heads = d_attended.reshape(rows_dev, seq_dev, KV_HEADS, group_size, HEAD_DIM).transpose(
        0, 2, 3, 1, 4
    )
    delta = jnp.sum(d_heads.astype(jnp.float32) * attended, axis=-1)

    def cycle_turn(turn_index, carry):
        pair16, grad_pair, d_queries = carry
        source = (seq_index + turn_index) % cycle_size
        key_places = source * seq_dev + local_places
        key_docs, _ = doc_tables(doc_starts, key_places)
        allowed = mask_of(query_docs, places, key_docs, key_places)
        key_block = pair16[0].reshape(rows_dev, seq_dev, KV_HEADS, HEAD_DIM)
        value_block = pair16[1].reshape(rows_dev, seq_dev, KV_HEADS, HEAD_DIM)
        scores = jnp.einsum(
            "rqkgh,rtkh->rkgqt", query16, key_block, preferred_element_type=jnp.float32
        )
        scores = jnp.where(allowed, scores, MASKED_SCORE)
        probs = jnp.where(allowed, jnp.exp(scores - log_total[..., None]), 0.0)
        d_values = jnp.einsum(
            "rkgqt,rkgqh->rtkh",
            probs.astype(jnp.bfloat16),
            d_heads,
            preferred_element_type=jnp.float32,
        )
        d_probs = jnp.einsum(
            "rkgqh,rtkh->rkgqt", d_heads, value_block, preferred_element_type=jnp.float32
        )
        d_scores = (probs * (d_probs - delta[..., None])).astype(jnp.bfloat16)
        d_queries = d_queries + jnp.einsum(
            "rkgqt,rtkh->rkgqh", d_scores, key_block, preferred_element_type=jnp.float32
        )
        d_keys = jnp.einsum(
            "rkgqt,rqkgh->rtkh", d_scores, query16, preferred_element_type=jnp.float32
        )
        grad_pair = grad_pair + jnp.stack(
            [
                d_keys.reshape(rows_dev, seq_dev, kv_width),
                d_values.reshape(rows_dev, seq_dev, kv_width),
            ]
        )
        grad_pair = from_behind(grad_pair.astype(jnp.bfloat16), "seq", -1).astype(grad_pair.dtype)
        pair16 = from_behind(pair16, "seq", -1)
        return (pair16, grad_pair, d_queries)

    start_pair = jnp.stack([keys16, values16])
    start_grads = jnp.zeros((2, rows_dev, seq_dev, kv_width), jnp.float32)
    start_queries = jnp.zeros(stat_shape + (HEAD_DIM,), jnp.float32)
    _, grad_pair, d_queries = lax.fori_loop(
        0, cycle_size, cycle_turn, (start_pair, start_grads, start_queries)
    )
    d_queries = d_queries.transpose(0, 3, 1, 2, 4).reshape(rows_dev, seq_dev, HEADS, HEAD_DIM)
    d_keys_home = grad_pair[0].reshape(rows_dev, seq_dev, KV_HEADS, HEAD_DIM)
    _, heads_back = jax.vjp(head_fn, projected, gain_query, gain_key)
    d_projected, grad_gain_query, grad_gain_key = heads_back((d_queries, d_keys_home))
    d_projected = jnp.concatenate(
        [d_projected[..., : att_width + kv_width], grad_pair[1]], axis=-1
    ).astype(jnp.bfloat16)
    term_qkv = jnp.einsum("rtd,rte->de", normed, d_projected, preferred_element_type=jnp.float32)
    d_normed = jnp.einsum("rte,de->rtd", d_projected, w_qkv, preferred_element_type=jnp.float32)
    _, attn_norm_back = jax.vjp(norm_rows, tokens_wide, gain_attn)
    d_tokens_part, grad_gain_attn = attn_norm_back(d_normed)
    grad_tokens = (d_hidden_in + d_tokens_part).astype(jnp.bfloat16)
    grad_qkv, grad_out_proj = (
        lax.psum_scatter(term_qkv, ("seq", "rows"), scatter_dimension=0, tiled=True),
        lax.psum_scatter(term_out, ("seq", "rows"), scatter_dimension=0, tiled=True),
    )
    gain_local = jnp.concatenate([grad_gain_attn, grad_gain_ffn, grad_gain_query, grad_gain_key])
    grads = (grad_qkv, grad_out_proj, grad_gate_up, grad_down)
    updated = optimizer_step(
        grads, gain_local, (qkv_master, out_master, gate_up_master, down_master), gains,
        (qkv_rows, out_rows, gate_up_rows, down_rows), col_moments, gain_moments,
        lambda vector: lax.psum(vector, ("seq", "rows")),
    )
    return (output.astype(jnp.bfloat16), grad_tokens, *grads, *updated)


MESH = pl.DeviceIdType.MESH
PLACES = 32
VMEM_BYTES = 61 * 1024 * 1024
CHUNK = 16


def here():
    seq = lax.axis_index("seq")
    return lax.div(seq, 2), lax.rem(seq, 2), lax.axis_index("rows")


def flips(chip):
    return (chip + 1 - 2 * lax.rem(chip, 2), lax.rem(chip + 2, 4), 3 - chip)


def ahead(z, step):
    return lax.rem(z + step, 4)


def at_place(chip, core, z):
    return (2 * chip + core, z)


def greet(peers):
    barrier = pltpu.get_barrier_semaphore()
    for peer in peers:
        pl.semaphore_signal(barrier, inc=1, device_id=peer, device_id_type=MESH)
    pl.semaphore_wait(barrier, len(peers))


class Mover:
    def __init__(self, send_sem, recv_sem, local_sem):
        self.send_sem, self.recv_sem, self.local_sem = send_sem, recv_sem, local_sem
        self.remote, self.own, self.lines, self.scattered = [], [], [], []
        self.used = 0

    def copy_of(self, src, dst, peer, send_slot, recv_slot):
        return pltpu.make_async_remote_copy(
            src_ref=src,
            dst_ref=dst,
            send_sem=self.send_sem.at[send_slot],
            recv_sem=self.recv_sem.at[recv_slot],
            device_id=peer,
            device_id_type=MESH,
        )

    def send_parts(self, pairs, whole, peer):
        slot = self.used
        self.used += 1
        for src, dst in pairs:
            self.copy_of(src, dst, peer, slot, slot).start()
        copy = self.copy_of(whole[0], whole[1], peer, slot, slot)
        handle = [copy, False, copy.wait_recv, False]
        self.remote.append(handle)
        return handle

    def send(self, src, dst, peer):
        return self.send_parts([(src, dst)], (src, dst), peer)

    def keep_parts(self, pairs, whole):
        sem = self.local_sem.at[len(self.own)]
        for src, dst in pairs:
            pltpu.make_async_copy(src, dst, sem).start()
        copy = pltpu.make_async_copy(whole[0], whole[1], sem)
        handle = [copy, False, copy.wait]
        self.own.append(handle)
        return handle

    def keep(self, src, dst):
        return self.keep_parts([(src, dst)], (src, dst))

    def line(self, source, block_of, chip, core, z):
        line = (self.used, block_of, chip, core, z)
        self.used += 5
        base = line[0]
        up, low = at_place(chip, core, z + 1), at_place(chip, core, z - 1)
        rising = self.copy_of(source, block_of(z), up, base, base + 3)
        falling = self.copy_of(source, block_of(z), low, base + 4, base + 1)
        pl.when(z < 3)(rising.start)
        pl.when(z > 0)(falling.start)
        self.lines += [(z < 3, rising), (z > 0, falling)]
        return line

    def wait_line(self, line, step, when=None):
        base, block_of, chip, core, z = line
        block = block_of(ahead(z, step))
        peer = at_place(chip, core, ahead(z, step))
        copy = self.copy_of(block, block, peer, base + step, base + step)
        if when is None:
            copy.wait_recv()
        else:
            pl.when(when)(copy.wait_recv)
        return block

    def arrive_line(self, line, step, when=None):
        base, _, chip, core, z = line
        block = self.wait_line(line, step, when)
        rises, falls = (z + step >= 4) & (z < 3), (z + step < 4) & (z > 0)
        up, low = at_place(chip, core, z + 1), at_place(chip, core, z - 1)
        rising = self.copy_of(block, block, up, base + step, base + step - 1)
        falling = self.copy_of(block, block, low, base + step, base + step + 1)
        for moves, copy in ((rises, rising), (falls, falling)):
            moves = moves if when is None else moves & when
            pl.when(moves)(copy.start)
            self.lines.append((moves, copy))
        return block

    def scatter(self, source, target, steps, chip, core, z):
        base = self.used
        self.used += 3

        def start(index):
            at = ahead(z, steps[index])
            copy = self.copy_of(
                source(at), target(z), at_place(chip, core, at), base + index, base + 3 - steps[index]
            )
            copy.start()
            self.scattered.append(copy)

        def wait():
            for step in (1, 2, 3):
                at = ahead(z, step)
                peer = at_place(chip, core, at)
                self.copy_of(source(at), target(at), peer, base, base + step - 1).wait_recv()

        return start, wait

    def arrive(self, *handles):
        for handle in handles:
            if not handle[1]:
                handle[1] = True
                handle[2]()

    def sent(self, *handles):
        for handle in handles:
            if not handle[3]:
                handle[3] = True
                handle[0].wait_send()

    def sent_lines(self):
        for when, copy in self.lines:
            pl.when(when)(copy.wait_send)
        self.lines = []

    def sent_sums(self):
        for copy in self.scattered:
            copy.wait_send()
        self.scattered = []

    def finish(self):
        assert self.used <= self.send_sem.shape[0] and len(self.own) <= self.local_sem.shape[0]
        self.arrive(*self.own, *self.remote)
        self.sent(*self.remote)
        self.sent_lines()
        self.sent_sums()


def semaphores(remote, own):
    return [
        pltpu.SemaphoreType.DMA((remote,)),
        pltpu.SemaphoreType.DMA((remote,)),
        pltpu.SemaphoreType.DMA((max(own, 1),)),
    ]


def exchange(kernel, ident, inputs, outputs, scratch, copies, moved, flops=0):
    spaces = {True: pltpu.VMEM, False: pl.ANY, None: pltpu.SMEM}
    specs = {near: pl.BlockSpec(memory_space=space) for near, space in spaces.items()}
    return pl.pallas_call(
        kernel,
        out_shape=[jax.ShapeDtypeStruct(shape, kind) for shape, kind, _ in outputs],
        in_specs=[specs[near] for _, near in inputs],
        out_specs=[specs[near] for _, _, near in outputs],
        scratch_shapes=scratch + semaphores(*copies),
        compiler_params=pltpu.CompilerParams(
            collective_id=ident, has_side_effects=True, vmem_limit_bytes=VMEM_BYTES
        ),
        cost_estimate=pl.CostEstimate(flops=flops, bytes_accessed=moved, transcendentals=0),
    )(*[array for array, _ in inputs])


def chunks(length, body):
    @pl.loop(0, length // CHUNK)
    def _(step):
        body(pl.ds(pl.multiple_of(step * CHUNK, CHUNK), CHUNK))


def add_blocks(first, second, result):
    for row in range(2):

        def body(part):
            total = first[row, part].astype(jnp.float32) + second[row, part].astype(jnp.float32)
            result[row, part] = total.astype(result.dtype)

        chunks(64, body)


def lower_half(shape):
    return lax.broadcasted_iota(jnp.int32, shape, len(shape) - 1) < 64


def swap_halves(entries):
    lane = lax.broadcasted_iota(jnp.int32, entries.shape, 1)
    return jnp.where(lax.rem(lane, 64) < 32, pltpu.roll(entries, 96, 1), pltpu.roll(entries, 32, 1))


def head_means(entries):
    lower = lower_half(entries.shape)
    low = jnp.sum(jnp.where(lower, entries, 0.0), axis=-1, keepdims=True)
    high = jnp.sum(jnp.where(lower, 0.0, entries), axis=-1, keepdims=True)
    return jnp.where(lower, low, high) * (1.0 / HEAD_DIM)


def wide(start, size):
    return pl.ds(pl.multiple_of(start, size), size)


def plain(left, right):
    return jnp.dot(left, right, preferred_element_type=jnp.float32)


def across(left, right):
    return lax.dot_general(
        left, right, (((1,), (1,)), ((), ())), preferred_element_type=jnp.float32
    )


def down(left, right):
    return lax.dot_general(
        left, right, (((0,), (0,)), ((), ())), preferred_element_type=jnp.float32
    )


def attention_probs(queries, keys, first, part):
    scores = across(queries, keys)
    place = lax.broadcasted_iota(jnp.int32, scores.shape, 1)
    query = lax.broadcasted_iota(jnp.int32, scores.shape, 0) + part * 128
    allowed = (place >= first) & (place <= query)
    scores = jnp.where(allowed, scores, MASKED_SCORE)
    best = jnp.max(scores, axis=-1, keepdims=True)
    weights = jnp.where(allowed, jnp.exp(scores - best), 0.0)
    return weights / jnp.sum(weights, axis=-1, keepdims=True)


COL_ROWS, GAIN_ROWS = 184, 33
COLS = COL_ROWS * 128
MATRICES = ((64, QKV, 0, 0), (64, D, 64, 24), (64, 2 * FF, 128, 40), (256, D, 192, 168))
ROW_TOTALS = (D, HEADS * HEAD_DIM, D, FF)
BETA = 1.0 - STEP ** (-0.8)


def lane_value(vector, lane):
    lanes = lax.broadcasted_iota(jnp.int32, (1, 128), 1)
    return jnp.sum(jnp.where(lanes == lane, vector, 0.0), axis=-1, keepdims=True)


def total(entries):
    return jnp.sum(jnp.sum(entries, axis=-1, keepdims=True), axis=0, keepdims=True)


def document_start(starts, row, place):
    start = jnp.zeros_like(place)
    for document in range(starts.shape[1]):
        begin = starts[row, document]
        start = jnp.maximum(start, jnp.where(place >= begin, begin, 0))
    return start


def place_tables(length):
    rates = ROPE_BASE ** (-(np.arange(128) % 32) * 2.0 / HEAD_DIM)
    angles = np.arange(length)[:, None] * rates
    return np.stack([np.cos(angles), np.sin(angles)]).astype(np.float32)


def derive_updates(
    flat, col_moments, gain_moments, gains,
    cols_new, col_factors, moments_new, gains_new, grad_gains, spreads,
):
    first = 2 * COL_ROWS
    stats = flat[first + 33 : first + 34]
    lanes = lax.broadcasted_iota(jnp.int32, (1, 128), 1)
    out = jnp.zeros((1, 128), jnp.float32)
    for slot, (_, width, _, col_at) in enumerate(MATRICES):
        own = pl.ds(col_at, width // 128)
        entries_all = float(ROW_TOTALS[slot] * width)
        new = BETA * col_moments[own] + (1.0 - BETA) * (flat[own] / ROW_TOTALS[slot])
        cols_new[own] = new
        mean_rows = lane_value(stats, slot) / ROW_TOTALS[slot]
        ratio = total(flat[pl.ds(COL_ROWS + col_at, width // 128)] / new)
        spread = jnp.sqrt(mean_rows * ratio / entries_all)
        scale = STEP_RATE * jnp.maximum(
            SCALE_EPSILON, jnp.sqrt(lane_value(stats, 4 + slot) / entries_all)
        )
        factor = scale * jnp.sqrt(mean_rows) / jnp.maximum(1.0, spread / CLIP_LEVEL)
        factors = lax.rsqrt(new) * factor
        for row in range(width // 128):
            col_factors[:, pl.ds((col_at + row) * 128, 128)] = factors[row : row + 1]
        out = jnp.where(lanes == slot, spread, out)
    gradient = flat[first : first + GAIN_ROWS]
    grad_gains[...] = gradient
    old = gains[...]
    new = BETA * gain_moments[...] + (1.0 - BETA) * (gradient * gradient + SQUARE_EPSILON)
    moments_new[...] = new
    unit = gradient * lax.rsqrt(new)
    row = lax.broadcasted_iota(jnp.int32, (GAIN_ROWS, 128), 0)
    lane = lax.broadcasted_iota(jnp.int32, (GAIN_ROWS, 128), 1)
    segment = jnp.where(row < 16, 0, jnp.where(row < 32, 1, jnp.where(lane < 64, 2, 3)))
    factors = jnp.zeros((GAIN_ROWS, 128), jnp.float32)
    for slot, count in enumerate((D, D, HEAD_DIM, HEAD_DIM)):
        mask = segment == slot
        spread = jnp.sqrt(total(jnp.where(mask, unit * unit, 0.0)) / count)
        mean = total(jnp.where(mask, old * old, 0.0)) / count
        scale = STEP_RATE * jnp.maximum(SCALE_EPSILON, jnp.sqrt(mean))
        factors = jnp.where(mask, scale / jnp.maximum(1.0, spread / CLIP_LEVEL), factors)
        out = jnp.where(lanes == 4 + slot, spread, out)
    gains_new[...] = old - factors * unit
    spreads[...] = out


def layer_kernel(
    tok, starts, rates, places_at, gain_attn, gain_ffn, gain_heads, gains, grad_out,
    m_qkv, m_out, m_down, m_gate_up, rows, col_moments, gain_moments,
    out_sum, grad_tok, g_qkv, gate_up_came, out_came, down_came, rows_new, row_factors,
    cols_new, col_factors, moments_new, gains_new, grad_gains, spreads,
    gate_up_in, gate_up_mid, kept_tok,
    projected, queries, keys_values, attended, document_tables,
    wq_send, normed, all_tok, all_wq, all_wo, partial, from_partner, came,
    hidden_in, all_norm, all_out, all_wg, wd, hidden, d_gate_up,
    d_queries, d_keys_values, qkv_in, d_hidden_in, gain_part, gain_part2, gain_qk, weight_sums, qkv_came,
    packed, plane_came, plane_sum, line_came, line_sum, line_all, totals, credit, tokens_used, *sems,
):
    half, full = jnp.bfloat16, jnp.float32
    chip, core, z = here()
    others = flips(chip)
    other = 1 - core
    me = 2 * chip + core
    partner = at_place(chip, other, z)
    plane = [at_place(peer_chip, core, z) for peer_chip in others]
    plane_cross = [at_place(peer_chip, other, z) for peer_chip in others]
    steps = (2, 1, 3)
    line = [at_place(chip, core, ahead(z, step)) for step in steps]
    cross = [at_place(chip, other, ahead(z, step)) for step in steps]
    everyone = [partner] + plane + plane_cross
    greet(everyone + line + cross)
    move = Mover(*sems)

    for head in range(8):
        wq_send[head, :, pl.ds(0, 256)] = m_qkv[:, pl.ds(head * 256, 256)].astype(half)
    low = lower_half((64, 128))
    for pair in range(4):
        keys = m_qkv[:, pl.ds(2048 + pair * 128, 128)]
        values = m_qkv[:, pl.ds(2560 + pair * 128, 128)]
        tail = pl.ds(256, 128)
        wq_send[2 * pair, :, tail] = jnp.where(low, keys, pltpu.roll(values, 64, 1)).astype(half)
        wq_send[2 * pair + 1, :, tail] = jnp.where(low, pltpu.roll(keys, 64, 1), values).astype(half)
    heads = [move.keep(wq_send.at[me], all_wq.at[me, z])]
    for peer in everyone:
        heads.append(move.send(wq_send.at[peer[0]], all_wq.at[me, z], peer))

    for row in range(2):

        def body0(part):
            result = tok[row, part].astype(full)
            scale = lax.rsqrt(jnp.mean(result * result, axis=-1, keepdims=True) + EPSILON)
            normed[row, part] = (result * scale * gain_attn[...]).astype(half)

        chunks(64, body0)
    token_copies = [move.send(normed, all_tok.at[me], peer) for peer in plane]
    token_copies.append(move.send(normed, all_tok.at[me], partner))
    tokens_here = move.keep(normed, all_tok.at[me])
    move.arrive(*heads)
    line_wq = move.line(all_wq.at[:, z], lambda at: all_wq.at[:, at], chip, core, z)
    flat_d = d_gate_up.reshape(1024, 2048)
    weight_sums[...] = jnp.zeros_like(weight_sums)
    for row in range(2):
        for document in range(starts.shape[1]):
            angle = starts[row, document].astype(full) * rates[0:1]
            document_tables[row, 2 * document] = jnp.cos(angle)
            document_tables[row, 2 * document + 1] = jnp.sin(angle)

    def cast_all(slot, blocks):
        loads = [move.keep(blocks[0][0], hidden_in.at[0])]
        for index, (_, target) in enumerate(blocks):
            if index + 1 < len(blocks):
                loads.append(move.keep(blocks[index + 1][0], hidden_in.at[(index + 1) % 2]))
            move.arrive(loads[index])

            def body(part, index=index, target=target):
                entries = hidden_in[index % 2, part]
                weight_sums[slot] += jnp.sum((entries * entries).reshape(2, 8, D), axis=0)
                target(part, entries.astype(half))

            chunks(64, body)

    def into(ref):
        def store(part, entries):
            ref[part] = entries

        return store

    def by_device(block):
        cols = pl.ds((block // 4) * 1024 + (block % 4) * 256, 256)

        def store(part, entries):
            for index in range(8):
                place = (index % 4) * 2 + index // 4
                rows_at = wide(place * 64 + part.start, CHUNK)
                flat_d[rows_at, cols] = entries[:, index * 256 : (index + 1) * 256]

        return store

    cast_all(1, [(m_out, into(all_wo.at[z]))])
    wo_copies = [move.send(all_wo.at[z], all_wo.at[z], peer) for peer in line]
    cast_all(
        3,
        [
            (m_down.at[pl.ds(64 * block, 64)], into(wd.at[chip, pl.ds(64 * block, 64)]))
            for block in range(4)
        ],
    )
    by_x, by_y = plane[0], plane[1]
    front, back = wd.at[chip, pl.ds(0, 128)], wd.at[chip, pl.ds(128, 128)]
    down_copies = [
        move.send(front, front, by_x), move.send(back, back, by_y),
        move.send(back, back, by_x), move.send(front, front, by_y),
    ]
    move.arrive_line(line_wq, 3)
    move.arrive_line(line_wq, 1)
    cast_all(
        2,
        [(m_gate_up.at[:, pl.ds(2048 * block, 2048)], by_device(block)) for block in range(8)],
    )
    move.arrive_line(line_wq, 2)

    def turn_block(to_core, to_z, side):
        lanes = pl.ds(side * 1024, 1024)
        src = flat_d.at[wide((to_z * 2 + to_core) * 64, 64), lanes]
        return src, all_wg.at[chip, core, z, :, lanes]

    turned, turned_own = ([], []), []
    for side in range(2):
        for step, peer, peer_cross in zip(steps, line, cross):
            to = ahead(z, step)
            turned[side].append(move.send(*turn_block(core, to, side), peer))
            turned[side].append(move.send(*turn_block(other, to, side), peer_cross))
        turned[side].append(move.send(*turn_block(other, z, side), partner))
        turned_own.append(move.keep(*turn_block(core, z, side)))
    line_grads = move.line(grad_out, lambda at: all_out.at[at, core], chip, core, z)
    own = [
        move.keep(grad_out, all_out.at[z, core]),
        move.send(grad_out, all_out.at[z, core], partner),
    ]

    for peer_chip, handle in zip(others, tuple(token_copies)):
        move.arrive(handle)
        block = all_tok.at[2 * peer_chip + core]
        token_copies.append(move.send(block, block, partner))
    move.arrive(tokens_here, *token_copies, *wo_copies)
    saved = [move.keep(all_tok, kept_tok)]

    def tables_of(block, row):
        place = lax.broadcasted_iota(jnp.int32, (64, 1), 0) + block * 64
        start_cos, start_sin = document_tables[row, 0], document_tables[row, 1]
        for document in range(1, starts.shape[1]):
            inside = place >= starts[row, document]
            start_cos = jnp.where(inside, document_tables[row, 2 * document], start_cos)
            start_sin = jnp.where(inside, document_tables[row, 2 * document + 1], start_sin)
        at = wide(block * 64, 64)
        place_cos, place_sin = places_at[0, at], places_at[1, at]
        cosine = place_cos * start_cos + place_sin * start_sin
        return cosine, (place_sin * start_cos - place_cos * start_sin) * rates[1:2]

    def first_of(row, part):
        place = lax.broadcasted_iota(jnp.int32, (128, 1), 0) + part * 128
        return document_start(starts, row, place)

    flat_tok, flat_wq = all_tok.reshape(1024, D), all_wq.reshape(D, 384)
    flat_wo = all_wo.reshape(256, D)

    @pl.loop(0, 4)
    def _(step):
        block = plain(flat_tok[wide(step * 256, 256)], flat_wq[...])
        projected[wide(step * 2, 2)] = block.reshape(2, 2, 64, 384)

    @pl.loop(0, 8)
    def _(block):
        for row in range(2):
            cosine, sine = tables_of(block, row)
            places = wide(block * 64, 64)
            for tile in range(3):
                entries = projected[block, row, :, pl.ds(tile * 128, 128)]
                gain = gain_heads[min(tile, 2) // 2 : min(tile, 2) // 2 + 1]
                scale = lax.rsqrt(head_means(entries * entries) + EPSILON)
                turned_entries = entries * scale * gain
                turned_entries = turned_entries * cosine + swap_halves(turned_entries) * sine
                if tile < 2:
                    queries[row, tile, places] = (turned_entries * HEAD_DIM ** (-0.5)).astype(half)
                else:
                    zero = jnp.zeros_like(entries)
                    rolled = pltpu.roll(turned_entries, 64, 1)
                    values = pltpu.roll(entries, 64, 1)
                    keys_values[row, 0, places] = jnp.where(low, turned_entries, zero).astype(half)
                    keys_values[row, 1, places] = jnp.where(low, zero, rolled).astype(half)
                    keys_values[row, 2, places] = jnp.where(low, values, zero).astype(half)
                    keys_values[row, 3, places] = jnp.where(low, zero, entries).astype(half)

    move.arrive(*down_copies[:2])
    front, back = wd.at[others[0], pl.ds(0, 128)], wd.at[others[1], pl.ds(128, 128)]
    down_copies += [move.send(front, front, by_y), move.send(back, back, by_x)]

    @pl.loop(0, 2)
    def _(row):
        for tile in range(2):
            for part in range(4):
                own_places, upto = pl.ds(part * 128, 128), pl.ds(0, (part + 1) * 128)
                result = jnp.zeros((128, 128), full)
                for side in range(2):
                    probs = attention_probs(
                        queries[row, tile, own_places], keys_values[row, side, upto],
                        first_of(row, part), part,
                    )
                    result += plain(probs.astype(half), keys_values[row, 2 + side, upto])
                attended[pl.ds(2 * part, 2), row, :, pl.ds(tile * 128, 128)] = result.reshape(2, 64, 128)

    flat_attended = attended.reshape(1024, 256)

    @pl.loop(0, 4)
    def _(step):
        rows = flat_attended[wide(step * 256, 256)].astype(half)

        @pl.loop(0, 4)
        def _(col):
            cols = wide(col * 512, 512)
            block = plain(rows, flat_wo[:, cols])
            partial[wide(step * 2, 2), :, :, cols] = block.reshape(2, 2, 64, 512).astype(half)

    order = tuple(others) + (chip,)
    halves = [move.send(partial.at[2 * to + other], from_partner.at[to], partner) for to in order]
    sums = []
    for to, arrived, peer in zip(others, halves, plane):
        move.arrive(arrived)
        add_blocks(partial.at[2 * to + core], from_partner.at[to], from_partner.at[to])
        sums.append(move.send(from_partner.at[to], came.at[chip], peer))
    def gather_weights(side):
        move.arrive(turned_own[side], *turned[side])
        lanes = pl.ds(side * 1024, 1024)
        front, back = all_wg.at[chip, 0, :, :, lanes], all_wg.at[chip, 1, :, :, lanes]
        return [
            move.send(front, front, by_x), move.send(back, back, by_y),
            move.send(back, back, by_x), move.send(front, front, by_y),
        ]

    def pass_weights(side, copies):
        move.arrive(*copies[:2])
        lanes = pl.ds(side * 1024, 1024)
        front, back = all_wg.at[others[0], 0, :, :, lanes], all_wg.at[others[1], 1, :, :, lanes]
        return [move.send(front, front, by_y), move.send(back, back, by_x)]

    gate_copies = gather_weights(0)
    move.sent(*token_copies)
    move.arrive(halves[3], *sums)
    for row in range(2):

        def body(part):
            result = tok[row, part].astype(full)
            result += partial[me, row, part].astype(full)
            result += from_partner[chip, row, part].astype(full)
            for peer_chip in others:
                result += came[peer_chip, row, part].astype(full)
            hidden_in[row, part] = result
            scale = lax.rsqrt(jnp.mean(result * result, axis=-1, keepdims=True) + EPSILON)
            normed[row, part] = (result * scale * gain_ffn[...]).astype(half)

        chunks(64, body)
    move.sent(*sums, *halves)
    move.arrive(*saved)
    line_norms = move.line(normed, lambda at: all_norm.at[at, core], chip, core, z)
    own.append(move.send(normed, all_norm.at[z, core], partner))
    own.append(move.keep(normed, all_norm.at[z, core]))

    up_copies = gather_weights(1)
    at_first, at_last = lax.div(3 - z, 3), lax.div(z, 3)
    arrivals = (3 - 2 * at_first, 1 + at_first + at_last, 2 + at_first - at_last)
    inner = (z > 0) & (z < 3)
    shared = []

    def share(step, wait_only=False):
        for line_of in (line_grads, line_norms):
            if wait_only:
                block = move.wait_line(line_of, step, jnp.logical_not(inner))
            else:
                block = move.arrive_line(line_of, step)
            shared.append(move.send(block, block, partner))

    flat_wg, flat_wd = all_wg.reshape(D, 2048), wd.reshape(1024, D)

    def d_hidden_of(zb):
        @pl.loop(0, 4)
        def _(step):
            cols = wide(step * 256, 256)
            hidden[zb, :, cols] = across(all_out[zb].reshape(256, D), flat_wd[cols]).astype(half)

    share(arrivals[0])
    gate_copies += pass_weights(0, gate_copies)
    move.arrive(*own[:2], *down_copies)
    d_hidden_of(z)
    share(arrivals[1])
    up_copies += pass_weights(1, up_copies)
    move.arrive(shared[0])
    d_hidden_of(ahead(z, arrivals[0]))
    for line_of in (line_grads, line_norms):
        move.arrive_line(line_of, arrivals[2], inner)
    move.arrive(shared[2])
    d_hidden_of(ahead(z, arrivals[1]))
    weights = gate_copies + up_copies
    move.arrive(*weights, *own)
    move.sent(*turned[0], *turned[1])

    def block_of(zb):
        @pl.loop(0, 4)
        def _(step):
            cols, ups = wide(step * 256, 256), wide(1024 + step * 256, 256)
            rows = all_norm[zb].reshape(256, D)
            gate = plain(rows, flat_wg[:, cols])
            up = plain(rows, flat_wg[:, ups])
            d_hidden = hidden[zb, :, cols].astype(full)
            sigmoid = 1.0 / (1.0 + jnp.exp(-gate))
            silu = gate * sigmoid
            hidden[zb, :, cols] = (silu * up).astype(half)
            d_gate = d_hidden * up * (sigmoid * (1.0 + gate * (1.0 - sigmoid)))
            d_gate_up[zb, :, cols] = d_gate.astype(half)
            d_gate_up[zb, :, ups] = (d_hidden * silu).astype(half)

        @pl.loop(0, 8)
        def _(step):
            cols = wide(step * 256, 256)
            block = across(d_gate_up[zb], flat_wg[cols])
            partial[pl.ds(2 * zb, 2), :, :, cols] = block.reshape(2, 2, 64, 256).astype(half)

    def pair_sum(zb, handle, into, base):
        move.arrive(handle)
        add_blocks(partial.at[2 * zb + core], into.at[base + zb], into.at[base + zb])

    start_sum, wait_sums = move.scatter(
        lambda at: from_partner.at[at], lambda at: came.at[at], arrivals, chip, core, z
    )
    to_partner = []
    walk = [z] + [ahead(z, step) for step in arrivals]
    for index, zb in enumerate(walk):
        if index > 0:
            move.arrive(*shared[2 * index - 2 : 2 * index])
        if index == 3:
            d_hidden_of(zb)
        block_of(zb)
        to_partner.append(move.send(partial.at[2 * zb + other], from_partner.at[zb], partner))
        if index == 0:
            share(arrivals[2], True)
        if index > 0:
            pair_sum(walk[index - 1], to_partner[index - 1], from_partner, 0)
        if index > 1:
            start_sum(index - 2)
    pair_sum(walk[3], to_partner[3], from_partner, 0)
    start_sum(2)

    flat_norm, flat_grads = all_norm.reshape(1024, D), all_out.reshape(1024, D)
    flat_hidden = hidden.reshape(1024, 1024)
    move.sent(*weights)

    def gate_up_grad(to, side):
        rows, lanes = wide(to * 512, 512), pl.ds(side * 1024, 1024)

        @pl.loop(0, 2)
        def _(step):
            cols = wide(side * 1024 + step * 512, 512)
            flat_wg[rows, cols] = down(flat_norm[:, rows], flat_d[:, cols]).astype(half)

        return flat_wg.at[rows, lanes]

    passed = []
    for side in (0, 1):
        passed.append(move.send(gate_up_grad(others[2], side), gate_up_mid.at[side], plane[side]))
    direct = [gate_up_grad(others[side], side) for side in (0, 1)]
    handed = [gate_up_grad(others[1 - side], side) for side in (0, 1)]
    for side in (0, 1):
        gate_up_grad(chip, side)
    move.sent(*shared, own[2])
    move.sent_lines()
    for peer in [partner] + plane:
        pl.semaphore_signal(credit, inc=1, device_id=peer, device_id_type=MESH)

    wait_sums()
    gain_part[...] = jnp.zeros_like(gain_part)
    for row in range(2):

        def body2(part):
            result = from_partner[z, row, part].astype(full)
            for step in steps:
                result += came[ahead(z, step), row, part].astype(full)
            entries = hidden_in[row, part]
            scale = lax.rsqrt(jnp.mean(entries * entries, axis=-1, keepdims=True) + EPSILON)
            gain_part[...] += jnp.sum(result * entries * scale, axis=0, keepdims=True)
            result = result * gain_ffn[...]
            inside = jnp.mean(result * entries, axis=-1, keepdims=True) * (scale * scale * scale)
            grad = grad_out[row, part].astype(full) + result * scale - entries * inside
            d_hidden_in[row, part] = grad
            normed[row, part] = grad.astype(half)

        chunks(64, body2)
    pl.semaphore_wait(credit, 4)
    move.sent_sums()
    all_branch = all_norm.reshape(8, 2, 64, D)
    branches = [move.send(normed, all_branch.at[me], peer) for peer in plane]
    branch_copies = [
        move.send(normed, all_branch.at[me], partner), move.keep(normed, all_branch.at[me])
    ]
    pieces = [
        move.send(direct[side], gate_up_in.at[side, 0], plane[side]) for side in (0, 1)
    ]

    move.sent(*to_partner)
    to_partner, sums = [], []
    walk = [ahead(z, step) for step in steps] + [z]
    for index, zb in enumerate(walk):

        @pl.loop(0, 4)
        def _(step, zb=zb):
            cols = wide(step * 512, 512)
            block = plain(hidden[zb], flat_wd[:, cols])
            partial[pl.ds(2 * zb, 2), :, :, cols] = block.reshape(2, 2, 64, 512).astype(half)

        to_partner.append(move.send(partial.at[2 * zb + other], all_tok.at[zb], partner))
        if index > 0:
            before = walk[index - 1]
            pair_sum(before, to_partner[index - 1], all_tok, 0)
            sums.append(move.send(all_tok.at[before], all_tok.at[4 + z], line[index - 1]))
    pair_sum(z, to_partner[3], all_tok, 0)

    move.sent(*down_copies, *wo_copies)

    @pl.loop(0, 4)
    def _(to):
        rows_at = wide(to * 256, 256)

        @pl.loop(0, 4)
        def _(step):
            cols = wide(step * 512, 512)
            flat_wd[rows_at, cols] = down(flat_hidden[:, rows_at], flat_grads[:, cols]).astype(half)

    load_tok = move.keep(kept_tok, all_out.reshape(8, 2, 64, D))

    def load(source):
        return [
            move.keep(source(side), flat_d.at[pl.ds(side * 512, 512), pl.ds(0, 1024)])
            for side in (0, 1)
        ]

    def add_loaded(side, chunk):
        @pl.loop(0, 512 // CHUNK)
        def _(step):
            lanes = pl.ds(side * 1024, 1024)
            rows = wide(chunk * 512 + step * CHUNK, CHUNK)
            extra = flat_d[wide(side * 512 + step * CHUNK, CHUNK), pl.ds(0, 1024)]
            result = flat_wg[rows, lanes].astype(full) + extra.astype(full)
            flat_wg[rows, lanes] = result.astype(half)

    move.arrive(*passed)
    loads = load(lambda side: gate_up_mid.at[side])
    later = []
    for side in (0, 1):
        move.arrive(loads[side])
        add_loaded(side, others[1 - side])
        later.append(move.send(handed[side], gate_up_in.at[side, 1], plane[1 - side]))
    for peer_chip, handle in zip(others, branches):
        move.arrive(handle)
        block = all_branch.at[2 * peer_chip + core]
        branch_copies.append(move.send(block, block, partner))
    move.arrive(*branch_copies)

    flat_branch = all_branch.reshape(1024, D)
    flat_wo = all_wo.reshape(256, D)
    d_heads_at, d_projected_at = pl.ds(0, 256), pl.ds(256, 384)

    @pl.loop(0, 4)
    def _(step):
        rows = wide(step * 256, 256)
        flat_hidden[rows, d_heads_at] = across(flat_branch[rows], flat_wo[...]).astype(half)

    @pl.loop(0, 4)
    def _(step):
        cols = wide(step * 512, 512)
        block = down(flat_attended[...].astype(half), flat_branch[:, cols])
        flat_wo[:, cols] = block.astype(half)

    outs = [
        move.send(all_wo.at[ahead(z, step)], out_came.at[z], peer) for step, peer in zip(steps, line)
    ]
    outs.append(move.keep(all_wo.at[z], out_came.at[z]))
    lower = lower_half((128, 128))
    line_low = lower_half((1, 128))
    gain_qk[...] = jnp.zeros_like(gain_qk)

    @pl.loop(0, 2)
    def _(row):
        d_keys_values[...] = jnp.zeros_like(d_keys_values)

        def token_rows(block):
            return wide((2 * block + row) * 64, 64)

        for tile in range(2):
            lanes = pl.ds(tile * 128, 128)
            for part in range(4):
                own_places, upto = pl.ds(part * 128, 128), pl.ds(0, (part + 1) * 128)
                d_heads = jnp.concatenate(
                    [flat_hidden[token_rows(2 * part + index), lanes] for index in range(2)], axis=0
                )
                products = d_heads.astype(full) * attended[pl.ds(2 * part, 2), row, :, lanes].reshape(128, 128)
                query = queries[row, tile, own_places]
                result = jnp.zeros((128, 128), full)
                for side in range(2):
                    mask = lower if side == 0 else jnp.logical_not(lower)
                    delta = jnp.sum(jnp.where(mask, products, 0.0), axis=-1, keepdims=True)
                    keys = keys_values[row, side, upto]
                    probs = attention_probs(query, keys, first_of(row, part), part)
                    d_probs = across(d_heads, keys_values[row, 2 + side, upto])
                    d_scores = (probs * (d_probs - delta)).astype(half)
                    result += plain(d_scores, keys)
                    d_keys_values[side, upto] += down(d_scores, query)
                    d_keys_values[2 + side, upto] += down(probs.astype(half), d_heads)
                d_queries[tile, own_places] = result

        @pl.loop(0, 8)
        def _(block):
            cosine, sine = tables_of(block, row)
            places = wide(block * 64, 64)
            for tile in range(3):
                entries = projected[block, row, :, pl.ds(tile * 128, 128)]
                gain = gain_heads[tile // 2 : tile // 2 + 1]
                scale = lax.rsqrt(head_means(entries * entries) + EPSILON)
                if tile < 2:
                    grad = d_queries[tile, places] * HEAD_DIM ** (-0.5)
                else:
                    from_low, from_high = d_keys_values[0, places], d_keys_values[1, places]
                    grad = jnp.where(low, from_low + pltpu.roll(from_high, 64, 1), 0.0)
                grad = grad * cosine + swap_halves(grad * sine)
                for_gain = jnp.sum(grad * entries * scale, axis=0, keepdims=True)
                if tile < 2:
                    for_gain = jnp.where(line_low, for_gain + pltpu.roll(for_gain, 64, 1), 0.0)
                else:
                    for_gain = jnp.where(line_low, 0.0, pltpu.roll(for_gain, 64, 1))
                gain_qk[...] += for_gain
                grad = grad * gain
                inside = head_means(grad * entries) * (scale * scale * scale)
                grad = grad * scale - entries * inside
                if tile == 2:
                    values = pltpu.roll(d_keys_values[2, places], 64, 1)
                    grad = jnp.where(low, grad, values + d_keys_values[3, places])
                flat_hidden[token_rows(block), pl.ds(256 + tile * 128, 128)] = grad.astype(half)

    move.sent(*to_partner)

    @pl.loop(0, 4)
    def _(step):
        rows = flat_hidden[wide(step * 256, 256), d_projected_at]

        @pl.loop(0, 4)
        def _(col):
            cols = wide(col * 512, 512)
            block = across(rows, flat_wq[cols])
            partial[wide(step * 2, 2), :, :, cols] = block.reshape(2, 2, 64, 512).astype(half)

    halves = [move.send(partial.at[2 * to + other], from_partner.at[to], partner) for to in order]
    move.arrive(load_tok)

    for block in range(4):
        strip = pl.ds(1024 + 384 * (block // 2), 384)
        product = down(
            flat_grads[:, pl.ds(block * 512, 512)], flat_hidden[:, d_projected_at]
        )
        flat_d[pl.ds(512 * (block % 2), 512), strip] = product.astype(half)

    for peer in [partner] + line + cross:
        pl.semaphore_signal(tokens_used, inc=1, device_id=peer, device_id_type=MESH)

    def head_block(head, at):
        rows = wide(((head % 4) * 4 + at) * 64, 64)
        return flat_d.at[rows, pl.ds(1024 + 384 * (head // 4), 384)]

    qkv_pieces = []
    for step, peer in zip(steps, line):
        pairs = [(head_block(head, ahead(z, step)), qkv_in.at[z, head]) for head in range(8)]
        qkv_pieces.append(move.send_parts(pairs, (qkv_in.at[z], qkv_in.at[z]), peer))
    d_norms = []
    for to, arrived, peer in zip(others, halves, plane):
        move.arrive(arrived)
        add_blocks(partial.at[2 * to + core], from_partner.at[to], from_partner.at[to])
        d_norms.append(move.send(from_partner.at[to], came.at[chip], peer))
    downs = [move.send(wd.at[to], down_came.at[chip], peer) for to, peer in zip(others, plane)]
    downs.append(move.keep(wd.at[chip], down_came.at[chip]))
    move.arrive(halves[3])
    add_blocks(partial.at[me], from_partner.at[chip], from_partner.at[chip])

    for slot, handles in ((0, pieces), (1, later)):
        move.arrive(*handles)
        loads = load(lambda side, slot=slot: gate_up_in.at[side, slot])
        for side in (0, 1):
            move.arrive(loads[side])
            add_loaded(side, chip)

    blocks = all_out.reshape(16, 64, D)

    def back_block(to_core, to_z):
        return all_wg.at[chip, to_core, to_z], blocks.at[8 + 2 * z + core]

    pl.semaphore_wait(tokens_used, 7)
    gate_ups = []
    for step, peer, peer_cross in zip(steps, line, cross):
        to = ahead(z, step)
        gate_ups.append(move.send(*back_block(core, to), peer))
        gate_ups.append(move.send(*back_block(other, to), peer_cross))
    gate_ups.append(move.send(*back_block(other, z), partner))
    gate_ups.append(move.keep(*back_block(core, z)))

    move.arrive(*sums)
    for row in range(2):

        def body3(part):
            result = hidden_in[row, part] + all_tok[z, row, part].astype(full)
            for step in steps:
                result += all_tok[4 + ahead(z, step), row, part].astype(full)
            out_sum[row, part] = result.astype(half)

        chunks(64, body3)

    move.arrive(*d_norms)
    gain_part2[...] = jnp.zeros_like(gain_part2)
    for row in range(2):

        def body4(part):
            result = from_partner[chip, row, part].astype(full)
            for peer_chip in others:
                result += came[peer_chip, row, part].astype(full)
            entries = tok[row, part].astype(full)
            scale = lax.rsqrt(jnp.mean(entries * entries, axis=-1, keepdims=True) + EPSILON)
            gain_part2[...] += jnp.sum(result * entries * scale, axis=0, keepdims=True)
            result = result * gain_attn[...]
            inside = jnp.mean(result * entries, axis=-1, keepdims=True) * (scale * scale * scale)
            result = d_hidden_in[row, part] + result * scale - entries * inside
            grad_tok[row, part] = result.astype(half)

        chunks(64, body4)

    def send_heads():
        move.arrive(*qkv_pieces)
        move.sent(*heads[1:])
        for head in range(8):
            result = head_block(head, z)[...].astype(full)
            for step in steps:
                result += qkv_in[ahead(z, step), head].astype(full)
            wq_send[head] = result.astype(half)
        copies = [move.send(wq_send.at[peer[0]], qkv_came.at[me], peer) for peer in everyone]
        return copies + [move.keep(wq_send.at[me], qkv_came.at[me])]

    flat_packed = packed.reshape(512, 128)
    first = 2 * COL_ROWS
    line_lanes = lax.broadcasted_iota(jnp.int32, (1, 128), 1)
    flat_packed[pl.ds(first + 33, 512 - first - 33)] = jnp.zeros((512 - first - 33, 128), full)

    def statistics(slot, read):
        count, width, row_at, col_at = MATRICES[slot]
        own_rows, some = pl.ds(row_at, count), pl.ds(0, count)
        d_queries[0, some] = jnp.zeros((count, 128), full)

        @pl.loop(0, width // 128)
        def _(step):
            entries = read(step)
            d_queries[0, some] += entries * entries

        mean = jnp.sum(d_queries[0, some], axis=-1, keepdims=True) / width + SQUARE_EPSILON
        new = BETA * rows[own_rows] + (1.0 - BETA) * mean
        rows_new[own_rows] = new
        row_factors[own_rows] = lax.rsqrt(new)
        d_keys_values[0, some] = jnp.broadcast_to(1.0 / new, (count, 128))

        @pl.loop(0, width // 128)
        def _(step):
            entries = read(step)
            square = entries * entries
            flat_packed[pl.ds(col_at + step, 1)] = (
                jnp.sum(square, axis=0, keepdims=True) + count * SQUARE_EPSILON
            )
            flat_packed[pl.ds(COL_ROWS + col_at + step, 1)] = jnp.sum(
                square * d_keys_values[0, some], axis=0, keepdims=True
            )

        stats = flat_packed[pl.ds(first + 33, 1)]
        stats = jnp.where(line_lanes == slot, jnp.sum(new, axis=0, keepdims=True), stats)
        stats = jnp.where(line_lanes == 4 + slot, total(weight_sums[slot]), stats)
        flat_packed[pl.ds(first + 33, 1)] = stats

    def lanes_of(step):
        return wide(step * 128, 128)

    def four(buffer):
        def read(step):
            result = buffer[0, :, lanes_of(step)].astype(full)
            for slot in range(1, 4):
                result += buffer[slot, :, lanes_of(step)].astype(full)
            return result

        return read

    out_here, down_here = blocks, all_norm.reshape(4, 256, D)
    move.arrive(*outs)
    out_load = move.keep(out_came, out_here.at[pl.ds(0, 4)])
    qkv_copies = send_heads()
    move.arrive(*downs)
    move.sent(*branch_copies[2:])
    down_load = move.keep(down_came, down_here)
    move.arrive(out_load)
    statistics(1, four(out_here))
    move.arrive(down_load)
    statistics(3, four(down_here))

    move.arrive(*qkv_copies)
    for head in range(8):
        for part in range(2):
            strip = qkv_came[head, :, pl.ds(part * 128, 128)]
            g_qkv[:, pl.ds(head * 256 + part * 128, 128)] = strip.astype(full)
    for pair in range(4):
        keys = qkv_came[2 * pair, :, pl.ds(256, 128)].astype(full)
        values = qkv_came[2 * pair + 1, :, pl.ds(256, 128)].astype(full)
        g_qkv[:, pl.ds(2048 + pair * 128, 128)] = jnp.where(low, keys, pltpu.roll(values, 64, 1))
        g_qkv[:, pl.ds(2560 + pair * 128, 128)] = jnp.where(low, pltpu.roll(keys, 64, 1), values)

    @pl.loop(0, QKV // 128)
    def _(step):
        entries = m_qkv[:, lanes_of(step)]
        weight_sums[0, :, pl.ds(0, 128)] += jnp.sum((entries * entries).reshape(8, 8, 128), axis=0)

    statistics(0, lambda step: g_qkv[:, lanes_of(step)])
    for slot in range(16):
        strip = pl.ds(slot * 128, 128)
        flat_packed[pl.ds(first + slot, 1)] = gain_part2[:, strip]
        flat_packed[pl.ds(first + 16 + slot, 1)] = gain_part[:, strip]
    flat_packed[pl.ds(first + 32, 1)] = gain_qk[...]

    move.arrive(*gate_ups)
    move.sent(*qkv_pieces)

    def read_gate_up(step):
        inside = lax.rem(step, 64)
        owner = lax.div(inside, 2)
        block = 2 * lax.rem(owner, 4) + lax.rem(lax.div(owner, 4), 2)
        begin = lax.div(step, 64) * 1024 + lax.div(owner, 8) * 256 + lax.rem(inside, 2) * 128
        strip = blocks[8 + block, :, wide(begin, 128)]
        flat_d[wide(lax.div(step, 16) * 64, 64), lanes_of(lax.rem(step, 16))] = strip
        return strip.astype(full)

    statistics(2, read_gate_up)
    for block in range(8):
        move.keep(flat_d.at[pl.ds(64 * block, 64)], gate_up_came.at[:, pl.ds(2048 * block, 2048)])

    copies = [move.send(packed.at[peer[0]], plane_came.at[me], peer) for peer in everyone]
    plane_came[me] = packed[me]
    move.arrive(*copies)
    result = plane_came[0]
    for slot in range(1, 8):
        result = result + plane_came[slot]
    plane_sum[...] = result
    copies = [move.send(plane_sum.at[peer[1]], line_came.at[z], peer) for peer in line]
    line_came[z] = plane_sum[z]
    move.arrive(*copies)
    line_sum[...] = line_came[0] + line_came[1] + line_came[2] + line_came[3]
    copies = [move.send(line_sum, line_all.at[z], peer) for peer in line]
    line_all[z] = line_sum[...]
    move.arrive(*copies)
    copies = [move.send(line_all, totals.at[me], peer) for peer in everyone]
    totals[me] = line_all[...]
    move.arrive(*copies)
    derive_updates(
        totals.reshape(512, 128), col_moments, gain_moments, gains,
        cols_new, col_factors, moments_new, gains_new, grad_gains, spreads,
    )
    move.finish()


def split_local(
    tokens, doc_starts, grad_out, qkv_master, out_master, gate_up_master, down_master, gains,
    qkv_rows, out_rows, gate_up_rows, down_rows, col_moments, gain_moments,
):
    half, full = jnp.bfloat16, jnp.float32
    gain_query, gain_key = gains[2 * D : 2 * D + HEAD_DIM], gains[2 * D + HEAD_DIM :]
    gain_heads = jnp.stack(
        [jnp.concatenate([gain_query, gain_query]), jnp.concatenate([gain_key, gain_key])]
    )
    lane = np.arange(128)
    rates = ROPE_BASE ** (-(lane % 32) * 2.0 / HEAD_DIM)
    rates = jnp.asarray(np.stack([rates, np.where(lane % 64 < 32, -1.0, 1.0)]), full)

    def near(*shape, kind=half):
        return pltpu.VMEM(shape, kind)

    masters = (qkv_master, out_master, gate_up_master, down_master)
    stats_shape = (8, 4, 16, 128)
    (
        output, grad_tokens, grad_qkv, gate_up_came, out_came, down_came, rows_new, row_factors,
        cols_new, col_factors, moments_new, gains_new, grad_gains, spreads, *_,
    ) = exchange(
        layer_kernel, 0,
        [
            (tokens, True), (doc_starts, None), (rates, True), (jnp.asarray(place_tables(512)), True),
            (gains[None, :D], True),
            (gains[None, D : 2 * D], True), (gain_heads, True), (gains.reshape(-1, 128), True),
            (grad_out, True), (qkv_master, True), (out_master, False), (down_master, False),
            (gate_up_master, False),
            (jnp.concatenate([qkv_rows, out_rows, gate_up_rows, down_rows])[:, None], True),
            (col_moments.reshape(-1, 128), True), (gain_moments.reshape(-1, 128), True),
        ],
        [
            ((2, 64, D), half, True), ((2, 64, D), half, True), ((64, QKV), full, True),
            ((64, 2 * FF), half, False), ((4, 64, D), half, False), ((4, 256, D), half, False),
            ((448, 1), full, True), ((448, 1), full, True),
            ((COL_ROWS, 128), full, True), ((1, COLS), full, True),
            ((GAIN_ROWS, 128), full, True), ((GAIN_ROWS, 128), full, True),
            ((GAIN_ROWS, 128), full, True), ((1, 128), full, True),
            ((2, 2, 512, 1024), half, False), ((2, 512, 1024), half, False),
            ((8, 2, 64, D), half, False),
        ],
        [
            near(8, 2, 64, 384, kind=full), near(2, 2, 512, 128), near(2, 4, 512, 128),
            near(8, 2, 64, 256, kind=full), near(2, 8, 1, 128, kind=full),
            near(8, 64, 384), near(2, 64, D), near(8, 2, 64, D), near(8, 4, 64, 384), near(4, 64, D),
            near(8, 2, 64, D), near(4, 2, 64, D), near(4, 2, 64, D), near(2, 64, D, kind=full),
            near(4, 2, 2, 64, D), near(4, 2, 2, 64, D), near(4, 2, 4, 64, 2048), near(4, 256, D),
            near(4, 256, 1024), near(4, 256, 2048),
            near(2, 512, 128, kind=full), near(4, 512, 128, kind=full), near(4, 8, 64, 384),
            near(2, 64, D, kind=full), near(1, D, kind=full), near(1, D, kind=full),
            near(1, 128, kind=full), near(4, 8, D, kind=full), near(8, 64, 384),
            near(*stats_shape, kind=full), near(*stats_shape, kind=full),
            near(*stats_shape[1:], kind=full), near(*stats_shape[1:], kind=full),
            near(*stats_shape[2:], kind=full), near(*stats_shape[1:], kind=full),
            near(*stats_shape, kind=full),
            pltpu.SemaphoreType.REGULAR, pltpu.SemaphoreType.REGULAR,
        ],
        (176, 56), 170 << 20, 48 << 30,
    )
    grads = (
        grad_qkv, jnp.sum(out_came.astype(full), axis=0), gate_up_came.astype(full),
        jnp.sum(down_came.astype(full), axis=0),
    )
    new_masters = []
    for slot, (count, width, row_at, col_at) in enumerate(MATRICES):
        row_factor = row_factors[row_at : row_at + count]
        col_factor = col_factors[:, col_at * 128 : col_at * 128 + width]
        new_masters.append(masters[slot] - grads[slot] * row_factor * col_factor)
    return (
        output,
        grad_tokens,
        *grads,
        grad_gains.reshape(-1),
        *[rows_new[row_at : row_at + count, 0] for count, _, row_at, _ in MATRICES],
        cols_new.reshape(-1),
        moments_new.reshape(-1),
        *new_masters,
        *[master.astype(half) for master in new_masters],
        gains_new.reshape(-1),
        spreads[0, :8],
    )


def optimizer_step(
    grads, gain_local, masters, gains, row_states, col_moments, gain_moments, total_fn
):
    beta = 1.0 - STEP ** (-0.8)
    col_widths = (QKV, D, 2 * FF, D)
    row_totals = (D, HEADS * HEAD_DIM, D, FF)
    squares = [gradient * gradient + SQUARE_EPSILON for gradient in grads]
    rows_new = [
        beta * row_state + (1.0 - beta) * jnp.mean(square, axis=1)
        for row_state, square in zip(row_states, squares)
    ]
    col_local = [jnp.sum(square, axis=0) for square in squares]
    weighted_local = [
        jnp.sum(gradient * gradient / row_new[:, None], axis=0)
        for gradient, row_new in zip(grads, rows_new)
    ]
    stats_local = jnp.stack(
        [jnp.sum(row_new) for row_new in rows_new]
        + [jnp.sum(master * master) for master in masters]
    )
    totals = total_fn(jnp.concatenate(col_local + weighted_local + [stats_local, gain_local]))
    cols = sum(col_widths)
    col_sums, weighted = totals[:cols], totals[cols : 2 * cols]
    stats, grad_gains = totals[2 * cols : 2 * cols + 8], totals[2 * cols + 8 :]
    col_divisor = jnp.concatenate(
        [
            jnp.full((col_width,), float(row_total), jnp.float32)
            for col_width, row_total in zip(col_widths, row_totals)
        ]
    )
    cols_new = beta * col_moments + (1.0 - beta) * col_sums / col_divisor
    new_masters = []
    spreads = []
    begin_at = 0
    for slot in range(4):
        col_part = cols_new[begin_at : begin_at + col_widths[slot]]
        weighted_part = weighted[begin_at : begin_at + col_widths[slot]]
        begin_at = begin_at + col_widths[slot]
        mean_rows = stats[slot] / row_totals[slot]
        unit = (
            grads[slot]
            * lax.rsqrt(rows_new[slot] / mean_rows)[:, None]
            * lax.rsqrt(col_part)[None, :]
        )
        entries_all = float(row_totals[slot] * col_widths[slot])
        spread = jnp.sqrt(mean_rows * jnp.sum(weighted_part / col_part) / entries_all)
        scale = STEP_RATE * jnp.maximum(SCALE_EPSILON, jnp.sqrt(stats[4 + slot] / entries_all))
        new_masters.append(masters[slot] - scale * unit / jnp.maximum(1.0, spread / CLIP_LEVEL))
        spreads.append(spread)
    bounds = (0, D, 2 * D, 2 * D + HEAD_DIM, 2 * D + 2 * HEAD_DIM)
    moment_parts, gain_parts = ([], [])
    for segment in range(4):
        gradient = grad_gains[bounds[segment] : bounds[segment + 1]]
        gain_old = gains[bounds[segment] : bounds[segment + 1]]
        moment_new = beta * gain_moments[bounds[segment] : bounds[segment + 1]] + (1.0 - beta) * (
            gradient * gradient + SQUARE_EPSILON
        )
        unit = gradient * lax.rsqrt(moment_new)
        spread = jnp.sqrt(jnp.mean(unit * unit))
        scale = STEP_RATE * jnp.maximum(SCALE_EPSILON, jnp.sqrt(jnp.mean(gain_old * gain_old)))
        moment_parts.append(moment_new)
        gain_parts.append(gain_old - scale * unit / jnp.maximum(1.0, spread / CLIP_LEVEL))
        spreads.append(spread)
    return (
        grad_gains,
        *rows_new,
        cols_new,
        jnp.concatenate(moment_parts),
        *new_masters,
        *[master.astype(jnp.bfloat16) for master in new_masters],
        jnp.concatenate(gain_parts),
        jnp.stack(spreads),
    )


def solution(mesh):
    split = mesh.shape["seq"] == 8 and mesh.shape["rows"] == 4
    return jax.shard_map(
        split_local if split else gathered_local,
        mesh=mesh,
        in_specs=(
            P("rows", "seq", None),
            P("rows", None),
            P("rows", "seq", None),
            P(("seq", "rows"), None),
            P(("seq", "rows"), None),
            P(("seq", "rows"), None),
            P(("seq", "rows"), None),
            P(),
            P(("seq", "rows")),
            P(("seq", "rows")),
            P(("seq", "rows")),
            P(("seq", "rows")),
            P(),
            P(),
        ),
        out_specs=(
            P("rows", "seq", None),
            P("rows", "seq", None),
            P(("seq", "rows"), None),
            P(("seq", "rows"), None),
            P(("seq", "rows"), None),
            P(("seq", "rows"), None),
            P(),
            P(("seq", "rows")),
            P(("seq", "rows")),
            P(("seq", "rows")),
            P(("seq", "rows")),
            P(),
            P(),
            P(("seq", "rows"), None),
            P(("seq", "rows"), None),
            P(("seq", "rows"), None),
            P(("seq", "rows"), None),
            P(("seq", "rows"), None),
            P(("seq", "rows"), None),
            P(("seq", "rows"), None),
            P(("seq", "rows"), None),
            P(),
            P(),
        ),
        check_vma=False,
    )
```

```python
from functools import partial

import jax
import jax.numpy as jnp
import numpy as np
from jax import lax
from jax.experimental import pallas as pl
from jax.experimental.pallas import tpu as pltpu
from jax.sharding import PartitionSpec as P

D = 2048
HEADS = 32
KV_HEADS = 8
HEAD_DIM = 64
FF = 8192
STEP = 10
QKV = 3072


EPSILON = 1e-06
ROPE_BASE = 10000.0
MASKED_SCORE = -1e30
STEP_RATE = 0.3
CLIP_LEVEL = 1.0
SQUARE_EPSILON = 1e-30
SCALE_EPSILON = 0.001


def from_behind(value, axis, steps):
    count = lax.axis_size(axis)
    pairs = [(source, (source + steps) % count) for source in range(count)]
    return lax.ppermute(value, axis, pairs)


def norm_rows(entries, gain):
    return entries * lax.rsqrt(jnp.mean(entries * entries, axis=-1, keepdims=True) + EPSILON) * gain


def turn(entries, cos_wide, sin_wide):
    half_width = entries.shape[-1] // 2
    turned = jnp.concatenate([-entries[..., half_width:], entries[..., :half_width]], axis=-1)
    return entries * cos_wide + turned * sin_wide


def doc_tables(doc_starts, places):
    before = doc_starts[:, None, :] <= places[None, :, None]
    doc_ids = jnp.sum(before.astype(jnp.int32), axis=-1)
    doc_first = jnp.max(jnp.where(before, doc_starts[:, None, :], 0), axis=-1)
    return (doc_ids, places[None, :] - doc_first)


def rotary(offsets):
    frequency = ROPE_BASE ** (-(jnp.arange(HEAD_DIM // 2, dtype=jnp.float32) * 2.0 / HEAD_DIM))
    angles = offsets.astype(jnp.float32)[..., None] * frequency
    cos_table = jnp.concatenate([jnp.cos(angles), jnp.cos(angles)], axis=-1)
    sin_table = jnp.concatenate([jnp.sin(angles), jnp.sin(angles)], axis=-1)
    return (cos_table, sin_table)


def queries_keys(
    cos_table, sin_table, projected, gain_query, gain_key, heads=HEADS, kv_heads=KV_HEADS
):
    rows_here, seq_here = (projected.shape[0], projected.shape[1])
    att_width = heads * HEAD_DIM
    queries = projected[..., :att_width].reshape(rows_here, seq_here, heads, HEAD_DIM)
    keys_rot = projected[..., att_width : att_width + kv_heads * HEAD_DIM].reshape(
        rows_here, seq_here, kv_heads, HEAD_DIM
    )
    cos_wide = cos_table[:, :, None, :]
    sin_wide = sin_table[:, :, None, :]
    queries = turn(norm_rows(queries, gain_query), cos_wide, sin_wide) * HEAD_DIM ** (-0.5)
    keys_rot = turn(norm_rows(keys_rot, gain_key), cos_wide, sin_wide)
    return (queries, keys_rot)


def mask_of(query_docs, query_places, key_docs, key_places):
    same_doc = query_docs[:, :, None] == key_docs[:, None, :]
    causal = query_places[None, :, None] >= key_places[None, None, :]
    return (same_doc & causal)[:, None, None, :, :]


def gathered_local(
    tokens,
    doc_starts,
    grad_out,
    qkv_master,
    out_master,
    gate_up_master,
    down_master,
    gains,
    qkv_rows,
    out_rows,
    gate_up_rows,
    down_rows,
    col_moments,
    gain_moments,
):
    cycle_size = lax.axis_size("seq")
    seq_index = lax.axis_index("seq")
    rows_dev, seq_dev = (tokens.shape[0], tokens.shape[1])
    group_size = HEADS // KV_HEADS
    att_width = HEADS * HEAD_DIM
    kv_width = KV_HEADS * HEAD_DIM
    gain_attn = gains[:D]
    gain_ffn = gains[D : 2 * D]
    gain_query = gains[2 * D : 2 * D + HEAD_DIM]
    gain_key = gains[2 * D + HEAD_DIM :]
    local_places = jnp.arange(seq_dev, dtype=jnp.int32)
    places = seq_index * seq_dev + local_places
    query_docs, offsets = doc_tables(doc_starts, places)
    cos_table, sin_table = rotary(offsets)
    copies = (
        qkv_master.astype(jnp.bfloat16),
        out_master.astype(jnp.bfloat16),
        gate_up_master.astype(jnp.bfloat16),
        down_master.astype(jnp.bfloat16),
    )
    w_qkv, w_out, w_gate_up, w_down = (
        lax.all_gather(copies[0], ("seq", "rows"), axis=0, tiled=True),
        lax.all_gather(copies[1], ("seq", "rows"), axis=0, tiled=True),
        lax.all_gather(copies[2], ("seq", "rows"), axis=0, tiled=True),
        lax.all_gather(copies[3], ("seq", "rows"), axis=0, tiled=True),
    )
    tokens_wide = tokens.astype(jnp.float32)
    normed = norm_rows(tokens_wide, gain_attn).astype(jnp.bfloat16)
    projected = jnp.einsum("rtd,de->rte", normed, w_qkv, preferred_element_type=jnp.float32)
    head_fn = partial(queries_keys, cos_table, sin_table)
    queries, keys_rot = head_fn(projected, gain_query, gain_key)
    query16 = queries.astype(jnp.bfloat16).reshape(
        rows_dev, seq_dev, KV_HEADS, group_size, HEAD_DIM
    )
    keys16 = keys_rot.astype(jnp.bfloat16).reshape(rows_dev, seq_dev, kv_width)
    values16 = projected[..., att_width + kv_width :].astype(jnp.bfloat16)
    stat_shape = (rows_dev, KV_HEADS, group_size, seq_dev)
    initial = (
        jnp.full(stat_shape, MASKED_SCORE, jnp.float32),
        jnp.zeros(stat_shape, jnp.float32),
        jnp.zeros(stat_shape + (HEAD_DIM,), jnp.float32),
    )
    carry = initial
    key_piece = lax.all_gather(keys16, "seq", axis=1, tiled=True)
    value_piece = lax.all_gather(values16, "seq", axis=1, tiled=True)
    key_count = key_piece.shape[1]

    def absorb_block(state, block_index):
        best, total, summed = state
        block_begin = block_index * seq_dev
        key_block = lax.dynamic_slice_in_dim(key_piece, block_begin, seq_dev, 1).reshape(
            rows_dev, seq_dev, KV_HEADS, HEAD_DIM
        )
        value_block = lax.dynamic_slice_in_dim(value_piece, block_begin, seq_dev, 1).reshape(
            rows_dev, seq_dev, KV_HEADS, HEAD_DIM
        )
        key_places = block_begin + jnp.arange(seq_dev, dtype=jnp.int32)
        key_docs, _ = doc_tables(doc_starts, key_places)
        allowed = mask_of(query_docs, places, key_docs, key_places)
        scores = jnp.einsum(
            "rqkgh,rtkh->rkgqt", query16, key_block, preferred_element_type=jnp.float32
        )
        scores = jnp.where(allowed, scores, MASKED_SCORE)
        best_new = jnp.maximum(best, jnp.max(scores, axis=-1))
        weights = jnp.where(allowed, jnp.exp(scores - best_new[..., None]), 0.0)
        factor = jnp.exp(best - best_new)
        total = total * factor + jnp.sum(weights, axis=-1)
        summed = summed * factor[..., None] + jnp.einsum(
            "rkgqt,rtkh->rkgqh",
            weights.astype(jnp.bfloat16),
            value_block,
            preferred_element_type=jnp.float32,
        )
        return ((best_new, total, summed), None)

    carry, _ = lax.scan(absorb_block, carry, jnp.arange(key_count // seq_dev, dtype=jnp.int32))
    best, total, summed = carry
    log_total = best + jnp.log(total)
    attended = summed / total[..., None]
    attended16 = (
        attended.transpose(0, 3, 1, 2, 4).reshape(rows_dev, seq_dev, att_width).astype(jnp.bfloat16)
    )
    branch = jnp.einsum("rtc,cd->rtd", attended16, w_out, preferred_element_type=jnp.float32)
    hidden_in = tokens_wide + branch
    normed2 = norm_rows(hidden_in, gain_ffn).astype(jnp.bfloat16)
    gate_up = jnp.einsum("rtd,df->rtf", normed2, w_gate_up, preferred_element_type=jnp.float32)
    gate_part, up_part = (gate_up[..., :FF], gate_up[..., FF:])
    hidden = (jax.nn.silu(gate_part) * up_part).astype(jnp.bfloat16)
    output = hidden_in + jnp.einsum(
        "rtf,fd->rtd", hidden, w_down, preferred_element_type=jnp.float32
    )
    d_hidden = jnp.einsum("rtd,fd->rtf", grad_out, w_down, preferred_element_type=jnp.float32)
    silu_value, silu_back = jax.vjp(jax.nn.silu, gate_part)
    d_gate = silu_back(d_hidden * up_part)[0]
    d_gate_up = jnp.concatenate([d_gate, d_hidden * silu_value], axis=-1).astype(jnp.bfloat16)
    d_normed2 = jnp.einsum("rtf,df->rtd", d_gate_up, w_gate_up, preferred_element_type=jnp.float32)
    _, ffn_norm_back = jax.vjp(norm_rows, hidden_in, gain_ffn)
    d_inner, grad_gain_ffn = ffn_norm_back(d_normed2)
    d_hidden_in = grad_out.astype(jnp.float32) + d_inner
    term_down = jnp.einsum("rtf,rtd->fd", hidden, grad_out, preferred_element_type=jnp.float32)
    grad_down = lax.psum_scatter(term_down, ("seq", "rows"), scatter_dimension=0, tiled=True)
    term_gate_up = jnp.einsum("rtd,rtf->df", normed2, d_gate_up, preferred_element_type=jnp.float32)
    grad_gate_up = lax.psum_scatter(term_gate_up, ("seq", "rows"), scatter_dimension=0, tiled=True)
    d_branch = d_hidden_in.astype(jnp.bfloat16)
    term_out = jnp.einsum("rtc,rtd->cd", attended16, d_branch, preferred_element_type=jnp.float32)
    d_attended = jnp.einsum(
        "rtd,cd->rtc", d_branch, w_out, preferred_element_type=jnp.float32
    ).astype(jnp.bfloat16)
    d_heads = d_attended.reshape(rows_dev, seq_dev, KV_HEADS, group_size, HEAD_DIM).transpose(
        0, 2, 3, 1, 4
    )
    delta = jnp.sum(d_heads.astype(jnp.float32) * attended, axis=-1)

    def cycle_turn(turn_index, carry):
        pair16, grad_pair, d_queries = carry
        source = (seq_index + turn_index) % cycle_size
        key_places = source * seq_dev + local_places
        key_docs, _ = doc_tables(doc_starts, key_places)
        allowed = mask_of(query_docs, places, key_docs, key_places)
        key_block = pair16[0].reshape(rows_dev, seq_dev, KV_HEADS, HEAD_DIM)
        value_block = pair16[1].reshape(rows_dev, seq_dev, KV_HEADS, HEAD_DIM)
        scores = jnp.einsum(
            "rqkgh,rtkh->rkgqt", query16, key_block, preferred_element_type=jnp.float32
        )
        scores = jnp.where(allowed, scores, MASKED_SCORE)
        probs = jnp.where(allowed, jnp.exp(scores - log_total[..., None]), 0.0)
        d_values = jnp.einsum(
            "rkgqt,rkgqh->rtkh",
            probs.astype(jnp.bfloat16),
            d_heads,
            preferred_element_type=jnp.float32,
        )
        d_probs = jnp.einsum(
            "rkgqh,rtkh->rkgqt", d_heads, value_block, preferred_element_type=jnp.float32
        )
        d_scores = (probs * (d_probs - delta[..., None])).astype(jnp.bfloat16)
        d_queries = d_queries + jnp.einsum(
            "rkgqt,rtkh->rkgqh", d_scores, key_block, preferred_element_type=jnp.float32
        )
        d_keys = jnp.einsum(
            "rkgqt,rqkgh->rtkh", d_scores, query16, preferred_element_type=jnp.float32
        )
        grad_pair = grad_pair + jnp.stack(
            [
                d_keys.reshape(rows_dev, seq_dev, kv_width),
                d_values.reshape(rows_dev, seq_dev, kv_width),
            ]
        )
        grad_pair = from_behind(grad_pair.astype(jnp.bfloat16), "seq", -1).astype(grad_pair.dtype)
        pair16 = from_behind(pair16, "seq", -1)
        return (pair16, grad_pair, d_queries)

    start_pair = jnp.stack([keys16, values16])
    start_grads = jnp.zeros((2, rows_dev, seq_dev, kv_width), jnp.float32)
    start_queries = jnp.zeros(stat_shape + (HEAD_DIM,), jnp.float32)
    _, grad_pair, d_queries = lax.fori_loop(
        0, cycle_size, cycle_turn, (start_pair, start_grads, start_queries)
    )
    d_queries = d_queries.transpose(0, 3, 1, 2, 4).reshape(rows_dev, seq_dev, HEADS, HEAD_DIM)
    d_keys_home = grad_pair[0].reshape(rows_dev, seq_dev, KV_HEADS, HEAD_DIM)
    _, heads_back = jax.vjp(head_fn, projected, gain_query, gain_key)
    d_projected, grad_gain_query, grad_gain_key = heads_back((d_queries, d_keys_home))
    d_projected = jnp.concatenate(
        [d_projected[..., : att_width + kv_width], grad_pair[1]], axis=-1
    ).astype(jnp.bfloat16)
    term_qkv = jnp.einsum("rtd,rte->de", normed, d_projected, preferred_element_type=jnp.float32)
    d_normed = jnp.einsum("rte,de->rtd", d_projected, w_qkv, preferred_element_type=jnp.float32)
    _, attn_norm_back = jax.vjp(norm_rows, tokens_wide, gain_attn)
    d_tokens_part, grad_gain_attn = attn_norm_back(d_normed)
    grad_tokens = (d_hidden_in + d_tokens_part).astype(jnp.bfloat16)
    grad_qkv, grad_out_proj = (
        lax.psum_scatter(term_qkv, ("seq", "rows"), scatter_dimension=0, tiled=True),
        lax.psum_scatter(term_out, ("seq", "rows"), scatter_dimension=0, tiled=True),
    )
    gain_local = jnp.concatenate([grad_gain_attn, grad_gain_ffn, grad_gain_query, grad_gain_key])
    grads = (grad_qkv, grad_out_proj, grad_gate_up, grad_down)
    updated = optimizer_step(
        grads, gain_local, (qkv_master, out_master, gate_up_master, down_master), gains,
        (qkv_rows, out_rows, gate_up_rows, down_rows), col_moments, gain_moments,
        lambda vector: lax.psum(vector, ("seq", "rows")),
    )
    return (output.astype(jnp.bfloat16), grad_tokens, *grads, *updated)


MESH = pl.DeviceIdType.MESH
PLACES = 32
VMEM_BYTES = 61 * 1024 * 1024
CHUNK = 16


def here():
    seq = lax.axis_index("seq")
    return lax.div(seq, 2), lax.rem(seq, 2), lax.axis_index("rows")


def flips(chip):
    return (chip + 1 - 2 * lax.rem(chip, 2), lax.rem(chip + 2, 4), 3 - chip)


def ahead(z, step):
    return lax.rem(z + step, 4)


def at_place(chip, core, z):
    return (2 * chip + core, z)


def greet(peers):
    barrier = pltpu.get_barrier_semaphore()
    for peer in peers:
        pl.semaphore_signal(barrier, inc=1, device_id=peer, device_id_type=MESH)
    pl.semaphore_wait(barrier, len(peers))


class Mover:
    def __init__(self, send_sem, recv_sem, local_sem):
        self.send_sem, self.recv_sem, self.local_sem = send_sem, recv_sem, local_sem
        self.remote, self.own, self.lines, self.scattered = [], [], [], []
        self.used = 0

    def copy_of(self, src, dst, peer, send_slot, recv_slot):
        return pltpu.make_async_remote_copy(
            src_ref=src,
            dst_ref=dst,
            send_sem=self.send_sem.at[send_slot],
            recv_sem=self.recv_sem.at[recv_slot],
            device_id=peer,
            device_id_type=MESH,
        )

    def send_parts(self, pairs, whole, peer):
        slot = self.used
        self.used += 1
        for src, dst in pairs:
            self.copy_of(src, dst, peer, slot, slot).start()
        copy = self.copy_of(whole[0], whole[1], peer, slot, slot)
        handle = [copy, False, copy.wait_recv, False]
        self.remote.append(handle)
        return handle

    def send(self, src, dst, peer):
        return self.send_parts([(src, dst)], (src, dst), peer)

    def keep_parts(self, pairs, whole):
        sem = self.local_sem.at[len(self.own)]
        for src, dst in pairs:
            pltpu.make_async_copy(src, dst, sem).start()
        copy = pltpu.make_async_copy(whole[0], whole[1], sem)
        handle = [copy, False, copy.wait]
        self.own.append(handle)
        return handle

    def keep(self, src, dst):
        return self.keep_parts([(src, dst)], (src, dst))

    def line(self, source, block_of, chip, core, z):
        line = (self.used, block_of, chip, core, z)
        self.used += 5
        base = line[0]
        up, low = at_place(chip, core, z + 1), at_place(chip, core, z - 1)
        rising = self.copy_of(source, block_of(z), up, base, base + 3)
        falling = self.copy_of(source, block_of(z), low, base + 4, base + 1)
        pl.when(z < 3)(rising.start)
        pl.when(z > 0)(falling.start)
        self.lines += [(z < 3, rising), (z > 0, falling)]
        return line

    def wait_line(self, line, step, when=None):
        base, block_of, chip, core, z = line
        block = block_of(ahead(z, step))
        peer = at_place(chip, core, ahead(z, step))
        copy = self.copy_of(block, block, peer, base + step, base + step)
        if when is None:
            copy.wait_recv()
        else:
            pl.when(when)(copy.wait_recv)
        return block

    def arrive_line(self, line, step, when=None):
        base, _, chip, core, z = line
        block = self.wait_line(line, step, when)
        rises, falls = (z + step >= 4) & (z < 3), (z + step < 4) & (z > 0)
        up, low = at_place(chip, core, z + 1), at_place(chip, core, z - 1)
        rising = self.copy_of(block, block, up, base + step, base + step - 1)
        falling = self.copy_of(block, block, low, base + step, base + step + 1)
        for moves, copy in ((rises, rising), (falls, falling)):
            moves = moves if when is None else moves & when
            pl.when(moves)(copy.start)
            self.lines.append((moves, copy))
        return block

    def scatter(self, source, target, steps, chip, core, z):
        base = self.used
        self.used += 3

        def start(index):
            at = ahead(z, steps[index])
            copy = self.copy_of(
                source(at), target(z), at_place(chip, core, at), base + index, base + 3 - steps[index]
            )
            copy.start()
            self.scattered.append(copy)

        def wait():
            for step in (1, 2, 3):
                at = ahead(z, step)
                peer = at_place(chip, core, at)
                self.copy_of(source(at), target(at), peer, base, base + step - 1).wait_recv()

        return start, wait

    def arrive(self, *handles):
        for handle in handles:
            if not handle[1]:
                handle[1] = True
                handle[2]()

    def sent(self, *handles):
        for handle in handles:
            if not handle[3]:
                handle[3] = True
                handle[0].wait_send()

    def sent_lines(self):
        for when, copy in self.lines:
            pl.when(when)(copy.wait_send)
        self.lines = []

    def sent_sums(self):
        for copy in self.scattered:
            copy.wait_send()
        self.scattered = []

    def finish(self):
        assert self.used <= self.send_sem.shape[0] and len(self.own) <= self.local_sem.shape[0]
        self.arrive(*self.own, *self.remote)
        self.sent(*self.remote)
        self.sent_lines()
        self.sent_sums()


def semaphores(remote, own):
    return [
        pltpu.SemaphoreType.DMA((remote,)),
        pltpu.SemaphoreType.DMA((remote,)),
        pltpu.SemaphoreType.DMA((max(own, 1),)),
    ]


def exchange(kernel, ident, inputs, outputs, scratch, copies, moved, flops=0):
    spaces = {True: pltpu.VMEM, False: pl.ANY, None: pltpu.SMEM}
    specs = {near: pl.BlockSpec(memory_space=space) for near, space in spaces.items()}
    return pl.pallas_call(
        kernel,
        out_shape=[jax.ShapeDtypeStruct(shape, kind) for shape, kind, _ in outputs],
        in_specs=[specs[near] for _, near in inputs],
        out_specs=[specs[near] for _, _, near in outputs],
        scratch_shapes=scratch + semaphores(*copies),
        compiler_params=pltpu.CompilerParams(
            collective_id=ident, has_side_effects=True, vmem_limit_bytes=VMEM_BYTES
        ),
        cost_estimate=pl.CostEstimate(flops=flops, bytes_accessed=moved, transcendentals=0),
    )(*[array for array, _ in inputs])


def chunks(length, body):
    @pl.loop(0, length // CHUNK)
    def _(step):
        body(pl.ds(pl.multiple_of(step * CHUNK, CHUNK), CHUNK))


def add_blocks(first, second, result):
    for row in range(2):

        def body(part):
            total = first[row, part].astype(jnp.float32) + second[row, part].astype(jnp.float32)
            result[row, part] = total.astype(result.dtype)

        chunks(64, body)


def lower_half(shape):
    return lax.broadcasted_iota(jnp.int32, shape, len(shape) - 1) < 64


def swap_halves(entries):
    lane = lax.broadcasted_iota(jnp.int32, entries.shape, 1)
    return jnp.where(lax.rem(lane, 64) < 32, pltpu.roll(entries, 96, 1), pltpu.roll(entries, 32, 1))


def head_means(entries):
    lower = lower_half(entries.shape)
    low = jnp.sum(jnp.where(lower, entries, 0.0), axis=-1, keepdims=True)
    high = jnp.sum(jnp.where(lower, 0.0, entries), axis=-1, keepdims=True)
    return jnp.where(lower, low, high) * (1.0 / HEAD_DIM)


def wide(start, size):
    return pl.ds(pl.multiple_of(start, size), size)


def plain(left, right):
    return jnp.dot(left, right, preferred_element_type=jnp.float32)


def across(left, right):
    return lax.dot_general(
        left, right, (((1,), (1,)), ((), ())), preferred_element_type=jnp.float32
    )


def down(left, right):
    return lax.dot_general(
        left, right, (((0,), (0,)), ((), ())), preferred_element_type=jnp.float32
    )


def attention_probs(queries, keys, first, part):
    scores = across(queries, keys)
    place = lax.broadcasted_iota(jnp.int32, scores.shape, 1)
    query = lax.broadcasted_iota(jnp.int32, scores.shape, 0) + part * 128
    allowed = (place >= first) & (place <= query)
    scores = jnp.where(allowed, scores, MASKED_SCORE)
    best = jnp.max(scores, axis=-1, keepdims=True)
    weights = jnp.where(allowed, jnp.exp(scores - best), 0.0)
    return weights / jnp.sum(weights, axis=-1, keepdims=True)


COL_ROWS, GAIN_ROWS = 184, 33
COLS = COL_ROWS * 128
MATRICES = ((64, QKV, 0, 0), (64, D, 64, 24), (64, 2 * FF, 128, 40), (256, D, 192, 168))
ROW_TOTALS = (D, HEADS * HEAD_DIM, D, FF)
BETA = 1.0 - STEP ** (-0.8)


def lane_value(vector, lane):
    lanes = lax.broadcasted_iota(jnp.int32, (1, 128), 1)
    return jnp.sum(jnp.where(lanes == lane, vector, 0.0), axis=-1, keepdims=True)


def total(entries):
    return jnp.sum(jnp.sum(entries, axis=-1, keepdims=True), axis=0, keepdims=True)


def document_start(starts, row, place):
    start = jnp.zeros_like(place)
    for document in range(starts.shape[1]):
        begin = starts[row, document]
        start = jnp.maximum(start, jnp.where(place >= begin, begin, 0))
    return start


def place_tables(length):
    rates = ROPE_BASE ** (-(np.arange(128) % 32) * 2.0 / HEAD_DIM)
    angles = np.arange(length)[:, None] * rates
    return np.stack([np.cos(angles), np.sin(angles)]).astype(np.float32)


def derive_updates(
    flat, col_moments, gain_moments, gains,
    cols_new, col_factors, moments_new, gains_new, grad_gains, spreads,
):
    first = 2 * COL_ROWS
    stats = flat[first + 33 : first + 34]
    lanes = lax.broadcasted_iota(jnp.int32, (1, 128), 1)
    out = jnp.zeros((1, 128), jnp.float32)
    for slot, (_, width, _, col_at) in enumerate(MATRICES):
        own = pl.ds(col_at, width // 128)
        entries_all = float(ROW_TOTALS[slot] * width)
        new = BETA * col_moments[own] + (1.0 - BETA) * (flat[own] / ROW_TOTALS[slot])
        cols_new[own] = new
        mean_rows = lane_value(stats, slot) / ROW_TOTALS[slot]
        ratio = total(flat[pl.ds(COL_ROWS + col_at, width // 128)] / new)
        spread = jnp.sqrt(mean_rows * ratio / entries_all)
        scale = STEP_RATE * jnp.maximum(
            SCALE_EPSILON, jnp.sqrt(lane_value(stats, 4 + slot) / entries_all)
        )
        factor = scale * jnp.sqrt(mean_rows) / jnp.maximum(1.0, spread / CLIP_LEVEL)
        factors = lax.rsqrt(new) * factor
        for row in range(width // 128):
            col_factors[:, pl.ds((col_at + row) * 128, 128)] = factors[row : row + 1]
        out = jnp.where(lanes == slot, spread, out)
    gradient = flat[first : first + GAIN_ROWS]
    grad_gains[...] = gradient
    old = gains[...]
    new = BETA * gain_moments[...] + (1.0 - BETA) * (gradient * gradient + SQUARE_EPSILON)
    moments_new[...] = new
    unit = gradient * lax.rsqrt(new)
    row = lax.broadcasted_iota(jnp.int32, (GAIN_ROWS, 128), 0)
    lane = lax.broadcasted_iota(jnp.int32, (GAIN_ROWS, 128), 1)
    segment = jnp.where(row < 16, 0, jnp.where(row < 32, 1, jnp.where(lane < 64, 2, 3)))
    factors = jnp.zeros((GAIN_ROWS, 128), jnp.float32)
    for slot, count in enumerate((D, D, HEAD_DIM, HEAD_DIM)):
        mask = segment == slot
        spread = jnp.sqrt(total(jnp.where(mask, unit * unit, 0.0)) / count)
        mean = total(jnp.where(mask, old * old, 0.0)) / count
        scale = STEP_RATE * jnp.maximum(SCALE_EPSILON, jnp.sqrt(mean))
        factors = jnp.where(mask, scale / jnp.maximum(1.0, spread / CLIP_LEVEL), factors)
        out = jnp.where(lanes == 4 + slot, spread, out)
    gains_new[...] = old - factors * unit
    spreads[...] = out


def layer_kernel(
    tok, starts, rates, places_at, gain_attn, gain_ffn, gain_heads, gains, grad_out,
    m_qkv, m_out, m_down, m_gate_up, rows, col_moments, gain_moments,
    out_sum, grad_tok, g_qkv, gate_up_came, out_came, down_came, rows_new, row_factors,
    cols_new, col_factors, moments_new, gains_new, grad_gains, spreads,
    gate_up_in, gate_up_mid, kept_tok,
    projected, queries, keys_values, attended, document_tables,
    wq_send, normed, all_tok, all_wq, all_wo, partial, from_partner, came,
    hidden_in, all_norm, all_out, all_wg, wd, hidden, d_gate_up,
    d_queries, d_keys_values, qkv_in, d_hidden_in, gain_part, gain_part2, gain_qk, weight_sums, qkv_came,
    packed, plane_came, plane_sum, line_came, line_sum, line_all, totals, credit, place_free, *sems,
):
    half, full = jnp.bfloat16, jnp.float32
    chip, core, z = here()
    others = flips(chip)
    other = 1 - core
    me = 2 * chip + core
    partner = at_place(chip, other, z)
    plane = [at_place(peer_chip, core, z) for peer_chip in others]
    plane_cross = [at_place(peer_chip, other, z) for peer_chip in others]
    steps = (2, 1, 3)
    line = [at_place(chip, core, ahead(z, step)) for step in steps]
    cross = [at_place(chip, other, ahead(z, step)) for step in steps]
    everyone = [partner] + plane + plane_cross
    greet(everyone + line + cross)
    move = Mover(*sems)
    line_grads = move.line(grad_out, lambda at: all_out.at[at, core], chip, core, z)

    for head in range(8):
        wq_send[head, :, pl.ds(0, 256)] = m_qkv[:, pl.ds(head * 256, 256)].astype(half)
    low = lower_half((64, 128))
    for pair in range(4):
        keys = m_qkv[:, pl.ds(2048 + pair * 128, 128)]
        values = m_qkv[:, pl.ds(2560 + pair * 128, 128)]
        tail = pl.ds(256, 128)
        wq_send[2 * pair, :, tail] = jnp.where(low, keys, pltpu.roll(values, 64, 1)).astype(half)
        wq_send[2 * pair + 1, :, tail] = jnp.where(low, pltpu.roll(keys, 64, 1), values).astype(half)
    heads = [move.keep(wq_send.at[me], all_wq.at[me, z])]
    for peer in everyone:
        heads.append(move.send(wq_send.at[peer[0]], all_wq.at[me, z], peer))

    for row in range(2):

        def body0(part):
            result = tok[row, part].astype(full)
            scale = lax.rsqrt(jnp.mean(result * result, axis=-1, keepdims=True) + EPSILON)
            normed[row, part] = (result * scale * gain_attn[...]).astype(half)

        chunks(64, body0)
    token_copies = [move.send(normed, all_tok.at[me], peer) for peer in plane]
    token_copies.append(move.send(normed, all_tok.at[me], partner))
    tokens_here = move.keep(normed, all_tok.at[me])
    move.arrive(*heads)
    line_wq = move.line(all_wq.at[:, z], lambda at: all_wq.at[:, at], chip, core, z)
    flat_d = d_gate_up.reshape(1024, 2048)
    weight_sums[...] = jnp.zeros_like(weight_sums)
    for row in range(2):
        for document in range(starts.shape[1]):
            angle = starts[row, document].astype(full) * rates[0:1]
            document_tables[row, 2 * document] = jnp.cos(angle)
            document_tables[row, 2 * document + 1] = jnp.sin(angle)

    def cast_all(slot, blocks):
        loads = [move.keep(blocks[0][0], hidden_in.at[0])]
        for index, (_, target) in enumerate(blocks):
            if index + 1 < len(blocks):
                loads.append(move.keep(blocks[index + 1][0], hidden_in.at[(index + 1) % 2]))
            move.arrive(loads[index])

            def body(part, index=index, target=target):
                entries = hidden_in[index % 2, part]
                weight_sums[slot] += jnp.sum((entries * entries).reshape(2, 8, D), axis=0)
                target(part, entries.astype(half))

            chunks(64, body)

    def into(ref):
        def store(part, entries):
            ref[part] = entries

        return store

    def by_device(block):
        cols = pl.ds((block // 4) * 1024 + (block % 4) * 256, 256)

        def store(part, entries):
            for index in range(8):
                place = (index % 4) * 2 + index // 4
                rows_at = wide(place * 64 + part.start, CHUNK)
                flat_d[rows_at, cols] = entries[:, index * 256 : (index + 1) * 256]

        return store

    cast_all(1, [(m_out, into(all_wo.at[z]))])
    wo_copies = [move.send(all_wo.at[z], all_wo.at[z], peer) for peer in line]
    cast_all(
        3,
        [
            (m_down.at[pl.ds(64 * block, 64)], into(wd.at[chip, pl.ds(64 * block, 64)]))
            for block in range(4)
        ],
    )
    by_x, by_y = plane[0], plane[1]
    front, back = wd.at[chip, pl.ds(0, 128)], wd.at[chip, pl.ds(128, 128)]
    down_copies = [
        move.send(front, front, by_x), move.send(back, back, by_y),
        move.send(back, back, by_x), move.send(front, front, by_y),
    ]
    move.arrive_line(line_wq, 3)
    move.arrive_line(line_wq, 1)
    cast_all(
        2,
        [(m_gate_up.at[:, pl.ds(2048 * block, 2048)], by_device(block)) for block in range(8)],
    )
    move.arrive_line(line_wq, 2)

    def turn_block(to_core, to_z, side):
        lanes = pl.ds(side * 1024, 1024)
        src = flat_d.at[wide((to_z * 2 + to_core) * 64, 64), lanes]
        return src, all_wg.at[chip, core, z, :, lanes]

    turned, turned_own = ([], []), []
    for side in range(2):
        for step, peer, peer_cross in zip(steps, line, cross):
            to = ahead(z, step)
            turned[side].append(move.send(*turn_block(core, to, side), peer))
            turned[side].append(move.send(*turn_block(other, to, side), peer_cross))
        turned[side].append(move.send(*turn_block(other, z, side), partner))
        turned_own.append(move.keep(*turn_block(core, z, side)))
    own = [
        move.keep(grad_out, all_out.at[z, core]),
        move.send(grad_out, all_out.at[z, core], partner),
    ]

    for peer_chip, handle in zip(others, tuple(token_copies)):
        move.arrive(handle)
        block = all_tok.at[2 * peer_chip + core]
        token_copies.append(move.send(block, block, partner))
    move.arrive(tokens_here, *token_copies, *wo_copies)
    saved = [move.keep(all_tok, kept_tok)]

    def tables_of(block, row):
        place = lax.broadcasted_iota(jnp.int32, (64, 1), 0) + block * 64
        start_cos, start_sin = document_tables[row, 0], document_tables[row, 1]
        for document in range(1, starts.shape[1]):
            inside = place >= starts[row, document]
            start_cos = jnp.where(inside, document_tables[row, 2 * document], start_cos)
            start_sin = jnp.where(inside, document_tables[row, 2 * document + 1], start_sin)
        at = wide(block * 64, 64)
        place_cos, place_sin = places_at[0, at], places_at[1, at]
        cosine = place_cos * start_cos + place_sin * start_sin
        return cosine, (place_sin * start_cos - place_cos * start_sin) * rates[1:2]

    def first_of(row, part):
        place = lax.broadcasted_iota(jnp.int32, (128, 1), 0) + part * 128
        return document_start(starts, row, place)

    flat_tok, flat_wq = all_tok.reshape(1024, D), all_wq.reshape(D, 384)
    flat_wo = all_wo.reshape(256, D)

    @pl.loop(0, 4)
    def _(step):
        block = plain(flat_tok[wide(step * 256, 256)], flat_wq[...])
        projected[wide(step * 2, 2)] = block.reshape(2, 2, 64, 384)

    @pl.loop(0, 8)
    def _(block):
        for row in range(2):
            cosine, sine = tables_of(block, row)
            places = wide(block * 64, 64)
            for tile in range(3):
                entries = projected[block, row, :, pl.ds(tile * 128, 128)]
                gain = gain_heads[min(tile, 2) // 2 : min(tile, 2) // 2 + 1]
                scale = lax.rsqrt(head_means(entries * entries) + EPSILON)
                turned_entries = entries * scale * gain
                turned_entries = turned_entries * cosine + swap_halves(turned_entries) * sine
                if tile < 2:
                    queries[row, tile, places] = (turned_entries * HEAD_DIM ** (-0.5)).astype(half)
                else:
                    zero = jnp.zeros_like(entries)
                    rolled = pltpu.roll(turned_entries, 64, 1)
                    values = pltpu.roll(entries, 64, 1)
                    keys_values[row, 0, places] = jnp.where(low, turned_entries, zero).astype(half)
                    keys_values[row, 1, places] = jnp.where(low, zero, rolled).astype(half)
                    keys_values[row, 2, places] = jnp.where(low, values, zero).astype(half)
                    keys_values[row, 3, places] = jnp.where(low, zero, entries).astype(half)

    move.arrive(*down_copies[:2])
    front, back = wd.at[others[0], pl.ds(0, 128)], wd.at[others[1], pl.ds(128, 128)]
    down_copies += [move.send(front, front, by_y), move.send(back, back, by_x)]

    @pl.loop(0, 2)
    def _(row):
        for tile in range(2):
            for part in range(4):
                own_places, upto = pl.ds(part * 128, 128), pl.ds(0, (part + 1) * 128)
                result = jnp.zeros((128, 128), full)
                for side in range(2):
                    probs = attention_probs(
                        queries[row, tile, own_places], keys_values[row, side, upto],
                        first_of(row, part), part,
                    )
                    result += plain(probs.astype(half), keys_values[row, 2 + side, upto])
                attended[pl.ds(2 * part, 2), row, :, pl.ds(tile * 128, 128)] = result.reshape(2, 64, 128)

    flat_attended = attended.reshape(1024, 256)

    @pl.loop(0, 4)
    def _(step):
        rows = flat_attended[wide(step * 256, 256)].astype(half)

        @pl.loop(0, 4)
        def _(col):
            cols = wide(col * 512, 512)
            block = plain(rows, flat_wo[:, cols])
            partial[wide(step * 2, 2), :, :, cols] = block.reshape(2, 2, 64, 512).astype(half)

    order = tuple(others) + (chip,)
    halves = [move.send(partial.at[2 * to + other], from_partner.at[to], partner) for to in order]
    sums = []
    for to, arrived, peer in zip(others, halves, plane):
        move.arrive(arrived)
        add_blocks(partial.at[2 * to + core], from_partner.at[to], from_partner.at[to])
        sums.append(move.send(from_partner.at[to], came.at[chip], peer))
    def gather_weights(side):
        move.arrive(turned_own[side], *turned[side])
        lanes = pl.ds(side * 1024, 1024)
        front, back = all_wg.at[chip, 0, :, :, lanes], all_wg.at[chip, 1, :, :, lanes]
        return [
            move.send(front, front, by_x), move.send(back, back, by_y),
            move.send(back, back, by_x), move.send(front, front, by_y),
        ]

    def pass_weights(side, copies):
        move.arrive(*copies[:2])
        lanes = pl.ds(side * 1024, 1024)
        front, back = all_wg.at[others[0], 0, :, :, lanes], all_wg.at[others[1], 1, :, :, lanes]
        return [move.send(front, front, by_y), move.send(back, back, by_x)]

    gate_copies = gather_weights(0)
    move.sent(*token_copies)
    move.arrive(halves[3], *sums)
    for row in range(2):

        def body(part):
            result = tok[row, part].astype(full)
            result += partial[me, row, part].astype(full)
            result += from_partner[chip, row, part].astype(full)
            for peer_chip in others:
                result += came[peer_chip, row, part].astype(full)
            hidden_in[row, part] = result
            scale = lax.rsqrt(jnp.mean(result * result, axis=-1, keepdims=True) + EPSILON)
            normed[row, part] = (result * scale * gain_ffn[...]).astype(half)

        chunks(64, body)
    move.sent(*sums, *halves)
    move.arrive(*saved)
    line_norms = move.line(normed, lambda at: all_norm.at[at, core], chip, core, z)
    own.append(move.send(normed, all_norm.at[z, core], partner))
    own.append(move.keep(normed, all_norm.at[z, core]))

    up_copies = gather_weights(1)
    at_first, at_last = lax.div(3 - z, 3), lax.div(z, 3)
    arrivals = (3 - 2 * at_first, 1 + at_first + at_last, 2 + at_first - at_last)
    inner = (z > 0) & (z < 3)
    shared = []

    def share(step, wait_only=False):
        for line_of in (line_grads, line_norms):
            if wait_only:
                block = move.wait_line(line_of, step, jnp.logical_not(inner))
            else:
                block = move.arrive_line(line_of, step)
            shared.append(move.send(block, block, partner))

    flat_wg, flat_wd = all_wg.reshape(D, 2048), wd.reshape(1024, D)

    def d_hidden_of(zb):
        @pl.loop(0, 4)
        def _(step):
            cols = wide(step * 256, 256)
            hidden[zb, :, cols] = across(all_out[zb].reshape(256, D), flat_wd[cols]).astype(half)

    share(arrivals[0])
    gate_copies += pass_weights(0, gate_copies)
    move.arrive(*own[:2], *down_copies)
    d_hidden_of(z)
    share(arrivals[1])
    up_copies += pass_weights(1, up_copies)
    move.arrive(shared[0])
    d_hidden_of(ahead(z, arrivals[0]))
    for line_of in (line_grads, line_norms):
        move.arrive_line(line_of, arrivals[2], inner)
    move.arrive(shared[2])
    d_hidden_of(ahead(z, arrivals[1]))
    weights = gate_copies + up_copies
    move.arrive(*weights, *own)
    move.sent(*turned[0], *turned[1])

    def block_of(zb):
        @pl.loop(0, 4)
        def _(step):
            cols, ups = wide(step * 256, 256), wide(1024 + step * 256, 256)
            rows = all_norm[zb].reshape(256, D)
            gate = plain(rows, flat_wg[:, cols])
            up = plain(rows, flat_wg[:, ups])
            d_hidden = hidden[zb, :, cols].astype(full)
            sigmoid = 1.0 / (1.0 + jnp.exp(-gate))
            silu = gate * sigmoid
            hidden[zb, :, cols] = (silu * up).astype(half)
            d_gate = d_hidden * up * (sigmoid * (1.0 + gate * (1.0 - sigmoid)))
            d_gate_up[zb, :, cols] = d_gate.astype(half)
            d_gate_up[zb, :, ups] = (d_hidden * silu).astype(half)

        @pl.loop(0, 8)
        def _(step):
            cols = wide(step * 256, 256)
            block = across(d_gate_up[zb], flat_wg[cols])
            partial[pl.ds(2 * zb, 2), :, :, cols] = block.reshape(2, 2, 64, 256).astype(half)

    def pair_sum(zb, handle, into, base):
        move.arrive(handle)
        add_blocks(partial.at[2 * zb + core], into.at[base + zb], into.at[base + zb])

    start_sum, wait_sums = move.scatter(
        lambda at: from_partner.at[at], lambda at: came.at[at], arrivals, chip, core, z
    )
    to_partner = []
    walk = [z] + [ahead(z, step) for step in arrivals]
    for index, zb in enumerate(walk):
        if index > 0:
            move.arrive(*shared[2 * index - 2 : 2 * index])
        if index == 3:
            d_hidden_of(zb)
        block_of(zb)
        to_partner.append(move.send(partial.at[2 * zb + other], from_partner.at[zb], partner))
        if index == 0:
            share(arrivals[2], True)
        if index > 0:
            pair_sum(walk[index - 1], to_partner[index - 1], from_partner, 0)
        if index > 1:
            start_sum(index - 2)
    pair_sum(walk[3], to_partner[3], from_partner, 0)
    start_sum(2)

    flat_norm, flat_grads = all_norm.reshape(1024, D), all_out.reshape(1024, D)
    flat_hidden = hidden.reshape(1024, 1024)
    move.sent(*weights)

    def gate_up_grad(to, side):
        rows, lanes = wide(to * 512, 512), pl.ds(side * 1024, 1024)

        @pl.loop(0, 2)
        def _(step):
            cols = wide(side * 1024 + step * 512, 512)
            flat_wg[rows, cols] = down(flat_norm[:, rows], flat_d[:, cols]).astype(half)

        return flat_wg.at[rows, lanes]

    passed = []
    for side in (0, 1):
        passed.append(move.send(gate_up_grad(others[2], side), gate_up_mid.at[side], plane[side]))
    move.sent(*to_partner)
    to_partner, sums = [], []
    walk = [ahead(z, step) for step in steps] + [z]
    for index, zb in enumerate(walk):

        @pl.loop(0, 4)
        def _(step, zb=zb):
            cols = wide(step * 512, 512)
            block = plain(hidden[zb], flat_wd[:, cols])
            partial[pl.ds(2 * zb, 2), :, :, cols] = block.reshape(2, 2, 64, 512).astype(half)

        to_partner.append(move.send(partial.at[2 * zb + other], all_tok.at[zb], partner))
        if index > 0:
            before = walk[index - 1]
            pair_sum(before, to_partner[index - 1], all_tok, 0)
            sums.append(move.send(all_tok.at[before], all_tok.at[4 + z], line[index - 1]))
    pair_sum(z, to_partner[3], all_tok, 0)

    direct = [gate_up_grad(others[side], side) for side in (0, 1)]
    handed = [gate_up_grad(others[1 - side], side) for side in (0, 1)]
    for side in (0, 1):
        gate_up_grad(chip, side)
    move.sent(*shared, own[2])
    move.sent_lines()
    for peer in [partner] + plane:
        pl.semaphore_signal(credit, inc=1, device_id=peer, device_id_type=MESH)

    wait_sums()
    gain_part[...] = jnp.zeros_like(gain_part)
    for row in range(2):

        def body2(part):
            result = from_partner[z, row, part].astype(full)
            for step in steps:
                result += came[ahead(z, step), row, part].astype(full)
            entries = hidden_in[row, part]
            scale = lax.rsqrt(jnp.mean(entries * entries, axis=-1, keepdims=True) + EPSILON)
            gain_part[...] += jnp.sum(result * entries * scale, axis=0, keepdims=True)
            result = result * gain_ffn[...]
            inside = jnp.mean(result * entries, axis=-1, keepdims=True) * (scale * scale * scale)
            grad = grad_out[row, part].astype(full) + result * scale - entries * inside
            d_hidden_in[row, part] = grad
            normed[row, part] = grad.astype(half)

        chunks(64, body2)
    pl.semaphore_wait(credit, 4)
    move.sent_sums()
    all_branch = all_norm.reshape(8, 2, 64, D)
    branches = [move.send(normed, all_branch.at[me], peer) for peer in plane]
    branch_copies = [
        move.send(normed, all_branch.at[me], partner), move.keep(normed, all_branch.at[me])
    ]
    pieces = [
        move.send(direct[side], gate_up_in.at[side, 0], plane[side]) for side in (0, 1)
    ]

    move.sent(*down_copies, *wo_copies)

    @pl.loop(0, 4)
    def _(to):
        rows_at = wide(to * 256, 256)

        @pl.loop(0, 4)
        def _(step):
            cols = wide(step * 512, 512)
            flat_wd[rows_at, cols] = down(flat_hidden[:, rows_at], flat_grads[:, cols]).astype(half)

    load_tok = move.keep(kept_tok, all_out.reshape(8, 2, 64, D))

    def load(source):
        return [
            move.keep(source(side), flat_d.at[pl.ds(side * 512, 512), pl.ds(0, 1024)])
            for side in (0, 1)
        ]

    def add_loaded(side, chunk):
        @pl.loop(0, 512 // CHUNK)
        def _(step):
            lanes = pl.ds(side * 1024, 1024)
            rows = wide(chunk * 512 + step * CHUNK, CHUNK)
            extra = flat_d[wide(side * 512 + step * CHUNK, CHUNK), pl.ds(0, 1024)]
            result = flat_wg[rows, lanes].astype(full) + extra.astype(full)
            flat_wg[rows, lanes] = result.astype(half)

    move.arrive(*passed)
    move.sent(*passed)
    for peer in [partner] + line + cross:
        pl.semaphore_signal(place_free, inc=1, device_id=peer, device_id_type=MESH)
    loads = load(lambda side: gate_up_mid.at[side])
    later = []
    for side in (0, 1):
        move.arrive(loads[side])
        add_loaded(side, others[1 - side])
        later.append(move.send(handed[side], gate_up_in.at[side, 1], plane[1 - side]))
    for peer_chip, handle in zip(others, branches):
        move.arrive(handle)
        block = all_branch.at[2 * peer_chip + core]
        branch_copies.append(move.send(block, block, partner))
    move.arrive(*branch_copies)

    flat_branch = all_branch.reshape(1024, D)
    flat_wo = all_wo.reshape(256, D)
    d_heads_at, d_projected_at = pl.ds(0, 256), pl.ds(256, 384)

    @pl.loop(0, 4)
    def _(step):
        rows = wide(step * 256, 256)
        flat_hidden[rows, d_heads_at] = across(flat_branch[rows], flat_wo[...]).astype(half)

    @pl.loop(0, 4)
    def _(step):
        cols = wide(step * 512, 512)
        block = down(flat_attended[...].astype(half), flat_branch[:, cols])
        flat_wo[:, cols] = block.astype(half)

    outs = [
        move.send(all_wo.at[ahead(z, step)], out_came.at[z], peer) for step, peer in zip(steps, line)
    ]
    outs.append(move.keep(all_wo.at[z], out_came.at[z]))
    lower = lower_half((128, 128))
    line_low = lower_half((1, 128))
    gain_qk[...] = jnp.zeros_like(gain_qk)

    @pl.loop(0, 2)
    def _(row):
        d_keys_values[...] = jnp.zeros_like(d_keys_values)

        def token_rows(block):
            return wide((2 * block + row) * 64, 64)

        for tile in range(2):
            lanes = pl.ds(tile * 128, 128)
            for part in range(4):
                own_places, upto = pl.ds(part * 128, 128), pl.ds(0, (part + 1) * 128)
                d_heads = jnp.concatenate(
                    [flat_hidden[token_rows(2 * part + index), lanes] for index in range(2)], axis=0
                )
                products = d_heads.astype(full) * attended[pl.ds(2 * part, 2), row, :, lanes].reshape(128, 128)
                query = queries[row, tile, own_places]
                result = jnp.zeros((128, 128), full)
                for side in range(2):
                    mask = lower if side == 0 else jnp.logical_not(lower)
                    delta = jnp.sum(jnp.where(mask, products, 0.0), axis=-1, keepdims=True)
                    keys = keys_values[row, side, upto]
                    probs = attention_probs(query, keys, first_of(row, part), part)
                    d_probs = across(d_heads, keys_values[row, 2 + side, upto])
                    d_scores = (probs * (d_probs - delta)).astype(half)
                    result += plain(d_scores, keys)
                    d_keys_values[side, upto] += down(d_scores, query)
                    d_keys_values[2 + side, upto] += down(probs.astype(half), d_heads)
                d_queries[tile, own_places] = result

        @pl.loop(0, 8)
        def _(block):
            cosine, sine = tables_of(block, row)
            places = wide(block * 64, 64)
            for tile in range(3):
                entries = projected[block, row, :, pl.ds(tile * 128, 128)]
                gain = gain_heads[tile // 2 : tile // 2 + 1]
                scale = lax.rsqrt(head_means(entries * entries) + EPSILON)
                if tile < 2:
                    grad = d_queries[tile, places] * HEAD_DIM ** (-0.5)
                else:
                    from_low, from_high = d_keys_values[0, places], d_keys_values[1, places]
                    grad = jnp.where(low, from_low + pltpu.roll(from_high, 64, 1), 0.0)
                grad = grad * cosine + swap_halves(grad * sine)
                for_gain = jnp.sum(grad * entries * scale, axis=0, keepdims=True)
                if tile < 2:
                    for_gain = jnp.where(line_low, for_gain + pltpu.roll(for_gain, 64, 1), 0.0)
                else:
                    for_gain = jnp.where(line_low, 0.0, pltpu.roll(for_gain, 64, 1))
                gain_qk[...] += for_gain
                grad = grad * gain
                inside = head_means(grad * entries) * (scale * scale * scale)
                grad = grad * scale - entries * inside
                if tile == 2:
                    values = pltpu.roll(d_keys_values[2, places], 64, 1)
                    grad = jnp.where(low, grad, values + d_keys_values[3, places])
                flat_hidden[token_rows(block), pl.ds(256 + tile * 128, 128)] = grad.astype(half)

    for slot, handles in ((0, pieces), (1, later)):
        move.arrive(*handles)
        loads = load(lambda side, slot=slot: gate_up_in.at[side, slot])
        for side in (0, 1):
            move.arrive(loads[side])
            add_loaded(side, chip)

    def back_block(to_core, to_z):
        return all_wg.at[chip, to_core, to_z], all_wg.at[others[2], core, z]

    pl.semaphore_wait(place_free, 7)
    gate_ups = []
    for step, peer, peer_cross in zip(steps, line, cross):
        to = ahead(z, step)
        gate_ups.append(move.send(*back_block(core, to), peer))
        gate_ups.append(move.send(*back_block(other, to), peer_cross))
    gate_ups.append(move.send(*back_block(other, z), partner))
    gate_ups.append(move.keep(*back_block(core, z)))

    move.sent(*to_partner)

    @pl.loop(0, 4)
    def _(step):
        rows = flat_hidden[wide(step * 256, 256), d_projected_at]

        @pl.loop(0, 4)
        def _(col):
            cols = wide(col * 512, 512)
            block = across(rows, flat_wq[cols])
            partial[wide(step * 2, 2), :, :, cols] = block.reshape(2, 2, 64, 512).astype(half)

    halves = [move.send(partial.at[2 * to + other], from_partner.at[to], partner) for to in order]
    move.arrive(load_tok)

    for block in range(4):
        strip = pl.ds(1024 + 384 * (block // 2), 384)
        product = down(
            flat_grads[:, pl.ds(block * 512, 512)], flat_hidden[:, d_projected_at]
        )
        flat_d[pl.ds(512 * (block % 2), 512), strip] = product.astype(half)

    def head_block(head, at):
        rows = wide(((head % 4) * 4 + at) * 64, 64)
        return flat_d.at[rows, pl.ds(1024 + 384 * (head // 4), 384)]

    qkv_pieces = []
    for step, peer in zip(steps, line):
        pairs = [(head_block(head, ahead(z, step)), qkv_in.at[z, head]) for head in range(8)]
        qkv_pieces.append(move.send_parts(pairs, (qkv_in.at[z], qkv_in.at[z]), peer))
    d_norms = []
    for to, arrived, peer in zip(others, halves, plane):
        move.arrive(arrived)
        add_blocks(partial.at[2 * to + core], from_partner.at[to], from_partner.at[to])
        d_norms.append(move.send(from_partner.at[to], came.at[chip], peer))
    downs = [move.send(wd.at[to], down_came.at[chip], peer) for to, peer in zip(others, plane)]
    downs.append(move.keep(wd.at[chip], down_came.at[chip]))
    move.arrive(halves[3])
    add_blocks(partial.at[me], from_partner.at[chip], from_partner.at[chip])

    move.arrive(*sums)
    for row in range(2):

        def body3(part):
            result = hidden_in[row, part] + all_tok[z, row, part].astype(full)
            for step in steps:
                result += all_tok[4 + ahead(z, step), row, part].astype(full)
            out_sum[row, part] = result.astype(half)

        chunks(64, body3)

    move.arrive(*d_norms)
    gain_part2[...] = jnp.zeros_like(gain_part2)
    for row in range(2):

        def body4(part):
            result = from_partner[chip, row, part].astype(full)
            for peer_chip in others:
                result += came[peer_chip, row, part].astype(full)
            entries = tok[row, part].astype(full)
            scale = lax.rsqrt(jnp.mean(entries * entries, axis=-1, keepdims=True) + EPSILON)
            gain_part2[...] += jnp.sum(result * entries * scale, axis=0, keepdims=True)
            result = result * gain_attn[...]
            inside = jnp.mean(result * entries, axis=-1, keepdims=True) * (scale * scale * scale)
            result = d_hidden_in[row, part] + result * scale - entries * inside
            grad_tok[row, part] = result.astype(half)

        chunks(64, body4)

    def send_heads():
        move.arrive(*qkv_pieces)
        move.sent(*heads[1:])
        for head in range(8):
            result = head_block(head, z)[...].astype(full)
            for step in steps:
                result += qkv_in[ahead(z, step), head].astype(full)
            wq_send[head] = result.astype(half)
        copies = [move.send(wq_send.at[peer[0]], qkv_came.at[me], peer) for peer in everyone]
        return copies + [move.keep(wq_send.at[me], qkv_came.at[me])]

    flat_packed = packed.reshape(512, 128)
    first = 2 * COL_ROWS
    line_lanes = lax.broadcasted_iota(jnp.int32, (1, 128), 1)
    flat_packed[pl.ds(first + 33, 512 - first - 33)] = jnp.zeros((512 - first - 33, 128), full)

    def statistics(slot, read):
        count, width, row_at, col_at = MATRICES[slot]
        own_rows, some = pl.ds(row_at, count), pl.ds(0, count)
        d_queries[0, some] = jnp.zeros((count, 128), full)

        @pl.loop(0, width // 128)
        def _(step):
            entries = read(step)
            d_queries[0, some] += entries * entries

        mean = jnp.sum(d_queries[0, some], axis=-1, keepdims=True) / width + SQUARE_EPSILON
        new = BETA * rows[own_rows] + (1.0 - BETA) * mean
        rows_new[own_rows] = new
        row_factors[own_rows] = lax.rsqrt(new)
        d_keys_values[0, some] = jnp.broadcast_to(1.0 / new, (count, 128))

        @pl.loop(0, width // 128)
        def _(step):
            entries = read(step)
            square = entries * entries
            flat_packed[pl.ds(col_at + step, 1)] = (
                jnp.sum(square, axis=0, keepdims=True) + count * SQUARE_EPSILON
            )
            flat_packed[pl.ds(COL_ROWS + col_at + step, 1)] = jnp.sum(
                square * d_keys_values[0, some], axis=0, keepdims=True
            )

        stats = flat_packed[pl.ds(first + 33, 1)]
        stats = jnp.where(line_lanes == slot, jnp.sum(new, axis=0, keepdims=True), stats)
        stats = jnp.where(line_lanes == 4 + slot, total(weight_sums[slot]), stats)
        flat_packed[pl.ds(first + 33, 1)] = stats

    def lanes_of(step):
        return wide(step * 128, 128)

    def four(buffer):
        def read(step):
            result = buffer[0, :, lanes_of(step)].astype(full)
            for slot in range(1, 4):
                result += buffer[slot, :, lanes_of(step)].astype(full)
            return result

        return read

    out_here, down_here = all_out.reshape(16, 64, D), all_norm.reshape(4, 256, D)
    move.arrive(*outs)
    out_load = move.keep(out_came, out_here.at[pl.ds(0, 4)])
    move.arrive(*downs)
    move.sent(*branch_copies[2:])
    down_load = move.keep(down_came, down_here)
    move.arrive(out_load)
    statistics(1, four(out_here))
    move.arrive(down_load)
    statistics(3, four(down_here))

    move.arrive(*gate_ups)
    move.sent(*pieces, *later)

    def read_gate_up(step):
        inside = lax.rem(step, 64)
        owner = lax.div(inside, 2)
        begin = lax.div(step, 64) * 1024 + lax.div(owner, 8) * 256 + lax.rem(inside, 2) * 128
        strip = all_wg[others[2], lax.rem(lax.div(owner, 4), 2), lax.rem(owner, 4), :, wide(begin, 128)]
        in_order = wide(others[0] * 512 + lax.div(step, 16) * 64, 64)
        flat_wg[in_order, lanes_of(lax.rem(step, 16))] = strip
        return strip.astype(full)

    statistics(2, read_gate_up)
    for block in range(8):
        strip = flat_wg.at[wide(others[0] * 512 + block * 64, 64)]
        move.keep(strip, gate_up_came.at[:, pl.ds(2048 * block, 2048)])
    qkv_copies = send_heads()
    move.arrive(*qkv_copies)
    for head in range(8):
        for part in range(2):
            strip = qkv_came[head, :, pl.ds(part * 128, 128)]
            g_qkv[:, pl.ds(head * 256 + part * 128, 128)] = strip.astype(full)
    for pair in range(4):
        keys = qkv_came[2 * pair, :, pl.ds(256, 128)].astype(full)
        values = qkv_came[2 * pair + 1, :, pl.ds(256, 128)].astype(full)
        g_qkv[:, pl.ds(2048 + pair * 128, 128)] = jnp.where(low, keys, pltpu.roll(values, 64, 1))
        g_qkv[:, pl.ds(2560 + pair * 128, 128)] = jnp.where(low, pltpu.roll(keys, 64, 1), values)

    @pl.loop(0, QKV // 128)
    def _(step):
        entries = m_qkv[:, lanes_of(step)]
        weight_sums[0, :, pl.ds(0, 128)] += jnp.sum((entries * entries).reshape(8, 8, 128), axis=0)

    statistics(0, lambda step: g_qkv[:, lanes_of(step)])
    for slot in range(16):
        strip = pl.ds(slot * 128, 128)
        flat_packed[pl.ds(first + slot, 1)] = gain_part2[:, strip]
        flat_packed[pl.ds(first + 16 + slot, 1)] = gain_part[:, strip]
    flat_packed[pl.ds(first + 32, 1)] = gain_qk[...]

    copies = [move.send(packed.at[peer[0]], plane_came.at[me], peer) for peer in everyone]
    plane_came[me] = packed[me]
    move.arrive(*copies)
    result = plane_came[0]
    for slot in range(1, 8):
        result = result + plane_came[slot]
    plane_sum[...] = result
    copies = [move.send(plane_sum.at[peer[1]], line_came.at[z], peer) for peer in line]
    line_came[z] = plane_sum[z]
    move.arrive(*copies)
    line_sum[...] = line_came[0] + line_came[1] + line_came[2] + line_came[3]
    copies = [move.send(line_sum, line_all.at[z], peer) for peer in line]
    line_all[z] = line_sum[...]
    move.arrive(*copies)
    copies = [move.send(line_all, totals.at[me], peer) for peer in everyone]
    totals[me] = line_all[...]
    move.arrive(*copies)
    derive_updates(
        totals.reshape(512, 128), col_moments, gain_moments, gains,
        cols_new, col_factors, moments_new, gains_new, grad_gains, spreads,
    )
    move.finish()


def split_local(
    tokens, doc_starts, grad_out, qkv_master, out_master, gate_up_master, down_master, gains,
    qkv_rows, out_rows, gate_up_rows, down_rows, col_moments, gain_moments,
):
    half, full = jnp.bfloat16, jnp.float32
    gain_query, gain_key = gains[2 * D : 2 * D + HEAD_DIM], gains[2 * D + HEAD_DIM :]
    gain_heads = jnp.stack(
        [jnp.concatenate([gain_query, gain_query]), jnp.concatenate([gain_key, gain_key])]
    )
    lane = np.arange(128)
    rates = ROPE_BASE ** (-(lane % 32) * 2.0 / HEAD_DIM)
    rates = jnp.asarray(np.stack([rates, np.where(lane % 64 < 32, -1.0, 1.0)]), full)

    def near(*shape, kind=half):
        return pltpu.VMEM(shape, kind)

    masters = (qkv_master, out_master, gate_up_master, down_master)
    stats_shape = (8, 4, 16, 128)
    (
        output, grad_tokens, grad_qkv, gate_up_came, out_came, down_came, rows_new, row_factors,
        cols_new, col_factors, moments_new, gains_new, grad_gains, spreads, *_,
    ) = exchange(
        layer_kernel, 0,
        [
            (tokens, True), (doc_starts, None), (rates, True), (jnp.asarray(place_tables(512)), True),
            (gains[None, :D], True),
            (gains[None, D : 2 * D], True), (gain_heads, True), (gains.reshape(-1, 128), True),
            (grad_out, True), (qkv_master, True), (out_master, False), (down_master, False),
            (gate_up_master, False),
            (jnp.concatenate([qkv_rows, out_rows, gate_up_rows, down_rows])[:, None], True),
            (col_moments.reshape(-1, 128), True), (gain_moments.reshape(-1, 128), True),
        ],
        [
            ((2, 64, D), half, True), ((2, 64, D), half, True), ((64, QKV), full, True),
            ((64, 2 * FF), half, False), ((4, 64, D), half, False), ((4, 256, D), half, False),
            ((448, 1), full, True), ((448, 1), full, True),
            ((COL_ROWS, 128), full, True), ((1, COLS), full, True),
            ((GAIN_ROWS, 128), full, True), ((GAIN_ROWS, 128), full, True),
            ((GAIN_ROWS, 128), full, True), ((1, 128), full, True),
            ((2, 2, 512, 1024), half, False), ((2, 512, 1024), half, False),
            ((8, 2, 64, D), half, False),
        ],
        [
            near(8, 2, 64, 384, kind=full), near(2, 2, 512, 128), near(2, 4, 512, 128),
            near(8, 2, 64, 256, kind=full), near(2, 8, 1, 128, kind=full),
            near(8, 64, 384), near(2, 64, D), near(8, 2, 64, D), near(8, 4, 64, 384), near(4, 64, D),
            near(8, 2, 64, D), near(4, 2, 64, D), near(4, 2, 64, D), near(2, 64, D, kind=full),
            near(4, 2, 2, 64, D), near(4, 2, 2, 64, D), near(4, 2, 4, 64, 2048), near(4, 256, D),
            near(4, 256, 1024), near(4, 256, 2048),
            near(2, 512, 128, kind=full), near(4, 512, 128, kind=full), near(4, 8, 64, 384),
            near(2, 64, D, kind=full), near(1, D, kind=full), near(1, D, kind=full),
            near(1, 128, kind=full), near(4, 8, D, kind=full), near(8, 64, 384),
            near(*stats_shape, kind=full), near(*stats_shape, kind=full),
            near(*stats_shape[1:], kind=full), near(*stats_shape[1:], kind=full),
            near(*stats_shape[2:], kind=full), near(*stats_shape[1:], kind=full),
            near(*stats_shape, kind=full),
            pltpu.SemaphoreType.REGULAR, pltpu.SemaphoreType.REGULAR,
        ],
        (176, 56), 170 << 20, 48 << 30,
    )
    grads = (
        grad_qkv, jnp.sum(out_came.astype(full), axis=0), gate_up_came.astype(full),
        jnp.sum(down_came.astype(full), axis=0),
    )
    new_masters = []
    for slot, (count, width, row_at, col_at) in enumerate(MATRICES):
        row_factor = row_factors[row_at : row_at + count]
        col_factor = col_factors[:, col_at * 128 : col_at * 128 + width]
        new_masters.append(masters[slot] - grads[slot] * row_factor * col_factor)
    return (
        output,
        grad_tokens,
        *grads,
        grad_gains.reshape(-1),
        *[rows_new[row_at : row_at + count, 0] for count, _, row_at, _ in MATRICES],
        cols_new.reshape(-1),
        moments_new.reshape(-1),
        *new_masters,
        *[master.astype(half) for master in new_masters],
        gains_new.reshape(-1),
        spreads[0, :8],
    )


def optimizer_step(
    grads, gain_local, masters, gains, row_states, col_moments, gain_moments, total_fn
):
    beta = 1.0 - STEP ** (-0.8)
    col_widths = (QKV, D, 2 * FF, D)
    row_totals = (D, HEADS * HEAD_DIM, D, FF)
    squares = [gradient * gradient + SQUARE_EPSILON for gradient in grads]
    rows_new = [
        beta * row_state + (1.0 - beta) * jnp.mean(square, axis=1)
        for row_state, square in zip(row_states, squares)
    ]
    col_local = [jnp.sum(square, axis=0) for square in squares]
    weighted_local = [
        jnp.sum(gradient * gradient / row_new[:, None], axis=0)
        for gradient, row_new in zip(grads, rows_new)
    ]
    stats_local = jnp.stack(
        [jnp.sum(row_new) for row_new in rows_new]
        + [jnp.sum(master * master) for master in masters]
    )
    totals = total_fn(jnp.concatenate(col_local + weighted_local + [stats_local, gain_local]))
    cols = sum(col_widths)
    col_sums, weighted = totals[:cols], totals[cols : 2 * cols]
    stats, grad_gains = totals[2 * cols : 2 * cols + 8], totals[2 * cols + 8 :]
    col_divisor = jnp.concatenate(
        [
            jnp.full((col_width,), float(row_total), jnp.float32)
            for col_width, row_total in zip(col_widths, row_totals)
        ]
    )
    cols_new = beta * col_moments + (1.0 - beta) * col_sums / col_divisor
    new_masters = []
    spreads = []
    begin_at = 0
    for slot in range(4):
        col_part = cols_new[begin_at : begin_at + col_widths[slot]]
        weighted_part = weighted[begin_at : begin_at + col_widths[slot]]
        begin_at = begin_at + col_widths[slot]
        mean_rows = stats[slot] / row_totals[slot]
        unit = (
            grads[slot]
            * lax.rsqrt(rows_new[slot] / mean_rows)[:, None]
            * lax.rsqrt(col_part)[None, :]
        )
        entries_all = float(row_totals[slot] * col_widths[slot])
        spread = jnp.sqrt(mean_rows * jnp.sum(weighted_part / col_part) / entries_all)
        scale = STEP_RATE * jnp.maximum(SCALE_EPSILON, jnp.sqrt(stats[4 + slot] / entries_all))
        new_masters.append(masters[slot] - scale * unit / jnp.maximum(1.0, spread / CLIP_LEVEL))
        spreads.append(spread)
    bounds = (0, D, 2 * D, 2 * D + HEAD_DIM, 2 * D + 2 * HEAD_DIM)
    moment_parts, gain_parts = ([], [])
    for segment in range(4):
        gradient = grad_gains[bounds[segment] : bounds[segment + 1]]
        gain_old = gains[bounds[segment] : bounds[segment + 1]]
        moment_new = beta * gain_moments[bounds[segment] : bounds[segment + 1]] + (1.0 - beta) * (
            gradient * gradient + SQUARE_EPSILON
        )
        unit = gradient * lax.rsqrt(moment_new)
        spread = jnp.sqrt(jnp.mean(unit * unit))
        scale = STEP_RATE * jnp.maximum(SCALE_EPSILON, jnp.sqrt(jnp.mean(gain_old * gain_old)))
        moment_parts.append(moment_new)
        gain_parts.append(gain_old - scale * unit / jnp.maximum(1.0, spread / CLIP_LEVEL))
        spreads.append(spread)
    return (
        grad_gains,
        *rows_new,
        cols_new,
        jnp.concatenate(moment_parts),
        *new_masters,
        *[master.astype(jnp.bfloat16) for master in new_masters],
        jnp.concatenate(gain_parts),
        jnp.stack(spreads),
    )


def solution(mesh):
    split = mesh.shape["seq"] == 8 and mesh.shape["rows"] == 4
    return jax.shard_map(
        split_local if split else gathered_local,
        mesh=mesh,
        in_specs=(
            P("rows", "seq", None),
            P("rows", None),
            P("rows", "seq", None),
            P(("seq", "rows"), None),
            P(("seq", "rows"), None),
            P(("seq", "rows"), None),
            P(("seq", "rows"), None),
            P(),
            P(("seq", "rows")),
            P(("seq", "rows")),
            P(("seq", "rows")),
            P(("seq", "rows")),
            P(),
            P(),
        ),
        out_specs=(
            P("rows", "seq", None),
            P("rows", "seq", None),
            P(("seq", "rows"), None),
            P(("seq", "rows"), None),
            P(("seq", "rows"), None),
            P(("seq", "rows"), None),
            P(),
            P(("seq", "rows")),
            P(("seq", "rows")),
            P(("seq", "rows")),
            P(("seq", "rows")),
            P(),
            P(),
            P(("seq", "rows"), None),
            P(("seq", "rows"), None),
            P(("seq", "rows"), None),
            P(("seq", "rows"), None),
            P(("seq", "rows"), None),
            P(("seq", "rows"), None),
            P(("seq", "rows"), None),
            P(("seq", "rows"), None),
            P(),
            P(),
        ),
        check_vma=False,
    )
```

```python
from functools import partial

import jax
import jax.numpy as jnp
import numpy as np
from jax import lax
from jax.experimental import pallas as pl
from jax.experimental.pallas import tpu as pltpu
from jax.sharding import PartitionSpec as P

D = 2048
HEADS = 32
KV_HEADS = 8
HEAD_DIM = 64
FF = 8192
STEP = 10
QKV = 3072


EPSILON = 1e-06
ROPE_BASE = 10000.0
MASKED_SCORE = -1e30
STEP_RATE = 0.3
CLIP_LEVEL = 1.0
SQUARE_EPSILON = 1e-30
SCALE_EPSILON = 0.001


def from_behind(value, axis, steps):
    count = lax.axis_size(axis)
    pairs = [(source, (source + steps) % count) for source in range(count)]
    return lax.ppermute(value, axis, pairs)


def norm_rows(entries, gain):
    return entries * lax.rsqrt(jnp.mean(entries * entries, axis=-1, keepdims=True) + EPSILON) * gain


def turn(entries, cos_wide, sin_wide):
    half_width = entries.shape[-1] // 2
    turned = jnp.concatenate([-entries[..., half_width:], entries[..., :half_width]], axis=-1)
    return entries * cos_wide + turned * sin_wide


def doc_tables(doc_starts, places):
    before = doc_starts[:, None, :] <= places[None, :, None]
    doc_ids = jnp.sum(before.astype(jnp.int32), axis=-1)
    doc_first = jnp.max(jnp.where(before, doc_starts[:, None, :], 0), axis=-1)
    return (doc_ids, places[None, :] - doc_first)


def rotary(offsets):
    frequency = ROPE_BASE ** (-(jnp.arange(HEAD_DIM // 2, dtype=jnp.float32) * 2.0 / HEAD_DIM))
    angles = offsets.astype(jnp.float32)[..., None] * frequency
    cos_table = jnp.concatenate([jnp.cos(angles), jnp.cos(angles)], axis=-1)
    sin_table = jnp.concatenate([jnp.sin(angles), jnp.sin(angles)], axis=-1)
    return (cos_table, sin_table)


def queries_keys(
    cos_table, sin_table, projected, gain_query, gain_key, heads=HEADS, kv_heads=KV_HEADS
):
    rows_here, seq_here = (projected.shape[0], projected.shape[1])
    att_width = heads * HEAD_DIM
    queries = projected[..., :att_width].reshape(rows_here, seq_here, heads, HEAD_DIM)
    keys_rot = projected[..., att_width : att_width + kv_heads * HEAD_DIM].reshape(
        rows_here, seq_here, kv_heads, HEAD_DIM
    )
    cos_wide = cos_table[:, :, None, :]
    sin_wide = sin_table[:, :, None, :]
    queries = turn(norm_rows(queries, gain_query), cos_wide, sin_wide) * HEAD_DIM ** (-0.5)
    keys_rot = turn(norm_rows(keys_rot, gain_key), cos_wide, sin_wide)
    return (queries, keys_rot)


def mask_of(query_docs, query_places, key_docs, key_places):
    same_doc = query_docs[:, :, None] == key_docs[:, None, :]
    causal = query_places[None, :, None] >= key_places[None, None, :]
    return (same_doc & causal)[:, None, None, :, :]


def gathered_local(
    tokens,
    doc_starts,
    grad_out,
    qkv_master,
    out_master,
    gate_up_master,
    down_master,
    gains,
    qkv_rows,
    out_rows,
    gate_up_rows,
    down_rows,
    col_moments,
    gain_moments,
):
    cycle_size = lax.axis_size("seq")
    seq_index = lax.axis_index("seq")
    rows_dev, seq_dev = (tokens.shape[0], tokens.shape[1])
    group_size = HEADS // KV_HEADS
    att_width = HEADS * HEAD_DIM
    kv_width = KV_HEADS * HEAD_DIM
    gain_attn = gains[:D]
    gain_ffn = gains[D : 2 * D]
    gain_query = gains[2 * D : 2 * D + HEAD_DIM]
    gain_key = gains[2 * D + HEAD_DIM :]
    local_places = jnp.arange(seq_dev, dtype=jnp.int32)
    places = seq_index * seq_dev + local_places
    query_docs, offsets = doc_tables(doc_starts, places)
    cos_table, sin_table = rotary(offsets)
    copies = (
        qkv_master.astype(jnp.bfloat16),
        out_master.astype(jnp.bfloat16),
        gate_up_master.astype(jnp.bfloat16),
        down_master.astype(jnp.bfloat16),
    )
    w_qkv, w_out, w_gate_up, w_down = (
        lax.all_gather(copies[0], ("seq", "rows"), axis=0, tiled=True),
        lax.all_gather(copies[1], ("seq", "rows"), axis=0, tiled=True),
        lax.all_gather(copies[2], ("seq", "rows"), axis=0, tiled=True),
        lax.all_gather(copies[3], ("seq", "rows"), axis=0, tiled=True),
    )
    tokens_wide = tokens.astype(jnp.float32)
    normed = norm_rows(tokens_wide, gain_attn).astype(jnp.bfloat16)
    projected = jnp.einsum("rtd,de->rte", normed, w_qkv, preferred_element_type=jnp.float32)
    head_fn = partial(queries_keys, cos_table, sin_table)
    queries, keys_rot = head_fn(projected, gain_query, gain_key)
    query16 = queries.astype(jnp.bfloat16).reshape(
        rows_dev, seq_dev, KV_HEADS, group_size, HEAD_DIM
    )
    keys16 = keys_rot.astype(jnp.bfloat16).reshape(rows_dev, seq_dev, kv_width)
    values16 = projected[..., att_width + kv_width :].astype(jnp.bfloat16)
    stat_shape = (rows_dev, KV_HEADS, group_size, seq_dev)
    initial = (
        jnp.full(stat_shape, MASKED_SCORE, jnp.float32),
        jnp.zeros(stat_shape, jnp.float32),
        jnp.zeros(stat_shape + (HEAD_DIM,), jnp.float32),
    )
    carry = initial
    key_piece = lax.all_gather(keys16, "seq", axis=1, tiled=True)
    value_piece = lax.all_gather(values16, "seq", axis=1, tiled=True)
    key_count = key_piece.shape[1]

    def absorb_block(state, block_index):
        best, total, summed = state
        block_begin = block_index * seq_dev
        key_block = lax.dynamic_slice_in_dim(key_piece, block_begin, seq_dev, 1).reshape(
            rows_dev, seq_dev, KV_HEADS, HEAD_DIM
        )
        value_block = lax.dynamic_slice_in_dim(value_piece, block_begin, seq_dev, 1).reshape(
            rows_dev, seq_dev, KV_HEADS, HEAD_DIM
        )
        key_places = block_begin + jnp.arange(seq_dev, dtype=jnp.int32)
        key_docs, _ = doc_tables(doc_starts, key_places)
        allowed = mask_of(query_docs, places, key_docs, key_places)
        scores = jnp.einsum(
            "rqkgh,rtkh->rkgqt", query16, key_block, preferred_element_type=jnp.float32
        )
        scores = jnp.where(allowed, scores, MASKED_SCORE)
        best_new = jnp.maximum(best, jnp.max(scores, axis=-1))
        weights = jnp.where(allowed, jnp.exp(scores - best_new[..., None]), 0.0)
        factor = jnp.exp(best - best_new)
        total = total * factor + jnp.sum(weights, axis=-1)
        summed = summed * factor[..., None] + jnp.einsum(
            "rkgqt,rtkh->rkgqh",
            weights.astype(jnp.bfloat16),
            value_block,
            preferred_element_type=jnp.float32,
        )
        return ((best_new, total, summed), None)

    carry, _ = lax.scan(absorb_block, carry, jnp.arange(key_count // seq_dev, dtype=jnp.int32))
    best, total, summed = carry
    log_total = best + jnp.log(total)
    attended = summed / total[..., None]
    attended16 = (
        attended.transpose(0, 3, 1, 2, 4).reshape(rows_dev, seq_dev, att_width).astype(jnp.bfloat16)
    )
    branch = jnp.einsum("rtc,cd->rtd", attended16, w_out, preferred_element_type=jnp.float32)
    hidden_in = tokens_wide + branch
    normed2 = norm_rows(hidden_in, gain_ffn).astype(jnp.bfloat16)
    gate_up = jnp.einsum("rtd,df->rtf", normed2, w_gate_up, preferred_element_type=jnp.float32)
    gate_part, up_part = (gate_up[..., :FF], gate_up[..., FF:])
    hidden = (jax.nn.silu(gate_part) * up_part).astype(jnp.bfloat16)
    output = hidden_in + jnp.einsum(
        "rtf,fd->rtd", hidden, w_down, preferred_element_type=jnp.float32
    )
    d_hidden = jnp.einsum("rtd,fd->rtf", grad_out, w_down, preferred_element_type=jnp.float32)
    silu_value, silu_back = jax.vjp(jax.nn.silu, gate_part)
    d_gate = silu_back(d_hidden * up_part)[0]
    d_gate_up = jnp.concatenate([d_gate, d_hidden * silu_value], axis=-1).astype(jnp.bfloat16)
    d_normed2 = jnp.einsum("rtf,df->rtd", d_gate_up, w_gate_up, preferred_element_type=jnp.float32)
    _, ffn_norm_back = jax.vjp(norm_rows, hidden_in, gain_ffn)
    d_inner, grad_gain_ffn = ffn_norm_back(d_normed2)
    d_hidden_in = grad_out.astype(jnp.float32) + d_inner
    term_down = jnp.einsum("rtf,rtd->fd", hidden, grad_out, preferred_element_type=jnp.float32)
    grad_down = lax.psum_scatter(term_down, ("seq", "rows"), scatter_dimension=0, tiled=True)
    term_gate_up = jnp.einsum("rtd,rtf->df", normed2, d_gate_up, preferred_element_type=jnp.float32)
    grad_gate_up = lax.psum_scatter(term_gate_up, ("seq", "rows"), scatter_dimension=0, tiled=True)
    d_branch = d_hidden_in.astype(jnp.bfloat16)
    term_out = jnp.einsum("rtc,rtd->cd", attended16, d_branch, preferred_element_type=jnp.float32)
    d_attended = jnp.einsum(
        "rtd,cd->rtc", d_branch, w_out, preferred_element_type=jnp.float32
    ).astype(jnp.bfloat16)
    d_heads = d_attended.reshape(rows_dev, seq_dev, KV_HEADS, group_size, HEAD_DIM).transpose(
        0, 2, 3, 1, 4
    )
    delta = jnp.sum(d_heads.astype(jnp.float32) * attended, axis=-1)

    def cycle_turn(turn_index, carry):
        pair16, grad_pair, d_queries = carry
        source = (seq_index + turn_index) % cycle_size
        key_places = source * seq_dev + local_places
        key_docs, _ = doc_tables(doc_starts, key_places)
        allowed = mask_of(query_docs, places, key_docs, key_places)
        key_block = pair16[0].reshape(rows_dev, seq_dev, KV_HEADS, HEAD_DIM)
        value_block = pair16[1].reshape(rows_dev, seq_dev, KV_HEADS, HEAD_DIM)
        scores = jnp.einsum(
            "rqkgh,rtkh->rkgqt", query16, key_block, preferred_element_type=jnp.float32
        )
        scores = jnp.where(allowed, scores, MASKED_SCORE)
        probs = jnp.where(allowed, jnp.exp(scores - log_total[..., None]), 0.0)
        d_values = jnp.einsum(
            "rkgqt,rkgqh->rtkh",
            probs.astype(jnp.bfloat16),
            d_heads,
            preferred_element_type=jnp.float32,
        )
        d_probs = jnp.einsum(
            "rkgqh,rtkh->rkgqt", d_heads, value_block, preferred_element_type=jnp.float32
        )
        d_scores = (probs * (d_probs - delta[..., None])).astype(jnp.bfloat16)
        d_queries = d_queries + jnp.einsum(
            "rkgqt,rtkh->rkgqh", d_scores, key_block, preferred_element_type=jnp.float32
        )
        d_keys = jnp.einsum(
            "rkgqt,rqkgh->rtkh", d_scores, query16, preferred_element_type=jnp.float32
        )
        grad_pair = grad_pair + jnp.stack(
            [
                d_keys.reshape(rows_dev, seq_dev, kv_width),
                d_values.reshape(rows_dev, seq_dev, kv_width),
            ]
        )
        grad_pair = from_behind(grad_pair.astype(jnp.bfloat16), "seq", -1).astype(grad_pair.dtype)
        pair16 = from_behind(pair16, "seq", -1)
        return (pair16, grad_pair, d_queries)

    start_pair = jnp.stack([keys16, values16])
    start_grads = jnp.zeros((2, rows_dev, seq_dev, kv_width), jnp.float32)
    start_queries = jnp.zeros(stat_shape + (HEAD_DIM,), jnp.float32)
    _, grad_pair, d_queries = lax.fori_loop(
        0, cycle_size, cycle_turn, (start_pair, start_grads, start_queries)
    )
    d_queries = d_queries.transpose(0, 3, 1, 2, 4).reshape(rows_dev, seq_dev, HEADS, HEAD_DIM)
    d_keys_home = grad_pair[0].reshape(rows_dev, seq_dev, KV_HEADS, HEAD_DIM)
    _, heads_back = jax.vjp(head_fn, projected, gain_query, gain_key)
    d_projected, grad_gain_query, grad_gain_key = heads_back((d_queries, d_keys_home))
    d_projected = jnp.concatenate(
        [d_projected[..., : att_width + kv_width], grad_pair[1]], axis=-1
    ).astype(jnp.bfloat16)
    term_qkv = jnp.einsum("rtd,rte->de", normed, d_projected, preferred_element_type=jnp.float32)
    d_normed = jnp.einsum("rte,de->rtd", d_projected, w_qkv, preferred_element_type=jnp.float32)
    _, attn_norm_back = jax.vjp(norm_rows, tokens_wide, gain_attn)
    d_tokens_part, grad_gain_attn = attn_norm_back(d_normed)
    grad_tokens = (d_hidden_in + d_tokens_part).astype(jnp.bfloat16)
    grad_qkv, grad_out_proj = (
        lax.psum_scatter(term_qkv, ("seq", "rows"), scatter_dimension=0, tiled=True),
        lax.psum_scatter(term_out, ("seq", "rows"), scatter_dimension=0, tiled=True),
    )
    gain_local = jnp.concatenate([grad_gain_attn, grad_gain_ffn, grad_gain_query, grad_gain_key])
    grads = (grad_qkv, grad_out_proj, grad_gate_up, grad_down)
    updated = optimizer_step(
        grads, gain_local, (qkv_master, out_master, gate_up_master, down_master), gains,
        (qkv_rows, out_rows, gate_up_rows, down_rows), col_moments, gain_moments,
        lambda vector: lax.psum(vector, ("seq", "rows")),
    )
    return (output.astype(jnp.bfloat16), grad_tokens, *grads, *updated)


MESH = pl.DeviceIdType.MESH
PLACES = 32
VMEM_BYTES = 61 * 1024 * 1024
CHUNK = 16


def here():
    seq = lax.axis_index("seq")
    return lax.div(seq, 2), lax.rem(seq, 2), lax.axis_index("rows")


def flips(chip):
    return (chip + 1 - 2 * lax.rem(chip, 2), lax.rem(chip + 2, 4), 3 - chip)


def ahead(z, step):
    return lax.rem(z + step, 4)


def at_place(chip, core, z):
    return (2 * chip + core, z)


def greet(peers):
    barrier = pltpu.get_barrier_semaphore()
    for peer in peers:
        pl.semaphore_signal(barrier, inc=1, device_id=peer, device_id_type=MESH)
    pl.semaphore_wait(barrier, len(peers))


class Mover:
    def __init__(self, send_sem, recv_sem, local_sem):
        self.send_sem, self.recv_sem, self.local_sem = send_sem, recv_sem, local_sem
        self.remote, self.own, self.lines, self.scattered = [], [], [], []
        self.used = 0

    def copy_of(self, src, dst, peer, send_slot, recv_slot):
        return pltpu.make_async_remote_copy(
            src_ref=src,
            dst_ref=dst,
            send_sem=self.send_sem.at[send_slot],
            recv_sem=self.recv_sem.at[recv_slot],
            device_id=peer,
            device_id_type=MESH,
        )

    def send_parts(self, pairs, whole, peer):
        slot = self.used
        self.used += 1
        for src, dst in pairs:
            self.copy_of(src, dst, peer, slot, slot).start()
        copy = self.copy_of(whole[0], whole[1], peer, slot, slot)
        handle = [copy, False, copy.wait_recv, False]
        self.remote.append(handle)
        return handle

    def send(self, src, dst, peer):
        return self.send_parts([(src, dst)], (src, dst), peer)

    def keep_parts(self, pairs, whole):
        sem = self.local_sem.at[len(self.own)]
        for src, dst in pairs:
            pltpu.make_async_copy(src, dst, sem).start()
        copy = pltpu.make_async_copy(whole[0], whole[1], sem)
        handle = [copy, False, copy.wait]
        self.own.append(handle)
        return handle

    def keep(self, src, dst):
        return self.keep_parts([(src, dst)], (src, dst))

    def line(self, source, block_of, chip, core, z):
        line = (self.used, block_of, chip, core, z)
        self.used += 5
        base = line[0]
        up, low = at_place(chip, core, z + 1), at_place(chip, core, z - 1)
        rising = self.copy_of(source, block_of(z), up, base, base + 3)
        falling = self.copy_of(source, block_of(z), low, base + 4, base + 1)
        pl.when(z < 3)(rising.start)
        pl.when(z > 0)(falling.start)
        self.lines += [(z < 3, rising), (z > 0, falling)]
        return line

    def wait_line(self, line, step, when=None):
        base, block_of, chip, core, z = line
        block = block_of(ahead(z, step))
        peer = at_place(chip, core, ahead(z, step))
        copy = self.copy_of(block, block, peer, base + step, base + step)
        if when is None:
            copy.wait_recv()
        else:
            pl.when(when)(copy.wait_recv)
        return block

    def arrive_line(self, line, step, when=None):
        base, _, chip, core, z = line
        block = self.wait_line(line, step, when)
        rises, falls = (z + step >= 4) & (z < 3), (z + step < 4) & (z > 0)
        up, low = at_place(chip, core, z + 1), at_place(chip, core, z - 1)
        rising = self.copy_of(block, block, up, base + step, base + step - 1)
        falling = self.copy_of(block, block, low, base + step, base + step + 1)
        for moves, copy in ((rises, rising), (falls, falling)):
            moves = moves if when is None else moves & when
            pl.when(moves)(copy.start)
            self.lines.append((moves, copy))
        return block

    def scatter(self, source, target, steps, chip, core, z):
        base = self.used
        self.used += 3

        def start(index):
            at = ahead(z, steps[index])
            copy = self.copy_of(
                source(at), target(z), at_place(chip, core, at), base + index, base + 3 - steps[index]
            )
            copy.start()
            self.scattered.append(copy)

        def wait():
            for step in (1, 2, 3):
                at = ahead(z, step)
                peer = at_place(chip, core, at)
                self.copy_of(source(at), target(at), peer, base, base + step - 1).wait_recv()

        return start, wait

    def arrive(self, *handles):
        for handle in handles:
            if not handle[1]:
                handle[1] = True
                handle[2]()

    def sent(self, *handles):
        for handle in handles:
            if not handle[3]:
                handle[3] = True
                handle[0].wait_send()

    def sent_lines(self):
        for when, copy in self.lines:
            pl.when(when)(copy.wait_send)
        self.lines = []

    def sent_sums(self):
        for copy in self.scattered:
            copy.wait_send()
        self.scattered = []

    def finish(self):
        assert self.used <= self.send_sem.shape[0] and len(self.own) <= self.local_sem.shape[0]
        self.arrive(*self.own, *self.remote)
        self.sent(*self.remote)
        self.sent_lines()
        self.sent_sums()


def semaphores(remote, own):
    return [
        pltpu.SemaphoreType.DMA((remote,)),
        pltpu.SemaphoreType.DMA((remote,)),
        pltpu.SemaphoreType.DMA((max(own, 1),)),
    ]


def exchange(kernel, ident, inputs, outputs, scratch, copies, moved, flops=0):
    spaces = {True: pltpu.VMEM, False: pl.ANY, None: pltpu.SMEM}
    specs = {near: pl.BlockSpec(memory_space=space) for near, space in spaces.items()}
    return pl.pallas_call(
        kernel,
        out_shape=[jax.ShapeDtypeStruct(shape, kind) for shape, kind, _ in outputs],
        in_specs=[specs[near] for _, near in inputs],
        out_specs=[specs[near] for _, _, near in outputs],
        scratch_shapes=scratch + semaphores(*copies),
        compiler_params=pltpu.CompilerParams(
            collective_id=ident, has_side_effects=True, vmem_limit_bytes=VMEM_BYTES
        ),
        cost_estimate=pl.CostEstimate(flops=flops, bytes_accessed=moved, transcendentals=0),
    )(*[array for array, _ in inputs])


def chunks(length, body):
    @pl.loop(0, length // CHUNK)
    def _(step):
        body(pl.ds(pl.multiple_of(step * CHUNK, CHUNK), CHUNK))


def add_blocks(first, second, result):
    for row in range(2):

        def body(part):
            total = first[row, part].astype(jnp.float32) + second[row, part].astype(jnp.float32)
            result[row, part] = total.astype(result.dtype)

        chunks(64, body)


def lower_half(shape):
    return lax.broadcasted_iota(jnp.int32, shape, len(shape) - 1) < 64


def swap_halves(entries):
    lane = lax.broadcasted_iota(jnp.int32, entries.shape, 1)
    return jnp.where(lax.rem(lane, 64) < 32, pltpu.roll(entries, 96, 1), pltpu.roll(entries, 32, 1))


def head_means(entries):
    lower = lower_half(entries.shape)
    low = jnp.sum(jnp.where(lower, entries, 0.0), axis=-1, keepdims=True)
    high = jnp.sum(jnp.where(lower, 0.0, entries), axis=-1, keepdims=True)
    return jnp.where(lower, low, high) * (1.0 / HEAD_DIM)


def wide(start, size):
    return pl.ds(pl.multiple_of(start, size), size)


def plain(left, right):
    return jnp.dot(left, right, preferred_element_type=jnp.float32)


def across(left, right):
    return lax.dot_general(
        left, right, (((1,), (1,)), ((), ())), preferred_element_type=jnp.float32
    )


def down(left, right):
    return lax.dot_general(
        left, right, (((0,), (0,)), ((), ())), preferred_element_type=jnp.float32
    )


def attention_probs(queries, keys, first, part):
    scores = across(queries, keys)
    place = lax.broadcasted_iota(jnp.int32, scores.shape, 1)
    query = lax.broadcasted_iota(jnp.int32, scores.shape, 0) + part * 128
    allowed = (place >= first) & (place <= query)
    scores = jnp.where(allowed, scores, MASKED_SCORE)
    best = jnp.max(scores, axis=-1, keepdims=True)
    weights = jnp.where(allowed, jnp.exp(scores - best), 0.0)
    return weights / jnp.sum(weights, axis=-1, keepdims=True)


COL_ROWS, GAIN_ROWS = 184, 33
COLS = COL_ROWS * 128
MATRICES = ((64, QKV, 0, 0), (64, D, 64, 24), (64, 2 * FF, 128, 40), (256, D, 192, 168))
ROW_TOTALS = (D, HEADS * HEAD_DIM, D, FF)
BETA = 1.0 - STEP ** (-0.8)


def lane_value(vector, lane):
    lanes = lax.broadcasted_iota(jnp.int32, (1, 128), 1)
    return jnp.sum(jnp.where(lanes == lane, vector, 0.0), axis=-1, keepdims=True)


def total(entries):
    return jnp.sum(jnp.sum(entries, axis=-1, keepdims=True), axis=0, keepdims=True)


def document_start(starts, row, place):
    start = jnp.zeros_like(place)
    for document in range(starts.shape[1]):
        begin = starts[row, document]
        start = jnp.maximum(start, jnp.where(place >= begin, begin, 0))
    return start


def place_tables(length):
    rates = ROPE_BASE ** (-(np.arange(128) % 32) * 2.0 / HEAD_DIM)
    angles = np.arange(length)[:, None] * rates
    return np.stack([np.cos(angles), np.sin(angles)]).astype(np.float32)


def derive_updates(
    flat, col_moments, gain_moments, gains,
    cols_new, col_factors, moments_new, gains_new, grad_gains, spreads,
):
    first = 2 * COL_ROWS
    stats = flat[first + 33 : first + 34]
    lanes = lax.broadcasted_iota(jnp.int32, (1, 128), 1)
    out = jnp.zeros((1, 128), jnp.float32)
    for slot, (_, width, _, col_at) in enumerate(MATRICES):
        own = pl.ds(col_at, width // 128)
        entries_all = float(ROW_TOTALS[slot] * width)
        new = BETA * col_moments[own] + (1.0 - BETA) * (flat[own] / ROW_TOTALS[slot])
        cols_new[own] = new
        mean_rows = lane_value(stats, slot) / ROW_TOTALS[slot]
        ratio = total(flat[pl.ds(COL_ROWS + col_at, width // 128)] / new)
        spread = jnp.sqrt(mean_rows * ratio / entries_all)
        scale = STEP_RATE * jnp.maximum(
            SCALE_EPSILON, jnp.sqrt(lane_value(stats, 4 + slot) / entries_all)
        )
        factor = scale * jnp.sqrt(mean_rows) / jnp.maximum(1.0, spread / CLIP_LEVEL)
        factors = lax.rsqrt(new) * factor
        for row in range(width // 128):
            col_factors[:, pl.ds((col_at + row) * 128, 128)] = factors[row : row + 1]
        out = jnp.where(lanes == slot, spread, out)
    gradient = flat[first : first + GAIN_ROWS]
    grad_gains[...] = gradient
    old = gains[...]
    new = BETA * gain_moments[...] + (1.0 - BETA) * (gradient * gradient + SQUARE_EPSILON)
    moments_new[...] = new
    unit = gradient * lax.rsqrt(new)
    row = lax.broadcasted_iota(jnp.int32, (GAIN_ROWS, 128), 0)
    lane = lax.broadcasted_iota(jnp.int32, (GAIN_ROWS, 128), 1)
    segment = jnp.where(row < 16, 0, jnp.where(row < 32, 1, jnp.where(lane < 64, 2, 3)))
    factors = jnp.zeros((GAIN_ROWS, 128), jnp.float32)
    for slot, count in enumerate((D, D, HEAD_DIM, HEAD_DIM)):
        mask = segment == slot
        spread = jnp.sqrt(total(jnp.where(mask, unit * unit, 0.0)) / count)
        mean = total(jnp.where(mask, old * old, 0.0)) / count
        scale = STEP_RATE * jnp.maximum(SCALE_EPSILON, jnp.sqrt(mean))
        factors = jnp.where(mask, scale / jnp.maximum(1.0, spread / CLIP_LEVEL), factors)
        out = jnp.where(lanes == 4 + slot, spread, out)
    gains_new[...] = old - factors * unit
    spreads[...] = out


def layer_kernel(
    tok, starts, rates, places_at, gain_attn, gain_ffn, gain_heads, gains, grad_out,
    m_qkv, m_out, m_down, m_gate_up, rows, col_moments, gain_moments,
    out_sum, grad_tok, g_qkv, gate_up_came, out_came, down_came, rows_new, row_factors,
    cols_new, col_factors, moments_new, gains_new, grad_gains, spreads,
    gate_up_in, gate_up_mid, kept_tok,
    projected, queries, keys_values, attended, document_tables,
    wq_send, normed, all_tok, all_wq, all_wo, partial, from_partner, came,
    hidden_in, all_norm, all_out, all_wg, wd, hidden, d_gate_up,
    d_queries, d_keys_values, qkv_in, d_hidden_in, gain_part, gain_part2, gain_qk, weight_sums, qkv_came,
    packed, plane_came, plane_sum, line_came, line_sum, line_all, totals, credit, tokens_used, *sems,
):
    half, full = jnp.bfloat16, jnp.float32
    chip, core, z = here()
    others = flips(chip)
    other = 1 - core
    me = 2 * chip + core
    partner = at_place(chip, other, z)
    plane = [at_place(peer_chip, core, z) for peer_chip in others]
    plane_cross = [at_place(peer_chip, other, z) for peer_chip in others]
    steps = (2, 1, 3)
    line = [at_place(chip, core, ahead(z, step)) for step in steps]
    cross = [at_place(chip, other, ahead(z, step)) for step in steps]
    everyone = [partner] + plane + plane_cross
    greet(everyone + line + cross)
    move = Mover(*sems)

    for head in range(8):
        wq_send[head, :, pl.ds(0, 256)] = m_qkv[:, pl.ds(head * 256, 256)].astype(half)
    low = lower_half((64, 128))
    for pair in range(4):
        keys = m_qkv[:, pl.ds(2048 + pair * 128, 128)]
        values = m_qkv[:, pl.ds(2560 + pair * 128, 128)]
        tail = pl.ds(256, 128)
        wq_send[2 * pair, :, tail] = jnp.where(low, keys, pltpu.roll(values, 64, 1)).astype(half)
        wq_send[2 * pair + 1, :, tail] = jnp.where(low, pltpu.roll(keys, 64, 1), values).astype(half)
    heads = [move.keep(wq_send.at[me], all_wq.at[me, z])]
    for peer in everyone:
        heads.append(move.send(wq_send.at[peer[0]], all_wq.at[me, z], peer))

    for row in range(2):

        def body0(part):
            result = tok[row, part].astype(full)
            scale = lax.rsqrt(jnp.mean(result * result, axis=-1, keepdims=True) + EPSILON)
            normed[row, part] = (result * scale * gain_attn[...]).astype(half)

        chunks(64, body0)
    token_copies = [move.send(normed, all_tok.at[me], peer) for peer in plane]
    token_copies.append(move.send(normed, all_tok.at[me], partner))
    tokens_here = move.keep(normed, all_tok.at[me])
    move.arrive(*heads)
    line_wq = move.line(all_wq.at[:, z], lambda at: all_wq.at[:, at], chip, core, z)
    flat_d = d_gate_up.reshape(1024, 2048)
    weight_sums[...] = jnp.zeros_like(weight_sums)
    for row in range(2):
        for document in range(starts.shape[1]):
            angle = starts[row, document].astype(full) * rates[0:1]
            document_tables[row, 2 * document] = jnp.cos(angle)
            document_tables[row, 2 * document + 1] = jnp.sin(angle)

    def cast_all(slot, blocks):
        loads = [move.keep(blocks[0][0], hidden_in.at[0])]
        for index, (_, target) in enumerate(blocks):
            if index + 1 < len(blocks):
                loads.append(move.keep(blocks[index + 1][0], hidden_in.at[(index + 1) % 2]))
            move.arrive(loads[index])

            def body(part, index=index, target=target):
                entries = hidden_in[index % 2, part]
                weight_sums[slot] += jnp.sum((entries * entries).reshape(2, 8, D), axis=0)
                target(part, entries.astype(half))

            chunks(64, body)

    def into(ref):
        def store(part, entries):
            ref[part] = entries

        return store

    def by_device(block):
        cols = pl.ds((block // 4) * 1024 + (block % 4) * 256, 256)

        def store(part, entries):
            for index in range(8):
                place = (index % 4) * 2 + index // 4
                rows_at = wide(place * 64 + part.start, CHUNK)
                flat_d[rows_at, cols] = entries[:, index * 256 : (index + 1) * 256]

        return store

    cast_all(1, [(m_out, into(all_wo.at[z]))])
    cast_all(
        3,
        [
            (m_down.at[pl.ds(64 * block, 64)], into(wd.at[chip, pl.ds(64 * block, 64)]))
            for block in range(4)
        ],
    )
    by_x, by_y = plane[0], plane[1]
    front, back = wd.at[chip, pl.ds(0, 128)], wd.at[chip, pl.ds(128, 128)]
    down_copies = [
        move.send(front, front, by_x), move.send(back, back, by_y),
        move.send(back, back, by_x), move.send(front, front, by_y),
    ]
    move.arrive_line(line_wq, 3)
    move.arrive_line(line_wq, 1)
    cast_all(
        2,
        [(m_gate_up.at[:, pl.ds(2048 * block, 2048)], by_device(block)) for block in range(8)],
    )
    move.arrive_line(line_wq, 2)
    wo_copies = [move.send(all_wo.at[z], all_wo.at[z], peer) for peer in line]

    def turn_block(to_core, to_z, side):
        lanes = pl.ds(side * 1024, 1024)
        src = flat_d.at[wide((to_z * 2 + to_core) * 64, 64), lanes]
        return src, all_wg.at[chip, core, z, :, lanes]

    own = [
        move.keep(grad_out, all_out.at[z, core]),
        move.send(grad_out, all_out.at[z, core], partner),
    ]

    for peer_chip, handle in zip(others, tuple(token_copies)):
        move.arrive(handle)
        block = all_tok.at[2 * peer_chip + core]
        token_copies.append(move.send(block, block, partner))
    move.arrive(tokens_here, *token_copies)
    saved = [move.keep(all_tok, kept_tok)]

    def tables_of(block, row):
        place = lax.broadcasted_iota(jnp.int32, (64, 1), 0) + block * 64
        start_cos, start_sin = document_tables[row, 0], document_tables[row, 1]
        for document in range(1, starts.shape[1]):
            inside = place >= starts[row, document]
            start_cos = jnp.where(inside, document_tables[row, 2 * document], start_cos)
            start_sin = jnp.where(inside, document_tables[row, 2 * document + 1], start_sin)
        at = wide(block * 64, 64)
        place_cos, place_sin = places_at[0, at], places_at[1, at]
        cosine = place_cos * start_cos + place_sin * start_sin
        return cosine, (place_sin * start_cos - place_cos * start_sin) * rates[1:2]

    def first_of(row, part):
        place = lax.broadcasted_iota(jnp.int32, (128, 1), 0) + part * 128
        return document_start(starts, row, place)

    flat_tok, flat_wq = all_tok.reshape(1024, D), all_wq.reshape(D, 384)
    flat_wo = all_wo.reshape(256, D)

    @pl.loop(0, 4)
    def _(step):
        block = plain(flat_tok[wide(step * 256, 256)], flat_wq[...])
        projected[wide(step * 2, 2)] = block.reshape(2, 2, 64, 384)

    @pl.loop(0, 8)
    def _(block):
        for row in range(2):
            cosine, sine = tables_of(block, row)
            places = wide(block * 64, 64)
            for tile in range(3):
                entries = projected[block, row, :, pl.ds(tile * 128, 128)]
                gain = gain_heads[min(tile, 2) // 2 : min(tile, 2) // 2 + 1]
                scale = lax.rsqrt(head_means(entries * entries) + EPSILON)
                turned_entries = entries * scale * gain
                turned_entries = turned_entries * cosine + swap_halves(turned_entries) * sine
                if tile < 2:
                    queries[row, tile, places] = (turned_entries * HEAD_DIM ** (-0.5)).astype(half)
                else:
                    zero = jnp.zeros_like(entries)
                    rolled = pltpu.roll(turned_entries, 64, 1)
                    values = pltpu.roll(entries, 64, 1)
                    keys_values[row, 0, places] = jnp.where(low, turned_entries, zero).astype(half)
                    keys_values[row, 1, places] = jnp.where(low, zero, rolled).astype(half)
                    keys_values[row, 2, places] = jnp.where(low, values, zero).astype(half)
                    keys_values[row, 3, places] = jnp.where(low, zero, entries).astype(half)

    turned, turned_own = ([], []), []
    for side in range(2):
        for step, peer, peer_cross in zip(steps, line, cross):
            to = ahead(z, step)
            turned[side].append(move.send(*turn_block(core, to, side), peer))
            turned[side].append(move.send(*turn_block(other, to, side), peer_cross))
        turned[side].append(move.send(*turn_block(other, z, side), partner))
        turned_own.append(move.keep(*turn_block(core, z, side)))
    line_grads = move.line(grad_out, lambda at: all_out.at[at, core], chip, core, z)
    move.arrive(*down_copies[:2])
    front, back = wd.at[others[0], pl.ds(0, 128)], wd.at[others[1], pl.ds(128, 128)]
    down_copies += [move.send(front, front, by_y), move.send(back, back, by_x)]

    @pl.loop(0, 2)
    def _(row):
        for tile in range(2):
            for part in range(4):
                own_places, upto = pl.ds(part * 128, 128), pl.ds(0, (part + 1) * 128)
                result = jnp.zeros((128, 128), full)
                for side in range(2):
                    probs = attention_probs(
                        queries[row, tile, own_places], keys_values[row, side, upto],
                        first_of(row, part), part,
                    )
                    result += plain(probs.astype(half), keys_values[row, 2 + side, upto])
                attended[pl.ds(2 * part, 2), row, :, pl.ds(tile * 128, 128)] = result.reshape(2, 64, 128)

    flat_attended = attended.reshape(1024, 256)
    move.arrive(*wo_copies)

    @pl.loop(0, 4)
    def _(step):
        rows = flat_attended[wide(step * 256, 256)].astype(half)

        @pl.loop(0, 4)
        def _(col):
            cols = wide(col * 512, 512)
            block = plain(rows, flat_wo[:, cols])
            partial[wide(step * 2, 2), :, :, cols] = block.reshape(2, 2, 64, 512).astype(half)

    order = tuple(others) + (chip,)
    halves = [move.send(partial.at[2 * to + other], from_partner.at[to], partner) for to in order]
    sums = []
    for to, arrived, peer in zip(others, halves, plane):
        move.arrive(arrived)
        add_blocks(partial.at[2 * to + core], from_partner.at[to], from_partner.at[to])
        sums.append(move.send(from_partner.at[to], came.at[chip], peer))
    def gather_weights(side):
        move.arrive(turned_own[side], *turned[side])
        lanes = pl.ds(side * 1024, 1024)
        front, back = all_wg.at[chip, 0, :, :, lanes], all_wg.at[chip, 1, :, :, lanes]
        return [
            move.send(front, front, by_x), move.send(back, back, by_y),
            move.send(back, back, by_x), move.send(front, front, by_y),
        ]

    def pass_weights(side, copies):
        move.arrive(*copies[:2])
        lanes = pl.ds(side * 1024, 1024)
        front, back = all_wg.at[others[0], 0, :, :, lanes], all_wg.at[others[1], 1, :, :, lanes]
        return [move.send(front, front, by_y), move.send(back, back, by_x)]

    gate_copies = gather_weights(0)
    move.sent(*token_copies)
    move.arrive(halves[3], *sums)
    for row in range(2):

        def body(part):
            result = tok[row, part].astype(full)
            result += partial[me, row, part].astype(full)
            result += from_partner[chip, row, part].astype(full)
            for peer_chip in others:
                result += came[peer_chip, row, part].astype(full)
            hidden_in[row, part] = result
            scale = lax.rsqrt(jnp.mean(result * result, axis=-1, keepdims=True) + EPSILON)
            normed[row, part] = (result * scale * gain_ffn[...]).astype(half)

        chunks(64, body)
    move.sent(*sums, *halves)
    move.arrive(*saved)
    line_norms = move.line(normed, lambda at: all_norm.at[at, core], chip, core, z)
    own.append(move.send(normed, all_norm.at[z, core], partner))
    own.append(move.keep(normed, all_norm.at[z, core]))

    up_copies = gather_weights(1)
    at_first, at_last = lax.div(3 - z, 3), lax.div(z, 3)
    arrivals = (3 - 2 * at_first, 1 + at_first + at_last, 2 + at_first - at_last)
    inner = (z > 0) & (z < 3)
    shared = []

    def share(step, wait_only=False):
        for line_of in (line_grads, line_norms):
            if wait_only:
                block = move.wait_line(line_of, step, jnp.logical_not(inner))
            else:
                block = move.arrive_line(line_of, step)
            shared.append(move.send(block, block, partner))

    flat_wg, flat_wd = all_wg.reshape(D, 2048), wd.reshape(1024, D)

    def d_hidden_of(zb):
        @pl.loop(0, 4)
        def _(step):
            cols = wide(step * 256, 256)
            hidden[zb, :, cols] = across(all_out[zb].reshape(256, D), flat_wd[cols]).astype(half)

    share(arrivals[0])
    gate_copies += pass_weights(0, gate_copies)
    move.arrive(*own[:2], *down_copies)
    d_hidden_of(z)
    share(arrivals[1])
    up_copies += pass_weights(1, up_copies)
    move.arrive(shared[0])
    d_hidden_of(ahead(z, arrivals[0]))
    for line_of in (line_grads, line_norms):
        move.arrive_line(line_of, arrivals[2], inner)
    move.arrive(shared[2])
    d_hidden_of(ahead(z, arrivals[1]))
    weights = gate_copies + up_copies
    move.arrive(*weights, *own)
    move.sent(*turned[0], *turned[1])

    def block_of(zb):
        @pl.loop(0, 4)
        def _(step):
            cols, ups = wide(step * 256, 256), wide(1024 + step * 256, 256)
            rows = all_norm[zb].reshape(256, D)
            gate = plain(rows, flat_wg[:, cols])
            up = plain(rows, flat_wg[:, ups])
            d_hidden = hidden[zb, :, cols].astype(full)
            sigmoid = 1.0 / (1.0 + jnp.exp(-gate))
            silu = gate * sigmoid
            hidden[zb, :, cols] = (silu * up).astype(half)
            d_gate = d_hidden * up * (sigmoid * (1.0 + gate * (1.0 - sigmoid)))
            d_gate_up[zb, :, cols] = d_gate.astype(half)
            d_gate_up[zb, :, ups] = (d_hidden * silu).astype(half)

        @pl.loop(0, 8)
        def _(step):
            cols = wide(step * 256, 256)
            block = across(d_gate_up[zb], flat_wg[cols])
            partial[pl.ds(2 * zb, 2), :, :, cols] = block.reshape(2, 2, 64, 256).astype(half)

    def pair_sum(zb, handle, into, base):
        move.arrive(handle)
        add_blocks(partial.at[2 * zb + core], into.at[base + zb], into.at[base + zb])

    start_sum, wait_sums = move.scatter(
        lambda at: from_partner.at[at], lambda at: came.at[at], arrivals, chip, core, z
    )
    to_partner = []
    walk = [z] + [ahead(z, step) for step in arrivals]
    for index, zb in enumerate(walk):
        if index > 0:
            move.arrive(*shared[2 * index - 2 : 2 * index])
        if index == 3:
            d_hidden_of(zb)
        block_of(zb)
        to_partner.append(move.send(partial.at[2 * zb + other], from_partner.at[zb], partner))
        if index == 0:
            share(arrivals[2], True)
        if index > 0:
            pair_sum(walk[index - 1], to_partner[index - 1], from_partner, 0)
        if index > 1:
            start_sum(index - 2)
    pair_sum(walk[3], to_partner[3], from_partner, 0)
    start_sum(2)

    flat_norm, flat_grads = all_norm.reshape(1024, D), all_out.reshape(1024, D)
    flat_hidden = hidden.reshape(1024, 1024)
    move.sent(*weights)

    def gate_up_grad(to, side):
        rows, lanes = wide(to * 512, 512), pl.ds(side * 1024, 1024)

        @pl.loop(0, 2)
        def _(step):
            cols = wide(side * 1024 + step * 512, 512)
            flat_wg[rows, cols] = down(flat_norm[:, rows], flat_d[:, cols]).astype(half)

        return flat_wg.at[rows, lanes]

    passed = []
    for side in (0, 1):
        passed.append(move.send(gate_up_grad(others[2], side), gate_up_mid.at[side], plane[side]))
    direct = [gate_up_grad(others[side], side) for side in (0, 1)]
    handed = [gate_up_grad(others[1 - side], side) for side in (0, 1)]
    for side in (0, 1):
        gate_up_grad(chip, side)
    move.sent(*shared, own[2])
    move.sent_lines()
    for peer in [partner] + plane:
        pl.semaphore_signal(credit, inc=1, device_id=peer, device_id_type=MESH)

    wait_sums()
    gain_part[...] = jnp.zeros_like(gain_part)
    for row in range(2):

        def body2(part):
            result = from_partner[z, row, part].astype(full)
            for step in steps:
                result += came[ahead(z, step), row, part].astype(full)
            entries = hidden_in[row, part]
            scale = lax.rsqrt(jnp.mean(entries * entries, axis=-1, keepdims=True) + EPSILON)
            gain_part[...] += jnp.sum(result * entries * scale, axis=0, keepdims=True)
            result = result * gain_ffn[...]
            inside = jnp.mean(result * entries, axis=-1, keepdims=True) * (scale * scale * scale)
            grad = grad_out[row, part].astype(full) + result * scale - entries * inside
            d_hidden_in[row, part] = grad
            normed[row, part] = grad.astype(half)

        chunks(64, body2)
    pl.semaphore_wait(credit, 4)
    move.sent_sums()
    all_branch = all_norm.reshape(8, 2, 64, D)
    branches = [move.send(normed, all_branch.at[me], peer) for peer in plane]
    branch_copies = [
        move.send(normed, all_branch.at[me], partner), move.keep(normed, all_branch.at[me])
    ]

    move.sent(*to_partner)
    to_partner, sums = [], []
    walk = [ahead(z, step) for step in steps] + [z]
    for index, zb in enumerate(walk):

        @pl.loop(0, 4)
        def _(step, zb=zb):
            cols = wide(step * 512, 512)
            block = plain(hidden[zb], flat_wd[:, cols])
            partial[pl.ds(2 * zb, 2), :, :, cols] = block.reshape(2, 2, 64, 512).astype(half)

        to_partner.append(move.send(partial.at[2 * zb + other], all_tok.at[zb], partner))
        if index > 0:
            before = walk[index - 1]
            pair_sum(before, to_partner[index - 1], all_tok, 0)
            sums.append(move.send(all_tok.at[before], all_tok.at[4 + z], line[index - 1]))
    pair_sum(z, to_partner[3], all_tok, 0)

    move.sent(*down_copies, *wo_copies)

    @pl.loop(0, 4)
    def _(to):
        rows_at = wide(to * 256, 256)

        @pl.loop(0, 4)
        def _(step):
            cols = wide(step * 512, 512)
            flat_wd[rows_at, cols] = down(flat_hidden[:, rows_at], flat_grads[:, cols]).astype(half)

    load_tok = move.keep(kept_tok, all_out.reshape(8, 2, 64, D))

    def load(source):
        return [
            move.keep(source(side), flat_d.at[pl.ds(side * 512, 512), pl.ds(0, 1024)])
            for side in (0, 1)
        ]

    def add_loaded(side, chunk):
        @pl.loop(0, 512 // CHUNK)
        def _(step):
            lanes = pl.ds(side * 1024, 1024)
            rows = wide(chunk * 512 + step * CHUNK, CHUNK)
            extra = flat_d[wide(side * 512 + step * CHUNK, CHUNK), pl.ds(0, 1024)]
            result = flat_wg[rows, lanes].astype(full) + extra.astype(full)
            flat_wg[rows, lanes] = result.astype(half)

    move.arrive(*branches)
    pieces = [
        move.send(direct[side], gate_up_in.at[side, 0], plane[side]) for side in (0, 1)
    ]
    for peer_chip in others:
        block = all_branch.at[2 * peer_chip + core]
        branch_copies.append(move.send(block, block, partner))
    move.arrive(*passed)
    loads = load(lambda side: gate_up_mid.at[side])
    later = []
    for side in (0, 1):
        move.arrive(loads[side])
        add_loaded(side, others[1 - side])
        later.append(move.send(handed[side], gate_up_in.at[side, 1], plane[1 - side]))
    move.arrive(*branch_copies)

    flat_branch = all_branch.reshape(1024, D)
    flat_wo = all_wo.reshape(256, D)
    d_heads_at, d_projected_at = pl.ds(0, 256), pl.ds(256, 384)

    @pl.loop(0, 4)
    def _(step):
        rows = wide(step * 256, 256)
        flat_hidden[rows, d_heads_at] = across(flat_branch[rows], flat_wo[...]).astype(half)

    @pl.loop(0, 4)
    def _(step):
        cols = wide(step * 512, 512)
        block = down(flat_attended[...].astype(half), flat_branch[:, cols])
        flat_wo[:, cols] = block.astype(half)

    outs = [
        move.send(all_wo.at[ahead(z, step)], out_came.at[z], peer) for step, peer in zip(steps, line)
    ]
    outs.append(move.keep(all_wo.at[z], out_came.at[z]))
    lower = lower_half((128, 128))
    line_low = lower_half((1, 128))
    gain_qk[...] = jnp.zeros_like(gain_qk)

    @pl.loop(0, 2)
    def _(row):
        d_keys_values[...] = jnp.zeros_like(d_keys_values)

        def token_rows(block):
            return wide((2 * block + row) * 64, 64)

        for tile in range(2):
            lanes = pl.ds(tile * 128, 128)
            for part in range(4):
                own_places, upto = pl.ds(part * 128, 128), pl.ds(0, (part + 1) * 128)
                d_heads = jnp.concatenate(
                    [flat_hidden[token_rows(2 * part + index), lanes] for index in range(2)], axis=0
                )
                products = d_heads.astype(full) * attended[pl.ds(2 * part, 2), row, :, lanes].reshape(128, 128)
                query = queries[row, tile, own_places]
                result = jnp.zeros((128, 128), full)
                for side in range(2):
                    mask = lower if side == 0 else jnp.logical_not(lower)
                    delta = jnp.sum(jnp.where(mask, products, 0.0), axis=-1, keepdims=True)
                    keys = keys_values[row, side, upto]
                    probs = attention_probs(query, keys, first_of(row, part), part)
                    d_probs = across(d_heads, keys_values[row, 2 + side, upto])
                    d_scores = (probs * (d_probs - delta)).astype(half)
                    result += plain(d_scores, keys)
                    d_keys_values[side, upto] += down(d_scores, query)
                    d_keys_values[2 + side, upto] += down(probs.astype(half), d_heads)
                d_queries[tile, own_places] = result

        @pl.loop(0, 8)
        def _(block):
            cosine, sine = tables_of(block, row)
            places = wide(block * 64, 64)
            for tile in range(3):
                entries = projected[block, row, :, pl.ds(tile * 128, 128)]
                gain = gain_heads[tile // 2 : tile // 2 + 1]
                scale = lax.rsqrt(head_means(entries * entries) + EPSILON)
                if tile < 2:
                    grad = d_queries[tile, places] * HEAD_DIM ** (-0.5)
                else:
                    from_low, from_high = d_keys_values[0, places], d_keys_values[1, places]
                    grad = jnp.where(low, from_low + pltpu.roll(from_high, 64, 1), 0.0)
                grad = grad * cosine + swap_halves(grad * sine)
                for_gain = jnp.sum(grad * entries * scale, axis=0, keepdims=True)
                if tile < 2:
                    for_gain = jnp.where(line_low, for_gain + pltpu.roll(for_gain, 64, 1), 0.0)
                else:
                    for_gain = jnp.where(line_low, 0.0, pltpu.roll(for_gain, 64, 1))
                gain_qk[...] += for_gain
                grad = grad * gain
                inside = head_means(grad * entries) * (scale * scale * scale)
                grad = grad * scale - entries * inside
                if tile == 2:
                    values = pltpu.roll(d_keys_values[2, places], 64, 1)
                    grad = jnp.where(low, grad, values + d_keys_values[3, places])
                flat_hidden[token_rows(block), pl.ds(256 + tile * 128, 128)] = grad.astype(half)

    move.sent(*to_partner)

    @pl.loop(0, 4)
    def _(step):
        rows = flat_hidden[wide(step * 256, 256), d_projected_at]

        @pl.loop(0, 4)
        def _(col):
            cols = wide(col * 512, 512)
            block = across(rows, flat_wq[cols])
            partial[wide(step * 2, 2), :, :, cols] = block.reshape(2, 2, 64, 512).astype(half)

    halves = [move.send(partial.at[2 * to + other], from_partner.at[to], partner) for to in order]
    move.arrive(load_tok)

    for block in range(4):
        strip = pl.ds(1024 + 384 * (block // 2), 384)
        product = down(
            flat_grads[:, pl.ds(block * 512, 512)], flat_hidden[:, d_projected_at]
        )
        flat_d[pl.ds(512 * (block % 2), 512), strip] = product.astype(half)

    for peer in [partner] + line + cross:
        pl.semaphore_signal(tokens_used, inc=1, device_id=peer, device_id_type=MESH)

    def head_block(head, at):
        rows = wide(((head % 4) * 4 + at) * 64, 64)
        return flat_d.at[rows, pl.ds(1024 + 384 * (head // 4), 384)]

    qkv_pieces = []
    for step, peer in zip(steps, line):
        pairs = [(head_block(head, ahead(z, step)), qkv_in.at[z, head]) for head in range(8)]
        qkv_pieces.append(move.send_parts(pairs, (qkv_in.at[z], qkv_in.at[z]), peer))
    d_norms = []
    for to, arrived, peer in zip(others, halves, plane):
        move.arrive(arrived)
        add_blocks(partial.at[2 * to + core], from_partner.at[to], from_partner.at[to])
        d_norms.append(move.send(from_partner.at[to], came.at[chip], peer))
    downs = [move.send(wd.at[to], down_came.at[chip], peer) for to, peer in zip(others, plane)]
    downs.append(move.keep(wd.at[chip], down_came.at[chip]))
    move.arrive(halves[3])
    add_blocks(partial.at[me], from_partner.at[chip], from_partner.at[chip])

    for slot, handles in ((0, pieces), (1, later)):
        move.arrive(*handles)
        loads = load(lambda side, slot=slot: gate_up_in.at[side, slot])
        for side in (0, 1):
            move.arrive(loads[side])
            add_loaded(side, chip)

    blocks = all_out.reshape(16, 64, D)

    def back_block(to_core, to_z):
        return all_wg.at[chip, to_core, to_z], blocks.at[8 + 2 * z + core]

    pl.semaphore_wait(tokens_used, 7)
    gate_ups = []
    for step, peer, peer_cross in zip(steps, line, cross):
        to = ahead(z, step)
        gate_ups.append(move.send(*back_block(core, to), peer))
        gate_ups.append(move.send(*back_block(other, to), peer_cross))
    gate_ups.append(move.send(*back_block(other, z), partner))
    gate_ups.append(move.keep(*back_block(core, z)))

    move.arrive(*sums)
    for row in range(2):

        def body3(part):
            result = hidden_in[row, part] + all_tok[z, row, part].astype(full)
            for step in steps:
                result += all_tok[4 + ahead(z, step), row, part].astype(full)
            out_sum[row, part] = result.astype(half)

        chunks(64, body3)

    move.arrive(*d_norms)
    gain_part2[...] = jnp.zeros_like(gain_part2)
    for row in range(2):

        def body4(part):
            result = from_partner[chip, row, part].astype(full)
            for peer_chip in others:
                result += came[peer_chip, row, part].astype(full)
            entries = tok[row, part].astype(full)
            scale = lax.rsqrt(jnp.mean(entries * entries, axis=-1, keepdims=True) + EPSILON)
            gain_part2[...] += jnp.sum(result * entries * scale, axis=0, keepdims=True)
            result = result * gain_attn[...]
            inside = jnp.mean(result * entries, axis=-1, keepdims=True) * (scale * scale * scale)
            result = d_hidden_in[row, part] + result * scale - entries * inside
            grad_tok[row, part] = result.astype(half)

        chunks(64, body4)

    def send_heads():
        move.arrive(*qkv_pieces)
        move.sent(*heads[1:])
        for head in range(8):
            result = head_block(head, z)[...].astype(full)
            for step in steps:
                result += qkv_in[ahead(z, step), head].astype(full)
            wq_send[head] = result.astype(half)
        copies = [move.send(wq_send.at[peer[0]], qkv_came.at[me], peer) for peer in everyone]
        return copies + [move.keep(wq_send.at[me], qkv_came.at[me])]

    flat_packed = packed.reshape(512, 128)
    first = 2 * COL_ROWS
    line_lanes = lax.broadcasted_iota(jnp.int32, (1, 128), 1)
    flat_packed[pl.ds(first + 33, 512 - first - 33)] = jnp.zeros((512 - first - 33, 128), full)

    def statistics(slot, read):
        count, width, row_at, col_at = MATRICES[slot]
        own_rows, some = pl.ds(row_at, count), pl.ds(0, count)
        d_queries[0, some] = jnp.zeros((count, 128), full)

        @pl.loop(0, width // 128)
        def _(step):
            entries = read(step)
            d_queries[0, some] += entries * entries

        mean = jnp.sum(d_queries[0, some], axis=-1, keepdims=True) / width + SQUARE_EPSILON
        new = BETA * rows[own_rows] + (1.0 - BETA) * mean
        rows_new[own_rows] = new
        row_factors[own_rows] = lax.rsqrt(new)
        d_keys_values[0, some] = jnp.broadcast_to(1.0 / new, (count, 128))

        @pl.loop(0, width // 128)
        def _(step):
            entries = read(step)
            square = entries * entries
            flat_packed[pl.ds(col_at + step, 1)] = (
                jnp.sum(square, axis=0, keepdims=True) + count * SQUARE_EPSILON
            )
            flat_packed[pl.ds(COL_ROWS + col_at + step, 1)] = jnp.sum(
                square * d_keys_values[0, some], axis=0, keepdims=True
            )

        stats = flat_packed[pl.ds(first + 33, 1)]
        stats = jnp.where(line_lanes == slot, jnp.sum(new, axis=0, keepdims=True), stats)
        stats = jnp.where(line_lanes == 4 + slot, total(weight_sums[slot]), stats)
        flat_packed[pl.ds(first + 33, 1)] = stats

    def lanes_of(step):
        return wide(step * 128, 128)

    def four(buffer):
        def read(step):
            result = buffer[0, :, lanes_of(step)].astype(full)
            for slot in range(1, 4):
                result += buffer[slot, :, lanes_of(step)].astype(full)
            return result

        return read

    out_here, down_here = blocks, all_norm.reshape(4, 256, D)
    move.arrive(*outs)
    out_load = move.keep(out_came, out_here.at[pl.ds(0, 4)])
    qkv_copies = send_heads()
    move.arrive(*downs)
    move.sent(*branch_copies[2:])
    down_load = move.keep(down_came, down_here)
    move.arrive(out_load)
    statistics(1, four(out_here))
    move.arrive(down_load)
    statistics(3, four(down_here))

    move.arrive(*qkv_copies)
    for head in range(8):
        for part in range(2):
            strip = qkv_came[head, :, pl.ds(part * 128, 128)]
            g_qkv[:, pl.ds(head * 256 + part * 128, 128)] = strip.astype(full)
    for pair in range(4):
        keys = qkv_came[2 * pair, :, pl.ds(256, 128)].astype(full)
        values = qkv_came[2 * pair + 1, :, pl.ds(256, 128)].astype(full)
        g_qkv[:, pl.ds(2048 + pair * 128, 128)] = jnp.where(low, keys, pltpu.roll(values, 64, 1))
        g_qkv[:, pl.ds(2560 + pair * 128, 128)] = jnp.where(low, pltpu.roll(keys, 64, 1), values)

    @pl.loop(0, QKV // 128)
    def _(step):
        entries = m_qkv[:, lanes_of(step)]
        weight_sums[0, :, pl.ds(0, 128)] += jnp.sum((entries * entries).reshape(8, 8, 128), axis=0)

    statistics(0, lambda step: g_qkv[:, lanes_of(step)])
    for slot in range(16):
        strip = pl.ds(slot * 128, 128)
        flat_packed[pl.ds(first + slot, 1)] = gain_part2[:, strip]
        flat_packed[pl.ds(first + 16 + slot, 1)] = gain_part[:, strip]
    flat_packed[pl.ds(first + 32, 1)] = gain_qk[...]

    move.arrive(*gate_ups)
    move.sent(*qkv_pieces)

    def read_gate_up(step):
        inside = lax.rem(step, 64)
        owner = lax.div(inside, 2)
        block = 2 * lax.rem(owner, 4) + lax.rem(lax.div(owner, 4), 2)
        begin = lax.div(step, 64) * 1024 + lax.div(owner, 8) * 256 + lax.rem(inside, 2) * 128
        strip = blocks[8 + block, :, wide(begin, 128)]
        flat_d[wide(lax.div(step, 16) * 64, 64), lanes_of(lax.rem(step, 16))] = strip
        return strip.astype(full)

    statistics(2, read_gate_up)
    for block in range(8):
        move.keep(flat_d.at[pl.ds(64 * block, 64)], gate_up_came.at[:, pl.ds(2048 * block, 2048)])

    copies = [move.send(packed.at[peer[0]], plane_came.at[me], peer) for peer in everyone]
    plane_came[me] = packed[me]
    move.arrive(*copies)
    result = plane_came[0]
    for slot in range(1, 8):
        result = result + plane_came[slot]
    plane_sum[...] = result
    copies = [move.send(plane_sum.at[peer[1]], line_came.at[z], peer) for peer in line]
    line_came[z] = plane_sum[z]
    move.arrive(*copies)
    line_sum[...] = line_came[0] + line_came[1] + line_came[2] + line_came[3]
    copies = [move.send(line_sum, line_all.at[z], peer) for peer in line]
    line_all[z] = line_sum[...]
    move.arrive(*copies)
    copies = [move.send(line_all, totals.at[me], peer) for peer in everyone]
    totals[me] = line_all[...]
    move.arrive(*copies)
    derive_updates(
        totals.reshape(512, 128), col_moments, gain_moments, gains,
        cols_new, col_factors, moments_new, gains_new, grad_gains, spreads,
    )
    move.finish()


def split_local(
    tokens, doc_starts, grad_out, qkv_master, out_master, gate_up_master, down_master, gains,
    qkv_rows, out_rows, gate_up_rows, down_rows, col_moments, gain_moments,
):
    half, full = jnp.bfloat16, jnp.float32
    gain_query, gain_key = gains[2 * D : 2 * D + HEAD_DIM], gains[2 * D + HEAD_DIM :]
    gain_heads = jnp.stack(
        [jnp.concatenate([gain_query, gain_query]), jnp.concatenate([gain_key, gain_key])]
    )
    lane = np.arange(128)
    rates = ROPE_BASE ** (-(lane % 32) * 2.0 / HEAD_DIM)
    rates = jnp.asarray(np.stack([rates, np.where(lane % 64 < 32, -1.0, 1.0)]), full)

    def near(*shape, kind=half):
        return pltpu.VMEM(shape, kind)

    masters = (qkv_master, out_master, gate_up_master, down_master)
    stats_shape = (8, 4, 16, 128)
    (
        output, grad_tokens, grad_qkv, gate_up_came, out_came, down_came, rows_new, row_factors,
        cols_new, col_factors, moments_new, gains_new, grad_gains, spreads, *_,
    ) = exchange(
        layer_kernel, 0,
        [
            (tokens, True), (doc_starts, None), (rates, True), (jnp.asarray(place_tables(512)), True),
            (gains[None, :D], True),
            (gains[None, D : 2 * D], True), (gain_heads, True), (gains.reshape(-1, 128), True),
            (grad_out, True), (qkv_master, True), (out_master, False), (down_master, False),
            (gate_up_master, False),
            (jnp.concatenate([qkv_rows, out_rows, gate_up_rows, down_rows])[:, None], True),
            (col_moments.reshape(-1, 128), True), (gain_moments.reshape(-1, 128), True),
        ],
        [
            ((2, 64, D), half, True), ((2, 64, D), half, True), ((64, QKV), full, True),
            ((64, 2 * FF), half, False), ((4, 64, D), half, False), ((4, 256, D), half, False),
            ((448, 1), full, True), ((448, 1), full, True),
            ((COL_ROWS, 128), full, True), ((1, COLS), full, True),
            ((GAIN_ROWS, 128), full, True), ((GAIN_ROWS, 128), full, True),
            ((GAIN_ROWS, 128), full, True), ((1, 128), full, True),
            ((2, 2, 512, 1024), half, False), ((2, 512, 1024), half, False),
            ((8, 2, 64, D), half, False),
        ],
        [
            near(8, 2, 64, 384, kind=full), near(2, 2, 512, 128), near(2, 4, 512, 128),
            near(8, 2, 64, 256, kind=full), near(2, 8, 1, 128, kind=full),
            near(8, 64, 384), near(2, 64, D), near(8, 2, 64, D), near(8, 4, 64, 384), near(4, 64, D),
            near(8, 2, 64, D), near(4, 2, 64, D), near(4, 2, 64, D), near(2, 64, D, kind=full),
            near(4, 2, 2, 64, D), near(4, 2, 2, 64, D), near(4, 2, 4, 64, 2048), near(4, 256, D),
            near(4, 256, 1024), near(4, 256, 2048),
            near(2, 512, 128, kind=full), near(4, 512, 128, kind=full), near(4, 8, 64, 384),
            near(2, 64, D, kind=full), near(1, D, kind=full), near(1, D, kind=full),
            near(1, 128, kind=full), near(4, 8, D, kind=full), near(8, 64, 384),
            near(*stats_shape, kind=full), near(*stats_shape, kind=full),
            near(*stats_shape[1:], kind=full), near(*stats_shape[1:], kind=full),
            near(*stats_shape[2:], kind=full), near(*stats_shape[1:], kind=full),
            near(*stats_shape, kind=full),
            pltpu.SemaphoreType.REGULAR, pltpu.SemaphoreType.REGULAR,
        ],
        (176, 56), 170 << 20, 48 << 30,
    )
    grads = (
        grad_qkv, jnp.sum(out_came.astype(full), axis=0), gate_up_came.astype(full),
        jnp.sum(down_came.astype(full), axis=0),
    )
    new_masters = []
    for slot, (count, width, row_at, col_at) in enumerate(MATRICES):
        row_factor = row_factors[row_at : row_at + count]
        col_factor = col_factors[:, col_at * 128 : col_at * 128 + width]
        new_masters.append(masters[slot] - grads[slot] * row_factor * col_factor)
    return (
        output,
        grad_tokens,
        *grads,
        grad_gains.reshape(-1),
        *[rows_new[row_at : row_at + count, 0] for count, _, row_at, _ in MATRICES],
        cols_new.reshape(-1),
        moments_new.reshape(-1),
        *new_masters,
        *[master.astype(half) for master in new_masters],
        gains_new.reshape(-1),
        spreads[0, :8],
    )


def optimizer_step(
    grads, gain_local, masters, gains, row_states, col_moments, gain_moments, total_fn
):
    beta = 1.0 - STEP ** (-0.8)
    col_widths = (QKV, D, 2 * FF, D)
    row_totals = (D, HEADS * HEAD_DIM, D, FF)
    squares = [gradient * gradient + SQUARE_EPSILON for gradient in grads]
    rows_new = [
        beta * row_state + (1.0 - beta) * jnp.mean(square, axis=1)
        for row_state, square in zip(row_states, squares)
    ]
    col_local = [jnp.sum(square, axis=0) for square in squares]
    weighted_local = [
        jnp.sum(gradient * gradient / row_new[:, None], axis=0)
        for gradient, row_new in zip(grads, rows_new)
    ]
    stats_local = jnp.stack(
        [jnp.sum(row_new) for row_new in rows_new]
        + [jnp.sum(master * master) for master in masters]
    )
    totals = total_fn(jnp.concatenate(col_local + weighted_local + [stats_local, gain_local]))
    cols = sum(col_widths)
    col_sums, weighted = totals[:cols], totals[cols : 2 * cols]
    stats, grad_gains = totals[2 * cols : 2 * cols + 8], totals[2 * cols + 8 :]
    col_divisor = jnp.concatenate(
        [
            jnp.full((col_width,), float(row_total), jnp.float32)
            for col_width, row_total in zip(col_widths, row_totals)
        ]
    )
    cols_new = beta * col_moments + (1.0 - beta) * col_sums / col_divisor
    new_masters = []
    spreads = []
    begin_at = 0
    for slot in range(4):
        col_part = cols_new[begin_at : begin_at + col_widths[slot]]
        weighted_part = weighted[begin_at : begin_at + col_widths[slot]]
        begin_at = begin_at + col_widths[slot]
        mean_rows = stats[slot] / row_totals[slot]
        unit = (
            grads[slot]
            * lax.rsqrt(rows_new[slot] / mean_rows)[:, None]
            * lax.rsqrt(col_part)[None, :]
        )
        entries_all = float(row_totals[slot] * col_widths[slot])
        spread = jnp.sqrt(mean_rows * jnp.sum(weighted_part / col_part) / entries_all)
        scale = STEP_RATE * jnp.maximum(SCALE_EPSILON, jnp.sqrt(stats[4 + slot] / entries_all))
        new_masters.append(masters[slot] - scale * unit / jnp.maximum(1.0, spread / CLIP_LEVEL))
        spreads.append(spread)
    bounds = (0, D, 2 * D, 2 * D + HEAD_DIM, 2 * D + 2 * HEAD_DIM)
    moment_parts, gain_parts = ([], [])
    for segment in range(4):
        gradient = grad_gains[bounds[segment] : bounds[segment + 1]]
        gain_old = gains[bounds[segment] : bounds[segment + 1]]
        moment_new = beta * gain_moments[bounds[segment] : bounds[segment + 1]] + (1.0 - beta) * (
            gradient * gradient + SQUARE_EPSILON
        )
        unit = gradient * lax.rsqrt(moment_new)
        spread = jnp.sqrt(jnp.mean(unit * unit))
        scale = STEP_RATE * jnp.maximum(SCALE_EPSILON, jnp.sqrt(jnp.mean(gain_old * gain_old)))
        moment_parts.append(moment_new)
        gain_parts.append(gain_old - scale * unit / jnp.maximum(1.0, spread / CLIP_LEVEL))
        spreads.append(spread)
    return (
        grad_gains,
        *rows_new,
        cols_new,
        jnp.concatenate(moment_parts),
        *new_masters,
        *[master.astype(jnp.bfloat16) for master in new_masters],
        jnp.concatenate(gain_parts),
        jnp.stack(spreads),
    )


def solution(mesh):
    split = mesh.shape["seq"] == 8 and mesh.shape["rows"] == 4
    return jax.shard_map(
        split_local if split else gathered_local,
        mesh=mesh,
        in_specs=(
            P("rows", "seq", None),
            P("rows", None),
            P("rows", "seq", None),
            P(("seq", "rows"), None),
            P(("seq", "rows"), None),
            P(("seq", "rows"), None),
            P(("seq", "rows"), None),
            P(),
            P(("seq", "rows")),
            P(("seq", "rows")),
            P(("seq", "rows")),
            P(("seq", "rows")),
            P(),
            P(),
        ),
        out_specs=(
            P("rows", "seq", None),
            P("rows", "seq", None),
            P(("seq", "rows"), None),
            P(("seq", "rows"), None),
            P(("seq", "rows"), None),
            P(("seq", "rows"), None),
            P(),
            P(("seq", "rows")),
            P(("seq", "rows")),
            P(("seq", "rows")),
            P(("seq", "rows")),
            P(),
            P(),
            P(("seq", "rows"), None),
            P(("seq", "rows"), None),
            P(("seq", "rows"), None),
            P(("seq", "rows"), None),
            P(("seq", "rows"), None),
            P(("seq", "rows"), None),
            P(("seq", "rows"), None),
            P(("seq", "rows"), None),
            P(),
            P(),
        ),
        check_vma=False,
    )
```

```python
from functools import partial

import jax
import jax.numpy as jnp
import numpy as np
from jax import lax
from jax.experimental import pallas as pl
from jax.experimental.pallas import tpu as pltpu
from jax.sharding import PartitionSpec as P

D = 2048
HEADS = 32
KV_HEADS = 8
HEAD_DIM = 64
FF = 8192
STEP = 10
QKV = 3072


EPSILON = 1e-06
ROPE_BASE = 10000.0
MASKED_SCORE = -1e30
STEP_RATE = 0.3
CLIP_LEVEL = 1.0
SQUARE_EPSILON = 1e-30
SCALE_EPSILON = 0.001


def from_behind(value, axis, steps):
    count = lax.axis_size(axis)
    pairs = [(source, (source + steps) % count) for source in range(count)]
    return lax.ppermute(value, axis, pairs)


def norm_rows(entries, gain):
    return entries * lax.rsqrt(jnp.mean(entries * entries, axis=-1, keepdims=True) + EPSILON) * gain


def turn(entries, cos_wide, sin_wide):
    half_width = entries.shape[-1] // 2
    turned = jnp.concatenate([-entries[..., half_width:], entries[..., :half_width]], axis=-1)
    return entries * cos_wide + turned * sin_wide


def doc_tables(doc_starts, places):
    before = doc_starts[:, None, :] <= places[None, :, None]
    doc_ids = jnp.sum(before.astype(jnp.int32), axis=-1)
    doc_first = jnp.max(jnp.where(before, doc_starts[:, None, :], 0), axis=-1)
    return (doc_ids, places[None, :] - doc_first)


def rotary(offsets):
    frequency = ROPE_BASE ** (-(jnp.arange(HEAD_DIM // 2, dtype=jnp.float32) * 2.0 / HEAD_DIM))
    angles = offsets.astype(jnp.float32)[..., None] * frequency
    cos_table = jnp.concatenate([jnp.cos(angles), jnp.cos(angles)], axis=-1)
    sin_table = jnp.concatenate([jnp.sin(angles), jnp.sin(angles)], axis=-1)
    return (cos_table, sin_table)


def queries_keys(
    cos_table, sin_table, projected, gain_query, gain_key, heads=HEADS, kv_heads=KV_HEADS
):
    rows_here, seq_here = (projected.shape[0], projected.shape[1])
    att_width = heads * HEAD_DIM
    queries = projected[..., :att_width].reshape(rows_here, seq_here, heads, HEAD_DIM)
    keys_rot = projected[..., att_width : att_width + kv_heads * HEAD_DIM].reshape(
        rows_here, seq_here, kv_heads, HEAD_DIM
    )
    cos_wide = cos_table[:, :, None, :]
    sin_wide = sin_table[:, :, None, :]
    queries = turn(norm_rows(queries, gain_query), cos_wide, sin_wide) * HEAD_DIM ** (-0.5)
    keys_rot = turn(norm_rows(keys_rot, gain_key), cos_wide, sin_wide)
    return (queries, keys_rot)


def mask_of(query_docs, query_places, key_docs, key_places):
    same_doc = query_docs[:, :, None] == key_docs[:, None, :]
    causal = query_places[None, :, None] >= key_places[None, None, :]
    return (same_doc & causal)[:, None, None, :, :]


def gathered_local(
    tokens,
    doc_starts,
    grad_out,
    qkv_master,
    out_master,
    gate_up_master,
    down_master,
    gains,
    qkv_rows,
    out_rows,
    gate_up_rows,
    down_rows,
    col_moments,
    gain_moments,
):
    cycle_size = lax.axis_size("seq")
    seq_index = lax.axis_index("seq")
    rows_dev, seq_dev = (tokens.shape[0], tokens.shape[1])
    group_size = HEADS // KV_HEADS
    att_width = HEADS * HEAD_DIM
    kv_width = KV_HEADS * HEAD_DIM
    gain_attn = gains[:D]
    gain_ffn = gains[D : 2 * D]
    gain_query = gains[2 * D : 2 * D + HEAD_DIM]
    gain_key = gains[2 * D + HEAD_DIM :]
    local_places = jnp.arange(seq_dev, dtype=jnp.int32)
    places = seq_index * seq_dev + local_places
    query_docs, offsets = doc_tables(doc_starts, places)
    cos_table, sin_table = rotary(offsets)
    copies = (
        qkv_master.astype(jnp.bfloat16),
        out_master.astype(jnp.bfloat16),
        gate_up_master.astype(jnp.bfloat16),
        down_master.astype(jnp.bfloat16),
    )
    w_qkv, w_out, w_gate_up, w_down = (
        lax.all_gather(copies[0], ("seq", "rows"), axis=0, tiled=True),
        lax.all_gather(copies[1], ("seq", "rows"), axis=0, tiled=True),
        lax.all_gather(copies[2], ("seq", "rows"), axis=0, tiled=True),
        lax.all_gather(copies[3], ("seq", "rows"), axis=0, tiled=True),
    )
    tokens_wide = tokens.astype(jnp.float32)
    normed = norm_rows(tokens_wide, gain_attn).astype(jnp.bfloat16)
    projected = jnp.einsum("rtd,de->rte", normed, w_qkv, preferred_element_type=jnp.float32)
    head_fn = partial(queries_keys, cos_table, sin_table)
    queries, keys_rot = head_fn(projected, gain_query, gain_key)
    query16 = queries.astype(jnp.bfloat16).reshape(
        rows_dev, seq_dev, KV_HEADS, group_size, HEAD_DIM
    )
    keys16 = keys_rot.astype(jnp.bfloat16).reshape(rows_dev, seq_dev, kv_width)
    values16 = projected[..., att_width + kv_width :].astype(jnp.bfloat16)
    stat_shape = (rows_dev, KV_HEADS, group_size, seq_dev)
    initial = (
        jnp.full(stat_shape, MASKED_SCORE, jnp.float32),
        jnp.zeros(stat_shape, jnp.float32),
        jnp.zeros(stat_shape + (HEAD_DIM,), jnp.float32),
    )
    carry = initial
    key_piece = lax.all_gather(keys16, "seq", axis=1, tiled=True)
    value_piece = lax.all_gather(values16, "seq", axis=1, tiled=True)
    key_count = key_piece.shape[1]

    def absorb_block(state, block_index):
        best, total, summed = state
        block_begin = block_index * seq_dev
        key_block = lax.dynamic_slice_in_dim(key_piece, block_begin, seq_dev, 1).reshape(
            rows_dev, seq_dev, KV_HEADS, HEAD_DIM
        )
        value_block = lax.dynamic_slice_in_dim(value_piece, block_begin, seq_dev, 1).reshape(
            rows_dev, seq_dev, KV_HEADS, HEAD_DIM
        )
        key_places = block_begin + jnp.arange(seq_dev, dtype=jnp.int32)
        key_docs, _ = doc_tables(doc_starts, key_places)
        allowed = mask_of(query_docs, places, key_docs, key_places)
        scores = jnp.einsum(
            "rqkgh,rtkh->rkgqt", query16, key_block, preferred_element_type=jnp.float32
        )
        scores = jnp.where(allowed, scores, MASKED_SCORE)
        best_new = jnp.maximum(best, jnp.max(scores, axis=-1))
        weights = jnp.where(allowed, jnp.exp(scores - best_new[..., None]), 0.0)
        factor = jnp.exp(best - best_new)
        total = total * factor + jnp.sum(weights, axis=-1)
        summed = summed * factor[..., None] + jnp.einsum(
            "rkgqt,rtkh->rkgqh",
            weights.astype(jnp.bfloat16),
            value_block,
            preferred_element_type=jnp.float32,
        )
        return ((best_new, total, summed), None)

    carry, _ = lax.scan(absorb_block, carry, jnp.arange(key_count // seq_dev, dtype=jnp.int32))
    best, total, summed = carry
    log_total = best + jnp.log(total)
    attended = summed / total[..., None]
    attended16 = (
        attended.transpose(0, 3, 1, 2, 4).reshape(rows_dev, seq_dev, att_width).astype(jnp.bfloat16)
    )
    branch = jnp.einsum("rtc,cd->rtd", attended16, w_out, preferred_element_type=jnp.float32)
    hidden_in = tokens_wide + branch
    normed2 = norm_rows(hidden_in, gain_ffn).astype(jnp.bfloat16)
    gate_up = jnp.einsum("rtd,df->rtf", normed2, w_gate_up, preferred_element_type=jnp.float32)
    gate_part, up_part = (gate_up[..., :FF], gate_up[..., FF:])
    hidden = (jax.nn.silu(gate_part) * up_part).astype(jnp.bfloat16)
    output = hidden_in + jnp.einsum(
        "rtf,fd->rtd", hidden, w_down, preferred_element_type=jnp.float32
    )
    d_hidden = jnp.einsum("rtd,fd->rtf", grad_out, w_down, preferred_element_type=jnp.float32)
    silu_value, silu_back = jax.vjp(jax.nn.silu, gate_part)
    d_gate = silu_back(d_hidden * up_part)[0]
    d_gate_up = jnp.concatenate([d_gate, d_hidden * silu_value], axis=-1).astype(jnp.bfloat16)
    d_normed2 = jnp.einsum("rtf,df->rtd", d_gate_up, w_gate_up, preferred_element_type=jnp.float32)
    _, ffn_norm_back = jax.vjp(norm_rows, hidden_in, gain_ffn)
    d_inner, grad_gain_ffn = ffn_norm_back(d_normed2)
    d_hidden_in = grad_out.astype(jnp.float32) + d_inner
    term_down = jnp.einsum("rtf,rtd->fd", hidden, grad_out, preferred_element_type=jnp.float32)
    grad_down = lax.psum_scatter(term_down, ("seq", "rows"), scatter_dimension=0, tiled=True)
    term_gate_up = jnp.einsum("rtd,rtf->df", normed2, d_gate_up, preferred_element_type=jnp.float32)
    grad_gate_up = lax.psum_scatter(term_gate_up, ("seq", "rows"), scatter_dimension=0, tiled=True)
    d_branch = d_hidden_in.astype(jnp.bfloat16)
    term_out = jnp.einsum("rtc,rtd->cd", attended16, d_branch, preferred_element_type=jnp.float32)
    d_attended = jnp.einsum(
        "rtd,cd->rtc", d_branch, w_out, preferred_element_type=jnp.float32
    ).astype(jnp.bfloat16)
    d_heads = d_attended.reshape(rows_dev, seq_dev, KV_HEADS, group_size, HEAD_DIM).transpose(
        0, 2, 3, 1, 4
    )
    delta = jnp.sum(d_heads.astype(jnp.float32) * attended, axis=-1)

    def cycle_turn(turn_index, carry):
        pair16, grad_pair, d_queries = carry
        source = (seq_index + turn_index) % cycle_size
        key_places = source * seq_dev + local_places
        key_docs, _ = doc_tables(doc_starts, key_places)
        allowed = mask_of(query_docs, places, key_docs, key_places)
        key_block = pair16[0].reshape(rows_dev, seq_dev, KV_HEADS, HEAD_DIM)
        value_block = pair16[1].reshape(rows_dev, seq_dev, KV_HEADS, HEAD_DIM)
        scores = jnp.einsum(
            "rqkgh,rtkh->rkgqt", query16, key_block, preferred_element_type=jnp.float32
        )
        scores = jnp.where(allowed, scores, MASKED_SCORE)
        probs = jnp.where(allowed, jnp.exp(scores - log_total[..., None]), 0.0)
        d_values = jnp.einsum(
            "rkgqt,rkgqh->rtkh",
            probs.astype(jnp.bfloat16),
            d_heads,
            preferred_element_type=jnp.float32,
        )
        d_probs = jnp.einsum(
            "rkgqh,rtkh->rkgqt", d_heads, value_block, preferred_element_type=jnp.float32
        )
        d_scores = (probs * (d_probs - delta[..., None])).astype(jnp.bfloat16)
        d_queries = d_queries + jnp.einsum(
            "rkgqt,rtkh->rkgqh", d_scores, key_block, preferred_element_type=jnp.float32
        )
        d_keys = jnp.einsum(
            "rkgqt,rqkgh->rtkh", d_scores, query16, preferred_element_type=jnp.float32
        )
        grad_pair = grad_pair + jnp.stack(
            [
                d_keys.reshape(rows_dev, seq_dev, kv_width),
                d_values.reshape(rows_dev, seq_dev, kv_width),
            ]
        )
        grad_pair = from_behind(grad_pair.astype(jnp.bfloat16), "seq", -1).astype(grad_pair.dtype)
        pair16 = from_behind(pair16, "seq", -1)
        return (pair16, grad_pair, d_queries)

    start_pair = jnp.stack([keys16, values16])
    start_grads = jnp.zeros((2, rows_dev, seq_dev, kv_width), jnp.float32)
    start_queries = jnp.zeros(stat_shape + (HEAD_DIM,), jnp.float32)
    _, grad_pair, d_queries = lax.fori_loop(
        0, cycle_size, cycle_turn, (start_pair, start_grads, start_queries)
    )
    d_queries = d_queries.transpose(0, 3, 1, 2, 4).reshape(rows_dev, seq_dev, HEADS, HEAD_DIM)
    d_keys_home = grad_pair[0].reshape(rows_dev, seq_dev, KV_HEADS, HEAD_DIM)
    _, heads_back = jax.vjp(head_fn, projected, gain_query, gain_key)
    d_projected, grad_gain_query, grad_gain_key = heads_back((d_queries, d_keys_home))
    d_projected = jnp.concatenate(
        [d_projected[..., : att_width + kv_width], grad_pair[1]], axis=-1
    ).astype(jnp.bfloat16)
    term_qkv = jnp.einsum("rtd,rte->de", normed, d_projected, preferred_element_type=jnp.float32)
    d_normed = jnp.einsum("rte,de->rtd", d_projected, w_qkv, preferred_element_type=jnp.float32)
    _, attn_norm_back = jax.vjp(norm_rows, tokens_wide, gain_attn)
    d_tokens_part, grad_gain_attn = attn_norm_back(d_normed)
    grad_tokens = (d_hidden_in + d_tokens_part).astype(jnp.bfloat16)
    grad_qkv, grad_out_proj = (
        lax.psum_scatter(term_qkv, ("seq", "rows"), scatter_dimension=0, tiled=True),
        lax.psum_scatter(term_out, ("seq", "rows"), scatter_dimension=0, tiled=True),
    )
    gain_local = jnp.concatenate([grad_gain_attn, grad_gain_ffn, grad_gain_query, grad_gain_key])
    grads = (grad_qkv, grad_out_proj, grad_gate_up, grad_down)
    updated = optimizer_step(
        grads, gain_local, (qkv_master, out_master, gate_up_master, down_master), gains,
        (qkv_rows, out_rows, gate_up_rows, down_rows), col_moments, gain_moments,
        lambda vector: lax.psum(vector, ("seq", "rows")),
    )
    return (output.astype(jnp.bfloat16), grad_tokens, *grads, *updated)


MESH = pl.DeviceIdType.MESH
PLACES = 32
VMEM_BYTES = 61 * 1024 * 1024
CHUNK = 16


def here():
    seq = lax.axis_index("seq")
    return lax.div(seq, 2), lax.rem(seq, 2), lax.axis_index("rows")


def flips(chip):
    return (chip + 1 - 2 * lax.rem(chip, 2), lax.rem(chip + 2, 4), 3 - chip)


def ahead(z, step):
    return lax.rem(z + step, 4)


def at_place(chip, core, z):
    return (2 * chip + core, z)


def greet(peers):
    barrier = pltpu.get_barrier_semaphore()
    for peer in peers:
        pl.semaphore_signal(barrier, inc=1, device_id=peer, device_id_type=MESH)
    pl.semaphore_wait(barrier, len(peers))


class Mover:
    def __init__(self, send_sem, recv_sem, local_sem):
        self.send_sem, self.recv_sem, self.local_sem = send_sem, recv_sem, local_sem
        self.remote, self.own, self.lines, self.scattered = [], [], [], []
        self.used = 0

    def copy_of(self, src, dst, peer, send_slot, recv_slot):
        return pltpu.make_async_remote_copy(
            src_ref=src,
            dst_ref=dst,
            send_sem=self.send_sem.at[send_slot],
            recv_sem=self.recv_sem.at[recv_slot],
            device_id=peer,
            device_id_type=MESH,
        )

    def send_parts(self, pairs, whole, peer):
        slot = self.used
        self.used += 1
        for src, dst in pairs:
            self.copy_of(src, dst, peer, slot, slot).start()
        copy = self.copy_of(whole[0], whole[1], peer, slot, slot)
        handle = [copy, False, copy.wait_recv, False]
        self.remote.append(handle)
        return handle

    def send(self, src, dst, peer):
        return self.send_parts([(src, dst)], (src, dst), peer)

    def keep_parts(self, pairs, whole):
        sem = self.local_sem.at[len(self.own)]
        for src, dst in pairs:
            pltpu.make_async_copy(src, dst, sem).start()
        copy = pltpu.make_async_copy(whole[0], whole[1], sem)
        handle = [copy, False, copy.wait]
        self.own.append(handle)
        return handle

    def keep(self, src, dst):
        return self.keep_parts([(src, dst)], (src, dst))

    def line(self, source, block_of, chip, core, z):
        line = (self.used, block_of, chip, core, z)
        self.used += 5
        base = line[0]
        up, low = at_place(chip, core, z + 1), at_place(chip, core, z - 1)
        rising = self.copy_of(source, block_of(z), up, base, base + 3)
        falling = self.copy_of(source, block_of(z), low, base + 4, base + 1)
        pl.when(z < 3)(rising.start)
        pl.when(z > 0)(falling.start)
        self.lines += [(z < 3, rising), (z > 0, falling)]
        return line

    def wait_line(self, line, step, when=None):
        base, block_of, chip, core, z = line
        block = block_of(ahead(z, step))
        peer = at_place(chip, core, ahead(z, step))
        copy = self.copy_of(block, block, peer, base + step, base + step)
        if when is None:
            copy.wait_recv()
        else:
            pl.when(when)(copy.wait_recv)
        return block

    def arrive_line(self, line, step, when=None):
        base, _, chip, core, z = line
        block = self.wait_line(line, step, when)
        rises, falls = (z + step >= 4) & (z < 3), (z + step < 4) & (z > 0)
        up, low = at_place(chip, core, z + 1), at_place(chip, core, z - 1)
        rising = self.copy_of(block, block, up, base + step, base + step - 1)
        falling = self.copy_of(block, block, low, base + step, base + step + 1)
        for moves, copy in ((rises, rising), (falls, falling)):
            moves = moves if when is None else moves & when
            pl.when(moves)(copy.start)
            self.lines.append((moves, copy))
        return block

    def scatter(self, source, target, steps, chip, core, z):
        base = self.used
        self.used += 3

        def start(index):
            at = ahead(z, steps[index])
            copy = self.copy_of(
                source(at), target(z), at_place(chip, core, at), base + index, base + 3 - steps[index]
            )
            copy.start()
            self.scattered.append(copy)

        def wait():
            for step in (1, 2, 3):
                at = ahead(z, step)
                peer = at_place(chip, core, at)
                self.copy_of(source(at), target(at), peer, base, base + step - 1).wait_recv()

        return start, wait

    def arrive(self, *handles):
        for handle in handles:
            if not handle[1]:
                handle[1] = True
                handle[2]()

    def sent(self, *handles):
        for handle in handles:
            if not handle[3]:
                handle[3] = True
                handle[0].wait_send()

    def sent_lines(self):
        for when, copy in self.lines:
            pl.when(when)(copy.wait_send)
        self.lines = []

    def sent_sums(self):
        for copy in self.scattered:
            copy.wait_send()
        self.scattered = []

    def finish(self):
        assert self.used <= self.send_sem.shape[0] and len(self.own) <= self.local_sem.shape[0]
        self.arrive(*self.own, *self.remote)
        self.sent(*self.remote)
        self.sent_lines()
        self.sent_sums()


def semaphores(remote, own):
    return [
        pltpu.SemaphoreType.DMA((remote,)),
        pltpu.SemaphoreType.DMA((remote,)),
        pltpu.SemaphoreType.DMA((max(own, 1),)),
    ]


def exchange(kernel, ident, inputs, outputs, scratch, copies, moved, flops=0):
    spaces = {True: pltpu.VMEM, False: pl.ANY, None: pltpu.SMEM}
    specs = {near: pl.BlockSpec(memory_space=space) for near, space in spaces.items()}
    return pl.pallas_call(
        kernel,
        out_shape=[jax.ShapeDtypeStruct(shape, kind) for shape, kind, _ in outputs],
        in_specs=[specs[near] for _, near in inputs],
        out_specs=[specs[near] for _, _, near in outputs],
        scratch_shapes=scratch + semaphores(*copies),
        compiler_params=pltpu.CompilerParams(
            collective_id=ident, has_side_effects=True, vmem_limit_bytes=VMEM_BYTES
        ),
        cost_estimate=pl.CostEstimate(flops=flops, bytes_accessed=moved, transcendentals=0),
    )(*[array for array, _ in inputs])


def chunks(length, body):
    @pl.loop(0, length // CHUNK)
    def _(step):
        body(pl.ds(pl.multiple_of(step * CHUNK, CHUNK), CHUNK))


def add_blocks(first, second, result):
    for row in range(2):

        def body(part):
            total = first[row, part].astype(jnp.float32) + second[row, part].astype(jnp.float32)
            result[row, part] = total.astype(result.dtype)

        chunks(64, body)


def lower_half(shape):
    return lax.broadcasted_iota(jnp.int32, shape, len(shape) - 1) < 64


def swap_halves(entries):
    lane = lax.broadcasted_iota(jnp.int32, entries.shape, 1)
    return jnp.where(lax.rem(lane, 64) < 32, pltpu.roll(entries, 96, 1), pltpu.roll(entries, 32, 1))


def head_means(entries):
    lower = lower_half(entries.shape)
    low = jnp.sum(jnp.where(lower, entries, 0.0), axis=-1, keepdims=True)
    high = jnp.sum(jnp.where(lower, 0.0, entries), axis=-1, keepdims=True)
    return jnp.where(lower, low, high) * (1.0 / HEAD_DIM)


def wide(start, size):
    return pl.ds(pl.multiple_of(start, size), size)


def plain(left, right):
    return jnp.dot(left, right, preferred_element_type=jnp.float32)


def across(left, right):
    return lax.dot_general(
        left, right, (((1,), (1,)), ((), ())), preferred_element_type=jnp.float32
    )


def down(left, right):
    return lax.dot_general(
        left, right, (((0,), (0,)), ((), ())), preferred_element_type=jnp.float32
    )


def attention_probs(queries, keys, first, part):
    scores = across(queries, keys)
    place = lax.broadcasted_iota(jnp.int32, scores.shape, 1)
    query = lax.broadcasted_iota(jnp.int32, scores.shape, 0) + part * 128
    allowed = (place >= first) & (place <= query)
    scores = jnp.where(allowed, scores, MASKED_SCORE)
    best = jnp.max(scores, axis=-1, keepdims=True)
    weights = jnp.where(allowed, jnp.exp(scores - best), 0.0)
    return weights / jnp.sum(weights, axis=-1, keepdims=True)


COL_ROWS, GAIN_ROWS = 184, 33
COLS = COL_ROWS * 128
MATRICES = ((64, QKV, 0, 0), (64, D, 64, 24), (64, 2 * FF, 128, 40), (256, D, 192, 168))
ROW_TOTALS = (D, HEADS * HEAD_DIM, D, FF)
BETA = 1.0 - STEP ** (-0.8)


def lane_value(vector, lane):
    lanes = lax.broadcasted_iota(jnp.int32, (1, 128), 1)
    return jnp.sum(jnp.where(lanes == lane, vector, 0.0), axis=-1, keepdims=True)


def total(entries):
    return jnp.sum(jnp.sum(entries, axis=-1, keepdims=True), axis=0, keepdims=True)


def document_start(starts, row, place):
    start = jnp.zeros_like(place)
    for document in range(starts.shape[1]):
        begin = starts[row, document]
        start = jnp.maximum(start, jnp.where(place >= begin, begin, 0))
    return start


def place_tables(length):
    rates = ROPE_BASE ** (-(np.arange(128) % 32) * 2.0 / HEAD_DIM)
    angles = np.arange(length)[:, None] * rates
    return np.stack([np.cos(angles), np.sin(angles)]).astype(np.float32)


def derive_updates(
    flat, col_moments, gain_moments, gains,
    cols_new, col_factors, moments_new, gains_new, grad_gains, spreads,
):
    first = 2 * COL_ROWS
    stats = flat[first + 33 : first + 34]
    lanes = lax.broadcasted_iota(jnp.int32, (1, 128), 1)
    out = jnp.zeros((1, 128), jnp.float32)
    for slot, (_, width, _, col_at) in enumerate(MATRICES):
        own = pl.ds(col_at, width // 128)
        entries_all = float(ROW_TOTALS[slot] * width)
        new = BETA * col_moments[own] + (1.0 - BETA) * (flat[own] / ROW_TOTALS[slot])
        cols_new[own] = new
        mean_rows = lane_value(stats, slot) / ROW_TOTALS[slot]
        ratio = total(flat[pl.ds(COL_ROWS + col_at, width // 128)] / new)
        spread = jnp.sqrt(mean_rows * ratio / entries_all)
        scale = STEP_RATE * jnp.maximum(
            SCALE_EPSILON, jnp.sqrt(lane_value(stats, 4 + slot) / entries_all)
        )
        factor = scale * jnp.sqrt(mean_rows) / jnp.maximum(1.0, spread / CLIP_LEVEL)
        factors = lax.rsqrt(new) * factor
        for row in range(width // 128):
            col_factors[:, pl.ds((col_at + row) * 128, 128)] = factors[row : row + 1]
        out = jnp.where(lanes == slot, spread, out)
    gradient = flat[first : first + GAIN_ROWS]
    grad_gains[...] = gradient
    old = gains[...]
    new = BETA * gain_moments[...] + (1.0 - BETA) * (gradient * gradient + SQUARE_EPSILON)
    moments_new[...] = new
    unit = gradient * lax.rsqrt(new)
    row = lax.broadcasted_iota(jnp.int32, (GAIN_ROWS, 128), 0)
    lane = lax.broadcasted_iota(jnp.int32, (GAIN_ROWS, 128), 1)
    segment = jnp.where(row < 16, 0, jnp.where(row < 32, 1, jnp.where(lane < 64, 2, 3)))
    factors = jnp.zeros((GAIN_ROWS, 128), jnp.float32)
    for slot, count in enumerate((D, D, HEAD_DIM, HEAD_DIM)):
        mask = segment == slot
        spread = jnp.sqrt(total(jnp.where(mask, unit * unit, 0.0)) / count)
        mean = total(jnp.where(mask, old * old, 0.0)) / count
        scale = STEP_RATE * jnp.maximum(SCALE_EPSILON, jnp.sqrt(mean))
        factors = jnp.where(mask, scale / jnp.maximum(1.0, spread / CLIP_LEVEL), factors)
        out = jnp.where(lanes == 4 + slot, spread, out)
    gains_new[...] = old - factors * unit
    spreads[...] = out


def layer_kernel(
    tok, starts, rates, places_at, gain_attn, gain_ffn, gain_heads, gains, grad_out,
    m_qkv, m_out, m_down, m_gate_up, rows, col_moments, gain_moments,
    out_sum, grad_tok, g_qkv, gate_up_came, out_came, down_came, rows_new, row_factors,
    cols_new, col_factors, moments_new, gains_new, grad_gains, spreads,
    gate_up_in, gate_up_mid, kept_tok,
    projected, queries, keys_values, attended, document_tables,
    wq_send, normed, all_tok, all_wq, all_wo, partial, from_partner, came,
    hidden_in, all_norm, all_out, all_wg, wd, hidden, d_gate_up,
    d_queries, d_keys_values, qkv_in, d_hidden_in, gain_part, gain_part2, gain_qk, weight_sums, qkv_came,
    packed, plane_came, plane_sum, line_came, line_sum, line_all, totals, credit, tokens_used, *sems,
):
    half, full = jnp.bfloat16, jnp.float32
    chip, core, z = here()
    others = flips(chip)
    other = 1 - core
    me = 2 * chip + core
    partner = at_place(chip, other, z)
    plane = [at_place(peer_chip, core, z) for peer_chip in others]
    plane_cross = [at_place(peer_chip, other, z) for peer_chip in others]
    steps = (2, 1, 3)
    line = [at_place(chip, core, ahead(z, step)) for step in steps]
    cross = [at_place(chip, other, ahead(z, step)) for step in steps]
    everyone = [partner] + plane + plane_cross
    greet(everyone + line + cross)
    move = Mover(*sems)

    for head in range(8):
        wq_send[head, :, pl.ds(0, 256)] = m_qkv[:, pl.ds(head * 256, 256)].astype(half)
    low = lower_half((64, 128))
    for pair in range(4):
        keys = m_qkv[:, pl.ds(2048 + pair * 128, 128)]
        values = m_qkv[:, pl.ds(2560 + pair * 128, 128)]
        tail = pl.ds(256, 128)
        wq_send[2 * pair, :, tail] = jnp.where(low, keys, pltpu.roll(values, 64, 1)).astype(half)
        wq_send[2 * pair + 1, :, tail] = jnp.where(low, pltpu.roll(keys, 64, 1), values).astype(half)
    heads = [move.keep(wq_send.at[me], all_wq.at[me, z])]
    for peer in everyone:
        heads.append(move.send(wq_send.at[peer[0]], all_wq.at[me, z], peer))

    for row in range(2):

        def body0(part):
            result = tok[row, part].astype(full)
            scale = lax.rsqrt(jnp.mean(result * result, axis=-1, keepdims=True) + EPSILON)
            normed[row, part] = (result * scale * gain_attn[...]).astype(half)

        chunks(64, body0)
    token_copies = [move.send(normed, all_tok.at[me], peer) for peer in plane]
    token_copies.append(move.send(normed, all_tok.at[me], partner))
    tokens_here = move.keep(normed, all_tok.at[me])
    move.arrive(*heads)
    line_wq = move.line(all_wq.at[:, z], lambda at: all_wq.at[:, at], chip, core, z)
    flat_d = d_gate_up.reshape(1024, 2048)
    weight_sums[...] = jnp.zeros_like(weight_sums)
    for row in range(2):
        for document in range(starts.shape[1]):
            angle = starts[row, document].astype(full) * rates[0:1]
            document_tables[row, 2 * document] = jnp.cos(angle)
            document_tables[row, 2 * document + 1] = jnp.sin(angle)

    def cast_all(slot, blocks):
        loads = [move.keep(blocks[0][0], hidden_in.at[0])]
        for index, (_, target) in enumerate(blocks):
            if index + 1 < len(blocks):
                loads.append(move.keep(blocks[index + 1][0], hidden_in.at[(index + 1) % 2]))
            move.arrive(loads[index])

            def body(part, index=index, target=target):
                entries = hidden_in[index % 2, part]
                weight_sums[slot] += jnp.sum((entries * entries).reshape(2, 8, D), axis=0)
                target(part, entries.astype(half))

            chunks(64, body)

    def into(ref):
        def store(part, entries):
            ref[part] = entries

        return store

    def by_device(block):
        cols = pl.ds((block // 4) * 1024 + (block % 4) * 256, 256)

        def store(part, entries):
            for index in range(8):
                place = (index % 4) * 2 + index // 4
                rows_at = wide(place * 64 + part.start, CHUNK)
                flat_d[rows_at, cols] = entries[:, index * 256 : (index + 1) * 256]

        return store

    cast_all(1, [(m_out, into(all_wo.at[z]))])
    cast_all(
        3,
        [
            (m_down.at[pl.ds(64 * block, 64)], into(wd.at[chip, pl.ds(64 * block, 64)]))
            for block in range(4)
        ],
    )
    by_x, by_y = plane[0], plane[1]
    front, back = wd.at[chip, pl.ds(0, 128)], wd.at[chip, pl.ds(128, 128)]
    down_copies = [
        move.send(front, front, by_x), move.send(back, back, by_y),
        move.send(back, back, by_x), move.send(front, front, by_y),
    ]
    move.arrive_line(line_wq, 3)
    move.arrive_line(line_wq, 1)
    cast_all(
        2,
        [(m_gate_up.at[:, pl.ds(2048 * block, 2048)], by_device(block)) for block in range(8)],
    )
    move.arrive_line(line_wq, 2)
    wo_copies = [move.send(all_wo.at[z], all_wo.at[z], peer) for peer in line]

    def turn_block(to_core, to_z, side):
        lanes = pl.ds(side * 1024, 1024)
        src = flat_d.at[wide((to_z * 2 + to_core) * 64, 64), lanes]
        return src, all_wg.at[chip, core, z, :, lanes]

    own = [
        move.keep(grad_out, all_out.at[z, core]),
        move.send(grad_out, all_out.at[z, core], partner),
    ]

    for peer_chip, handle in zip(others, tuple(token_copies)):
        move.arrive(handle)
        block = all_tok.at[2 * peer_chip + core]
        token_copies.append(move.send(block, block, partner))
    move.arrive(tokens_here, *token_copies)
    saved = [move.keep(all_tok, kept_tok)]

    def tables_of(block, row):
        place = lax.broadcasted_iota(jnp.int32, (64, 1), 0) + block * 64
        start_cos, start_sin = document_tables[row, 0], document_tables[row, 1]
        for document in range(1, starts.shape[1]):
            inside = place >= starts[row, document]
            start_cos = jnp.where(inside, document_tables[row, 2 * document], start_cos)
            start_sin = jnp.where(inside, document_tables[row, 2 * document + 1], start_sin)
        at = wide(block * 64, 64)
        place_cos, place_sin = places_at[0, at], places_at[1, at]
        cosine = place_cos * start_cos + place_sin * start_sin
        return cosine, (place_sin * start_cos - place_cos * start_sin) * rates[1:2]

    def first_of(row, part):
        place = lax.broadcasted_iota(jnp.int32, (128, 1), 0) + part * 128
        return document_start(starts, row, place)

    flat_tok, flat_wq = all_tok.reshape(1024, D), all_wq.reshape(D, 384)
    flat_wo = all_wo.reshape(256, D)

    @pl.loop(0, 4)
    def _(step):
        block = plain(flat_tok[wide(step * 256, 256)], flat_wq[...])
        projected[wide(step * 2, 2)] = block.reshape(2, 2, 64, 384)

    @pl.loop(0, 8)
    def _(block):
        for row in range(2):
            cosine, sine = tables_of(block, row)
            places = wide(block * 64, 64)
            for tile in range(3):
                entries = projected[block, row, :, pl.ds(tile * 128, 128)]
                gain = gain_heads[min(tile, 2) // 2 : min(tile, 2) // 2 + 1]
                scale = lax.rsqrt(head_means(entries * entries) + EPSILON)
                turned_entries = entries * scale * gain
                turned_entries = turned_entries * cosine + swap_halves(turned_entries) * sine
                if tile < 2:
                    queries[row, tile, places] = (turned_entries * HEAD_DIM ** (-0.5)).astype(half)
                else:
                    zero = jnp.zeros_like(entries)
                    rolled = pltpu.roll(turned_entries, 64, 1)
                    values = pltpu.roll(entries, 64, 1)
                    keys_values[row, 0, places] = jnp.where(low, turned_entries, zero).astype(half)
                    keys_values[row, 1, places] = jnp.where(low, zero, rolled).astype(half)
                    keys_values[row, 2, places] = jnp.where(low, values, zero).astype(half)
                    keys_values[row, 3, places] = jnp.where(low, zero, entries).astype(half)

    turned, turned_own = ([], []), []
    for side in range(2):
        for step, peer, peer_cross in zip(steps, line, cross):
            to = ahead(z, step)
            turned[side].append(move.send(*turn_block(core, to, side), peer))
            turned[side].append(move.send(*turn_block(other, to, side), peer_cross))
        turned[side].append(move.send(*turn_block(other, z, side), partner))
        turned_own.append(move.keep(*turn_block(core, z, side)))
    line_grads = move.line(grad_out, lambda at: all_out.at[at, core], chip, core, z)
    move.arrive(*down_copies[:2])
    front, back = wd.at[others[0], pl.ds(0, 128)], wd.at[others[1], pl.ds(128, 128)]
    down_copies += [move.send(front, front, by_y), move.send(back, back, by_x)]

    @pl.loop(0, 2)
    def _(row):
        for tile in range(2):
            for part in range(4):
                own_places, upto = pl.ds(part * 128, 128), pl.ds(0, (part + 1) * 128)
                result = jnp.zeros((128, 128), full)
                for side in range(2):
                    probs = attention_probs(
                        queries[row, tile, own_places], keys_values[row, side, upto],
                        first_of(row, part), part,
                    )
                    result += plain(probs.astype(half), keys_values[row, 2 + side, upto])
                attended[pl.ds(2 * part, 2), row, :, pl.ds(tile * 128, 128)] = result.reshape(2, 64, 128)

    flat_attended = attended.reshape(1024, 256)
    move.arrive(*wo_copies)

    @pl.loop(0, 4)
    def _(step):
        rows = flat_attended[wide(step * 256, 256)].astype(half)

        @pl.loop(0, 4)
        def _(col):
            cols = wide(col * 512, 512)
            block = plain(rows, flat_wo[:, cols])
            partial[wide(step * 2, 2), :, :, cols] = block.reshape(2, 2, 64, 512).astype(half)

    move.arrive(*saved)
    move.sent(*token_copies)
    order = tuple(others) + (chip,)
    halves = [move.send(partial.at[2 * to + other], from_partner.at[to], partner) for to in order]
    sums = []
    for to, arrived, peer in zip(others, halves, plane):
        move.arrive(arrived)
        add_blocks(partial.at[2 * to + core], from_partner.at[to], from_partner.at[to])
        sums.append(move.send(from_partner.at[to], came.at[chip], peer))
    def gather_weights(side):
        move.arrive(turned_own[side], *turned[side])
        lanes = pl.ds(side * 1024, 1024)
        front, back = all_wg.at[chip, 0, :, :, lanes], all_wg.at[chip, 1, :, :, lanes]
        return [
            move.send(front, front, by_x), move.send(back, back, by_y),
            move.send(back, back, by_x), move.send(front, front, by_y),
        ]

    def pass_weights(side, copies):
        move.arrive(*copies[:2])
        lanes = pl.ds(side * 1024, 1024)
        front, back = all_wg.at[others[0], 0, :, :, lanes], all_wg.at[others[1], 1, :, :, lanes]
        return [move.send(front, front, by_y), move.send(back, back, by_x)]

    gate_copies = gather_weights(0)
    move.sent(*token_copies)
    move.arrive(halves[3], *sums)
    for row in range(2):

        def body(part):
            result = tok[row, part].astype(full)
            result += partial[me, row, part].astype(full)
            result += from_partner[chip, row, part].astype(full)
            for peer_chip in others:
                result += came[peer_chip, row, part].astype(full)
            hidden_in[row, part] = result
            scale = lax.rsqrt(jnp.mean(result * result, axis=-1, keepdims=True) + EPSILON)
            normed[row, part] = (result * scale * gain_ffn[...]).astype(half)

        chunks(64, body)
    move.sent(*sums, *halves)
    move.arrive(*saved)
    line_norms = move.line(normed, lambda at: all_norm.at[at, core], chip, core, z)
    own.append(move.send(normed, all_norm.at[z, core], partner))
    own.append(move.keep(normed, all_norm.at[z, core]))

    up_copies = gather_weights(1)
    at_first, at_last = lax.div(3 - z, 3), lax.div(z, 3)
    arrivals = (3 - 2 * at_first, 1 + at_first + at_last, 2 + at_first - at_last)
    inner = (z > 0) & (z < 3)
    shared = []

    def share(step, wait_only=False):
        for line_of in (line_grads, line_norms):
            if wait_only:
                block = move.wait_line(line_of, step, jnp.logical_not(inner))
            else:
                block = move.arrive_line(line_of, step)
            shared.append(move.send(block, block, partner))

    flat_wg, flat_wd = all_wg.reshape(D, 2048), wd.reshape(1024, D)

    def d_hidden_of(zb):
        @pl.loop(0, 4)
        def _(step):
            cols = wide(step * 256, 256)
            hidden[zb, :, cols] = across(all_out[zb].reshape(256, D), flat_wd[cols]).astype(half)

    share(arrivals[0])
    gate_copies += pass_weights(0, gate_copies)
    move.arrive(*own[:2], *down_copies)
    d_hidden_of(z)
    share(arrivals[1])
    up_copies += pass_weights(1, up_copies)
    move.arrive(shared[0])
    d_hidden_of(ahead(z, arrivals[0]))
    for line_of in (line_grads, line_norms):
        move.arrive_line(line_of, arrivals[2], inner)
    move.arrive(shared[2])
    d_hidden_of(ahead(z, arrivals[1]))
    weights = gate_copies + up_copies
    move.arrive(*weights, *own)
    move.sent(*turned[0], *turned[1])

    def block_of(zb):
        @pl.loop(0, 4)
        def _(step):
            cols, ups = wide(step * 256, 256), wide(1024 + step * 256, 256)
            rows = all_norm[zb].reshape(256, D)
            gate = plain(rows, flat_wg[:, cols])
            up = plain(rows, flat_wg[:, ups])
            d_hidden = hidden[zb, :, cols].astype(full)
            sigmoid = 1.0 / (1.0 + jnp.exp(-gate))
            silu = gate * sigmoid
            hidden[zb, :, cols] = (silu * up).astype(half)
            d_gate = d_hidden * up * (sigmoid * (1.0 + gate * (1.0 - sigmoid)))
            d_gate_up[zb, :, cols] = d_gate.astype(half)
            d_gate_up[zb, :, ups] = (d_hidden * silu).astype(half)

        @pl.loop(0, 8)
        def _(step):
            cols = wide(step * 256, 256)
            block = across(d_gate_up[zb], flat_wg[cols])
            partial[pl.ds(2 * zb, 2), :, :, cols] = block.reshape(2, 2, 64, 256).astype(half)

    def pair_sum(zb, handle, into, base):
        move.arrive(handle)
        add_blocks(partial.at[2 * zb + core], into.at[base + zb], into.at[base + zb])

    start_sum, wait_sums = move.scatter(
        lambda at: from_partner.at[at], lambda at: came.at[at], arrivals, chip, core, z
    )
    to_partner = []
    walk = [z] + [ahead(z, step) for step in arrivals]
    for index, zb in enumerate(walk):
        if index > 0:
            move.arrive(*shared[2 * index - 2 : 2 * index])
        if index == 3:
            d_hidden_of(zb)
        block_of(zb)
        to_partner.append(move.send(partial.at[2 * zb + other], from_partner.at[zb], partner))
        if index == 0:
            share(arrivals[2], True)
        if index > 0:
            pair_sum(walk[index - 1], to_partner[index - 1], from_partner, 0)
        if index > 1:
            start_sum(index - 2)
    pair_sum(walk[3], to_partner[3], from_partner, 0)
    start_sum(2)

    flat_norm, flat_grads = all_norm.reshape(1024, D), all_out.reshape(1024, D)
    flat_hidden = hidden.reshape(1024, 1024)
    move.sent(*weights)

    def gate_up_grad(to, side):
        rows, lanes = wide(to * 512, 512), pl.ds(side * 1024, 1024)

        @pl.loop(0, 2)
        def _(step):
            cols = wide(side * 1024 + step * 512, 512)
            flat_wg[rows, cols] = down(flat_norm[:, rows], flat_d[:, cols]).astype(half)

        return flat_wg.at[rows, lanes]

    passed = []
    for side in (0, 1):
        passed.append(move.send(gate_up_grad(others[2], side), gate_up_mid.at[side], plane[side]))
    move.sent(*shared, own[2])
    move.sent_lines()
    wait_sums()
    gain_part[...] = jnp.zeros_like(gain_part)
    for row in range(2):

        def body2(part):
            result = from_partner[z, row, part].astype(full)
            for step in steps:
                result += came[ahead(z, step), row, part].astype(full)
            entries = hidden_in[row, part]
            scale = lax.rsqrt(jnp.mean(entries * entries, axis=-1, keepdims=True) + EPSILON)
            gain_part[...] += jnp.sum(result * entries * scale, axis=0, keepdims=True)
            result = result * gain_ffn[...]
            inside = jnp.mean(result * entries, axis=-1, keepdims=True) * (scale * scale * scale)
            grad = grad_out[row, part].astype(full) + result * scale - entries * inside
            d_hidden_in[row, part] = grad
            normed[row, part] = grad.astype(half)

        chunks(64, body2)
    move.sent_sums()
    all_branch = all_tok
    branches = [move.send(normed, all_branch.at[me], peer) for peer in plane]
    branch_copies = [
        move.send(normed, all_branch.at[me], partner), move.keep(normed, all_branch.at[me])
    ]

    direct = [gate_up_grad(others[side], side) for side in (0, 1)]
    handed = [gate_up_grad(others[1 - side], side) for side in (0, 1)]
    for side in (0, 1):
        gate_up_grad(chip, side)
    for peer in [partner] + line:
        pl.semaphore_signal(credit, inc=1, device_id=peer, device_id_type=MESH)

    move.sent(*to_partner)
    to_partner, sums = [], []
    out_sums = all_norm.reshape(8, 2, 64, D)
    pl.semaphore_wait(credit, 4)
    walk = [ahead(z, step) for step in steps] + [z]
    for index, zb in enumerate(walk):

        @pl.loop(0, 4)
        def _(step, zb=zb):
            cols = wide(step * 512, 512)
            block = plain(hidden[zb], flat_wd[:, cols])
            partial[pl.ds(2 * zb, 2), :, :, cols] = block.reshape(2, 2, 64, 512).astype(half)

        to_partner.append(move.send(partial.at[2 * zb + other], out_sums.at[zb], partner))
        if index > 0:
            before = walk[index - 1]
            pair_sum(before, to_partner[index - 1], out_sums, 0)
            sums.append(move.send(out_sums.at[before], out_sums.at[4 + z], line[index - 1]))
    pair_sum(z, to_partner[3], out_sums, 0)

    move.sent(*down_copies, *wo_copies)

    @pl.loop(0, 4)
    def _(to):
        rows_at = wide(to * 256, 256)

        @pl.loop(0, 4)
        def _(step):
            cols = wide(step * 512, 512)
            flat_wd[rows_at, cols] = down(flat_hidden[:, rows_at], flat_grads[:, cols]).astype(half)

    load_tok = move.keep(kept_tok, all_out.reshape(8, 2, 64, D))

    def load(source):
        return [
            move.keep(source(side), flat_d.at[pl.ds(side * 512, 512), pl.ds(0, 1024)])
            for side in (0, 1)
        ]

    def add_loaded(side, chunk):
        @pl.loop(0, 512 // CHUNK)
        def _(step):
            lanes = pl.ds(side * 1024, 1024)
            rows = wide(chunk * 512 + step * CHUNK, CHUNK)
            extra = flat_d[wide(side * 512 + step * CHUNK, CHUNK), pl.ds(0, 1024)]
            result = flat_wg[rows, lanes].astype(full) + extra.astype(full)
            flat_wg[rows, lanes] = result.astype(half)

    move.arrive(*branches)
    pieces = [
        move.send(direct[side], gate_up_in.at[side, 0], plane[side]) for side in (0, 1)
    ]
    for peer_chip in others:
        block = all_branch.at[2 * peer_chip + core]
        branch_copies.append(move.send(block, block, partner))
    move.arrive(*passed)
    loads = load(lambda side: gate_up_mid.at[side])
    later = []
    for side in (0, 1):
        move.arrive(loads[side])
        add_loaded(side, others[1 - side])
        later.append(move.send(handed[side], gate_up_in.at[side, 1], plane[1 - side]))
    move.arrive(*branch_copies)

    flat_branch = all_branch.reshape(1024, D)
    flat_wo = all_wo.reshape(256, D)
    d_heads_at, d_projected_at = pl.ds(0, 256), pl.ds(256, 384)

    @pl.loop(0, 4)
    def _(step):
        rows = wide(step * 256, 256)
        flat_hidden[rows, d_heads_at] = across(flat_branch[rows], flat_wo[...]).astype(half)

    @pl.loop(0, 4)
    def _(step):
        cols = wide(step * 512, 512)
        block = down(flat_attended[...].astype(half), flat_branch[:, cols])
        flat_wo[:, cols] = block.astype(half)

    outs = [
        move.send(all_wo.at[ahead(z, step)], out_came.at[z], peer) for step, peer in zip(steps, line)
    ]
    outs.append(move.keep(all_wo.at[z], out_came.at[z]))
    lower = lower_half((128, 128))
    line_low = lower_half((1, 128))
    gain_qk[...] = jnp.zeros_like(gain_qk)

    @pl.loop(0, 2)
    def _(row):
        d_keys_values[...] = jnp.zeros_like(d_keys_values)

        def token_rows(block):
            return wide((2 * block + row) * 64, 64)

        for tile in range(2):
            lanes = pl.ds(tile * 128, 128)
            for part in range(4):
                own_places, upto = pl.ds(part * 128, 128), pl.ds(0, (part + 1) * 128)
                d_heads = jnp.concatenate(
                    [flat_hidden[token_rows(2 * part + index), lanes] for index in range(2)], axis=0
                )
                products = d_heads.astype(full) * attended[pl.ds(2 * part, 2), row, :, lanes].reshape(128, 128)
                query = queries[row, tile, own_places]
                result = jnp.zeros((128, 128), full)
                for side in range(2):
                    mask = lower if side == 0 else jnp.logical_not(lower)
                    delta = jnp.sum(jnp.where(mask, products, 0.0), axis=-1, keepdims=True)
                    keys = keys_values[row, side, upto]
                    probs = attention_probs(query, keys, first_of(row, part), part)
                    d_probs = across(d_heads, keys_values[row, 2 + side, upto])
                    d_scores = (probs * (d_probs - delta)).astype(half)
                    result += plain(d_scores, keys)
                    d_keys_values[side, upto] += down(d_scores, query)
                    d_keys_values[2 + side, upto] += down(probs.astype(half), d_heads)
                d_queries[tile, own_places] = result

        @pl.loop(0, 8)
        def _(block):
            cosine, sine = tables_of(block, row)
            places = wide(block * 64, 64)
            for tile in range(3):
                entries = projected[block, row, :, pl.ds(tile * 128, 128)]
                gain = gain_heads[tile // 2 : tile // 2 + 1]
                scale = lax.rsqrt(head_means(entries * entries) + EPSILON)
                if tile < 2:
                    grad = d_queries[tile, places] * HEAD_DIM ** (-0.5)
                else:
                    from_low, from_high = d_keys_values[0, places], d_keys_values[1, places]
                    grad = jnp.where(low, from_low + pltpu.roll(from_high, 64, 1), 0.0)
                grad = grad * cosine + swap_halves(grad * sine)
                for_gain = jnp.sum(grad * entries * scale, axis=0, keepdims=True)
                if tile < 2:
                    for_gain = jnp.where(line_low, for_gain + pltpu.roll(for_gain, 64, 1), 0.0)
                else:
                    for_gain = jnp.where(line_low, 0.0, pltpu.roll(for_gain, 64, 1))
                gain_qk[...] += for_gain
                grad = grad * gain
                inside = head_means(grad * entries) * (scale * scale * scale)
                grad = grad * scale - entries * inside
                if tile == 2:
                    values = pltpu.roll(d_keys_values[2, places], 64, 1)
                    grad = jnp.where(low, grad, values + d_keys_values[3, places])
                flat_hidden[token_rows(block), pl.ds(256 + tile * 128, 128)] = grad.astype(half)

    move.arrive(load_tok)

    for block in range(4):
        strip = pl.ds(1024 + 384 * (block // 2), 384)
        product = down(
            flat_grads[:, pl.ds(block * 512, 512)], flat_hidden[:, d_projected_at]
        )
        flat_d[pl.ds(512 * (block % 2), 512), strip] = product.astype(half)

    for peer in [partner] + line + cross:
        pl.semaphore_signal(tokens_used, inc=1, device_id=peer, device_id_type=MESH)

    def head_block(head, at):
        rows = wide(((head % 4) * 4 + at) * 64, 64)
        return flat_d.at[rows, pl.ds(1024 + 384 * (head // 4), 384)]

    qkv_pieces = []
    for step, peer in zip(steps, line):
        pairs = [(head_block(head, ahead(z, step)), qkv_in.at[z, head]) for head in range(8)]
        qkv_pieces.append(move.send_parts(pairs, (qkv_in.at[z], qkv_in.at[z]), peer))
    move.sent(*to_partner)

    @pl.loop(0, 4)
    def _(step):
        rows = flat_hidden[wide(step * 256, 256), d_projected_at]

        @pl.loop(0, 4)
        def _(col):
            cols = wide(col * 512, 512)
            block = across(rows, flat_wq[cols])
            partial[wide(step * 2, 2), :, :, cols] = block.reshape(2, 2, 64, 512).astype(half)

    halves = [move.send(partial.at[2 * to + other], from_partner.at[to], partner) for to in order]
    d_norms = []
    for to, arrived, peer in zip(others, halves, plane):
        move.arrive(arrived)
        add_blocks(partial.at[2 * to + core], from_partner.at[to], from_partner.at[to])
        d_norms.append(move.send(from_partner.at[to], came.at[chip], peer))
    downs = [move.send(wd.at[to], down_came.at[chip], peer) for to, peer in zip(others, plane)]
    downs.append(move.keep(wd.at[chip], down_came.at[chip]))
    move.arrive(halves[3])
    add_blocks(partial.at[me], from_partner.at[chip], from_partner.at[chip])

    for slot, handles in ((0, pieces), (1, later)):
        move.arrive(*handles)
        loads = load(lambda side, slot=slot: gate_up_in.at[side, slot])
        for side in (0, 1):
            move.arrive(loads[side])
            add_loaded(side, chip)

    blocks = all_out.reshape(16, 64, D)

    def back_block(to_core, to_z):
        return all_wg.at[chip, to_core, to_z], blocks.at[8 + 2 * z + core]

    pl.semaphore_wait(tokens_used, 7)
    gate_ups = []
    for step, peer, peer_cross in zip(steps, line, cross):
        to = ahead(z, step)
        gate_ups.append(move.send(*back_block(core, to), peer))
        gate_ups.append(move.send(*back_block(other, to), peer_cross))
    gate_ups.append(move.send(*back_block(other, z), partner))
    gate_ups.append(move.keep(*back_block(core, z)))

    move.arrive(*sums)
    for row in range(2):

        def body3(part):
            result = hidden_in[row, part] + out_sums[z, row, part].astype(full)
            for step in steps:
                result += out_sums[4 + ahead(z, step), row, part].astype(full)
            out_sum[row, part] = result.astype(half)

        chunks(64, body3)

    move.arrive(*d_norms)
    gain_part2[...] = jnp.zeros_like(gain_part2)
    for row in range(2):

        def body4(part):
            result = from_partner[chip, row, part].astype(full)
            for peer_chip in others:
                result += came[peer_chip, row, part].astype(full)
            entries = tok[row, part].astype(full)
            scale = lax.rsqrt(jnp.mean(entries * entries, axis=-1, keepdims=True) + EPSILON)
            gain_part2[...] += jnp.sum(result * entries * scale, axis=0, keepdims=True)
            result = result * gain_attn[...]
            inside = jnp.mean(result * entries, axis=-1, keepdims=True) * (scale * scale * scale)
            result = d_hidden_in[row, part] + result * scale - entries * inside
            grad_tok[row, part] = result.astype(half)

        chunks(64, body4)

    def send_heads():
        move.arrive(*qkv_pieces)
        move.sent(*heads[1:])
        for head in range(8):
            result = head_block(head, z)[...].astype(full)
            for step in steps:
                result += qkv_in[ahead(z, step), head].astype(full)
            wq_send[head] = result.astype(half)
        copies = [move.send(wq_send.at[peer[0]], qkv_came.at[me], peer) for peer in everyone]
        return copies + [move.keep(wq_send.at[me], qkv_came.at[me])]

    flat_packed = packed.reshape(512, 128)
    first = 2 * COL_ROWS
    line_lanes = lax.broadcasted_iota(jnp.int32, (1, 128), 1)
    flat_packed[pl.ds(first + 33, 512 - first - 33)] = jnp.zeros((512 - first - 33, 128), full)

    def statistics(slot, read):
        count, width, row_at, col_at = MATRICES[slot]
        own_rows, some = pl.ds(row_at, count), pl.ds(0, count)
        d_queries[0, some] = jnp.zeros((count, 128), full)

        @pl.loop(0, width // 128)
        def _(step):
            entries = read(step)
            d_queries[0, some] += entries * entries

        mean = jnp.sum(d_queries[0, some], axis=-1, keepdims=True) / width + SQUARE_EPSILON
        new = BETA * rows[own_rows] + (1.0 - BETA) * mean
        rows_new[own_rows] = new
        row_factors[own_rows] = lax.rsqrt(new)
        d_keys_values[0, some] = jnp.broadcast_to(1.0 / new, (count, 128))

        @pl.loop(0, width // 128)
        def _(step):
            entries = read(step)
            square = entries * entries
            flat_packed[pl.ds(col_at + step, 1)] = (
                jnp.sum(square, axis=0, keepdims=True) + count * SQUARE_EPSILON
            )
            flat_packed[pl.ds(COL_ROWS + col_at + step, 1)] = jnp.sum(
                square * d_keys_values[0, some], axis=0, keepdims=True
            )

        stats = flat_packed[pl.ds(first + 33, 1)]
        stats = jnp.where(line_lanes == slot, jnp.sum(new, axis=0, keepdims=True), stats)
        stats = jnp.where(line_lanes == 4 + slot, total(weight_sums[slot]), stats)
        flat_packed[pl.ds(first + 33, 1)] = stats

    def lanes_of(step):
        return wide(step * 128, 128)

    def four(buffer):
        def read(step):
            result = buffer[0, :, lanes_of(step)].astype(full)
            for slot in range(1, 4):
                result += buffer[slot, :, lanes_of(step)].astype(full)
            return result

        return read

    out_here, down_here = blocks, all_norm.reshape(4, 256, D)
    move.arrive(*outs)
    out_load = move.keep(out_came, out_here.at[pl.ds(0, 4)])
    qkv_copies = send_heads()
    move.arrive(*downs)
    move.sent(*sums)
    down_load = move.keep(down_came, down_here)
    move.arrive(out_load)
    statistics(1, four(out_here))
    move.arrive(down_load)
    statistics(3, four(down_here))

    move.arrive(*qkv_copies)
    for head in range(8):
        for part in range(2):
            strip = qkv_came[head, :, pl.ds(part * 128, 128)]
            g_qkv[:, pl.ds(head * 256 + part * 128, 128)] = strip.astype(full)
    for pair in range(4):
        keys = qkv_came[2 * pair, :, pl.ds(256, 128)].astype(full)
        values = qkv_came[2 * pair + 1, :, pl.ds(256, 128)].astype(full)
        g_qkv[:, pl.ds(2048 + pair * 128, 128)] = jnp.where(low, keys, pltpu.roll(values, 64, 1))
        g_qkv[:, pl.ds(2560 + pair * 128, 128)] = jnp.where(low, pltpu.roll(keys, 64, 1), values)

    @pl.loop(0, QKV // 128)
    def _(step):
        entries = m_qkv[:, lanes_of(step)]
        weight_sums[0, :, pl.ds(0, 128)] += jnp.sum((entries * entries).reshape(8, 8, 128), axis=0)

    statistics(0, lambda step: g_qkv[:, lanes_of(step)])
    for slot in range(16):
        strip = pl.ds(slot * 128, 128)
        flat_packed[pl.ds(first + slot, 1)] = gain_part2[:, strip]
        flat_packed[pl.ds(first + 16 + slot, 1)] = gain_part[:, strip]
    flat_packed[pl.ds(first + 32, 1)] = gain_qk[...]

    move.arrive(*gate_ups)
    move.sent(*qkv_pieces)

    def read_gate_up(step):
        inside = lax.rem(step, 64)
        owner = lax.div(inside, 2)
        block = 2 * lax.rem(owner, 4) + lax.rem(lax.div(owner, 4), 2)
        begin = lax.div(step, 64) * 1024 + lax.div(owner, 8) * 256 + lax.rem(inside, 2) * 128
        strip = blocks[8 + block, :, wide(begin, 128)]
        flat_d[wide(lax.div(step, 16) * 64, 64), lanes_of(lax.rem(step, 16))] = strip
        return strip.astype(full)

    statistics(2, read_gate_up)
    for block in range(8):
        move.keep(flat_d.at[pl.ds(64 * block, 64)], gate_up_came.at[:, pl.ds(2048 * block, 2048)])

    copies = [move.send(packed.at[peer[0]], plane_came.at[me], peer) for peer in everyone]
    plane_came[me] = packed[me]
    move.arrive(*copies)
    result = plane_came[0]
    for slot in range(1, 8):
        result = result + plane_came[slot]
    plane_sum[...] = result
    copies = [move.send(plane_sum.at[peer[1]], line_came.at[z], peer) for peer in line]
    line_came[z] = plane_sum[z]
    move.arrive(*copies)
    line_sum[...] = line_came[0] + line_came[1] + line_came[2] + line_came[3]
    copies = [move.send(line_sum, line_all.at[z], peer) for peer in line]
    line_all[z] = line_sum[...]
    move.arrive(*copies)
    copies = [move.send(line_all, totals.at[me], peer) for peer in everyone]
    totals[me] = line_all[...]
    move.arrive(*copies)
    derive_updates(
        totals.reshape(512, 128), col_moments, gain_moments, gains,
        cols_new, col_factors, moments_new, gains_new, grad_gains, spreads,
    )
    move.finish()


def split_local(
    tokens, doc_starts, grad_out, qkv_master, out_master, gate_up_master, down_master, gains,
    qkv_rows, out_rows, gate_up_rows, down_rows, col_moments, gain_moments,
):
    half, full = jnp.bfloat16, jnp.float32
    gain_query, gain_key = gains[2 * D : 2 * D + HEAD_DIM], gains[2 * D + HEAD_DIM :]
    gain_heads = jnp.stack(
        [jnp.concatenate([gain_query, gain_query]), jnp.concatenate([gain_key, gain_key])]
    )
    lane = np.arange(128)
    rates = ROPE_BASE ** (-(lane % 32) * 2.0 / HEAD_DIM)
    rates = jnp.asarray(np.stack([rates, np.where(lane % 64 < 32, -1.0, 1.0)]), full)

    def near(*shape, kind=half):
        return pltpu.VMEM(shape, kind)

    masters = (qkv_master, out_master, gate_up_master, down_master)
    stats_shape = (8, 4, 16, 128)
    (
        output, grad_tokens, grad_qkv, gate_up_came, out_came, down_came, rows_new, row_factors,
        cols_new, col_factors, moments_new, gains_new, grad_gains, spreads, *_,
    ) = exchange(
        layer_kernel, 0,
        [
            (tokens, True), (doc_starts, None), (rates, True), (jnp.asarray(place_tables(512)), True),
            (gains[None, :D], True),
            (gains[None, D : 2 * D], True), (gain_heads, True), (gains.reshape(-1, 128), True),
            (grad_out, True), (qkv_master, True), (out_master, False), (down_master, False),
            (gate_up_master, False),
            (jnp.concatenate([qkv_rows, out_rows, gate_up_rows, down_rows])[:, None], True),
            (col_moments.reshape(-1, 128), True), (gain_moments.reshape(-1, 128), True),
        ],
        [
            ((2, 64, D), half, True), ((2, 64, D), half, True), ((64, QKV), full, True),
            ((64, 2 * FF), half, False), ((4, 64, D), half, False), ((4, 256, D), half, False),
            ((448, 1), full, True), ((448, 1), full, True),
            ((COL_ROWS, 128), full, True), ((1, COLS), full, True),
            ((GAIN_ROWS, 128), full, True), ((GAIN_ROWS, 128), full, True),
            ((GAIN_ROWS, 128), full, True), ((1, 128), full, True),
            ((2, 2, 512, 1024), half, False), ((2, 512, 1024), half, False),
            ((8, 2, 64, D), half, False),
        ],
        [
            near(8, 2, 64, 384, kind=full), near(2, 2, 512, 128), near(2, 4, 512, 128),
            near(8, 2, 64, 256, kind=full), near(2, 8, 1, 128, kind=full),
            near(8, 64, 384), near(2, 64, D), near(8, 2, 64, D), near(8, 4, 64, 384), near(4, 64, D),
            near(8, 2, 64, D), near(4, 2, 64, D), near(4, 2, 64, D), near(2, 64, D, kind=full),
            near(4, 2, 2, 64, D), near(4, 2, 2, 64, D), near(4, 2, 4, 64, 2048), near(4, 256, D),
            near(4, 256, 1024), near(4, 256, 2048),
            near(2, 512, 128, kind=full), near(4, 512, 128, kind=full), near(4, 8, 64, 384),
            near(2, 64, D, kind=full), near(1, D, kind=full), near(1, D, kind=full),
            near(1, 128, kind=full), near(4, 8, D, kind=full), near(8, 64, 384),
            near(*stats_shape, kind=full), near(*stats_shape, kind=full),
            near(*stats_shape[1:], kind=full), near(*stats_shape[1:], kind=full),
            near(*stats_shape[2:], kind=full), near(*stats_shape[1:], kind=full),
            near(*stats_shape, kind=full),
            pltpu.SemaphoreType.REGULAR, pltpu.SemaphoreType.REGULAR,
        ],
        (176, 56), 170 << 20, 48 << 30,
    )
    grads = (
        grad_qkv, jnp.sum(out_came.astype(full), axis=0), gate_up_came.astype(full),
        jnp.sum(down_came.astype(full), axis=0),
    )
    new_masters = []
    for slot, (count, width, row_at, col_at) in enumerate(MATRICES):
        row_factor = row_factors[row_at : row_at + count]
        col_factor = col_factors[:, col_at * 128 : col_at * 128 + width]
        new_masters.append(masters[slot] - grads[slot] * row_factor * col_factor)
    return (
        output,
        grad_tokens,
        *grads,
        grad_gains.reshape(-1),
        *[rows_new[row_at : row_at + count, 0] for count, _, row_at, _ in MATRICES],
        cols_new.reshape(-1),
        moments_new.reshape(-1),
        *new_masters,
        *[master.astype(half) for master in new_masters],
        gains_new.reshape(-1),
        spreads[0, :8],
    )


def optimizer_step(
    grads, gain_local, masters, gains, row_states, col_moments, gain_moments, total_fn
):
    beta = 1.0 - STEP ** (-0.8)
    col_widths = (QKV, D, 2 * FF, D)
    row_totals = (D, HEADS * HEAD_DIM, D, FF)
    squares = [gradient * gradient + SQUARE_EPSILON for gradient in grads]
    rows_new = [
        beta * row_state + (1.0 - beta) * jnp.mean(square, axis=1)
        for row_state, square in zip(row_states, squares)
    ]
    col_local = [jnp.sum(square, axis=0) for square in squares]
    weighted_local = [
        jnp.sum(gradient * gradient / row_new[:, None], axis=0)
        for gradient, row_new in zip(grads, rows_new)
    ]
    stats_local = jnp.stack(
        [jnp.sum(row_new) for row_new in rows_new]
        + [jnp.sum(master * master) for master in masters]
    )
    totals = total_fn(jnp.concatenate(col_local + weighted_local + [stats_local, gain_local]))
    cols = sum(col_widths)
    col_sums, weighted = totals[:cols], totals[cols : 2 * cols]
    stats, grad_gains = totals[2 * cols : 2 * cols + 8], totals[2 * cols + 8 :]
    col_divisor = jnp.concatenate(
        [
            jnp.full((col_width,), float(row_total), jnp.float32)
            for col_width, row_total in zip(col_widths, row_totals)
        ]
    )
    cols_new = beta * col_moments + (1.0 - beta) * col_sums / col_divisor
    new_masters = []
    spreads = []
    begin_at = 0
    for slot in range(4):
        col_part = cols_new[begin_at : begin_at + col_widths[slot]]
        weighted_part = weighted[begin_at : begin_at + col_widths[slot]]
        begin_at = begin_at + col_widths[slot]
        mean_rows = stats[slot] / row_totals[slot]
        unit = (
            grads[slot]
            * lax.rsqrt(rows_new[slot] / mean_rows)[:, None]
            * lax.rsqrt(col_part)[None, :]
        )
        entries_all = float(row_totals[slot] * col_widths[slot])
        spread = jnp.sqrt(mean_rows * jnp.sum(weighted_part / col_part) / entries_all)
        scale = STEP_RATE * jnp.maximum(SCALE_EPSILON, jnp.sqrt(stats[4 + slot] / entries_all))
        new_masters.append(masters[slot] - scale * unit / jnp.maximum(1.0, spread / CLIP_LEVEL))
        spreads.append(spread)
    bounds = (0, D, 2 * D, 2 * D + HEAD_DIM, 2 * D + 2 * HEAD_DIM)
    moment_parts, gain_parts = ([], [])
    for segment in range(4):
        gradient = grad_gains[bounds[segment] : bounds[segment + 1]]
        gain_old = gains[bounds[segment] : bounds[segment + 1]]
        moment_new = beta * gain_moments[bounds[segment] : bounds[segment + 1]] + (1.0 - beta) * (
            gradient * gradient + SQUARE_EPSILON
        )
        unit = gradient * lax.rsqrt(moment_new)
        spread = jnp.sqrt(jnp.mean(unit * unit))
        scale = STEP_RATE * jnp.maximum(SCALE_EPSILON, jnp.sqrt(jnp.mean(gain_old * gain_old)))
        moment_parts.append(moment_new)
        gain_parts.append(gain_old - scale * unit / jnp.maximum(1.0, spread / CLIP_LEVEL))
        spreads.append(spread)
    return (
        grad_gains,
        *rows_new,
        cols_new,
        jnp.concatenate(moment_parts),
        *new_masters,
        *[master.astype(jnp.bfloat16) for master in new_masters],
        jnp.concatenate(gain_parts),
        jnp.stack(spreads),
    )


def solution(mesh):
    split = mesh.shape["seq"] == 8 and mesh.shape["rows"] == 4
    return jax.shard_map(
        split_local if split else gathered_local,
        mesh=mesh,
        in_specs=(
            P("rows", "seq", None),
            P("rows", None),
            P("rows", "seq", None),
            P(("seq", "rows"), None),
            P(("seq", "rows"), None),
            P(("seq", "rows"), None),
            P(("seq", "rows"), None),
            P(),
            P(("seq", "rows")),
            P(("seq", "rows")),
            P(("seq", "rows")),
            P(("seq", "rows")),
            P(),
            P(),
        ),
        out_specs=(
            P("rows", "seq", None),
            P("rows", "seq", None),
            P(("seq", "rows"), None),
            P(("seq", "rows"), None),
            P(("seq", "rows"), None),
            P(("seq", "rows"), None),
            P(),
            P(("seq", "rows")),
            P(("seq", "rows")),
            P(("seq", "rows")),
            P(("seq", "rows")),
            P(),
            P(),
            P(("seq", "rows"), None),
            P(("seq", "rows"), None),
            P(("seq", "rows"), None),
            P(("seq", "rows"), None),
            P(("seq", "rows"), None),
            P(("seq", "rows"), None),
            P(("seq", "rows"), None),
            P(("seq", "rows"), None),
            P(),
            P(),
        ),
        check_vma=False,
    )
```

```python
from functools import partial

import jax
import jax.numpy as jnp
import numpy as np
from jax import lax
from jax.experimental import pallas as pl
from jax.experimental.pallas import tpu as pltpu
from jax.sharding import PartitionSpec as P

D = 2048
HEADS = 32
KV_HEADS = 8
HEAD_DIM = 64
FF = 8192
STEP = 10
QKV = 3072


EPSILON = 1e-06
ROPE_BASE = 10000.0
MASKED_SCORE = -1e30
STEP_RATE = 0.3
CLIP_LEVEL = 1.0
SQUARE_EPSILON = 1e-30
SCALE_EPSILON = 0.001


def from_behind(value, axis, steps):
    count = lax.axis_size(axis)
    pairs = [(source, (source + steps) % count) for source in range(count)]
    return lax.ppermute(value, axis, pairs)


def norm_rows(entries, gain):
    return entries * lax.rsqrt(jnp.mean(entries * entries, axis=-1, keepdims=True) + EPSILON) * gain


def turn(entries, cos_wide, sin_wide):
    half_width = entries.shape[-1] // 2
    turned = jnp.concatenate([-entries[..., half_width:], entries[..., :half_width]], axis=-1)
    return entries * cos_wide + turned * sin_wide


def doc_tables(doc_starts, places):
    before = doc_starts[:, None, :] <= places[None, :, None]
    doc_ids = jnp.sum(before.astype(jnp.int32), axis=-1)
    doc_first = jnp.max(jnp.where(before, doc_starts[:, None, :], 0), axis=-1)
    return (doc_ids, places[None, :] - doc_first)


def rotary(offsets):
    frequency = ROPE_BASE ** (-(jnp.arange(HEAD_DIM // 2, dtype=jnp.float32) * 2.0 / HEAD_DIM))
    angles = offsets.astype(jnp.float32)[..., None] * frequency
    cos_table = jnp.concatenate([jnp.cos(angles), jnp.cos(angles)], axis=-1)
    sin_table = jnp.concatenate([jnp.sin(angles), jnp.sin(angles)], axis=-1)
    return (cos_table, sin_table)


def queries_keys(
    cos_table, sin_table, projected, gain_query, gain_key, heads=HEADS, kv_heads=KV_HEADS
):
    rows_here, seq_here = (projected.shape[0], projected.shape[1])
    att_width = heads * HEAD_DIM
    queries = projected[..., :att_width].reshape(rows_here, seq_here, heads, HEAD_DIM)
    keys_rot = projected[..., att_width : att_width + kv_heads * HEAD_DIM].reshape(
        rows_here, seq_here, kv_heads, HEAD_DIM
    )
    cos_wide = cos_table[:, :, None, :]
    sin_wide = sin_table[:, :, None, :]
    queries = turn(norm_rows(queries, gain_query), cos_wide, sin_wide) * HEAD_DIM ** (-0.5)
    keys_rot = turn(norm_rows(keys_rot, gain_key), cos_wide, sin_wide)
    return (queries, keys_rot)


def mask_of(query_docs, query_places, key_docs, key_places):
    same_doc = query_docs[:, :, None] == key_docs[:, None, :]
    causal = query_places[None, :, None] >= key_places[None, None, :]
    return (same_doc & causal)[:, None, None, :, :]


def gathered_local(
    tokens,
    doc_starts,
    grad_out,
    qkv_master,
    out_master,
    gate_up_master,
    down_master,
    gains,
    qkv_rows,
    out_rows,
    gate_up_rows,
    down_rows,
    col_moments,
    gain_moments,
):
    cycle_size = lax.axis_size("seq")
    seq_index = lax.axis_index("seq")
    rows_dev, seq_dev = (tokens.shape[0], tokens.shape[1])
    group_size = HEADS // KV_HEADS
    att_width = HEADS * HEAD_DIM
    kv_width = KV_HEADS * HEAD_DIM
    gain_attn = gains[:D]
    gain_ffn = gains[D : 2 * D]
    gain_query = gains[2 * D : 2 * D + HEAD_DIM]
    gain_key = gains[2 * D + HEAD_DIM :]
    local_places = jnp.arange(seq_dev, dtype=jnp.int32)
    places = seq_index * seq_dev + local_places
    query_docs, offsets = doc_tables(doc_starts, places)
    cos_table, sin_table = rotary(offsets)
    copies = (
        qkv_master.astype(jnp.bfloat16),
        out_master.astype(jnp.bfloat16),
        gate_up_master.astype(jnp.bfloat16),
        down_master.astype(jnp.bfloat16),
    )
    w_qkv, w_out, w_gate_up, w_down = (
        lax.all_gather(copies[0], ("seq", "rows"), axis=0, tiled=True),
        lax.all_gather(copies[1], ("seq", "rows"), axis=0, tiled=True),
        lax.all_gather(copies[2], ("seq", "rows"), axis=0, tiled=True),
        lax.all_gather(copies[3], ("seq", "rows"), axis=0, tiled=True),
    )
    tokens_wide = tokens.astype(jnp.float32)
    normed = norm_rows(tokens_wide, gain_attn).astype(jnp.bfloat16)
    projected = jnp.einsum("rtd,de->rte", normed, w_qkv, preferred_element_type=jnp.float32)
    head_fn = partial(queries_keys, cos_table, sin_table)
    queries, keys_rot = head_fn(projected, gain_query, gain_key)
    query16 = queries.astype(jnp.bfloat16).reshape(
        rows_dev, seq_dev, KV_HEADS, group_size, HEAD_DIM
    )
    keys16 = keys_rot.astype(jnp.bfloat16).reshape(rows_dev, seq_dev, kv_width)
    values16 = projected[..., att_width + kv_width :].astype(jnp.bfloat16)
    stat_shape = (rows_dev, KV_HEADS, group_size, seq_dev)
    initial = (
        jnp.full(stat_shape, MASKED_SCORE, jnp.float32),
        jnp.zeros(stat_shape, jnp.float32),
        jnp.zeros(stat_shape + (HEAD_DIM,), jnp.float32),
    )
    carry = initial
    key_piece = lax.all_gather(keys16, "seq", axis=1, tiled=True)
    value_piece = lax.all_gather(values16, "seq", axis=1, tiled=True)
    key_count = key_piece.shape[1]

    def absorb_block(state, block_index):
        best, total, summed = state
        block_begin = block_index * seq_dev
        key_block = lax.dynamic_slice_in_dim(key_piece, block_begin, seq_dev, 1).reshape(
            rows_dev, seq_dev, KV_HEADS, HEAD_DIM
        )
        value_block = lax.dynamic_slice_in_dim(value_piece, block_begin, seq_dev, 1).reshape(
            rows_dev, seq_dev, KV_HEADS, HEAD_DIM
        )
        key_places = block_begin + jnp.arange(seq_dev, dtype=jnp.int32)
        key_docs, _ = doc_tables(doc_starts, key_places)
        allowed = mask_of(query_docs, places, key_docs, key_places)
        scores = jnp.einsum(
            "rqkgh,rtkh->rkgqt", query16, key_block, preferred_element_type=jnp.float32
        )
        scores = jnp.where(allowed, scores, MASKED_SCORE)
        best_new = jnp.maximum(best, jnp.max(scores, axis=-1))
        weights = jnp.where(allowed, jnp.exp(scores - best_new[..., None]), 0.0)
        factor = jnp.exp(best - best_new)
        total = total * factor + jnp.sum(weights, axis=-1)
        summed = summed * factor[..., None] + jnp.einsum(
            "rkgqt,rtkh->rkgqh",
            weights.astype(jnp.bfloat16),
            value_block,
            preferred_element_type=jnp.float32,
        )
        return ((best_new, total, summed), None)

    carry, _ = lax.scan(absorb_block, carry, jnp.arange(key_count // seq_dev, dtype=jnp.int32))
    best, total, summed = carry
    log_total = best + jnp.log(total)
    attended = summed / total[..., None]
    attended16 = (
        attended.transpose(0, 3, 1, 2, 4).reshape(rows_dev, seq_dev, att_width).astype(jnp.bfloat16)
    )
    branch = jnp.einsum("rtc,cd->rtd", attended16, w_out, preferred_element_type=jnp.float32)
    hidden_in = tokens_wide + branch
    normed2 = norm_rows(hidden_in, gain_ffn).astype(jnp.bfloat16)
    gate_up = jnp.einsum("rtd,df->rtf", normed2, w_gate_up, preferred_element_type=jnp.float32)
    gate_part, up_part = (gate_up[..., :FF], gate_up[..., FF:])
    hidden = (jax.nn.silu(gate_part) * up_part).astype(jnp.bfloat16)
    output = hidden_in + jnp.einsum(
        "rtf,fd->rtd", hidden, w_down, preferred_element_type=jnp.float32
    )
    d_hidden = jnp.einsum("rtd,fd->rtf", grad_out, w_down, preferred_element_type=jnp.float32)
    silu_value, silu_back = jax.vjp(jax.nn.silu, gate_part)
    d_gate = silu_back(d_hidden * up_part)[0]
    d_gate_up = jnp.concatenate([d_gate, d_hidden * silu_value], axis=-1).astype(jnp.bfloat16)
    d_normed2 = jnp.einsum("rtf,df->rtd", d_gate_up, w_gate_up, preferred_element_type=jnp.float32)
    _, ffn_norm_back = jax.vjp(norm_rows, hidden_in, gain_ffn)
    d_inner, grad_gain_ffn = ffn_norm_back(d_normed2)
    d_hidden_in = grad_out.astype(jnp.float32) + d_inner
    term_down = jnp.einsum("rtf,rtd->fd", hidden, grad_out, preferred_element_type=jnp.float32)
    grad_down = lax.psum_scatter(term_down, ("seq", "rows"), scatter_dimension=0, tiled=True)
    term_gate_up = jnp.einsum("rtd,rtf->df", normed2, d_gate_up, preferred_element_type=jnp.float32)
    grad_gate_up = lax.psum_scatter(term_gate_up, ("seq", "rows"), scatter_dimension=0, tiled=True)
    d_branch = d_hidden_in.astype(jnp.bfloat16)
    term_out = jnp.einsum("rtc,rtd->cd", attended16, d_branch, preferred_element_type=jnp.float32)
    d_attended = jnp.einsum(
        "rtd,cd->rtc", d_branch, w_out, preferred_element_type=jnp.float32
    ).astype(jnp.bfloat16)
    d_heads = d_attended.reshape(rows_dev, seq_dev, KV_HEADS, group_size, HEAD_DIM).transpose(
        0, 2, 3, 1, 4
    )
    delta = jnp.sum(d_heads.astype(jnp.float32) * attended, axis=-1)

    def cycle_turn(turn_index, carry):
        pair16, grad_pair, d_queries = carry
        source = (seq_index + turn_index) % cycle_size
        key_places = source * seq_dev + local_places
        key_docs, _ = doc_tables(doc_starts, key_places)
        allowed = mask_of(query_docs, places, key_docs, key_places)
        key_block = pair16[0].reshape(rows_dev, seq_dev, KV_HEADS, HEAD_DIM)
        value_block = pair16[1].reshape(rows_dev, seq_dev, KV_HEADS, HEAD_DIM)
        scores = jnp.einsum(
            "rqkgh,rtkh->rkgqt", query16, key_block, preferred_element_type=jnp.float32
        )
        scores = jnp.where(allowed, scores, MASKED_SCORE)
        probs = jnp.where(allowed, jnp.exp(scores - log_total[..., None]), 0.0)
        d_values = jnp.einsum(
            "rkgqt,rkgqh->rtkh",
            probs.astype(jnp.bfloat16),
            d_heads,
            preferred_element_type=jnp.float32,
        )
        d_probs = jnp.einsum(
            "rkgqh,rtkh->rkgqt", d_heads, value_block, preferred_element_type=jnp.float32
        )
        d_scores = (probs * (d_probs - delta[..., None])).astype(jnp.bfloat16)
        d_queries = d_queries + jnp.einsum(
            "rkgqt,rtkh->rkgqh", d_scores, key_block, preferred_element_type=jnp.float32
        )
        d_keys = jnp.einsum(
            "rkgqt,rqkgh->rtkh", d_scores, query16, preferred_element_type=jnp.float32
        )
        grad_pair = grad_pair + jnp.stack(
            [
                d_keys.reshape(rows_dev, seq_dev, kv_width),
                d_values.reshape(rows_dev, seq_dev, kv_width),
            ]
        )
        grad_pair = from_behind(grad_pair.astype(jnp.bfloat16), "seq", -1).astype(grad_pair.dtype)
        pair16 = from_behind(pair16, "seq", -1)
        return (pair16, grad_pair, d_queries)

    start_pair = jnp.stack([keys16, values16])
    start_grads = jnp.zeros((2, rows_dev, seq_dev, kv_width), jnp.float32)
    start_queries = jnp.zeros(stat_shape + (HEAD_DIM,), jnp.float32)
    _, grad_pair, d_queries = lax.fori_loop(
        0, cycle_size, cycle_turn, (start_pair, start_grads, start_queries)
    )
    d_queries = d_queries.transpose(0, 3, 1, 2, 4).reshape(rows_dev, seq_dev, HEADS, HEAD_DIM)
    d_keys_home = grad_pair[0].reshape(rows_dev, seq_dev, KV_HEADS, HEAD_DIM)
    _, heads_back = jax.vjp(head_fn, projected, gain_query, gain_key)
    d_projected, grad_gain_query, grad_gain_key = heads_back((d_queries, d_keys_home))
    d_projected = jnp.concatenate(
        [d_projected[..., : att_width + kv_width], grad_pair[1]], axis=-1
    ).astype(jnp.bfloat16)
    term_qkv = jnp.einsum("rtd,rte->de", normed, d_projected, preferred_element_type=jnp.float32)
    d_normed = jnp.einsum("rte,de->rtd", d_projected, w_qkv, preferred_element_type=jnp.float32)
    _, attn_norm_back = jax.vjp(norm_rows, tokens_wide, gain_attn)
    d_tokens_part, grad_gain_attn = attn_norm_back(d_normed)
    grad_tokens = (d_hidden_in + d_tokens_part).astype(jnp.bfloat16)
    grad_qkv, grad_out_proj = (
        lax.psum_scatter(term_qkv, ("seq", "rows"), scatter_dimension=0, tiled=True),
        lax.psum_scatter(term_out, ("seq", "rows"), scatter_dimension=0, tiled=True),
    )
    gain_local = jnp.concatenate([grad_gain_attn, grad_gain_ffn, grad_gain_query, grad_gain_key])
    grads = (grad_qkv, grad_out_proj, grad_gate_up, grad_down)
    updated = optimizer_step(
        grads, gain_local, (qkv_master, out_master, gate_up_master, down_master), gains,
        (qkv_rows, out_rows, gate_up_rows, down_rows), col_moments, gain_moments,
        lambda vector: lax.psum(vector, ("seq", "rows")),
    )
    return (output.astype(jnp.bfloat16), grad_tokens, *grads, *updated)


MESH = pl.DeviceIdType.MESH
PLACES = 32
VMEM_BYTES = 61 * 1024 * 1024
CHUNK = 16


def here():
    seq = lax.axis_index("seq")
    return lax.div(seq, 2), lax.rem(seq, 2), lax.axis_index("rows")


def flips(chip):
    return (chip + 1 - 2 * lax.rem(chip, 2), lax.rem(chip + 2, 4), 3 - chip)


def ahead(z, step):
    return lax.rem(z + step, 4)


def at_place(chip, core, z):
    return (2 * chip + core, z)


def greet(peers):
    barrier = pltpu.get_barrier_semaphore()
    for peer in peers:
        pl.semaphore_signal(barrier, inc=1, device_id=peer, device_id_type=MESH)
    pl.semaphore_wait(barrier, len(peers))


class Mover:
    def __init__(self, send_sem, recv_sem, local_sem):
        self.send_sem, self.recv_sem, self.local_sem = send_sem, recv_sem, local_sem
        self.remote, self.own, self.lines, self.scattered = [], [], [], []
        self.used = 0

    def copy_of(self, src, dst, peer, send_slot, recv_slot):
        return pltpu.make_async_remote_copy(
            src_ref=src,
            dst_ref=dst,
            send_sem=self.send_sem.at[send_slot],
            recv_sem=self.recv_sem.at[recv_slot],
            device_id=peer,
            device_id_type=MESH,
        )

    def send_parts(self, pairs, whole, peer):
        slot = self.used
        self.used += 1
        for src, dst in pairs:
            self.copy_of(src, dst, peer, slot, slot).start()
        copy = self.copy_of(whole[0], whole[1], peer, slot, slot)
        handle = [copy, False, copy.wait_recv, False]
        self.remote.append(handle)
        return handle

    def send(self, src, dst, peer):
        return self.send_parts([(src, dst)], (src, dst), peer)

    def keep_parts(self, pairs, whole):
        sem = self.local_sem.at[len(self.own)]
        for src, dst in pairs:
            pltpu.make_async_copy(src, dst, sem).start()
        copy = pltpu.make_async_copy(whole[0], whole[1], sem)
        handle = [copy, False, copy.wait]
        self.own.append(handle)
        return handle

    def keep(self, src, dst):
        return self.keep_parts([(src, dst)], (src, dst))

    def line(self, source, block_of, chip, core, z):
        line = (self.used, block_of, chip, core, z)
        self.used += 5
        base = line[0]
        up, low = at_place(chip, core, z + 1), at_place(chip, core, z - 1)
        rising = self.copy_of(source, block_of(z), up, base, base + 3)
        falling = self.copy_of(source, block_of(z), low, base + 4, base + 1)
        pl.when(z < 3)(rising.start)
        pl.when(z > 0)(falling.start)
        self.lines += [(z < 3, rising), (z > 0, falling)]
        return line

    def wait_line(self, line, step, when=None):
        base, block_of, chip, core, z = line
        block = block_of(ahead(z, step))
        peer = at_place(chip, core, ahead(z, step))
        copy = self.copy_of(block, block, peer, base + step, base + step)
        if when is None:
            copy.wait_recv()
        else:
            pl.when(when)(copy.wait_recv)
        return block

    def arrive_line(self, line, step, when=None):
        base, _, chip, core, z = line
        block = self.wait_line(line, step, when)
        rises, falls = (z + step >= 4) & (z < 3), (z + step < 4) & (z > 0)
        up, low = at_place(chip, core, z + 1), at_place(chip, core, z - 1)
        rising = self.copy_of(block, block, up, base + step, base + step - 1)
        falling = self.copy_of(block, block, low, base + step, base + step + 1)
        for moves, copy in ((rises, rising), (falls, falling)):
            moves = moves if when is None else moves & when
            pl.when(moves)(copy.start)
            self.lines.append((moves, copy))
        return block

    def scatter(self, source, target, steps, chip, core, z):
        base = self.used
        self.used += 3

        def start(index):
            at = ahead(z, steps[index])
            copy = self.copy_of(
                source(at), target(z), at_place(chip, core, at), base + index, base + 3 - steps[index]
            )
            copy.start()
            self.scattered.append(copy)

        def wait():
            for step in (1, 2, 3):
                at = ahead(z, step)
                peer = at_place(chip, core, at)
                self.copy_of(source(at), target(at), peer, base, base + step - 1).wait_recv()

        return start, wait

    def arrive(self, *handles):
        for handle in handles:
            if not handle[1]:
                handle[1] = True
                handle[2]()

    def sent(self, *handles):
        for handle in handles:
            if not handle[3]:
                handle[3] = True
                handle[0].wait_send()

    def sent_lines(self):
        for when, copy in self.lines:
            pl.when(when)(copy.wait_send)
        self.lines = []

    def sent_sums(self):
        for copy in self.scattered:
            copy.wait_send()
        self.scattered = []

    def finish(self):
        assert self.used <= self.send_sem.shape[0] and len(self.own) <= self.local_sem.shape[0]
        self.arrive(*self.own, *self.remote)
        self.sent(*self.remote)
        self.sent_lines()
        self.sent_sums()


def semaphores(remote, own):
    return [
        pltpu.SemaphoreType.DMA((remote,)),
        pltpu.SemaphoreType.DMA((remote,)),
        pltpu.SemaphoreType.DMA((max(own, 1),)),
    ]


def exchange(kernel, ident, inputs, outputs, scratch, copies, moved, flops=0):
    spaces = {True: pltpu.VMEM, False: pl.ANY, None: pltpu.SMEM}
    specs = {near: pl.BlockSpec(memory_space=space) for near, space in spaces.items()}
    return pl.pallas_call(
        kernel,
        out_shape=[jax.ShapeDtypeStruct(shape, kind) for shape, kind, _ in outputs],
        in_specs=[specs[near] for _, near in inputs],
        out_specs=[specs[near] for _, _, near in outputs],
        scratch_shapes=scratch + semaphores(*copies),
        compiler_params=pltpu.CompilerParams(
            collective_id=ident, has_side_effects=True, vmem_limit_bytes=VMEM_BYTES
        ),
        cost_estimate=pl.CostEstimate(flops=flops, bytes_accessed=moved, transcendentals=0),
    )(*[array for array, _ in inputs])


def chunks(length, body):
    @pl.loop(0, length // CHUNK)
    def _(step):
        body(pl.ds(pl.multiple_of(step * CHUNK, CHUNK), CHUNK))


def add_blocks(first, second, result):
    for row in range(2):

        def body(part):
            total = first[row, part].astype(jnp.float32) + second[row, part].astype(jnp.float32)
            result[row, part] = total.astype(result.dtype)

        chunks(64, body)


def lower_half(shape):
    return lax.broadcasted_iota(jnp.int32, shape, len(shape) - 1) < 64


def swap_halves(entries):
    lane = lax.broadcasted_iota(jnp.int32, entries.shape, 1)
    return jnp.where(lax.rem(lane, 64) < 32, pltpu.roll(entries, 96, 1), pltpu.roll(entries, 32, 1))


def head_means(entries):
    lower = lower_half(entries.shape)
    low = jnp.sum(jnp.where(lower, entries, 0.0), axis=-1, keepdims=True)
    high = jnp.sum(jnp.where(lower, 0.0, entries), axis=-1, keepdims=True)
    return jnp.where(lower, low, high) * (1.0 / HEAD_DIM)


def wide(start, size):
    return pl.ds(pl.multiple_of(start, size), size)


def plain(left, right):
    return jnp.dot(left, right, preferred_element_type=jnp.float32)


def across(left, right):
    return lax.dot_general(
        left, right, (((1,), (1,)), ((), ())), preferred_element_type=jnp.float32
    )


def down(left, right):
    return lax.dot_general(
        left, right, (((0,), (0,)), ((), ())), preferred_element_type=jnp.float32
    )


def attention_probs(queries, keys, first, part):
    scores = across(queries, keys)
    place = lax.broadcasted_iota(jnp.int32, scores.shape, 1)
    query = lax.broadcasted_iota(jnp.int32, scores.shape, 0) + part * 128
    allowed = (place >= first) & (place <= query)
    scores = jnp.where(allowed, scores, MASKED_SCORE)
    best = jnp.max(scores, axis=-1, keepdims=True)
    weights = jnp.where(allowed, jnp.exp(scores - best), 0.0)
    return weights / jnp.sum(weights, axis=-1, keepdims=True)


COL_ROWS, GAIN_ROWS = 184, 33
COLS = COL_ROWS * 128
MATRICES = ((64, QKV, 0, 0), (64, D, 64, 24), (64, 2 * FF, 128, 40), (256, D, 192, 168))
ROW_TOTALS = (D, HEADS * HEAD_DIM, D, FF)
BETA = 1.0 - STEP ** (-0.8)


def lane_value(vector, lane):
    lanes = lax.broadcasted_iota(jnp.int32, (1, 128), 1)
    return jnp.sum(jnp.where(lanes == lane, vector, 0.0), axis=-1, keepdims=True)


def total(entries):
    return jnp.sum(jnp.sum(entries, axis=-1, keepdims=True), axis=0, keepdims=True)


def document_start(starts, row, place):
    start = jnp.zeros_like(place)
    for document in range(starts.shape[1]):
        begin = starts[row, document]
        start = jnp.maximum(start, jnp.where(place >= begin, begin, 0))
    return start


def place_tables(length):
    rates = ROPE_BASE ** (-(np.arange(128) % 32) * 2.0 / HEAD_DIM)
    angles = np.arange(length)[:, None] * rates
    return np.stack([np.cos(angles), np.sin(angles)]).astype(np.float32)


def derive_updates(
    flat, col_moments, gain_moments, gains,
    cols_new, col_factors, moments_new, gains_new, grad_gains, spreads,
):
    first = 2 * COL_ROWS
    stats = flat[first + 33 : first + 34]
    lanes = lax.broadcasted_iota(jnp.int32, (1, 128), 1)
    out = jnp.zeros((1, 128), jnp.float32)
    for slot, (_, width, _, col_at) in enumerate(MATRICES):
        own = pl.ds(col_at, width // 128)
        entries_all = float(ROW_TOTALS[slot] * width)
        new = BETA * col_moments[own] + (1.0 - BETA) * (flat[own] / ROW_TOTALS[slot])
        cols_new[own] = new
        mean_rows = lane_value(stats, slot) / ROW_TOTALS[slot]
        ratio = total(flat[pl.ds(COL_ROWS + col_at, width // 128)] / new)
        spread = jnp.sqrt(mean_rows * ratio / entries_all)
        scale = STEP_RATE * jnp.maximum(
            SCALE_EPSILON, jnp.sqrt(lane_value(stats, 4 + slot) / entries_all)
        )
        factor = scale * jnp.sqrt(mean_rows) / jnp.maximum(1.0, spread / CLIP_LEVEL)
        factors = lax.rsqrt(new) * factor
        for row in range(width // 128):
            col_factors[:, pl.ds((col_at + row) * 128, 128)] = factors[row : row + 1]
        out = jnp.where(lanes == slot, spread, out)
    gradient = flat[first : first + GAIN_ROWS]
    grad_gains[...] = gradient
    old = gains[...]
    new = BETA * gain_moments[...] + (1.0 - BETA) * (gradient * gradient + SQUARE_EPSILON)
    moments_new[...] = new
    unit = gradient * lax.rsqrt(new)
    row = lax.broadcasted_iota(jnp.int32, (GAIN_ROWS, 128), 0)
    lane = lax.broadcasted_iota(jnp.int32, (GAIN_ROWS, 128), 1)
    segment = jnp.where(row < 16, 0, jnp.where(row < 32, 1, jnp.where(lane < 64, 2, 3)))
    factors = jnp.zeros((GAIN_ROWS, 128), jnp.float32)
    for slot, count in enumerate((D, D, HEAD_DIM, HEAD_DIM)):
        mask = segment == slot
        spread = jnp.sqrt(total(jnp.where(mask, unit * unit, 0.0)) / count)
        mean = total(jnp.where(mask, old * old, 0.0)) / count
        scale = STEP_RATE * jnp.maximum(SCALE_EPSILON, jnp.sqrt(mean))
        factors = jnp.where(mask, scale / jnp.maximum(1.0, spread / CLIP_LEVEL), factors)
        out = jnp.where(lanes == 4 + slot, spread, out)
    gains_new[...] = old - factors * unit
    spreads[...] = out


def layer_kernel(
    tok, starts, rates, places_at, gain_attn, gain_ffn, gain_heads, gains, grad_out,
    m_qkv, m_out, m_down, m_gate_up, rows, col_moments, gain_moments,
    out_sum, grad_tok, g_qkv, gate_up_came, out_came, down_came, rows_new, row_factors,
    cols_new, col_factors, moments_new, gains_new, grad_gains, spreads,
    gate_up_in, gate_up_mid, kept_tok,
    projected, queries, keys_values, attended, document_tables,
    wq_send, normed, all_tok, all_wq, all_wo, partial, from_partner, came,
    hidden_in, all_norm, all_out, all_wg, wd, hidden, d_gate_up,
    d_queries, d_keys_values, qkv_in, d_hidden_in, gain_part, gain_part2, gain_qk, weight_sums, qkv_came,
    packed, plane_came, plane_sum, line_came, line_sum, line_all, totals, credit, tokens_used, *sems,
):
    half, full = jnp.bfloat16, jnp.float32
    chip, core, z = here()
    others = flips(chip)
    other = 1 - core
    me = 2 * chip + core
    partner = at_place(chip, other, z)
    plane = [at_place(peer_chip, core, z) for peer_chip in others]
    plane_cross = [at_place(peer_chip, other, z) for peer_chip in others]
    steps = (2, 1, 3)
    line = [at_place(chip, core, ahead(z, step)) for step in steps]
    cross = [at_place(chip, other, ahead(z, step)) for step in steps]
    everyone = [partner] + plane + plane_cross
    greet(everyone + line + cross)
    move = Mover(*sems)
    line_grads = move.line(grad_out, lambda at: all_out.at[at, core], chip, core, z)

    for head in range(8):
        wq_send[head, :, pl.ds(0, 256)] = m_qkv[:, pl.ds(head * 256, 256)].astype(half)
    low = lower_half((64, 128))
    for pair in range(4):
        keys = m_qkv[:, pl.ds(2048 + pair * 128, 128)]
        values = m_qkv[:, pl.ds(2560 + pair * 128, 128)]
        tail = pl.ds(256, 128)
        wq_send[2 * pair, :, tail] = jnp.where(low, keys, pltpu.roll(values, 64, 1)).astype(half)
        wq_send[2 * pair + 1, :, tail] = jnp.where(low, pltpu.roll(keys, 64, 1), values).astype(half)
    heads = [move.keep(wq_send.at[me], all_wq.at[me, z])]
    for peer in everyone:
        heads.append(move.send(wq_send.at[peer[0]], all_wq.at[me, z], peer))

    for row in range(2):

        def body0(part):
            result = tok[row, part].astype(full)
            scale = lax.rsqrt(jnp.mean(result * result, axis=-1, keepdims=True) + EPSILON)
            normed[row, part] = (result * scale * gain_attn[...]).astype(half)

        chunks(64, body0)
    token_copies = [move.send(normed, all_tok.at[me], peer) for peer in plane]
    token_copies.append(move.send(normed, all_tok.at[me], partner))
    tokens_here = move.keep(normed, all_tok.at[me])
    move.arrive(*heads)
    line_wq = move.line(all_wq.at[:, z], lambda at: all_wq.at[:, at], chip, core, z)
    flat_d = d_gate_up.reshape(1024, 2048)
    weight_sums[...] = jnp.zeros_like(weight_sums)
    for row in range(2):
        for document in range(starts.shape[1]):
            angle = starts[row, document].astype(full) * rates[0:1]
            document_tables[row, 2 * document] = jnp.cos(angle)
            document_tables[row, 2 * document + 1] = jnp.sin(angle)

    def cast_all(slot, blocks):
        loads = [move.keep(blocks[0][0], hidden_in.at[0])]
        for index, (_, target) in enumerate(blocks):
            if index + 1 < len(blocks):
                loads.append(move.keep(blocks[index + 1][0], hidden_in.at[(index + 1) % 2]))
            move.arrive(loads[index])

            def body(part, index=index, target=target):
                entries = hidden_in[index % 2, part]
                weight_sums[slot] += jnp.sum((entries * entries).reshape(2, 8, D), axis=0)
                target(part, entries.astype(half))

            chunks(64, body)

    def into(ref):
        def store(part, entries):
            ref[part] = entries

        return store

    def by_device(block):
        cols = pl.ds((block // 4) * 1024 + (block % 4) * 256, 256)

        def store(part, entries):
            for index in range(8):
                place = (index % 4) * 2 + index // 4
                rows_at = wide(place * 64 + part.start, CHUNK)
                flat_d[rows_at, cols] = entries[:, index * 256 : (index + 1) * 256]

        return store

    cast_all(1, [(m_out, into(all_wo.at[z]))])
    cast_all(
        3,
        [
            (m_down.at[pl.ds(64 * block, 64)], into(wd.at[chip, pl.ds(64 * block, 64)]))
            for block in range(4)
        ],
    )
    by_x, by_y = plane[0], plane[1]
    front, back = wd.at[chip, pl.ds(0, 128)], wd.at[chip, pl.ds(128, 128)]
    down_copies = [
        move.send(front, front, by_x), move.send(back, back, by_y),
        move.send(back, back, by_x), move.send(front, front, by_y),
    ]
    move.arrive_line(line_wq, 3)
    move.arrive_line(line_wq, 1)
    cast_all(
        2,
        [(m_gate_up.at[:, pl.ds(2048 * block, 2048)], by_device(block)) for block in range(8)],
    )
    move.arrive_line(line_wq, 2)
    wo_copies = [move.send(all_wo.at[z], all_wo.at[z], peer) for peer in line]

    def turn_block(to_core, to_z, side):
        lanes = pl.ds(side * 1024, 1024)
        src = flat_d.at[wide((to_z * 2 + to_core) * 64, 64), lanes]
        return src, all_wg.at[chip, core, z, :, lanes]

    own = [
        move.keep(grad_out, all_out.at[z, core]),
        move.send(grad_out, all_out.at[z, core], partner),
    ]

    for peer_chip, handle in zip(others, tuple(token_copies)):
        move.arrive(handle)
        block = all_tok.at[2 * peer_chip + core]
        token_copies.append(move.send(block, block, partner))
    move.arrive(tokens_here, *token_copies)
    saved = [move.keep(all_tok, kept_tok)]

    def tables_of(block, row):
        place = lax.broadcasted_iota(jnp.int32, (64, 1), 0) + block * 64
        start_cos, start_sin = document_tables[row, 0], document_tables[row, 1]
        for document in range(1, starts.shape[1]):
            inside = place >= starts[row, document]
            start_cos = jnp.where(inside, document_tables[row, 2 * document], start_cos)
            start_sin = jnp.where(inside, document_tables[row, 2 * document + 1], start_sin)
        at = wide(block * 64, 64)
        place_cos, place_sin = places_at[0, at], places_at[1, at]
        cosine = place_cos * start_cos + place_sin * start_sin
        return cosine, (place_sin * start_cos - place_cos * start_sin) * rates[1:2]

    def first_of(row, part):
        place = lax.broadcasted_iota(jnp.int32, (128, 1), 0) + part * 128
        return document_start(starts, row, place)

    flat_tok, flat_wq = all_tok.reshape(1024, D), all_wq.reshape(D, 384)
    flat_wo = all_wo.reshape(256, D)

    @pl.loop(0, 4)
    def _(step):
        block = plain(flat_tok[wide(step * 256, 256)], flat_wq[...])
        projected[wide(step * 2, 2)] = block.reshape(2, 2, 64, 384)

    @pl.loop(0, 8)
    def _(block):
        for row in range(2):
            cosine, sine = tables_of(block, row)
            places = wide(block * 64, 64)
            for tile in range(3):
                entries = projected[block, row, :, pl.ds(tile * 128, 128)]
                gain = gain_heads[min(tile, 2) // 2 : min(tile, 2) // 2 + 1]
                scale = lax.rsqrt(head_means(entries * entries) + EPSILON)
                turned_entries = entries * scale * gain
                turned_entries = turned_entries * cosine + swap_halves(turned_entries) * sine
                if tile < 2:
                    queries[row, tile, places] = (turned_entries * HEAD_DIM ** (-0.5)).astype(half)
                else:
                    zero = jnp.zeros_like(entries)
                    rolled = pltpu.roll(turned_entries, 64, 1)
                    values = pltpu.roll(entries, 64, 1)
                    keys_values[row, 0, places] = jnp.where(low, turned_entries, zero).astype(half)
                    keys_values[row, 1, places] = jnp.where(low, zero, rolled).astype(half)
                    keys_values[row, 2, places] = jnp.where(low, values, zero).astype(half)
                    keys_values[row, 3, places] = jnp.where(low, zero, entries).astype(half)

    turned, turned_own = ([], []), []
    for side in range(2):
        for step, peer, peer_cross in zip(steps, line, cross):
            to = ahead(z, step)
            turned[side].append(move.send(*turn_block(core, to, side), peer))
            turned[side].append(move.send(*turn_block(other, to, side), peer_cross))
        turned[side].append(move.send(*turn_block(other, z, side), partner))
        turned_own.append(move.keep(*turn_block(core, z, side)))
    move.arrive(*down_copies[:2])
    front, back = wd.at[others[0], pl.ds(0, 128)], wd.at[others[1], pl.ds(128, 128)]
    down_copies += [move.send(front, front, by_y), move.send(back, back, by_x)]

    @pl.loop(0, 2)
    def _(row):
        for tile in range(2):
            for part in range(4):
                own_places, upto = pl.ds(part * 128, 128), pl.ds(0, (part + 1) * 128)
                result = jnp.zeros((128, 128), full)
                for side in range(2):
                    probs = attention_probs(
                        queries[row, tile, own_places], keys_values[row, side, upto],
                        first_of(row, part), part,
                    )
                    result += plain(probs.astype(half), keys_values[row, 2 + side, upto])
                attended[pl.ds(2 * part, 2), row, :, pl.ds(tile * 128, 128)] = result.reshape(2, 64, 128)

    flat_attended = attended.reshape(1024, 256)
    move.arrive(*wo_copies)

    @pl.loop(0, 4)
    def _(step):
        rows = flat_attended[wide(step * 256, 256)].astype(half)

        @pl.loop(0, 4)
        def _(col):
            cols = wide(col * 512, 512)
            block = plain(rows, flat_wo[:, cols])
            partial[wide(step * 2, 2), :, :, cols] = block.reshape(2, 2, 64, 512).astype(half)

    order = tuple(others) + (chip,)
    halves = [move.send(partial.at[2 * to + other], from_partner.at[to], partner) for to in order]
    sums = []
    for to, arrived, peer in zip(others, halves, plane):
        move.arrive(arrived)
        add_blocks(partial.at[2 * to + core], from_partner.at[to], from_partner.at[to])
        sums.append(move.send(from_partner.at[to], came.at[chip], peer))
    def gather_weights(side):
        move.arrive(turned_own[side], *turned[side])
        lanes = pl.ds(side * 1024, 1024)
        front, back = all_wg.at[chip, 0, :, :, lanes], all_wg.at[chip, 1, :, :, lanes]
        return [
            move.send(front, front, by_x), move.send(back, back, by_y),
            move.send(back, back, by_x), move.send(front, front, by_y),
        ]

    def pass_weights(side, copies):
        move.arrive(*copies[:2])
        lanes = pl.ds(side * 1024, 1024)
        front, back = all_wg.at[others[0], 0, :, :, lanes], all_wg.at[others[1], 1, :, :, lanes]
        return [move.send(front, front, by_y), move.send(back, back, by_x)]

    gate_copies = gather_weights(0)
    move.sent(*token_copies)
    move.arrive(halves[3], *sums)
    for row in range(2):

        def body(part):
            result = tok[row, part].astype(full)
            result += partial[me, row, part].astype(full)
            result += from_partner[chip, row, part].astype(full)
            for peer_chip in others:
                result += came[peer_chip, row, part].astype(full)
            hidden_in[row, part] = result
            scale = lax.rsqrt(jnp.mean(result * result, axis=-1, keepdims=True) + EPSILON)
            normed[row, part] = (result * scale * gain_ffn[...]).astype(half)

        chunks(64, body)
    move.sent(*sums, *halves)
    move.arrive(*saved)
    line_norms = move.line(normed, lambda at: all_norm.at[at, core], chip, core, z)
    own.append(move.send(normed, all_norm.at[z, core], partner))
    own.append(move.keep(normed, all_norm.at[z, core]))

    up_copies = gather_weights(1)
    at_first, at_last = lax.div(3 - z, 3), lax.div(z, 3)
    arrivals = (3 - 2 * at_first, 1 + at_first + at_last, 2 + at_first - at_last)
    inner = (z > 0) & (z < 3)
    shared = []

    def share(step, wait_only=False):
        for line_of in (line_grads, line_norms):
            if wait_only:
                block = move.wait_line(line_of, step, jnp.logical_not(inner))
            else:
                block = move.arrive_line(line_of, step)
            shared.append(move.send(block, block, partner))

    flat_wg, flat_wd = all_wg.reshape(D, 2048), wd.reshape(1024, D)

    def d_hidden_of(zb):
        @pl.loop(0, 4)
        def _(step):
            cols = wide(step * 256, 256)
            hidden[zb, :, cols] = across(all_out[zb].reshape(256, D), flat_wd[cols]).astype(half)

    share(arrivals[0])
    gate_copies += pass_weights(0, gate_copies)
    move.arrive(*own[:2], *down_copies)
    d_hidden_of(z)
    share(arrivals[1])
    up_copies += pass_weights(1, up_copies)
    move.arrive(shared[0])
    d_hidden_of(ahead(z, arrivals[0]))
    for line_of in (line_grads, line_norms):
        move.arrive_line(line_of, arrivals[2], inner)
    move.arrive(shared[2])
    d_hidden_of(ahead(z, arrivals[1]))
    weights = gate_copies + up_copies
    move.arrive(*weights, *own)
    move.sent(*turned[0], *turned[1])

    def block_of(zb):
        @pl.loop(0, 4)
        def _(step):
            cols, ups = wide(step * 256, 256), wide(1024 + step * 256, 256)
            rows = all_norm[zb].reshape(256, D)
            gate = plain(rows, flat_wg[:, cols])
            up = plain(rows, flat_wg[:, ups])
            d_hidden = hidden[zb, :, cols].astype(full)
            sigmoid = 1.0 / (1.0 + jnp.exp(-gate))
            silu = gate * sigmoid
            hidden[zb, :, cols] = (silu * up).astype(half)
            d_gate = d_hidden * up * (sigmoid * (1.0 + gate * (1.0 - sigmoid)))
            d_gate_up[zb, :, cols] = d_gate.astype(half)
            d_gate_up[zb, :, ups] = (d_hidden * silu).astype(half)

        @pl.loop(0, 8)
        def _(step):
            cols = wide(step * 256, 256)
            block = across(d_gate_up[zb], flat_wg[cols])
            partial[pl.ds(2 * zb, 2), :, :, cols] = block.reshape(2, 2, 64, 256).astype(half)

    def pair_sum(zb, handle, into, base):
        move.arrive(handle)
        add_blocks(partial.at[2 * zb + core], into.at[base + zb], into.at[base + zb])

    start_sum, wait_sums = move.scatter(
        lambda at: from_partner.at[at], lambda at: came.at[at], arrivals, chip, core, z
    )
    to_partner = []
    walk = [z] + [ahead(z, step) for step in arrivals]
    for index, zb in enumerate(walk):
        if index > 0:
            move.arrive(*shared[2 * index - 2 : 2 * index])
        if index == 3:
            d_hidden_of(zb)
        block_of(zb)
        to_partner.append(move.send(partial.at[2 * zb + other], from_partner.at[zb], partner))
        if index == 0:
            share(arrivals[2], True)
        if index > 0:
            pair_sum(walk[index - 1], to_partner[index - 1], from_partner, 0)
        if index > 1:
            start_sum(index - 2)
    pair_sum(walk[3], to_partner[3], from_partner, 0)
    start_sum(2)

    flat_norm, flat_grads = all_norm.reshape(1024, D), all_out.reshape(1024, D)
    flat_hidden = hidden.reshape(1024, 1024)
    move.sent(*weights)

    def gate_up_grad(to, side):
        rows, lanes = wide(to * 512, 512), pl.ds(side * 1024, 1024)

        @pl.loop(0, 2)
        def _(step):
            cols = wide(side * 1024 + step * 512, 512)
            flat_wg[rows, cols] = down(flat_norm[:, rows], flat_d[:, cols]).astype(half)

        return flat_wg.at[rows, lanes]

    passed = []
    for side in (0, 1):
        passed.append(move.send(gate_up_grad(others[2], side), gate_up_mid.at[side], plane[side]))
    move.sent(*to_partner)
    to_partner, sums = [], []
    walk = [ahead(z, step) for step in steps] + [z]
    for index, zb in enumerate(walk):

        @pl.loop(0, 4)
        def _(step, zb=zb):
            cols = wide(step * 512, 512)
            block = plain(hidden[zb], flat_wd[:, cols])
            partial[pl.ds(2 * zb, 2), :, :, cols] = block.reshape(2, 2, 64, 512).astype(half)

        to_partner.append(move.send(partial.at[2 * zb + other], all_tok.at[zb], partner))
        if index > 0:
            before = walk[index - 1]
            pair_sum(before, to_partner[index - 1], all_tok, 0)
            sums.append(move.send(all_tok.at[before], all_tok.at[4 + z], line[index - 1]))
    pair_sum(z, to_partner[3], all_tok, 0)

    direct = [gate_up_grad(others[side], side) for side in (0, 1)]
    handed = [gate_up_grad(others[1 - side], side) for side in (0, 1)]
    for side in (0, 1):
        gate_up_grad(chip, side)
    move.sent(*shared, own[2])
    move.sent_lines()
    for peer in [partner] + plane:
        pl.semaphore_signal(credit, inc=1, device_id=peer, device_id_type=MESH)

    wait_sums()
    gain_part[...] = jnp.zeros_like(gain_part)
    for row in range(2):

        def body2(part):
            result = from_partner[z, row, part].astype(full)
            for step in steps:
                result += came[ahead(z, step), row, part].astype(full)
            entries = hidden_in[row, part]
            scale = lax.rsqrt(jnp.mean(entries * entries, axis=-1, keepdims=True) + EPSILON)
            gain_part[...] += jnp.sum(result * entries * scale, axis=0, keepdims=True)
            result = result * gain_ffn[...]
            inside = jnp.mean(result * entries, axis=-1, keepdims=True) * (scale * scale * scale)
            grad = grad_out[row, part].astype(full) + result * scale - entries * inside
            d_hidden_in[row, part] = grad
            normed[row, part] = grad.astype(half)

        chunks(64, body2)
    pl.semaphore_wait(credit, 4)
    move.sent_sums()
    all_branch = all_norm.reshape(8, 2, 64, D)
    branches = [move.send(normed, all_branch.at[me], peer) for peer in plane]
    branch_copies = [
        move.send(normed, all_branch.at[me], partner), move.keep(normed, all_branch.at[me])
    ]

    move.sent(*down_copies, *wo_copies)

    @pl.loop(0, 4)
    def _(to):
        rows_at = wide(to * 256, 256)

        @pl.loop(0, 4)
        def _(step):
            cols = wide(step * 512, 512)
            flat_wd[rows_at, cols] = down(flat_hidden[:, rows_at], flat_grads[:, cols]).astype(half)

    load_tok = move.keep(kept_tok, all_out.reshape(8, 2, 64, D))

    def load(source):
        return [
            move.keep(source(side), flat_d.at[pl.ds(side * 512, 512), pl.ds(0, 1024)])
            for side in (0, 1)
        ]

    def add_loaded(side, chunk):
        @pl.loop(0, 512 // CHUNK)
        def _(step):
            lanes = pl.ds(side * 1024, 1024)
            rows = wide(chunk * 512 + step * CHUNK, CHUNK)
            extra = flat_d[wide(side * 512 + step * CHUNK, CHUNK), pl.ds(0, 1024)]
            result = flat_wg[rows, lanes].astype(full) + extra.astype(full)
            flat_wg[rows, lanes] = result.astype(half)

    move.arrive(*branches)
    pieces = [
        move.send(direct[side], gate_up_in.at[side, 0], plane[side]) for side in (0, 1)
    ]
    for peer_chip in others:
        block = all_branch.at[2 * peer_chip + core]
        branch_copies.append(move.send(block, block, partner))
    move.arrive(*passed)
    loads = load(lambda side: gate_up_mid.at[side])
    later = []
    for side in (0, 1):
        move.arrive(loads[side])
        add_loaded(side, others[1 - side])
        later.append(move.send(handed[side], gate_up_in.at[side, 1], plane[1 - side]))
    move.arrive(*branch_copies)

    flat_branch = all_branch.reshape(1024, D)
    flat_wo = all_wo.reshape(256, D)
    d_heads_at, d_projected_at = pl.ds(0, 256), pl.ds(256, 384)

    @pl.loop(0, 4)
    def _(step):
        rows = wide(step * 256, 256)
        flat_hidden[rows, d_heads_at] = across(flat_branch[rows], flat_wo[...]).astype(half)

    @pl.loop(0, 4)
    def _(step):
        cols = wide(step * 512, 512)
        block = down(flat_attended[...].astype(half), flat_branch[:, cols])
        flat_wo[:, cols] = block.astype(half)

    outs = [
        move.send(all_wo.at[ahead(z, step)], out_came.at[z], peer) for step, peer in zip(steps, line)
    ]
    outs.append(move.keep(all_wo.at[z], out_came.at[z]))
    lower = lower_half((128, 128))
    line_low = lower_half((1, 128))
    gain_qk[...] = jnp.zeros_like(gain_qk)

    @pl.loop(0, 2)
    def _(row):
        d_keys_values[...] = jnp.zeros_like(d_keys_values)

        def token_rows(block):
            return wide((2 * block + row) * 64, 64)

        for tile in range(2):
            lanes = pl.ds(tile * 128, 128)
            for part in range(4):
                own_places, upto = pl.ds(part * 128, 128), pl.ds(0, (part + 1) * 128)
                d_heads = jnp.concatenate(
                    [flat_hidden[token_rows(2 * part + index), lanes] for index in range(2)], axis=0
                )
                products = d_heads.astype(full) * attended[pl.ds(2 * part, 2), row, :, lanes].reshape(128, 128)
                query = queries[row, tile, own_places]
                result = jnp.zeros((128, 128), full)
                for side in range(2):
                    mask = lower if side == 0 else jnp.logical_not(lower)
                    delta = jnp.sum(jnp.where(mask, products, 0.0), axis=-1, keepdims=True)
                    keys = keys_values[row, side, upto]
                    probs = attention_probs(query, keys, first_of(row, part), part)
                    d_probs = across(d_heads, keys_values[row, 2 + side, upto])
                    d_scores = (probs * (d_probs - delta)).astype(half)
                    result += plain(d_scores, keys)
                    d_keys_values[side, upto] += down(d_scores, query)
                    d_keys_values[2 + side, upto] += down(probs.astype(half), d_heads)
                d_queries[tile, own_places] = result

        @pl.loop(0, 8)
        def _(block):
            cosine, sine = tables_of(block, row)
            places = wide(block * 64, 64)
            for tile in range(3):
                entries = projected[block, row, :, pl.ds(tile * 128, 128)]
                gain = gain_heads[tile // 2 : tile // 2 + 1]
                scale = lax.rsqrt(head_means(entries * entries) + EPSILON)
                if tile < 2:
                    grad = d_queries[tile, places] * HEAD_DIM ** (-0.5)
                else:
                    from_low, from_high = d_keys_values[0, places], d_keys_values[1, places]
                    grad = jnp.where(low, from_low + pltpu.roll(from_high, 64, 1), 0.0)
                grad = grad * cosine + swap_halves(grad * sine)
                for_gain = jnp.sum(grad * entries * scale, axis=0, keepdims=True)
                if tile < 2:
                    for_gain = jnp.where(line_low, for_gain + pltpu.roll(for_gain, 64, 1), 0.0)
                else:
                    for_gain = jnp.where(line_low, 0.0, pltpu.roll(for_gain, 64, 1))
                gain_qk[...] += for_gain
                grad = grad * gain
                inside = head_means(grad * entries) * (scale * scale * scale)
                grad = grad * scale - entries * inside
                if tile == 2:
                    values = pltpu.roll(d_keys_values[2, places], 64, 1)
                    grad = jnp.where(low, grad, values + d_keys_values[3, places])
                flat_hidden[token_rows(block), pl.ds(256 + tile * 128, 128)] = grad.astype(half)

    move.arrive(load_tok)

    for block in range(4):
        strip = pl.ds(1024 + 384 * (block // 2), 384)
        product = down(
            flat_grads[:, pl.ds(block * 512, 512)], flat_hidden[:, d_projected_at]
        )
        flat_d[pl.ds(512 * (block % 2), 512), strip] = product.astype(half)

    for peer in [partner] + line + cross:
        pl.semaphore_signal(tokens_used, inc=1, device_id=peer, device_id_type=MESH)

    def head_block(head, at):
        rows = wide(((head % 4) * 4 + at) * 64, 64)
        return flat_d.at[rows, pl.ds(1024 + 384 * (head // 4), 384)]

    qkv_pieces = []
    for step, peer in zip(steps, line):
        pairs = [(head_block(head, ahead(z, step)), qkv_in.at[z, head]) for head in range(8)]
        qkv_pieces.append(move.send_parts(pairs, (qkv_in.at[z], qkv_in.at[z]), peer))
    move.sent(*to_partner)

    @pl.loop(0, 4)
    def _(step):
        rows = flat_hidden[wide(step * 256, 256), d_projected_at]

        @pl.loop(0, 4)
        def _(col):
            cols = wide(col * 512, 512)
            block = across(rows, flat_wq[cols])
            partial[wide(step * 2, 2), :, :, cols] = block.reshape(2, 2, 64, 512).astype(half)

    halves = [move.send(partial.at[2 * to + other], from_partner.at[to], partner) for to in order]
    d_norms = []
    for to, arrived, peer in zip(others, halves, plane):
        move.arrive(arrived)
        add_blocks(partial.at[2 * to + core], from_partner.at[to], from_partner.at[to])
        d_norms.append(move.send(from_partner.at[to], came.at[chip], peer))
    downs = [move.send(wd.at[to], down_came.at[chip], peer) for to, peer in zip(others, plane)]
    downs.append(move.keep(wd.at[chip], down_came.at[chip]))
    move.arrive(halves[3])
    add_blocks(partial.at[me], from_partner.at[chip], from_partner.at[chip])

    for slot, handles in ((0, pieces), (1, later)):
        move.arrive(*handles)
        loads = load(lambda side, slot=slot: gate_up_in.at[side, slot])
        for side in (0, 1):
            move.arrive(loads[side])
            add_loaded(side, chip)

    blocks = all_out.reshape(16, 64, D)

    def back_block(to_core, to_z):
        return all_wg.at[chip, to_core, to_z], blocks.at[8 + 2 * z + core]

    pl.semaphore_wait(tokens_used, 7)
    gate_ups = []
    for step, peer, peer_cross in zip(steps, line, cross):
        to = ahead(z, step)
        gate_ups.append(move.send(*back_block(core, to), peer))
        gate_ups.append(move.send(*back_block(other, to), peer_cross))
    gate_ups.append(move.send(*back_block(other, z), partner))
    gate_ups.append(move.keep(*back_block(core, z)))

    move.arrive(*sums)
    for row in range(2):

        def body3(part):
            result = hidden_in[row, part] + all_tok[z, row, part].astype(full)
            for step in steps:
                result += all_tok[4 + ahead(z, step), row, part].astype(full)
            out_sum[row, part] = result.astype(half)

        chunks(64, body3)

    move.arrive(*d_norms)
    gain_part2[...] = jnp.zeros_like(gain_part2)
    for row in range(2):

        def body4(part):
            result = from_partner[chip, row, part].astype(full)
            for peer_chip in others:
                result += came[peer_chip, row, part].astype(full)
            entries = tok[row, part].astype(full)
            scale = lax.rsqrt(jnp.mean(entries * entries, axis=-1, keepdims=True) + EPSILON)
            gain_part2[...] += jnp.sum(result * entries * scale, axis=0, keepdims=True)
            result = result * gain_attn[...]
            inside = jnp.mean(result * entries, axis=-1, keepdims=True) * (scale * scale * scale)
            result = d_hidden_in[row, part] + result * scale - entries * inside
            grad_tok[row, part] = result.astype(half)

        chunks(64, body4)

    def send_heads():
        move.arrive(*qkv_pieces)
        move.sent(*heads[1:])
        for head in range(8):
            result = head_block(head, z)[...].astype(full)
            for step in steps:
                result += qkv_in[ahead(z, step), head].astype(full)
            wq_send[head] = result.astype(half)
        copies = [move.send(wq_send.at[peer[0]], qkv_came.at[me], peer) for peer in everyone]
        return copies + [move.keep(wq_send.at[me], qkv_came.at[me])]

    flat_packed = packed.reshape(512, 128)
    first = 2 * COL_ROWS
    line_lanes = lax.broadcasted_iota(jnp.int32, (1, 128), 1)
    flat_packed[pl.ds(first + 33, 512 - first - 33)] = jnp.zeros((512 - first - 33, 128), full)

    def statistics(slot, read):
        count, width, row_at, col_at = MATRICES[slot]
        own_rows, some = pl.ds(row_at, count), pl.ds(0, count)
        d_queries[0, some] = jnp.zeros((count, 128), full)

        @pl.loop(0, width // 128)
        def _(step):
            entries = read(step)
            d_queries[0, some] += entries * entries

        mean = jnp.sum(d_queries[0, some], axis=-1, keepdims=True) / width + SQUARE_EPSILON
        new = BETA * rows[own_rows] + (1.0 - BETA) * mean
        rows_new[own_rows] = new
        row_factors[own_rows] = lax.rsqrt(new)
        d_keys_values[0, some] = jnp.broadcast_to(1.0 / new, (count, 128))

        @pl.loop(0, width // 128)
        def _(step):
            entries = read(step)
            square = entries * entries
            flat_packed[pl.ds(col_at + step, 1)] = (
                jnp.sum(square, axis=0, keepdims=True) + count * SQUARE_EPSILON
            )
            flat_packed[pl.ds(COL_ROWS + col_at + step, 1)] = jnp.sum(
                square * d_keys_values[0, some], axis=0, keepdims=True
            )

        stats = flat_packed[pl.ds(first + 33, 1)]
        stats = jnp.where(line_lanes == slot, jnp.sum(new, axis=0, keepdims=True), stats)
        stats = jnp.where(line_lanes == 4 + slot, total(weight_sums[slot]), stats)
        flat_packed[pl.ds(first + 33, 1)] = stats

    def lanes_of(step):
        return wide(step * 128, 128)

    def four(buffer):
        def read(step):
            result = buffer[0, :, lanes_of(step)].astype(full)
            for slot in range(1, 4):
                result += buffer[slot, :, lanes_of(step)].astype(full)
            return result

        return read

    out_here, down_here = blocks, all_norm.reshape(4, 256, D)
    move.arrive(*outs)
    out_load = move.keep(out_came, out_here.at[pl.ds(0, 4)])
    qkv_copies = send_heads()
    move.arrive(*downs)
    move.sent(*branch_copies[2:])
    down_load = move.keep(down_came, down_here)
    move.arrive(out_load)
    statistics(1, four(out_here))
    move.arrive(down_load)
    statistics(3, four(down_here))

    move.arrive(*qkv_copies)
    for head in range(8):
        for part in range(2):
            strip = qkv_came[head, :, pl.ds(part * 128, 128)]
            g_qkv[:, pl.ds(head * 256 + part * 128, 128)] = strip.astype(full)
    for pair in range(4):
        keys = qkv_came[2 * pair, :, pl.ds(256, 128)].astype(full)
        values = qkv_came[2 * pair + 1, :, pl.ds(256, 128)].astype(full)
        g_qkv[:, pl.ds(2048 + pair * 128, 128)] = jnp.where(low, keys, pltpu.roll(values, 64, 1))
        g_qkv[:, pl.ds(2560 + pair * 128, 128)] = jnp.where(low, pltpu.roll(keys, 64, 1), values)

    @pl.loop(0, QKV // 128)
    def _(step):
        entries = m_qkv[:, lanes_of(step)]
        weight_sums[0, :, pl.ds(0, 128)] += jnp.sum((entries * entries).reshape(8, 8, 128), axis=0)

    statistics(0, lambda step: g_qkv[:, lanes_of(step)])
    for slot in range(16):
        strip = pl.ds(slot * 128, 128)
        flat_packed[pl.ds(first + slot, 1)] = gain_part2[:, strip]
        flat_packed[pl.ds(first + 16 + slot, 1)] = gain_part[:, strip]
    flat_packed[pl.ds(first + 32, 1)] = gain_qk[...]

    move.arrive(*gate_ups)
    move.sent(*qkv_pieces)

    def read_gate_up(step):
        inside = lax.rem(step, 64)
        owner = lax.div(inside, 2)
        block = 2 * lax.rem(owner, 4) + lax.rem(lax.div(owner, 4), 2)
        begin = lax.div(step, 64) * 1024 + lax.div(owner, 8) * 256 + lax.rem(inside, 2) * 128
        strip = blocks[8 + block, :, wide(begin, 128)]
        flat_d[wide(lax.div(step, 16) * 64, 64), lanes_of(lax.rem(step, 16))] = strip
        return strip.astype(full)

    statistics(2, read_gate_up)
    for block in range(8):
        move.keep(flat_d.at[pl.ds(64 * block, 64)], gate_up_came.at[:, pl.ds(2048 * block, 2048)])

    copies = [move.send(packed.at[peer[0]], plane_came.at[me], peer) for peer in everyone]
    plane_came[me] = packed[me]
    move.arrive(*copies)
    result = plane_came[0]
    for slot in range(1, 8):
        result = result + plane_came[slot]
    plane_sum[...] = result
    copies = [move.send(plane_sum.at[peer[1]], line_came.at[z], peer) for peer in line]
    line_came[z] = plane_sum[z]
    move.arrive(*copies)
    line_sum[...] = line_came[0] + line_came[1] + line_came[2] + line_came[3]
    copies = [move.send(line_sum, line_all.at[z], peer) for peer in line]
    line_all[z] = line_sum[...]
    move.arrive(*copies)
    copies = [move.send(line_all, totals.at[me], peer) for peer in everyone]
    totals[me] = line_all[...]
    move.arrive(*copies)
    derive_updates(
        totals.reshape(512, 128), col_moments, gain_moments, gains,
        cols_new, col_factors, moments_new, gains_new, grad_gains, spreads,
    )
    move.finish()


def split_local(
    tokens, doc_starts, grad_out, qkv_master, out_master, gate_up_master, down_master, gains,
    qkv_rows, out_rows, gate_up_rows, down_rows, col_moments, gain_moments,
):
    half, full = jnp.bfloat16, jnp.float32
    gain_query, gain_key = gains[2 * D : 2 * D + HEAD_DIM], gains[2 * D + HEAD_DIM :]
    gain_heads = jnp.stack(
        [jnp.concatenate([gain_query, gain_query]), jnp.concatenate([gain_key, gain_key])]
    )
    lane = np.arange(128)
    rates = ROPE_BASE ** (-(lane % 32) * 2.0 / HEAD_DIM)
    rates = jnp.asarray(np.stack([rates, np.where(lane % 64 < 32, -1.0, 1.0)]), full)

    def near(*shape, kind=half):
        return pltpu.VMEM(shape, kind)

    masters = (qkv_master, out_master, gate_up_master, down_master)
    stats_shape = (8, 4, 16, 128)
    (
        output, grad_tokens, grad_qkv, gate_up_came, out_came, down_came, rows_new, row_factors,
        cols_new, col_factors, moments_new, gains_new, grad_gains, spreads, *_,
    ) = exchange(
        layer_kernel, 0,
        [
            (tokens, True), (doc_starts, None), (rates, True), (jnp.asarray(place_tables(512)), True),
            (gains[None, :D], True),
            (gains[None, D : 2 * D], True), (gain_heads, True), (gains.reshape(-1, 128), True),
            (grad_out, True), (qkv_master, True), (out_master, False), (down_master, False),
            (gate_up_master, False),
            (jnp.concatenate([qkv_rows, out_rows, gate_up_rows, down_rows])[:, None], True),
            (col_moments.reshape(-1, 128), True), (gain_moments.reshape(-1, 128), True),
        ],
        [
            ((2, 64, D), half, True), ((2, 64, D), half, True), ((64, QKV), full, True),
            ((64, 2 * FF), half, False), ((4, 64, D), half, False), ((4, 256, D), half, False),
            ((448, 1), full, True), ((448, 1), full, True),
            ((COL_ROWS, 128), full, True), ((1, COLS), full, True),
            ((GAIN_ROWS, 128), full, True), ((GAIN_ROWS, 128), full, True),
            ((GAIN_ROWS, 128), full, True), ((1, 128), full, True),
            ((2, 2, 512, 1024), half, False), ((2, 512, 1024), half, False),
            ((8, 2, 64, D), half, False),
        ],
        [
            near(8, 2, 64, 384, kind=full), near(2, 2, 512, 128), near(2, 4, 512, 128),
            near(8, 2, 64, 256, kind=full), near(2, 8, 1, 128, kind=full),
            near(8, 64, 384), near(2, 64, D), near(8, 2, 64, D), near(8, 4, 64, 384), near(4, 64, D),
            near(8, 2, 64, D), near(4, 2, 64, D), near(4, 2, 64, D), near(2, 64, D, kind=full),
            near(4, 2, 2, 64, D), near(4, 2, 2, 64, D), near(4, 2, 4, 64, 2048), near(4, 256, D),
            near(4, 256, 1024), near(4, 256, 2048),
            near(2, 512, 128, kind=full), near(4, 512, 128, kind=full), near(4, 8, 64, 384),
            near(2, 64, D, kind=full), near(1, D, kind=full), near(1, D, kind=full),
            near(1, 128, kind=full), near(4, 8, D, kind=full), near(8, 64, 384),
            near(*stats_shape, kind=full), near(*stats_shape, kind=full),
            near(*stats_shape[1:], kind=full), near(*stats_shape[1:], kind=full),
            near(*stats_shape[2:], kind=full), near(*stats_shape[1:], kind=full),
            near(*stats_shape, kind=full),
            pltpu.SemaphoreType.REGULAR, pltpu.SemaphoreType.REGULAR,
        ],
        (176, 56), 170 << 20, 48 << 30,
    )
    grads = (
        grad_qkv, jnp.sum(out_came.astype(full), axis=0), gate_up_came.astype(full),
        jnp.sum(down_came.astype(full), axis=0),
    )
    new_masters = []
    for slot, (count, width, row_at, col_at) in enumerate(MATRICES):
        row_factor = row_factors[row_at : row_at + count]
        col_factor = col_factors[:, col_at * 128 : col_at * 128 + width]
        new_masters.append(masters[slot] - grads[slot] * row_factor * col_factor)
    return (
        output,
        grad_tokens,
        *grads,
        grad_gains.reshape(-1),
        *[rows_new[row_at : row_at + count, 0] for count, _, row_at, _ in MATRICES],
        cols_new.reshape(-1),
        moments_new.reshape(-1),
        *new_masters,
        *[master.astype(half) for master in new_masters],
        gains_new.reshape(-1),
        spreads[0, :8],
    )


def optimizer_step(
    grads, gain_local, masters, gains, row_states, col_moments, gain_moments, total_fn
):
    beta = 1.0 - STEP ** (-0.8)
    col_widths = (QKV, D, 2 * FF, D)
    row_totals = (D, HEADS * HEAD_DIM, D, FF)
    squares = [gradient * gradient + SQUARE_EPSILON for gradient in grads]
    rows_new = [
        beta * row_state + (1.0 - beta) * jnp.mean(square, axis=1)
        for row_state, square in zip(row_states, squares)
    ]
    col_local = [jnp.sum(square, axis=0) for square in squares]
    weighted_local = [
        jnp.sum(gradient * gradient / row_new[:, None], axis=0)
        for gradient, row_new in zip(grads, rows_new)
    ]
    stats_local = jnp.stack(
        [jnp.sum(row_new) for row_new in rows_new]
        + [jnp.sum(master * master) for master in masters]
    )
    totals = total_fn(jnp.concatenate(col_local + weighted_local + [stats_local, gain_local]))
    cols = sum(col_widths)
    col_sums, weighted = totals[:cols], totals[cols : 2 * cols]
    stats, grad_gains = totals[2 * cols : 2 * cols + 8], totals[2 * cols + 8 :]
    col_divisor = jnp.concatenate(
        [
            jnp.full((col_width,), float(row_total), jnp.float32)
            for col_width, row_total in zip(col_widths, row_totals)
        ]
    )
    cols_new = beta * col_moments + (1.0 - beta) * col_sums / col_divisor
    new_masters = []
    spreads = []
    begin_at = 0
    for slot in range(4):
        col_part = cols_new[begin_at : begin_at + col_widths[slot]]
        weighted_part = weighted[begin_at : begin_at + col_widths[slot]]
        begin_at = begin_at + col_widths[slot]
        mean_rows = stats[slot] / row_totals[slot]
        unit = (
            grads[slot]
            * lax.rsqrt(rows_new[slot] / mean_rows)[:, None]
            * lax.rsqrt(col_part)[None, :]
        )
        entries_all = float(row_totals[slot] * col_widths[slot])
        spread = jnp.sqrt(mean_rows * jnp.sum(weighted_part / col_part) / entries_all)
        scale = STEP_RATE * jnp.maximum(SCALE_EPSILON, jnp.sqrt(stats[4 + slot] / entries_all))
        new_masters.append(masters[slot] - scale * unit / jnp.maximum(1.0, spread / CLIP_LEVEL))
        spreads.append(spread)
    bounds = (0, D, 2 * D, 2 * D + HEAD_DIM, 2 * D + 2 * HEAD_DIM)
    moment_parts, gain_parts = ([], [])
    for segment in range(4):
        gradient = grad_gains[bounds[segment] : bounds[segment + 1]]
        gain_old = gains[bounds[segment] : bounds[segment + 1]]
        moment_new = beta * gain_moments[bounds[segment] : bounds[segment + 1]] + (1.0 - beta) * (
            gradient * gradient + SQUARE_EPSILON
        )
        unit = gradient * lax.rsqrt(moment_new)
        spread = jnp.sqrt(jnp.mean(unit * unit))
        scale = STEP_RATE * jnp.maximum(SCALE_EPSILON, jnp.sqrt(jnp.mean(gain_old * gain_old)))
        moment_parts.append(moment_new)
        gain_parts.append(gain_old - scale * unit / jnp.maximum(1.0, spread / CLIP_LEVEL))
        spreads.append(spread)
    return (
        grad_gains,
        *rows_new,
        cols_new,
        jnp.concatenate(moment_parts),
        *new_masters,
        *[master.astype(jnp.bfloat16) for master in new_masters],
        jnp.concatenate(gain_parts),
        jnp.stack(spreads),
    )


def solution(mesh):
    split = mesh.shape["seq"] == 8 and mesh.shape["rows"] == 4
    return jax.shard_map(
        split_local if split else gathered_local,
        mesh=mesh,
        in_specs=(
            P("rows", "seq", None),
            P("rows", None),
            P("rows", "seq", None),
            P(("seq", "rows"), None),
            P(("seq", "rows"), None),
            P(("seq", "rows"), None),
            P(("seq", "rows"), None),
            P(),
            P(("seq", "rows")),
            P(("seq", "rows")),
            P(("seq", "rows")),
            P(("seq", "rows")),
            P(),
            P(),
        ),
        out_specs=(
            P("rows", "seq", None),
            P("rows", "seq", None),
            P(("seq", "rows"), None),
            P(("seq", "rows"), None),
            P(("seq", "rows"), None),
            P(("seq", "rows"), None),
            P(),
            P(("seq", "rows")),
            P(("seq", "rows")),
            P(("seq", "rows")),
            P(("seq", "rows")),
            P(),
            P(),
            P(("seq", "rows"), None),
            P(("seq", "rows"), None),
            P(("seq", "rows"), None),
            P(("seq", "rows"), None),
            P(("seq", "rows"), None),
            P(("seq", "rows"), None),
            P(("seq", "rows"), None),
            P(("seq", "rows"), None),
            P(),
            P(),
        ),
        check_vma=False,
    )
```
